32 devices in a mesh: dp: 8 (over y, x, core), ctx: 4 (over z).
Axes of the slice: x: 2, y: 2, z: 4, core: 2. Of those that a mesh axis runs over, the one named last changes fastest.
Arguments:
- tokens: bfloat16 [8192, 1536], P(('dp', 'ctx')), may hold values from -6 to 6
- norm_attn: bfloat16 [1536], P(('dp', 'ctx')), may hold values from 0.5 to 1.5
- w_query: bfloat16 [1536, 1536], P(('dp', 'ctx')), may hold values from -0.15625 to 0.15625
- w_key: bfloat16 [1536, 256], P(('dp', 'ctx')), may hold values from -0.15625 to 0.15625
- w_value: bfloat16 [1536, 256], P(('dp', 'ctx')), may hold values from -0.15625 to 0.15625
- w_out: bfloat16 [1536, 1536], P(('dp', 'ctx')), may hold values from -0.625 to 0.625
- norm_moe: bfloat16 [1536], P(('dp', 'ctx')), may hold values from 0.5 to 1.5
- w_gate: bfloat16 [8, 1536, 768], P('dp'), may hold values from -0.15625 to 0.15625
- w_up: bfloat16 [8, 1536, 768], P('dp'), may hold values from -0.15625 to 0.15625
- w_down: bfloat16 [8, 768, 1536], P('dp'), may hold values from -0.21875 to 0.21875
- routes: int32 [8192, 4], P(('dp', 'ctx')), may hold values from 0 to 7, all different within a row; in each aligned block of 256 rows (0 to 255, 256 to 511, ...) at most 192 rows name the same one
- gate_values: float32 [8192, 4], P(('dp', 'ctx')), may hold values from 0.25 to 1
- lengths: int32 [8, 3], P('dp'), may hold values from 1 to 896, 1024 in all within a row
- cotangent: bfloat16 [8192, 1536], P(('dp', 'ctx')), may hold values from -6 to 6
Outputs:
- layer_out: bfloat16 [8192, 1536], P(('dp', 'ctx'))
- d_tokens: float32 [8192, 1536], P(('dp', 'ctx'))
- d_norm_attn: float32 [1536], P(('dp', 'ctx'))
- d_w_query: float32 [1536, 1536], P(('dp', 'ctx'))
- d_w_key: float32 [1536, 256], P(('dp', 'ctx'))
- d_w_value: float32 [1536, 256], P(('dp', 'ctx'))
- d_w_out: float32 [1536, 1536], P(('dp', 'ctx'))
- d_norm_moe: float32 [1536], P(('dp', 'ctx'))
- d_w_gate: float32 [8, 1536, 768], P('dp')
- d_w_up: float32 [8, 1536, 768], P('dp')
- d_w_down: float32 [8, 768, 1536], P('dp')
The draws below stay inside these ranges and needn't reach their ends.
Inputs may be any that keep to these rules, and one draw needn't show every extreme that they name: `routes`: each row names 4 different experts; among the rows of one device no expert is named by more than 192 rows, a bound that some block reaches. `lengths`: each row sums to 1024; its largest entry is exactly 896.
All inputs are finite; a program needn't handle non-finite values.
Results may differ from the reference program's by a relative error of at most 0.015.
Values may be sent and summed in bfloat16 or wider, within the bound.
A program may use at most 192 MiB of HBM per device.

```python
import math
import jax
import jax.numpy as jnp
import numpy as np
from jax import lax

D = 1536
HEADS = 12
KVH = 2
HD = 128
FF = 768
TOP = 4
TOK_DEV = 256
NSEQ = 3
EXPERTS = 8
GROUP = 1024
MOST = 896
CAP = 192
TOKENS = 8192
N_DP = 8
N_CTX = 4


def steps_of(key, dims, shards, low, top_value):
    loudness = 1.0
    for position, shards_of in shards:
        steps = jax.random.uniform(jax.random.fold_in(jax.random.fold_in(key, 6), position), (shards_of,), jnp.float32, low / len(shards), top_value / len(shards))
        loudness = loudness * jnp.repeat(jnp.exp(steps), dims[position] // shards_of).reshape((-1,) + (1,) * (len(dims) - 1 - position))
    return loudness


def split_up(count, total, limit, lean):
    weights = [(1 << 20) // math.isqrt(standing ** lean) + 1 for standing in range(2, count + 1)]
    rest, given = total - limit - (count - 1), [1] * (count - 1)
    while rest > 0:
        movable = [i for i in range(count - 1) if given[i] < limit]
        whole, budget = sum([weights[i] for i in movable]), rest
        for i in movable:
            more = min(limit - given[i], max(1, budget * weights[i] // whole), rest)
            given[i] = given[i] + more
            rest = rest - more
    return np.array([limit] + given)


def ragged_sizes(key, count, total, bound, slope):
    if count == 2:
        one = jax.random.randint(key, (), max(1, total - bound), min(bound, total - 1) + 1)
        return jnp.stack([one, total - one])
    sizes = jnp.asarray(split_up(count, total, bound, slope), jnp.int32)
    pairs = (count - 1) // 2
    source_of, sink = sizes[1:1 + 2 * pairs:2], sizes[2:2 + 2 * pairs:2]
    slack = jnp.minimum(source_of - 1, bound - sink)
    shifted = jax.random.randint(jax.random.fold_in(key, 1), (pairs,), 0, 1 << 20) % (slack + 1)
    sizes = sizes.at[1:1 + 2 * pairs:2].set(source_of - shifted).at[2:2 + 2 * pairs:2].set(sink + shifted)
    return sizes[jax.random.permutation(jax.random.fold_in(key, 2), count)]


def assign_block(own_key, own, number, rows, count, top, limit, slope):
    sequence = jax.random.permutation(own_key, count)
    heavy_load, common = portions_of(count, rows * top, limit, slope, True), portions_of(count, rows * top, limit, slope, False)
    places = jnp.arange(count)

    def named(sizes, turn):
        used = int((sizes > 0).sum())
        fixed = max(1, used // 4)
        shifted = fixed + (places - fixed + turn * (used - fixed)) % max(1, count - fixed)
        return jnp.zeros((count,), jnp.int32).at[sequence[jnp.where(places < fixed, places, shifted)]].set(jnp.asarray(sizes, jnp.int32))

    sizes = jnp.where(number % 4 == 0, named(heavy_load, number // 4), named(common, number - number // 4 - 1))
    mixed = jax.random.permutation(jax.random.fold_in(own, 3), count)
    donor, sink = mixed[0:count // 2 * 2:2], mixed[1:count // 2 * 2:2]
    margin = jnp.minimum(sizes[donor] - 1, limit - sizes[sink]) // 2
    margin = jnp.where((donor == sequence[0]) | (sink == sequence[0]) | (sizes[sink] == 0), 0, jnp.maximum(margin, 0))
    shifted = jax.random.randint(jax.random.fold_in(own, 4), (count // 2,), 0, 1 << 20) % (margin + 1)
    sizes = sizes.at[donor].add(-shifted).at[sink].add(shifted)
    labels = jnp.searchsorted(jnp.cumsum(sizes), jnp.arange(rows * top), side="right").astype(jnp.int32)
    table = labels.reshape(top, rows).T
    table = table[jax.random.permutation(jax.random.fold_in(own, 1), rows)]
    turn = jax.random.randint(jax.random.fold_in(own, 2), (rows, 1), 0, top)
    return jnp.take_along_axis(table, (jnp.arange(top)[None, :] + turn) % top, axis=1)


def portions_of(amount, total, reach, lean, full):
    weights = [(1 << 20) // math.isqrt(grade ** lean) + 1 for grade in range(1, amount + 1)]
    largest = reach if full else min(reach, max(-(-total // amount), total * weights[0] // sum(weights)))
    least = 1 if total - largest >= amount - 1 else 0
    counts, surplus = [largest] + [least] * (amount - 1), total - largest - least * (amount - 1)
    while surplus > 0:
        candidates = [i for i in range(1, amount) if counts[i] < largest] or [i for i in range(1, amount) if counts[i] < reach]
        whole, left = sum([weights[i] for i in candidates]), surplus
        for i in candidates:
            extra = min(reach - counts[i], max(1, left * weights[i] // whole), surplus)
            counts[i] = counts[i] + extra
            surplus = surplus - extra
    return np.array(counts)


def scatter_about(own_key, dims, spread, reach, pieces=(), held_as=jnp.bfloat16):
    factor_of = steps_of(own_key, dims, pieces, -0.22, 0.18) if pieces else 1.0
    values = jax.random.normal(own_key, dims, jnp.float32) * spread * factor_of
    return jnp.minimum(jnp.maximum(values, -reach), reach).astype(held_as)


def setup_inputs(seed: int = 0) -> dict:
    arg_keys = jax.random.split(jax.random.key(seed), 15)
    tokens = scatter_about(arg_keys[0], (TOKENS, D), 1.0, 6.0, ((0, 32),))
    norm_attn = jnp.clip(1.0 + 0.1 * jax.random.normal(arg_keys[1], (D,), jnp.float32), 0.5, 1.5).astype(jnp.bfloat16)
    w_query = scatter_about(arg_keys[2], (D, HEADS * HD), D ** -0.5, 0.15625, ((0, 32),))
    w_key = scatter_about(arg_keys[3], (D, KVH * HD), D ** -0.5, 0.15625, ((0, 32),))
    w_value = scatter_about(arg_keys[4], (D, KVH * HD), D ** -0.5, 0.15625, ((0, 32),))
    w_out = scatter_about(arg_keys[5], (HEADS * HD, D), (HEADS * HD // 16) ** -0.5, 0.625, ((0, 32),))
    norm_moe = jnp.clip(1.0 + 0.1 * jax.random.normal(arg_keys[6], (D,), jnp.float32), 0.5, 1.5).astype(jnp.bfloat16)
    w_gate = scatter_about(arg_keys[7], (EXPERTS, D, FF), D ** -0.5, 0.15625, ((0, 8),))
    w_up = scatter_about(arg_keys[8], (EXPERTS, D, FF), D ** -0.5, 0.15625, ((0, 8),))
    w_down = scatter_about(arg_keys[9], (EXPERTS, FF, D), FF ** -0.5, 0.21875, ((0, 8),))
    routes_keys = jax.random.split(jax.random.fold_in(arg_keys[10], 1), TOKENS // TOK_DEV)
    routes_turns = jax.random.permutation(jax.random.fold_in(arg_keys[10], 3), TOKENS // TOK_DEV)
    routes = jax.vmap(lambda own, number: assign_block(jax.random.fold_in(arg_keys[10], 2), own, number, TOK_DEV, EXPERTS, TOP, CAP, 1))(routes_keys, routes_turns).reshape((TOKENS, TOP))
    gate_values = jnp.clip(jnp.exp(math.log(1.0) - 1.3862944 * jax.random.uniform(arg_keys[11], (TOKENS, TOP), jnp.float32) ** steps_of(arg_keys[11], (TOKENS, TOP), ((0, 32),), -0.2, 0.2)), 0.25, 1.0)
    lengths = jax.vmap(lambda own: ragged_sizes(own, NSEQ, GROUP, MOST, 1))(jax.random.split(arg_keys[12], N_DP)).reshape((N_DP, NSEQ)).astype(jnp.int32)
    cotangent = scatter_about(arg_keys[13], (TOKENS, D), 1.0, 6.0, ((0, 32),))
    return dict(tokens=tokens, norm_attn=norm_attn, w_query=w_query, w_key=w_key, w_value=w_value, w_out=w_out, norm_moe=norm_moe, w_gate=w_gate, w_up=w_up, w_down=w_down, routes=routes, gate_values=gate_values, lengths=lengths, cotangent=cotangent)


@jax.custom_vjp
def low(v):
    return lax.optimization_barrier(v.astype(jnp.bfloat16)).astype(jnp.float32)

@jax.custom_vjp
def low_back(v):
    return v

def low_keep(v):
    return (low(v), None)

def low_pass(kept, grad):
    return (grad,)

def back_keep(v):
    return (v, None)

def back_low(kept, grad):
    return (low(grad),)
low.defvjp(low_keep, low_pass)
low_back.defvjp(back_keep, back_low)
epsilon = 1e-06
rope_base = 1000000.0
masked_score = -1e+30

def exact_dot(left, right):
    return jnp.dot(left, right, precision=lax.Precision.HIGHEST, preferred_element_type=jnp.float32)

def rms_norm(values, gain):
    return values * lax.rsqrt(lax.optimization_barrier(jnp.mean(values * values, axis=-1, keepdims=True)) + epsilon) * gain

def rotate(values, within, direction):
    half_size = values.shape[-1] // 2
    frequency = rope_base ** (-jnp.arange(half_size, dtype=jnp.float32) / half_size)
    angles = direction * within.astype(jnp.float32)[:, None] * frequency[None, :]
    cosine = jnp.cos(angles)[:, None, :]
    sine = jnp.sin(angles)[:, None, :]
    first_half = values[..., :half_size]
    second = values[..., half_size:]
    return jnp.concatenate([first_half * cosine - second * sine, second * cosine + first_half * sine], axis=-1)

def seq_tables(length_row, places):
    seq_ends = jnp.cumsum(length_row)
    passed = places[:, None] >= seq_ends[None, :]
    segment = lax.optimization_barrier(jnp.sum(passed.astype(jnp.int32), axis=1))
    within = places - lax.optimization_barrier(jnp.sum(jnp.where(passed, length_row[None, :], 0), axis=1))
    return (segment, within)

def group_attention(packed):
    query_g, key_g, value_g, segment_g = packed
    count = query_g.shape[0]
    places = jnp.arange(count, dtype=jnp.int32)
    allowed = (segment_g[:, None] == segment_g[None, :]) & (places[None, :] <= places[:, None])
    query_sets = query_g.reshape(count, KVH, HEADS // KVH, HD)
    raw = jnp.einsum('qgjd,kgd->gjqk', query_sets, key_g, precision=lax.Precision.HIGHEST, preferred_element_type=jnp.float32)
    scores = jnp.where(allowed[None, None], low_back(raw) * HD ** (-0.5), masked_score)
    row_top = lax.optimization_barrier(jnp.max(scores, axis=-1, keepdims=True))
    expo = jnp.exp(scores - row_top)
    probs = expo / lax.optimization_barrier(jnp.sum(expo, axis=-1, keepdims=True))
    mixed = jnp.einsum('gjqk,kgd->qgjd', low(probs), value_g, precision=lax.Precision.HIGHEST, preferred_element_type=jnp.float32)
    return mixed.reshape(count, HEADS * HD)

def device_slots(route_rows):
    flat_ids = route_rows.reshape(-1)
    onehot = (flat_ids[:, None] == jnp.arange(EXPERTS, dtype=jnp.int32)[None, :]).astype(jnp.int32)
    earlier = lax.optimization_barrier(jnp.sum((jnp.cumsum(onehot, axis=0) - onehot) * onehot, axis=1))
    return (flat_ids * CAP + earlier).astype(jnp.int32)

def expert_block(packed, w_gate, w_up, w_down):
    routed_rows, slot_index, gate_rows = packed
    count = routed_rows.shape[0]
    assign_count = count * TOP
    owner = jnp.full((EXPERTS * CAP,), assign_count, jnp.int32).at[slot_index].set(jnp.arange(assign_count, dtype=jnp.int32))
    padded = jnp.concatenate([routed_rows, jnp.zeros((1, D), routed_rows.dtype)], axis=0)
    sent = low_back(padded[owner // TOP]).reshape(EXPERTS, CAP, D)
    gate_act = low_back(jnp.einsum('ecd,edf->ecf', sent, w_gate, precision=lax.Precision.HIGHEST, preferred_element_type=jnp.float32))
    up_act = low_back(jnp.einsum('ecd,edf->ecf', sent, w_up, precision=lax.Precision.HIGHEST, preferred_element_type=jnp.float32))
    hidden = low(jax.nn.silu(gate_act) * up_act)
    produced = jnp.einsum('ecf,efd->ecd', hidden, w_down, precision=lax.Precision.HIGHEST, preferred_element_type=jnp.float32)
    produced = low(low_back(produced)).reshape(EXPERTS * CAP, D)
    picked = produced[slot_index].reshape(count, TOP, D)
    return lax.optimization_barrier(jnp.sum(picked * gate_rows[:, :, None], axis=1))

def reference(tokens, norm_attn, w_query, w_key, w_value, w_out, norm_moe, w_gate, w_up, w_down, routes, gate_values, lengths, cotangent):
    places = jnp.arange(GROUP, dtype=jnp.int32)
    segments, withins = jax.vmap(lambda length_row: seq_tables(length_row, places))(lengths)
    within_flat = withins.reshape(TOKENS)
    slots = jax.vmap(device_slots)(routes.reshape(N_DP * N_CTX, TOK_DEV, TOP))
    gate_blocks = gate_values.reshape(N_DP * N_CTX, TOK_DEV, TOP)

    def forward(inputs, gain_attn, wq, wk, wv, wo, gain_moe, wg, wu, wd):
        normed = low(rms_norm(inputs, gain_attn))
        query = low(rotate(low_back(exact_dot(normed, wq)).reshape(TOKENS, HEADS, HD), within_flat, 1.0))
        key = low(rotate(low_back(exact_dot(normed, wk)).reshape(TOKENS, KVH, HD), within_flat, 1.0))
        value = low(low_back(exact_dot(normed, wv))).reshape(TOKENS, KVH, HD)
        mixed = lax.map(jax.checkpoint(group_attention), (query.reshape(N_DP, GROUP, HEADS, HD), key.reshape(N_DP, GROUP, KVH, HD), value.reshape(N_DP, GROUP, KVH, HD), segments))
        mixed = low(low_back(mixed.reshape(TOKENS, HEADS * HD)))
        middle = inputs + low_back(exact_dot(mixed, wo))
        routed = low(rms_norm(middle, gain_moe))
        moe_out = lax.map(jax.checkpoint(lambda packed: expert_block(packed, wg, wu, wd)), (routed.reshape(N_DP * N_CTX, TOK_DEV, D), slots, gate_blocks))
        return middle + moe_out.reshape(TOKENS, D)
    primals = (tokens.astype(jnp.float32), norm_attn.astype(jnp.float32), w_query.astype(jnp.float32), w_key.astype(jnp.float32), w_value.astype(jnp.float32), w_out.astype(jnp.float32), norm_moe.astype(jnp.float32), w_gate.astype(jnp.float32), w_up.astype(jnp.float32), w_down.astype(jnp.float32))
    result, pullback = jax.vjp(forward, *primals)
    grads = pullback(cotangent.astype(jnp.float32))
    return (result.astype(jnp.bfloat16), grads[0], grads[1], grads[2], grads[3], grads[4], grads[5], grads[6], grads[7], grads[8], grads[9])
```

```python
import functools

import jax
import jax.numpy as jnp
from jax import lax
from jax.experimental import pallas as pl
from jax.experimental.pallas import tpu as pltpu
from jax.sharding import PartitionSpec as P

D = 1536
HEADS = 12
KVH = 2
HD = 128
TOP = 4
EXP_DEV = 1


epsilon = 1e-06
rope_base = 1000000.0
masked_score = -1e30


def rms_norm(values, gain):
    return values * lax.rsqrt(jnp.mean(values * values, axis=-1, keepdims=True) + epsilon) * gain


def rotate(values, within, direction):
    half_size = values.shape[-1] // 2
    frequency = rope_base ** (-jnp.arange(half_size, dtype=jnp.float32) / half_size)
    angles = direction * within.astype(jnp.float32)[:, None] * frequency[None, :]
    cosine = jnp.cos(angles)[:, None, :]
    sine = jnp.sin(angles)[:, None, :]
    first_half = values[..., :half_size]
    second = values[..., half_size:]
    return jnp.concatenate(
        [first_half * cosine - second * sine, second * cosine + first_half * sine], axis=-1
    )


def seq_tables(length_row, places):
    seq_ends = jnp.cumsum(length_row)
    passed = places[:, None] >= seq_ends[None, :]
    segment = jnp.sum(passed.astype(jnp.int32), axis=1)
    within = places - jnp.sum(jnp.where(passed, length_row[None, :], 0), axis=1)
    return (segment, within)


def collect_weights(gain_attn, w_query, w_key, w_value, w_out, gain_moe):
    return (
        lax.all_gather(gain_attn, ("dp", "ctx"), axis=0, tiled=True),
        lax.all_gather(w_query, ("dp", "ctx"), axis=0, tiled=True),
        lax.all_gather(w_key, ("dp", "ctx"), axis=0, tiled=True),
        lax.all_gather(w_value, ("dp", "ctx"), axis=0, tiled=True),
        lax.all_gather(w_out, ("dp", "ctx"), axis=0, tiled=True),
        lax.all_gather(gain_moe, ("dp", "ctx"), axis=0, tiled=True),
    )


def spread_grads(grad_gain_attn, grad_query, grad_key, grad_value, grad_outp, grad_gain_moe):
    return (
        lax.psum_scatter(grad_gain_attn, ("dp", "ctx"), scatter_dimension=0, tiled=True),
        lax.psum_scatter(grad_query, ("dp", "ctx"), scatter_dimension=0, tiled=True),
        lax.psum_scatter(grad_key, ("dp", "ctx"), scatter_dimension=0, tiled=True),
        lax.psum_scatter(grad_value, ("dp", "ctx"), scatter_dimension=0, tiled=True),
        lax.psum_scatter(grad_outp, ("dp", "ctx"), scatter_dimension=0, tiled=True),
        lax.psum_scatter(grad_gain_moe, ("dp", "ctx"), scatter_dimension=0, tiled=True),
    )


def on_device(
    tokens,
    norm_attn,
    w_query,
    w_key,
    w_value,
    w_out,
    norm_moe,
    w_gate,
    w_up,
    w_down,
    routes,
    gate_values,
    lengths,
    cotangent,
):
    tok_rows = tokens.shape[0]
    ctx_size = lax.axis_size("ctx")
    dp_size = lax.axis_size("dp")
    ctx_place = lax.axis_index("ctx")
    group_rows = tok_rows * ctx_size
    group_places = jnp.arange(group_rows, dtype=jnp.int32)
    seg_all, within_all = seq_tables(lengths[0], group_places)
    offset = ctx_place * tok_rows
    own_places = offset + jnp.arange(tok_rows, dtype=jnp.int32)
    seg_own = lax.dynamic_slice_in_dim(seg_all, offset, tok_rows)
    within_own = lax.dynamic_slice_in_dim(within_all, offset, tok_rows)
    allowed = (seg_own[:, None] == seg_all[None, :]) & (
        group_places[None, :] <= own_places[:, None]
    )
    gain_attn, full_q, full_k, full_v, full_o, gain_moe = collect_weights(
        norm_attn, w_query, w_key, w_value, w_out, norm_moe
    )
    gain_attn_f = gain_attn.astype(jnp.float32)
    gain_moe_f = gain_moe.astype(jnp.float32)
    inputs = tokens.astype(jnp.float32)
    normed_low = rms_norm(inputs, gain_attn_f).astype(jnp.bfloat16)
    query_pre = jnp.dot(normed_low, full_q, preferred_element_type=jnp.float32)
    key_pre = jnp.dot(normed_low, full_k, preferred_element_type=jnp.float32)
    value_pre = jnp.dot(normed_low, full_v, preferred_element_type=jnp.float32)
    query = rotate(query_pre.reshape(tok_rows, HEADS, HD), within_own, 1.0).astype(jnp.bfloat16)
    key_low = rotate(key_pre.reshape(tok_rows, KVH, HD), within_own, 1.0).astype(jnp.bfloat16)
    key_low = key_low.reshape(tok_rows, KVH * HD)
    value_low = value_pre.astype(jnp.bfloat16)
    all_keys, all_values = (
        lax.all_gather(key_low, "ctx", axis=0, tiled=True),
        lax.all_gather(value_low, "ctx", axis=0, tiled=True),
    )
    per_group = HEADS // KVH
    score_scale = HD ** (-0.5)
    query_groups = query.reshape(tok_rows, KVH, per_group, HD)

    def softmax_weights(group_number):
        keys_part = all_keys[:, group_number * HD : (group_number + 1) * HD]
        raw = jnp.einsum(
            "qjd,kd->jqk",
            query_groups[:, group_number],
            keys_part,
            preferred_element_type=jnp.float32,
        )
        scores = jnp.where(allowed[None], raw * score_scale, masked_score)
        row_top = jnp.max(scores, axis=-1, keepdims=True)
        expo = jnp.exp(scores - row_top)
        return expo / jnp.sum(expo, axis=-1, keepdims=True)

    mixed_parts = []
    for group_number in range(KVH):
        probs = softmax_weights(group_number)
        values_part = all_values[:, group_number * HD : (group_number + 1) * HD]
        mixed_group = jnp.einsum(
            "jqk,kd->qjd",
            probs.astype(jnp.bfloat16),
            values_part,
            preferred_element_type=jnp.float32,
        )
        mixed_parts.append(mixed_group.reshape(tok_rows, per_group * HD))
    mixed_low = jnp.concatenate(mixed_parts, axis=1).astype(jnp.bfloat16)
    middle = inputs + jnp.dot(mixed_low, full_o, preferred_element_type=jnp.float32)
    routed_low = rms_norm(middle, gain_moe_f).astype(jnp.bfloat16)
    experts_total = EXP_DEV * dp_size
    capacity = 3 * TOP * tok_rows // (2 * experts_total)
    assign_count = tok_rows * TOP
    flat_ids = routes.reshape(assign_count)
    onehot = (flat_ids[:, None] == jnp.arange(experts_total, dtype=jnp.int32)[None, :]).astype(
        jnp.int32
    )
    earlier = jnp.sum((jnp.cumsum(onehot, axis=0) - onehot) * onehot, axis=1)
    slot_index = flat_ids * capacity + earlier
    owner = (
        jnp.full((experts_total * capacity,), assign_count, jnp.int32)
        .at[slot_index]
        .set(jnp.arange(assign_count, dtype=jnp.int32))
    )
    padded = jnp.concatenate([routed_low, jnp.zeros((1, D), jnp.bfloat16)], axis=0)
    outgoing = padded[owner // TOP].reshape(experts_total, capacity, D)
    arrived = lax.all_to_all(outgoing, "dp", split_axis=0, concat_axis=0, tiled=True)
    arrived_sets = arrived.reshape(dp_size, EXP_DEV, capacity, D)
    gate_act = jnp.einsum(
        "secd,edf->secf", arrived_sets, w_gate, preferred_element_type=jnp.float32
    )
    up_act = jnp.einsum("secd,edf->secf", arrived_sets, w_up, preferred_element_type=jnp.float32)
    hidden_low = (jax.nn.silu(gate_act) * up_act).astype(jnp.bfloat16)
    produced = jnp.einsum("secf,efd->secd", hidden_low, w_down, preferred_element_type=jnp.float32)
    produced = produced.astype(jnp.bfloat16).reshape(experts_total, capacity, D)
    returned = lax.all_to_all(produced, "dp", split_axis=0, concat_axis=0, tiled=True)
    picked = returned.reshape(experts_total * capacity, D)[slot_index].reshape(tok_rows, TOP, D)
    moe_out = jnp.sum(picked.astype(jnp.float32) * gate_values[:, :, None], axis=1)
    layer_out = (middle + moe_out).astype(jnp.bfloat16)
    grad_out = cotangent.astype(jnp.float32)
    grad_assign = (grad_out[:, None, :] * gate_values[:, :, None]).astype(jnp.bfloat16)
    grad_padded = jnp.concatenate(
        [grad_assign.reshape(assign_count, D), jnp.zeros((1, D), jnp.bfloat16)], axis=0
    )
    grad_slots = grad_padded[owner].reshape(experts_total, capacity, D)
    grad_arrived = lax.all_to_all(grad_slots, "dp", split_axis=0, concat_axis=0, tiled=True)
    grad_arrived = grad_arrived.reshape(dp_size, EXP_DEV, capacity, D)
    grad_hidden = jnp.einsum(
        "secd,efd->secf", grad_arrived, w_down, preferred_element_type=jnp.float32
    )
    grad_w_down = jnp.einsum(
        "secf,secd->efd", hidden_low, grad_arrived, preferred_element_type=jnp.float32
    )
    glu_value, glu_pull = jax.vjp(
        lambda gate_in, up_in: jax.nn.silu(gate_in) * up_in, gate_act, up_act
    )
    grad_gate, grad_up = glu_pull(grad_hidden)
    grad_gate_low = grad_gate.astype(jnp.bfloat16)
    grad_up_low = grad_up.astype(jnp.bfloat16)
    grad_w_gate = jnp.einsum(
        "secd,secf->edf", arrived_sets, grad_gate_low, preferred_element_type=jnp.float32
    )
    grad_w_up = jnp.einsum(
        "secd,secf->edf", arrived_sets, grad_up_low, preferred_element_type=jnp.float32
    )
    grad_sent = jnp.einsum(
        "secf,edf->secd", grad_gate_low, w_gate, preferred_element_type=jnp.float32
    ) + jnp.einsum("secf,edf->secd", grad_up_low, w_up, preferred_element_type=jnp.float32)
    grad_sent = grad_sent.astype(jnp.bfloat16).reshape(experts_total, capacity, D)
    grad_back = lax.all_to_all(grad_sent, "dp", split_axis=0, concat_axis=0, tiled=True)
    grad_picked = grad_back.reshape(experts_total * capacity, D)[slot_index].reshape(
        tok_rows, TOP, D
    )
    grad_routed = jnp.sum(grad_picked.astype(jnp.float32), axis=1)
    expert_sums = (
        lax.psum(grad_w_gate.astype(jnp.bfloat16), "ctx").astype(jnp.float32),
        lax.psum(grad_w_up.astype(jnp.bfloat16), "ctx").astype(jnp.float32),
        lax.psum(grad_w_down.astype(jnp.bfloat16), "ctx").astype(jnp.float32),
    )
    norm_value, moe_pull = jax.vjp(rms_norm, middle, gain_moe_f)
    grad_mid_norm, grad_gain_moe = moe_pull(grad_routed)
    grad_middle = grad_out + grad_mid_norm
    grad_attn_low = grad_middle.astype(jnp.bfloat16)
    grad_w_out = jnp.einsum(
        "th,td->hd", mixed_low, grad_attn_low, preferred_element_type=jnp.float32
    )
    grad_mixed_low = jnp.einsum(
        "td,hd->th", grad_attn_low, full_o, preferred_element_type=jnp.float32
    ).astype(jnp.bfloat16)
    grad_mixed_groups = grad_mixed_low.reshape(tok_rows, KVH, per_group, HD)
    grad_query_parts = []
    prob_parts = []
    score_parts = []
    for group_number in range(KVH):
        probs = softmax_weights(group_number)
        keys_part = all_keys[:, group_number * HD : (group_number + 1) * HD]
        values_part = all_values[:, group_number * HD : (group_number + 1) * HD]
        grad_probs = jnp.einsum(
            "qjd,kd->jqk",
            grad_mixed_groups[:, group_number],
            values_part,
            preferred_element_type=jnp.float32,
        )
        grad_scores = probs * (grad_probs - jnp.sum(probs * grad_probs, axis=-1, keepdims=True))
        grad_raw_low = (grad_scores * score_scale).astype(jnp.bfloat16)
        grad_query_parts.append(
            jnp.einsum("jqk,kd->qjd", grad_raw_low, keys_part, preferred_element_type=jnp.float32)
        )
        prob_parts.append(probs.astype(jnp.bfloat16))
        score_parts.append(grad_raw_low)
    grad_query_rot = jnp.stack(grad_query_parts, axis=1).reshape(tok_rows, HEADS, HD)
    key_pieces = []
    value_pieces = []
    for group_number in range(KVH):
        score_piece = score_parts[group_number]
        prob_piece = prob_parts[group_number]
        key_pieces.append(
            jnp.einsum(
                "jqk,qjd->kd",
                score_piece,
                query_groups[:, group_number],
                preferred_element_type=jnp.float32,
            )
        )
        value_pieces.append(
            jnp.einsum(
                "jqk,qjd->kd",
                prob_piece,
                grad_mixed_groups[:, group_number],
                preferred_element_type=jnp.float32,
            )
        )
    key_value_grads = lax.psum_scatter(
        jnp.concatenate(key_pieces + value_pieces, axis=1).astype(jnp.bfloat16),
        "ctx",
        scatter_dimension=0,
        tiled=True,
    ).astype(jnp.float32)
    grad_query_low = (
        rotate(grad_query_rot, within_own, -1.0).astype(jnp.bfloat16).reshape(tok_rows, HEADS * HD)
    )
    grad_key_rot = key_value_grads[:, : KVH * HD].reshape(tok_rows, KVH, HD)
    grad_key_low = (
        rotate(grad_key_rot, within_own, -1.0).astype(jnp.bfloat16).reshape(tok_rows, KVH * HD)
    )
    grad_value_low = key_value_grads[:, KVH * HD :].astype(jnp.bfloat16)
    grad_w_query = jnp.einsum(
        "td,th->dh", normed_low, grad_query_low, preferred_element_type=jnp.float32
    )
    grad_w_key = jnp.einsum(
        "td,th->dh", normed_low, grad_key_low, preferred_element_type=jnp.float32
    )
    grad_w_value = jnp.einsum(
        "td,th->dh", normed_low, grad_value_low, preferred_element_type=jnp.float32
    )
    grad_normed = (
        jnp.einsum("th,dh->td", grad_query_low, full_q, preferred_element_type=jnp.float32)
        + jnp.einsum("th,dh->td", grad_key_low, full_k, preferred_element_type=jnp.float32)
        + jnp.einsum("th,dh->td", grad_value_low, full_v, preferred_element_type=jnp.float32)
    )
    first_value, attn_pull = jax.vjp(rms_norm, inputs, gain_attn_f)
    grad_inputs, grad_gain_attn = attn_pull(grad_normed)
    grad_tokens = grad_middle + grad_inputs
    dense_sums = spread_grads(
        grad_gain_attn, grad_w_query, grad_w_key, grad_w_value, grad_w_out, grad_gain_moe
    )
    return (
        layer_out,
        grad_tokens,
        dense_sums[0],
        dense_sums[1],
        dense_sums[2],
        dense_sums[3],
        dense_sums[4],
        dense_sums[5],
        expert_sums[0],
        expert_sums[1],
        expert_sums[2],
    )


MESH = pl.DeviceIdType.MESH
LANES = 128
MIB = 2**20
ANY = pl.BlockSpec(memory_space=pl.ANY)
VMEM = pl.BlockSpec(memory_space=pltpu.VMEM)


def flip(index, bit):
    return index + bit - 2 * bit * ((index // bit) % 2)


def masked(index, mask):
    for bit in (1, 2, 4):
        if mask & bit:
            index = flip(index, bit)
    return index


class Wires:
    def __init__(self, send, recv):
        self.send, self.recv, self.used = send, recv, 0
        self.dp, self.z = lax.axis_index("dp"), lax.axis_index("ctx")

    def take(self, count):
        first = self.used
        self.used += count
        return first

    def copy(self, src, dst, number, dp=None, z=None):
        return pltpu.make_async_remote_copy(
            src_ref=src,
            dst_ref=dst,
            send_sem=self.send.at[number],
            recv_sem=self.recv.at[number],
            device_id=(self.dp if dp is None else dp, self.z if z is None else z),
            device_id_type=MESH,
        )


def greet(wires, masks, line):
    barrier = pltpu.get_barrier_semaphore()
    dp, z = wires.dp, wires.z
    for mask in masks:
        pl.semaphore_signal(barrier, inc=1, device_id=(masked(dp, mask), z), device_id_type=MESH)
    for step in range(1, LINE) if line else ():
        pl.semaphore_signal(
            barrier, inc=1, device_id=(dp, lax.rem(z + step, LINE)), device_id_type=MESH
        )
    pl.semaphore_wait(barrier, len(masks) + (LINE - 1 if line else 0))


LINE = 4


class LineGather:
    COPIES = 2 * (LINE - 1)

    def __init__(self, wires, ref, rows_of):
        self.wires, self.ref, self.rows_of = wires, ref, rows_of
        self.first = wires.take(self.COPIES)

    def _copy(self, block, number, z):
        part = self.ref.at[self.rows_of(block)]
        return self.wires.copy(part, part, self.first + number, z=z)

    def start(self, step):
        z = self.wires.z

        @pl.when((z >= step) & (z < LINE - 1))
        def _():
            self._copy(z - step, step, z + 1).start()

        @pl.when((z + step < LINE) & (z > 0))
        def _():
            self._copy(z + step, LINE - 1 + step, z - 1).start()

    def wait(self, step):
        z = self.wires.z

        @pl.when(z - 1 - step >= 0)
        def _():
            self._copy(z - 1 - step, step, z).wait_recv()

        @pl.when(z + 1 + step < LINE)
        def _():
            self._copy(z + 1 + step, LINE - 1 + step, z).wait_recv()

    def finish(self):
        z = self.wires.z
        for step in range(LINE - 1):

            @pl.when((z >= step) & (z < LINE - 1))
            def _():
                self._copy(z - step, step, z + 1).wait_send()

            @pl.when((z + step < LINE) & (z > 0))
            def _():
                self._copy(z + step, LINE - 1 + step, z - 1).wait_send()


class PlaneGather:
    CHIP = (
        ((2, 0, 0), (4, 0, 1)),
        ((4, 0, 0), (4, 2, 0), (2, 0, 1), (2, 4, 1)),
    )
    CORE = (
        ((1, 0, 2),),
        ((1, 2, 0), (1, 4, 1)),
        ((1, 4, 0), (1, 6, 0), (1, 2, 1), (1, 6, 1)),
    )
    COPIES = 13

    def __init__(self, wires, ref, group):
        self.wires, self.ref, self.group = wires, ref, group
        first = wires.take(self.COPIES)
        self.number = {}
        for stage in self.CHIP + self.CORE:
            for one in stage:
                self.number[one] = first + len(self.number)

    def _copy(self, one, from_me):
        to, whose, half = one
        dp = self.wires.dp
        sender = dp if from_me else masked(dp, to)
        owner = masked(sender, whose)
        size = self.group if half == 2 else self.group // 2
        begin = owner * self.group + (self.group // 2 if half == 1 else 0)
        part = self.ref.at[pl.ds(pl.multiple_of(begin, 16), size)]
        return self.wires.copy(part, part, self.number[one], dp=masked(dp, to))

    def start(self, stage):
        for one in (self.CHIP[stage] if stage < 2 else ()) + self.CORE[stage]:
            self._copy(one, True).start()

    def wait(self, stage):
        for one in self.CHIP[stage]:
            self._copy(one, False).wait_recv()

    def finish(self):
        for stage in self.CORE:
            for one in stage:
                self._copy(one, False).wait_recv()
        for one in self.number:
            self._copy(one, True).wait_send()


def add_rows(out, out_row, left, left_row, right, right_row, rows):
    @pl.loop(0, rows // 16)
    def _(step):
        def cut(row):
            return pl.ds(pl.multiple_of(row + step * 16, 16), 16)

        out[cut(out_row), :] = (
            left[cut(left_row), :].astype(jnp.float32) + right[cut(right_row), :].astype(jnp.float32)
        ).astype(out.dtype)


class PlaneReduce:
    COPIES = 10

    def __init__(self, wires, part, group, core_in, first_in, second_in):
        self.wires, self.part, self.group, self.half = wires, part, group, group // 2
        self.core_in, self.first_in, self.second_in = core_in, first_in, second_in
        self.first = wires.take(self.COPIES)
        self.begun = []

    def _send(self, src, src_row, dst, dst_row, rows, number, to):
        return self.wires.copy(
            src.at[pl.ds(src_row, rows)],
            dst.at[pl.ds(dst_row, rows)],
            self.first + number,
            dp=masked(self.wires.dp, to),
        )

    def _core(self, slot):
        row = pl.multiple_of(masked(self.wires.dp, 1 + 2 * slot) * self.group, 16)
        return self._send(self.part, row, self.core_in, slot * self.group, self.group, slot, 1)

    def _far(self, number):
        g, h = self.group, self.half
        src_row, dst, dst_row, to = (
            (3 * g, self.first_in, h, 4),
            (3 * g + h, self.first_in, 3 * h, 2),
            (2 * g, self.first_in, 0, 4),
            (1 * g + h, self.first_in, 2 * h, 2),
            (1 * g, self.second_in, 0, 2),
            (2 * g + h, self.second_in, h, 4),
        )[number]
        return self._send(self.core_in, src_row, dst, dst_row, h, 4 + number, to)

    def start(self):
        for slot in (3, 2, 1, 0):
            self._core(slot).start()

    def _sum_core(self, slot):
        self._core(slot).wait()
        row = pl.multiple_of(masked(self.wires.dp, 2 * slot) * self.group, 16)
        add_rows(
            self.core_in, slot * self.group, self.part, row, self.core_in, slot * self.group, self.group
        )

    def middle(self):
        g, h = self.group, self.half
        self._sum_core(3)
        self._far(0).start()
        self._far(1).start()
        self._sum_core(2)
        self._far(2).start()
        self._sum_core(1)
        self._far(3).start()
        self._sum_core(0)
        self._far(0).wait()
        add_rows(self.core_in, 1 * g, self.core_in, 1 * g, self.first_in, h, h)
        self._far(4).start()
        self._far(1).wait()
        add_rows(self.core_in, 2 * g + h, self.core_in, 2 * g + h, self.first_in, 3 * h, h)
        self._far(5).start()
        self._far(2).wait()
        add_rows(self.core_in, 0, self.core_in, 0, self.first_in, 0, h)
        self._far(3).wait()
        add_rows(self.core_in, h, self.core_in, h, self.first_in, 2 * h, h)

    def finish(self, out):
        h = self.half
        self._far(4).wait()
        add_rows(out, 0, self.core_in, 0, self.second_in, 0, h)
        self._far(5).wait()
        add_rows(out, h, self.core_in, h, self.second_in, h, h)

    @staticmethod
    def scratch(group, columns):
        return [
            pltpu.VMEM((4 * group, columns), jnp.bfloat16),
            pltpu.VMEM((2 * group, columns), jnp.bfloat16),
            pltpu.VMEM((group, columns), jnp.bfloat16),
        ]


class LineReduce:
    COPIES = 2 * (LINE - 1) * LINE

    def __init__(self, wires, part, rows, landing):
        self.wires, self.part, self.rows, self.landing = wires, part, rows, landing
        self.first = wires.take(self.COPIES)

    def _copy(self, way, hop, block, z):
        number = ((0 if way == 1 else 1) * (LINE - 1) + hop) * LINE + block
        return self.wires.copy(
            self.part.at[pl.ds(block * self.rows, self.rows)],
            self.landing.at[pl.ds(((0 if way == 1 else 1) * LINE + block) * self.rows, self.rows)],
            self.first + number,
            z=z,
        )

    def run(self, out):
        z, rows = self.wires.z, self.rows
        sends = []
        for hop in range(LINE - 1):
            for way in (1, -1):
                source = hop if way == 1 else LINE - 1 - hop
                blocks = range(LINE - 1, hop, -1) if way == 1 else range(0, LINE - 1 - hop)
                for block in blocks:

                    @pl.when(z == source)
                    def _():
                        self._copy(way, hop, block, z + way).start()

                    sends.append((way, hop, block, source))
            for way in (1, -1):
                source = hop if way == 1 else LINE - 1 - hop
                blocks = range(LINE - 1, hop, -1) if way == 1 else range(0, LINE - 1 - hop)
                for block in blocks:

                    @pl.when(z == source + way)
                    def _():
                        self._copy(way, hop, block, z).wait_recv()
                        add_rows(
                            self.part,
                            block * rows,
                            self.part,
                            block * rows,
                            self.landing,
                            ((0 if way == 1 else 1) * LINE + block) * rows,
                            rows,
                        )

        @pl.loop(0, rows // 16)
        def _(step):
            row = pl.multiple_of(z * rows + step * 16, 16)
            out[pl.ds(pl.multiple_of(step * 16, 16), 16), :] = self.part[pl.ds(row, 16), :].astype(out.dtype)

        for way, hop, block, source in sends:

            @pl.when(z == source)
            def _():
                self._copy(way, hop, block, z + way).wait_send()

    @staticmethod
    def scratch(rows, columns):
        return pltpu.VMEM((2 * LINE * rows, columns), jnp.bfloat16)


def sems(count):
    return [pltpu.SemaphoreType.DMA((count,)), pltpu.SemaphoreType.DMA((count,))]


def kernel_params(collective_id, mib):
    return pltpu.CompilerParams(
        collective_id=collective_id, has_side_effects=True, vmem_limit_bytes=mib * MIB
    )


def gather_inputs(w_in, w_out, cotangent, gates):
    rows, tokens = w_in.shape[0], cotangent.shape[0]
    planes = 8
    group = LINE * rows

    def kernel(in_ref, out_ref, cot_ref, gate_ref, all_in, all_out, all_cot, all_gate, here, send, recv):
        wires = Wires(send, recv)
        dp, z = wires.dp, wires.z
        own = pl.ds(pl.multiple_of((dp * LINE + z) * rows, 16), rows)
        locals_ = [
            pltpu.make_async_copy(in_ref, all_in.at[own], here.at[0]),
            pltpu.make_async_copy(out_ref, all_out.at[own], here.at[1]),
            pltpu.make_async_copy(
                cot_ref, all_cot.at[pl.ds(pl.multiple_of(dp * tokens, 16), tokens)], here.at[2]
            ),
            pltpu.make_async_copy(gate_ref, all_gate.at[pl.ds(pl.multiple_of(dp * 8, 8), 8)], here.at[3]),
        ]
        for one in locals_:
            one.start()
        greet(wires, range(1, planes), True)
        for one in locals_:
            one.wait()

        def block_rows(block):
            return pl.ds(pl.multiple_of((dp * LINE + block) * rows, 16), rows)

        lines = [LineGather(wires, all_in, block_rows), LineGather(wires, all_out, block_rows)]
        spreads = [
            PlaneGather(wires, all_in, group),
            PlaneGather(wires, all_out, group),
            PlaneGather(wires, all_cot, tokens),
        ]
        first = wires.take(planes - 1)

        def gate_copy(mask, owner):
            part = all_gate.at[pl.ds(pl.multiple_of(owner * 8, 8), 8)]
            return wires.copy(part, part, first + mask - 1, dp=masked(dp, mask))

        for mask in range(1, planes):
            gate_copy(mask, dp).start()
        for step in range(LINE - 1):
            lines[0].start(step)
            lines[0].wait(step)
        spreads[0].start(0)
        for step in range(LINE - 1):
            lines[1].start(step)
            lines[1].wait(step)
        spreads[0].wait(0)
        spreads[0].start(1)
        spreads[1].start(0)
        spreads[2].start(0)
        spreads[0].wait(1)
        spreads[0].start(2)
        spreads[1].wait(0)
        spreads[1].start(1)
        spreads[2].wait(0)
        spreads[2].start(1)
        spreads[1].wait(1)
        spreads[1].start(2)
        spreads[2].wait(1)
        spreads[2].start(2)
        for one in lines + spreads:
            one.finish()
        for mask in range(1, planes):
            gate_copy(mask, masked(dp, mask)).wait_recv()
        for mask in range(1, planes):
            gate_copy(mask, dp).wait_send()

    copies = 2 * LineGather.COPIES + 3 * PlaneGather.COPIES + planes - 1
    return pl.pallas_call(
        kernel,
        out_shape=(
            jax.ShapeDtypeStruct((planes * group, w_in.shape[1]), jnp.bfloat16),
            jax.ShapeDtypeStruct((planes * group, w_out.shape[1]), jnp.bfloat16),
            jax.ShapeDtypeStruct((planes * tokens, cotangent.shape[1]), jnp.bfloat16),
            jax.ShapeDtypeStruct((planes * 8, tokens), jnp.float32),
        ),
        in_specs=[ANY] * 4,
        out_specs=(ANY,) * 4,
        scratch_shapes=[pltpu.SemaphoreType.DMA((4,))] + sems(copies),
        compiler_params=kernel_params(0, 60),
        name="gather_inputs",
    )(w_in, w_out, cotangent, gates)


def gather_line(block):
    rows, columns = block.shape

    def kernel(block_ref, all_ref, here, send, recv):
        wires = Wires(send, recv)
        own = pltpu.make_async_copy(
            block_ref, all_ref.at[pl.ds(pl.multiple_of(wires.z * rows, 16), rows)], here.at[0]
        )
        own.start()
        greet(wires, (), True)
        own.wait()
        line = LineGather(wires, all_ref, lambda b: pl.ds(pl.multiple_of(b * rows, 16), rows))
        for step in range(LINE - 1):
            line.start(step)
            line.wait(step)
        line.finish()

    return pl.pallas_call(
        kernel,
        out_shape=jax.ShapeDtypeStruct((LINE * rows, columns), block.dtype),
        in_specs=[VMEM],
        out_specs=VMEM,
        scratch_shapes=[pltpu.SemaphoreType.DMA((1,))] + sems(LineGather.COPIES),
        compiler_params=kernel_params(1, 60),
        name="gather_line",
    )(block)


def gather_plane(block):
    rows, columns = block.shape

    def kernel(block_ref, all_ref, here, send, recv):
        wires = Wires(send, recv)
        own = pltpu.make_async_copy(
            block_ref, all_ref.at[pl.ds(pl.multiple_of(wires.dp * rows, 16), rows)], here.at[0]
        )
        own.start()
        greet(wires, (1, 2, 4), False)
        own.wait()
        spread = PlaneGather(wires, all_ref, rows)
        spread.start(0)
        spread.wait(0)
        spread.start(1)
        spread.wait(1)
        spread.start(2)
        spread.finish()

    return pl.pallas_call(
        kernel,
        out_shape=jax.ShapeDtypeStruct((8 * rows, columns), block.dtype),
        in_specs=[VMEM],
        out_specs=VMEM,
        scratch_shapes=[pltpu.SemaphoreType.DMA((1,))] + sems(PlaneGather.COPIES),
        compiler_params=kernel_params(2, 60),
        name="gather_plane",
    )(block)


def reduce_plane(part, collective_id):
    rows, columns = part.shape[0] // 8, part.shape[1]

    def kernel(part_ref, out_ref, core_in, first_in, second_in, send, recv):
        wires = Wires(send, recv)
        greet(wires, (1, 2, 4), False)
        total = PlaneReduce(wires, part_ref, rows, core_in, first_in, second_in)
        total.start()
        total.middle()
        total.finish(out_ref)

    return pl.pallas_call(
        kernel,
        out_shape=jax.ShapeDtypeStruct((rows, columns), jnp.float32),
        in_specs=[VMEM],
        out_specs=VMEM,
        scratch_shapes=PlaneReduce.scratch(rows, columns) + sems(PlaneReduce.COPIES),
        compiler_params=kernel_params(collective_id, 60),
        name=f"reduce_plane_{collective_id}",
    )(part)


def reduce_line(part):
    rows, columns = part.shape[0] // LINE, part.shape[1]

    def kernel(part_ref, out_ref, sums, landing, here, send, recv):
        wires = Wires(send, recv)
        own = pltpu.make_async_copy(part_ref, sums, here.at[0])
        own.start()
        greet(wires, (), True)
        own.wait()
        LineReduce(wires, sums, rows, landing).run(out_ref)

    return pl.pallas_call(
        kernel,
        out_shape=jax.ShapeDtypeStruct((rows, columns), jnp.float32),
        in_specs=[VMEM],
        out_specs=VMEM,
        scratch_shapes=[
            pltpu.VMEM(part.shape, jnp.bfloat16),
            LineReduce.scratch(rows, columns),
            pltpu.SemaphoreType.DMA((1,)),
        ]
        + sems(LineReduce.COPIES),
        compiler_params=kernel_params(5, 60),
        name="reduce_line",
    )(part)


def reduce_all(part):
    rows, columns = part.shape[0] // (8 * LINE), part.shape[1]
    group = LINE * rows

    def kernel(part_ref, out_ref, core_in, first_in, second_in, sums, landing, send, recv):
        wires = Wires(send, recv)
        greet(wires, (1, 2, 4), True)
        total = PlaneReduce(wires, part_ref, group, core_in, first_in, second_in)
        total.start()
        total.middle()
        total.finish(sums)
        LineReduce(wires, sums, rows, landing).run(out_ref)

    return pl.pallas_call(
        kernel,
        out_shape=jax.ShapeDtypeStruct((rows, columns), jnp.float32),
        in_specs=[VMEM],
        out_specs=VMEM,
        scratch_shapes=PlaneReduce.scratch(group, columns)
        + [pltpu.VMEM((group, columns), jnp.bfloat16), LineReduce.scratch(rows, columns)]
        + sems(PlaneReduce.COPIES + LineReduce.COPIES),
        compiler_params=kernel_params(6, 60),
        name="reduce_all",
    )(part)


def on_plane_device(
    tokens,
    norm_attn,
    w_query,
    w_key,
    w_value,
    w_out,
    norm_moe,
    w_gate,
    w_up,
    w_down,
    routes,
    gate_values,
    lengths,
    cotangent,
):
    tok_rows = tokens.shape[0]
    ctx_size = lax.axis_size("ctx")
    ctx_place = lax.axis_index("ctx")
    group_rows = tok_rows * ctx_size
    group_places = jnp.arange(group_rows, dtype=jnp.int32)
    seg_all, within_all = seq_tables(lengths[0], group_places)
    offset = ctx_place * tok_rows
    own_places = offset + jnp.arange(tok_rows, dtype=jnp.int32)
    seg_own = lax.dynamic_slice_in_dim(seg_all, offset, tok_rows)
    within_own = lax.dynamic_slice_in_dim(within_all, offset, tok_rows)
    allowed = (seg_own[:, None] == seg_all[None, :]) & (
        group_places[None, :] <= own_places[:, None]
    )
    kv_columns = KVH * HD
    q_columns = HEADS * HD
    gains = jnp.pad(jnp.stack([norm_attn, norm_moe], axis=1), ((0, 0), (0, LANES - 2)))
    w_in = jnp.concatenate([w_query, w_key, w_value, gains], axis=1)
    experts = jnp.arange(8, dtype=jnp.int32)
    gates = jnp.sum(
        jnp.where(routes[None, :, :] == experts[:, None, None], gate_values[None], 0.0), axis=2
    )
    full_in, full_o, cot_all, gates_all = gather_inputs(w_in, w_out, cotangent, gates)
    full_q = full_in[:, :q_columns]
    full_k = full_in[:, q_columns : q_columns + kv_columns]
    full_v = full_in[:, q_columns + kv_columns : q_columns + 2 * kv_columns]
    both_gains = full_in[:, q_columns + 2 * kv_columns :][:, :2].astype(jnp.float32).T
    gain_attn_f, gain_moe_f = both_gains[0], both_gains[1]
    inputs = tokens.astype(jnp.float32)
    normed_low = rms_norm(inputs, gain_attn_f).astype(jnp.bfloat16)
    pre = jnp.dot(
        normed_low, full_in[:, : q_columns + 2 * kv_columns], preferred_element_type=jnp.float32
    )
    query_pre = pre[:, :q_columns]
    key_pre = pre[:, q_columns : q_columns + kv_columns]
    value_pre = pre[:, q_columns + kv_columns :]
    query = rotate(query_pre.reshape(tok_rows, HEADS, HD), within_own, 1.0).astype(jnp.bfloat16)
    key_low = rotate(key_pre.reshape(tok_rows, KVH, HD), within_own, 1.0).astype(jnp.bfloat16)
    key_low = key_low.reshape(tok_rows, kv_columns)
    all_kv = gather_line(jnp.concatenate([key_low, value_pre.astype(jnp.bfloat16)], axis=1))
    all_keys, all_values = all_kv[:, :kv_columns], all_kv[:, kv_columns:]
    per_group = HEADS // KVH
    score_scale = HD ** (-0.5)
    query_groups = query.reshape(tok_rows, KVH, per_group, HD)

    def softmax_weights(group_number):
        keys_part = all_keys[:, group_number * HD : (group_number + 1) * HD]
        raw = jnp.einsum(
            "qjd,kd->jqk",
            query_groups[:, group_number],
            keys_part,
            preferred_element_type=jnp.float32,
        )
        scores = jnp.where(allowed[None], raw * score_scale, masked_score)
        row_top = jnp.max(scores, axis=-1, keepdims=True)
        expo = jnp.exp(scores - row_top)
        return expo / jnp.sum(expo, axis=-1, keepdims=True)

    mixed_parts = []
    for group_number in range(KVH):
        probs = softmax_weights(group_number)
        values_part = all_values[:, group_number * HD : (group_number + 1) * HD]
        mixed_group = jnp.einsum(
            "jqk,kd->qjd",
            probs.astype(jnp.bfloat16),
            values_part,
            preferred_element_type=jnp.float32,
        )
        mixed_parts.append(mixed_group.reshape(tok_rows, per_group * HD))
    mixed_low = jnp.concatenate(mixed_parts, axis=1).astype(jnp.bfloat16)
    middle = inputs + jnp.dot(mixed_low, full_o, preferred_element_type=jnp.float32)
    routed_low = rms_norm(middle, gain_moe_f).astype(jnp.bfloat16)

    routed_all = gather_plane(routed_low)
    my_expert = lax.axis_index("dp")
    gate_mine = lax.dynamic_index_in_dim(
        gates_all.reshape(8, 8, tok_rows), my_expert, axis=1, keepdims=False
    ).reshape(8 * tok_rows, 1)
    w_gate_e, w_up_e, w_down_e = w_gate[0], w_up[0], w_down[0]
    gate_act = jnp.dot(routed_all, w_gate_e, preferred_element_type=jnp.float32)
    up_act = jnp.dot(routed_all, w_up_e, preferred_element_type=jnp.float32)
    hidden_low = (jax.nn.silu(gate_act) * up_act).astype(jnp.bfloat16)
    grad_arrived = (cot_all.astype(jnp.float32) * gate_mine).astype(jnp.bfloat16)
    grad_hidden = jnp.einsum(
        "cd,fd->cf", grad_arrived, w_down_e, preferred_element_type=jnp.float32
    )
    grad_w_down = jnp.einsum(
        "cf,cd->fd", hidden_low, grad_arrived, preferred_element_type=jnp.float32
    )
    glu_value, glu_pull = jax.vjp(
        lambda gate_in, up_in: jax.nn.silu(gate_in) * up_in, gate_act, up_act
    )
    grad_gate, grad_up = glu_pull(grad_hidden)
    grad_gate_low = grad_gate.astype(jnp.bfloat16)
    grad_up_low = grad_up.astype(jnp.bfloat16)
    grad_w_gate = jnp.einsum(
        "cd,cf->df", routed_all, grad_gate_low, preferred_element_type=jnp.float32
    )
    grad_w_up = jnp.einsum(
        "cd,cf->df", routed_all, grad_up_low, preferred_element_type=jnp.float32
    )
    expert_sums = (
        lax.psum(grad_w_gate.astype(jnp.bfloat16), "ctx").astype(jnp.float32),
        lax.psum(grad_w_up.astype(jnp.bfloat16), "ctx").astype(jnp.float32),
        lax.psum(grad_w_down.astype(jnp.bfloat16), "ctx").astype(jnp.float32),
    )
    grad_sent = (
        jnp.einsum("cf,df->cd", grad_gate_low, w_gate_e, preferred_element_type=jnp.float32)
        + jnp.einsum("cf,df->cd", grad_up_low, w_up_e, preferred_element_type=jnp.float32)
    ).astype(jnp.bfloat16)
    grad_routed = reduce_plane(grad_sent, 3)
    produced = jnp.dot(hidden_low, w_down_e, preferred_element_type=jnp.float32)
    produced = produced.astype(jnp.bfloat16).astype(jnp.float32) * gate_mine
    moe_out = reduce_plane(produced.astype(jnp.bfloat16), 4)
    layer_out = (middle + moe_out).astype(jnp.bfloat16)

    grad_out = cotangent.astype(jnp.float32)
    norm_value, moe_pull = jax.vjp(rms_norm, middle, gain_moe_f)
    grad_mid_norm, grad_gain_moe = moe_pull(grad_routed)
    grad_middle = grad_out + grad_mid_norm
    grad_attn_low = grad_middle.astype(jnp.bfloat16)
    grad_w_out = jnp.einsum(
        "th,td->hd", mixed_low, grad_attn_low, preferred_element_type=jnp.float32
    )
    grad_mixed_low = jnp.einsum(
        "td,hd->th", grad_attn_low, full_o, preferred_element_type=jnp.float32
    ).astype(jnp.bfloat16)
    grad_mixed_groups = grad_mixed_low.reshape(tok_rows, KVH, per_group, HD)
    grad_query_parts = []
    key_pieces = []
    value_pieces = []
    for group_number in range(KVH):
        probs = softmax_weights(group_number)
        keys_part = all_keys[:, group_number * HD : (group_number + 1) * HD]
        values_part = all_values[:, group_number * HD : (group_number + 1) * HD]
        grad_probs = jnp.einsum(
            "qjd,kd->jqk",
            grad_mixed_groups[:, group_number],
            values_part,
            preferred_element_type=jnp.float32,
        )
        grad_scores = probs * (grad_probs - jnp.sum(probs * grad_probs, axis=-1, keepdims=True))
        grad_raw_low = (grad_scores * score_scale).astype(jnp.bfloat16)
        grad_query_parts.append(
            jnp.einsum("jqk,kd->qjd", grad_raw_low, keys_part, preferred_element_type=jnp.float32)
        )
        key_pieces.append(
            jnp.einsum(
                "jqk,qjd->kd",
                grad_raw_low,
                query_groups[:, group_number],
                preferred_element_type=jnp.float32,
            )
        )
        value_pieces.append(
            jnp.einsum(
                "jqk,qjd->kd",
                probs.astype(jnp.bfloat16),
                grad_mixed_groups[:, group_number],
                preferred_element_type=jnp.float32,
            )
        )
    grad_query_rot = jnp.stack(grad_query_parts, axis=1).reshape(tok_rows, HEADS, HD)
    key_value_grads = reduce_line(
        jnp.concatenate(key_pieces + value_pieces, axis=1).astype(jnp.bfloat16)
    )
    grad_query_low = (
        rotate(grad_query_rot, within_own, -1.0).astype(jnp.bfloat16).reshape(tok_rows, q_columns)
    )
    grad_key_rot = key_value_grads[:, :kv_columns].reshape(tok_rows, KVH, HD)
    grad_key_low = (
        rotate(grad_key_rot, within_own, -1.0).astype(jnp.bfloat16).reshape(tok_rows, kv_columns)
    )
    grad_value_low = key_value_grads[:, kv_columns:].astype(jnp.bfloat16)
    grad_pre = jnp.concatenate([grad_query_low, grad_key_low, grad_value_low], axis=1)
    grad_w_in = jnp.einsum("td,th->dh", normed_low, grad_pre, preferred_element_type=jnp.float32)
    grad_normed = jnp.einsum(
        "th,dh->td",
        grad_pre,
        full_in[:, : q_columns + 2 * kv_columns],
        preferred_element_type=jnp.float32,
    )
    first_value, attn_pull = jax.vjp(rms_norm, inputs, gain_attn_f)
    grad_inputs, grad_gain_attn = attn_pull(grad_normed)
    grad_tokens = grad_middle + grad_inputs
    grad_gains = jnp.pad(jnp.stack([grad_gain_attn, grad_gain_moe], axis=1), ((0, 0), (0, LANES - 2)))
    dense = reduce_all(
        jnp.concatenate([grad_w_in, grad_gains, grad_w_out], axis=1).astype(jnp.bfloat16)
    )
    edge = q_columns + 2 * kv_columns
    return (
        layer_out,
        grad_tokens,
        dense[:, edge],
        dense[:, :q_columns],
        dense[:, q_columns : q_columns + kv_columns],
        dense[:, q_columns + kv_columns : edge],
        dense[:, edge + LANES :],
        dense[:, edge + 1],
        expert_sums[0][None],
        expert_sums[1][None],
        expert_sums[2][None],
    )


def solution(mesh):
    on_plane = mesh.shape["dp"] == 8 and mesh.shape["ctx"] == LINE
    return jax.shard_map(
        on_plane_device if on_plane else on_device,
        mesh=mesh,
        in_specs=(
            P(("dp", "ctx"), None),
            P(("dp", "ctx")),
            P(("dp", "ctx"), None),
            P(("dp", "ctx"), None),
            P(("dp", "ctx"), None),
            P(("dp", "ctx"), None),
            P(("dp", "ctx")),
            P("dp", None, None),
            P("dp", None, None),
            P("dp", None, None),
            P(("dp", "ctx"), None),
            P(("dp", "ctx"), None),
            P("dp", None),
            P(("dp", "ctx"), None),
        ),
        out_specs=(
            P(("dp", "ctx"), None),
            P(("dp", "ctx"), None),
            P(("dp", "ctx")),
            P(("dp", "ctx"), None),
            P(("dp", "ctx"), None),
            P(("dp", "ctx"), None),
            P(("dp", "ctx"), None),
            P(("dp", "ctx")),
            P("dp", None, None),
            P("dp", None, None),
            P("dp", None, None),
        ),
        check_vma=False,
    )
```

```python
import functools

import jax
import jax.numpy as jnp
from jax import lax
from jax.experimental import pallas as pl
from jax.experimental.pallas import tpu as pltpu
from jax.sharding import PartitionSpec as P

D = 1536
HEADS = 12
KVH = 2
HD = 128
TOP = 4
EXP_DEV = 1


epsilon = 1e-06
rope_base = 1000000.0
masked_score = -1e30


def rms_norm(values, gain):
    return values * lax.rsqrt(jnp.mean(values * values, axis=-1, keepdims=True) + epsilon) * gain


def rotate(values, within, direction):
    half_size = values.shape[-1] // 2
    frequency = rope_base ** (-jnp.arange(half_size, dtype=jnp.float32) / half_size)
    angles = direction * within.astype(jnp.float32)[:, None] * frequency[None, :]
    cosine = jnp.cos(angles)[:, None, :]
    sine = jnp.sin(angles)[:, None, :]
    first_half = values[..., :half_size]
    second = values[..., half_size:]
    return jnp.concatenate(
        [first_half * cosine - second * sine, second * cosine + first_half * sine], axis=-1
    )


def seq_tables(length_row, places):
    seq_ends = jnp.cumsum(length_row)
    passed = places[:, None] >= seq_ends[None, :]
    segment = jnp.sum(passed.astype(jnp.int32), axis=1)
    within = places - jnp.sum(jnp.where(passed, length_row[None, :], 0), axis=1)
    return (segment, within)


def collect_weights(gain_attn, w_query, w_key, w_value, w_out, gain_moe):
    return (
        lax.all_gather(gain_attn, ("dp", "ctx"), axis=0, tiled=True),
        lax.all_gather(w_query, ("dp", "ctx"), axis=0, tiled=True),
        lax.all_gather(w_key, ("dp", "ctx"), axis=0, tiled=True),
        lax.all_gather(w_value, ("dp", "ctx"), axis=0, tiled=True),
        lax.all_gather(w_out, ("dp", "ctx"), axis=0, tiled=True),
        lax.all_gather(gain_moe, ("dp", "ctx"), axis=0, tiled=True),
    )


def spread_grads(grad_gain_attn, grad_query, grad_key, grad_value, grad_outp, grad_gain_moe):
    return (
        lax.psum_scatter(grad_gain_attn, ("dp", "ctx"), scatter_dimension=0, tiled=True),
        lax.psum_scatter(grad_query, ("dp", "ctx"), scatter_dimension=0, tiled=True),
        lax.psum_scatter(grad_key, ("dp", "ctx"), scatter_dimension=0, tiled=True),
        lax.psum_scatter(grad_value, ("dp", "ctx"), scatter_dimension=0, tiled=True),
        lax.psum_scatter(grad_outp, ("dp", "ctx"), scatter_dimension=0, tiled=True),
        lax.psum_scatter(grad_gain_moe, ("dp", "ctx"), scatter_dimension=0, tiled=True),
    )


def on_device(
    tokens,
    norm_attn,
    w_query,
    w_key,
    w_value,
    w_out,
    norm_moe,
    w_gate,
    w_up,
    w_down,
    routes,
    gate_values,
    lengths,
    cotangent,
):
    tok_rows = tokens.shape[0]
    ctx_size = lax.axis_size("ctx")
    dp_size = lax.axis_size("dp")
    ctx_place = lax.axis_index("ctx")
    group_rows = tok_rows * ctx_size
    group_places = jnp.arange(group_rows, dtype=jnp.int32)
    seg_all, within_all = seq_tables(lengths[0], group_places)
    offset = ctx_place * tok_rows
    own_places = offset + jnp.arange(tok_rows, dtype=jnp.int32)
    seg_own = lax.dynamic_slice_in_dim(seg_all, offset, tok_rows)
    within_own = lax.dynamic_slice_in_dim(within_all, offset, tok_rows)
    allowed = (seg_own[:, None] == seg_all[None, :]) & (
        group_places[None, :] <= own_places[:, None]
    )
    gain_attn, full_q, full_k, full_v, full_o, gain_moe = collect_weights(
        norm_attn, w_query, w_key, w_value, w_out, norm_moe
    )
    gain_attn_f = gain_attn.astype(jnp.float32)
    gain_moe_f = gain_moe.astype(jnp.float32)
    inputs = tokens.astype(jnp.float32)
    normed_low = rms_norm(inputs, gain_attn_f).astype(jnp.bfloat16)
    query_pre = jnp.dot(normed_low, full_q, preferred_element_type=jnp.float32)
    key_pre = jnp.dot(normed_low, full_k, preferred_element_type=jnp.float32)
    value_pre = jnp.dot(normed_low, full_v, preferred_element_type=jnp.float32)
    query = rotate(query_pre.reshape(tok_rows, HEADS, HD), within_own, 1.0).astype(jnp.bfloat16)
    key_low = rotate(key_pre.reshape(tok_rows, KVH, HD), within_own, 1.0).astype(jnp.bfloat16)
    key_low = key_low.reshape(tok_rows, KVH * HD)
    value_low = value_pre.astype(jnp.bfloat16)
    all_keys, all_values = (
        lax.all_gather(key_low, "ctx", axis=0, tiled=True),
        lax.all_gather(value_low, "ctx", axis=0, tiled=True),
    )
    per_group = HEADS // KVH
    score_scale = HD ** (-0.5)
    query_groups = query.reshape(tok_rows, KVH, per_group, HD)

    def softmax_weights(group_number):
        keys_part = all_keys[:, group_number * HD : (group_number + 1) * HD]
        raw = jnp.einsum(
            "qjd,kd->jqk",
            query_groups[:, group_number],
            keys_part,
            preferred_element_type=jnp.float32,
        )
        scores = jnp.where(allowed[None], raw * score_scale, masked_score)
        row_top = jnp.max(scores, axis=-1, keepdims=True)
        expo = jnp.exp(scores - row_top)
        return expo / jnp.sum(expo, axis=-1, keepdims=True)

    mixed_parts = []
    for group_number in range(KVH):
        probs = softmax_weights(group_number)
        values_part = all_values[:, group_number * HD : (group_number + 1) * HD]
        mixed_group = jnp.einsum(
            "jqk,kd->qjd",
            probs.astype(jnp.bfloat16),
            values_part,
            preferred_element_type=jnp.float32,
        )
        mixed_parts.append(mixed_group.reshape(tok_rows, per_group * HD))
    mixed_low = jnp.concatenate(mixed_parts, axis=1).astype(jnp.bfloat16)
    middle = inputs + jnp.dot(mixed_low, full_o, preferred_element_type=jnp.float32)
    routed_low = rms_norm(middle, gain_moe_f).astype(jnp.bfloat16)
    experts_total = EXP_DEV * dp_size
    capacity = 3 * TOP * tok_rows // (2 * experts_total)
    assign_count = tok_rows * TOP
    flat_ids = routes.reshape(assign_count)
    onehot = (flat_ids[:, None] == jnp.arange(experts_total, dtype=jnp.int32)[None, :]).astype(
        jnp.int32
    )
    earlier = jnp.sum((jnp.cumsum(onehot, axis=0) - onehot) * onehot, axis=1)
    slot_index = flat_ids * capacity + earlier
    owner = (
        jnp.full((experts_total * capacity,), assign_count, jnp.int32)
        .at[slot_index]
        .set(jnp.arange(assign_count, dtype=jnp.int32))
    )
    padded = jnp.concatenate([routed_low, jnp.zeros((1, D), jnp.bfloat16)], axis=0)
    outgoing = padded[owner // TOP].reshape(experts_total, capacity, D)
    arrived = lax.all_to_all(outgoing, "dp", split_axis=0, concat_axis=0, tiled=True)
    arrived_sets = arrived.reshape(dp_size, EXP_DEV, capacity, D)
    gate_act = jnp.einsum(
        "secd,edf->secf", arrived_sets, w_gate, preferred_element_type=jnp.float32
    )
    up_act = jnp.einsum("secd,edf->secf", arrived_sets, w_up, preferred_element_type=jnp.float32)
    hidden_low = (jax.nn.silu(gate_act) * up_act).astype(jnp.bfloat16)
    produced = jnp.einsum("secf,efd->secd", hidden_low, w_down, preferred_element_type=jnp.float32)
    produced = produced.astype(jnp.bfloat16).reshape(experts_total, capacity, D)
    returned = lax.all_to_all(produced, "dp", split_axis=0, concat_axis=0, tiled=True)
    picked = returned.reshape(experts_total * capacity, D)[slot_index].reshape(tok_rows, TOP, D)
    moe_out = jnp.sum(picked.astype(jnp.float32) * gate_values[:, :, None], axis=1)
    layer_out = (middle + moe_out).astype(jnp.bfloat16)
    grad_out = cotangent.astype(jnp.float32)
    grad_assign = (grad_out[:, None, :] * gate_values[:, :, None]).astype(jnp.bfloat16)
    grad_padded = jnp.concatenate(
        [grad_assign.reshape(assign_count, D), jnp.zeros((1, D), jnp.bfloat16)], axis=0
    )
    grad_slots = grad_padded[owner].reshape(experts_total, capacity, D)
    grad_arrived = lax.all_to_all(grad_slots, "dp", split_axis=0, concat_axis=0, tiled=True)
    grad_arrived = grad_arrived.reshape(dp_size, EXP_DEV, capacity, D)
    grad_hidden = jnp.einsum(
        "secd,efd->secf", grad_arrived, w_down, preferred_element_type=jnp.float32
    )
    grad_w_down = jnp.einsum(
        "secf,secd->efd", hidden_low, grad_arrived, preferred_element_type=jnp.float32
    )
    glu_value, glu_pull = jax.vjp(
        lambda gate_in, up_in: jax.nn.silu(gate_in) * up_in, gate_act, up_act
    )
    grad_gate, grad_up = glu_pull(grad_hidden)
    grad_gate_low = grad_gate.astype(jnp.bfloat16)
    grad_up_low = grad_up.astype(jnp.bfloat16)
    grad_w_gate = jnp.einsum(
        "secd,secf->edf", arrived_sets, grad_gate_low, preferred_element_type=jnp.float32
    )
    grad_w_up = jnp.einsum(
        "secd,secf->edf", arrived_sets, grad_up_low, preferred_element_type=jnp.float32
    )
    grad_sent = jnp.einsum(
        "secf,edf->secd", grad_gate_low, w_gate, preferred_element_type=jnp.float32
    ) + jnp.einsum("secf,edf->secd", grad_up_low, w_up, preferred_element_type=jnp.float32)
    grad_sent = grad_sent.astype(jnp.bfloat16).reshape(experts_total, capacity, D)
    grad_back = lax.all_to_all(grad_sent, "dp", split_axis=0, concat_axis=0, tiled=True)
    grad_picked = grad_back.reshape(experts_total * capacity, D)[slot_index].reshape(
        tok_rows, TOP, D
    )
    grad_routed = jnp.sum(grad_picked.astype(jnp.float32), axis=1)
    expert_sums = (
        lax.psum(grad_w_gate.astype(jnp.bfloat16), "ctx").astype(jnp.float32),
        lax.psum(grad_w_up.astype(jnp.bfloat16), "ctx").astype(jnp.float32),
        lax.psum(grad_w_down.astype(jnp.bfloat16), "ctx").astype(jnp.float32),
    )
    norm_value, moe_pull = jax.vjp(rms_norm, middle, gain_moe_f)
    grad_mid_norm, grad_gain_moe = moe_pull(grad_routed)
    grad_middle = grad_out + grad_mid_norm
    grad_attn_low = grad_middle.astype(jnp.bfloat16)
    grad_w_out = jnp.einsum(
        "th,td->hd", mixed_low, grad_attn_low, preferred_element_type=jnp.float32
    )
    grad_mixed_low = jnp.einsum(
        "td,hd->th", grad_attn_low, full_o, preferred_element_type=jnp.float32
    ).astype(jnp.bfloat16)
    grad_mixed_groups = grad_mixed_low.reshape(tok_rows, KVH, per_group, HD)
    grad_query_parts = []
    prob_parts = []
    score_parts = []
    for group_number in range(KVH):
        probs = softmax_weights(group_number)
        keys_part = all_keys[:, group_number * HD : (group_number + 1) * HD]
        values_part = all_values[:, group_number * HD : (group_number + 1) * HD]
        grad_probs = jnp.einsum(
            "qjd,kd->jqk",
            grad_mixed_groups[:, group_number],
            values_part,
            preferred_element_type=jnp.float32,
        )
        grad_scores = probs * (grad_probs - jnp.sum(probs * grad_probs, axis=-1, keepdims=True))
        grad_raw_low = (grad_scores * score_scale).astype(jnp.bfloat16)
        grad_query_parts.append(
            jnp.einsum("jqk,kd->qjd", grad_raw_low, keys_part, preferred_element_type=jnp.float32)
        )
        prob_parts.append(probs.astype(jnp.bfloat16))
        score_parts.append(grad_raw_low)
    grad_query_rot = jnp.stack(grad_query_parts, axis=1).reshape(tok_rows, HEADS, HD)
    key_pieces = []
    value_pieces = []
    for group_number in range(KVH):
        score_piece = score_parts[group_number]
        prob_piece = prob_parts[group_number]
        key_pieces.append(
            jnp.einsum(
                "jqk,qjd->kd",
                score_piece,
                query_groups[:, group_number],
                preferred_element_type=jnp.float32,
            )
        )
        value_pieces.append(
            jnp.einsum(
                "jqk,qjd->kd",
                prob_piece,
                grad_mixed_groups[:, group_number],
                preferred_element_type=jnp.float32,
            )
        )
    key_value_grads = lax.psum_scatter(
        jnp.concatenate(key_pieces + value_pieces, axis=1).astype(jnp.bfloat16),
        "ctx",
        scatter_dimension=0,
        tiled=True,
    ).astype(jnp.float32)
    grad_query_low = (
        rotate(grad_query_rot, within_own, -1.0).astype(jnp.bfloat16).reshape(tok_rows, HEADS * HD)
    )
    grad_key_rot = key_value_grads[:, : KVH * HD].reshape(tok_rows, KVH, HD)
    grad_key_low = (
        rotate(grad_key_rot, within_own, -1.0).astype(jnp.bfloat16).reshape(tok_rows, KVH * HD)
    )
    grad_value_low = key_value_grads[:, KVH * HD :].astype(jnp.bfloat16)
    grad_w_query = jnp.einsum(
        "td,th->dh", normed_low, grad_query_low, preferred_element_type=jnp.float32
    )
    grad_w_key = jnp.einsum(
        "td,th->dh", normed_low, grad_key_low, preferred_element_type=jnp.float32
    )
    grad_w_value = jnp.einsum(
        "td,th->dh", normed_low, grad_value_low, preferred_element_type=jnp.float32
    )
    grad_normed = (
        jnp.einsum("th,dh->td", grad_query_low, full_q, preferred_element_type=jnp.float32)
        + jnp.einsum("th,dh->td", grad_key_low, full_k, preferred_element_type=jnp.float32)
        + jnp.einsum("th,dh->td", grad_value_low, full_v, preferred_element_type=jnp.float32)
    )
    first_value, attn_pull = jax.vjp(rms_norm, inputs, gain_attn_f)
    grad_inputs, grad_gain_attn = attn_pull(grad_normed)
    grad_tokens = grad_middle + grad_inputs
    dense_sums = spread_grads(
        grad_gain_attn, grad_w_query, grad_w_key, grad_w_value, grad_w_out, grad_gain_moe
    )
    return (
        layer_out,
        grad_tokens,
        dense_sums[0],
        dense_sums[1],
        dense_sums[2],
        dense_sums[3],
        dense_sums[4],
        dense_sums[5],
        expert_sums[0],
        expert_sums[1],
        expert_sums[2],
    )


MESH = pl.DeviceIdType.MESH
LANES = 128
MIB = 2**20
ANY = pl.BlockSpec(memory_space=pl.ANY)
VMEM = pl.BlockSpec(memory_space=pltpu.VMEM)


def flip(index, bit):
    return index + bit - 2 * bit * ((index // bit) % 2)


def masked(index, mask):
    for bit in (1, 2, 4):
        if mask & bit:
            index = flip(index, bit)
    return index


class Wires:
    def __init__(self, send, recv):
        self.send, self.recv, self.used = send, recv, 0
        self.dp, self.z = lax.axis_index("dp"), lax.axis_index("ctx")

    def take(self, count):
        first = self.used
        self.used += count
        return first

    def copy(self, src, dst, number, dp=None, z=None):
        return pltpu.make_async_remote_copy(
            src_ref=src,
            dst_ref=dst,
            send_sem=self.send.at[number],
            recv_sem=self.recv.at[number],
            device_id=(self.dp if dp is None else dp, self.z if z is None else z),
            device_id_type=MESH,
        )


def greet(wires, masks, line):
    barrier = pltpu.get_barrier_semaphore()
    dp, z = wires.dp, wires.z
    for mask in masks:
        pl.semaphore_signal(barrier, inc=1, device_id=(masked(dp, mask), z), device_id_type=MESH)
    for step in range(1, LINE) if line else ():
        pl.semaphore_signal(
            barrier, inc=1, device_id=(dp, lax.rem(z + step, LINE)), device_id_type=MESH
        )
    pl.semaphore_wait(barrier, len(masks) + (LINE - 1 if line else 0))


LINE = 4


class LineGather:
    COPIES = 2 * (LINE - 1)

    def __init__(self, wires, ref, rows_of):
        self.wires, self.ref, self.rows_of = wires, ref, rows_of
        self.first = wires.take(self.COPIES)

    def _copy(self, block, number, z):
        part = self.ref.at[self.rows_of(block)]
        return self.wires.copy(part, part, self.first + number, z=z)

    def start(self, step):
        z = self.wires.z

        @pl.when((z >= step) & (z < LINE - 1))
        def _():
            self._copy(z - step, step, z + 1).start()

        @pl.when((z + step < LINE) & (z > 0))
        def _():
            self._copy(z + step, LINE - 1 + step, z - 1).start()

    def wait(self, step):
        z = self.wires.z

        @pl.when(z - 1 - step >= 0)
        def _():
            self._copy(z - 1 - step, step, z).wait_recv()

        @pl.when(z + 1 + step < LINE)
        def _():
            self._copy(z + 1 + step, LINE - 1 + step, z).wait_recv()

    def finish(self):
        z = self.wires.z
        for step in range(LINE - 1):

            @pl.when((z >= step) & (z < LINE - 1))
            def _():
                self._copy(z - step, step, z + 1).wait_send()

            @pl.when((z + step < LINE) & (z > 0))
            def _():
                self._copy(z + step, LINE - 1 + step, z - 1).wait_send()


class PlaneGather:
    CHIP = (
        ((2, 0, 0), (4, 0, 1)),
        ((4, 0, 0), (4, 2, 0), (2, 0, 1), (2, 4, 1)),
    )
    CORE = (
        ((1, 0, 2),),
        ((1, 2, 0), (1, 4, 1)),
        ((1, 4, 0), (1, 6, 0), (1, 2, 1), (1, 6, 1)),
    )
    COPIES = 13

    def __init__(self, wires, ref, group):
        self.wires, self.ref, self.group = wires, ref, group
        first = wires.take(self.COPIES)
        self.number = {}
        for stage in self.CHIP + self.CORE:
            for one in stage:
                self.number[one] = first + len(self.number)

    def _copy(self, one, from_me):
        to, whose, half = one
        dp = self.wires.dp
        sender = dp if from_me else masked(dp, to)
        owner = masked(sender, whose)
        size = self.group if half == 2 else self.group // 2
        begin = owner * self.group + (self.group // 2 if half == 1 else 0)
        part = self.ref.at[pl.ds(pl.multiple_of(begin, 16), size)]
        return self.wires.copy(part, part, self.number[one], dp=masked(dp, to))

    def start(self, stage):
        for one in (self.CHIP[stage] if stage < 2 else ()) + self.CORE[stage]:
            self._copy(one, True).start()

    def wait(self, stage):
        for one in self.CHIP[stage]:
            self._copy(one, False).wait_recv()

    def finish(self):
        for stage in self.CORE:
            for one in stage:
                self._copy(one, False).wait_recv()
        for one in self.number:
            self._copy(one, True).wait_send()


def add_rows(out, out_row, left, left_row, right, right_row, rows):
    @pl.loop(0, rows // 16)
    def _(step):
        def cut(row):
            return pl.ds(pl.multiple_of(row + step * 16, 16), 16)

        out[cut(out_row), :] = (
            left[cut(left_row), :].astype(jnp.float32) + right[cut(right_row), :].astype(jnp.float32)
        ).astype(out.dtype)


class PlaneReduce:
    COPIES = 10
    STEPS = 6

    def __init__(self, wires, part, group, own, own_row, core_in, first_in, second_in, out):
        self.wires, self.part, self.group, self.half = wires, part, group, group // 2
        self.own, self.own_row, self.out = own, own_row, out
        self.core_in, self.first_in, self.second_in = core_in, first_in, second_in
        self.first = wires.take(self.COPIES)

    def _send(self, src, src_row, dst, dst_row, rows, number, to):
        return self.wires.copy(
            src.at[pl.ds(src_row, rows)],
            dst.at[pl.ds(dst_row, rows)],
            self.first + number,
            dp=masked(self.wires.dp, to),
        )

    def _core(self, slot):
        row = pl.multiple_of(masked(self.wires.dp, 1 + 2 * slot) * self.group, 16)
        return self._send(self.part, row, self.core_in, slot * self.group, self.group, slot, 1)

    def _far(self, number):
        g, h = self.group, self.half
        src_row, dst, dst_row, to = (
            (3 * g, self.first_in, h, 4),
            (3 * g + h, self.first_in, 3 * h, 2),
            (2 * g, self.first_in, 0, 4),
            (1 * g + h, self.first_in, 2 * h, 2),
            (1 * g, self.second_in, 0, 2),
            (2 * g + h, self.second_in, h, 4),
        )[number]
        return self._send(self.core_in, src_row, dst, dst_row, h, 4 + number, to)

    def _sum_core(self, slot):
        self._core(slot).wait()
        row = slot * self.group
        add_rows(self.core_in, row, self.own, self.own_row(slot), self.core_in, row, self.group)

    def _sum_far(self, number, row, in_row):
        self._far(number).wait()
        add_rows(self.core_in, row, self.core_in, row, self.first_in, in_row, self.half)

    def step(self, number):
        g, h = self.group, self.half
        if number == 0:
            for slot in (3, 2, 1, 0):
                self._core(slot).start()
        elif number == 1:
            self._sum_core(3)
            self._far(0).start()
            self._far(1).start()
        elif number == 2:
            self._sum_core(2)
            self._far(2).start()
            self._sum_core(1)
            self._far(3).start()
            self._sum_core(0)
        elif number == 3:
            self._sum_far(0, 1 * g, h)
            self._far(4).start()
            self._sum_far(1, 2 * g + h, 3 * h)
            self._far(5).start()
        elif number == 4:
            self._sum_far(2, 0, 0)
            self._sum_far(3, h, 2 * h)
        else:
            self._far(4).wait()
            add_rows(self.out, 0, self.core_in, 0, self.second_in, 0, h)
            self._far(5).wait()
            add_rows(self.out, h, self.core_in, h, self.second_in, h, h)

    @staticmethod
    def scratch(group, columns):
        return [
            pltpu.VMEM((4 * group, columns), jnp.bfloat16),
            pltpu.VMEM((2 * group, columns), jnp.bfloat16),
            pltpu.VMEM((group, columns), jnp.bfloat16),
        ]


class LineReduce:
    COPIES = 2 * (LINE - 1) * LINE

    def __init__(self, wires, part, rows, landing):
        self.wires, self.part, self.rows, self.landing = wires, part, rows, landing
        self.first = wires.take(self.COPIES)

    def _copy(self, way, hop, block, z):
        number = ((0 if way == 1 else 1) * (LINE - 1) + hop) * LINE + block
        return self.wires.copy(
            self.part.at[pl.ds(block * self.rows, self.rows)],
            self.landing.at[pl.ds(((0 if way == 1 else 1) * LINE + block) * self.rows, self.rows)],
            self.first + number,
            z=z,
        )

    def _moves(self, hop):
        for way in (1, -1):
            source = hop if way == 1 else LINE - 1 - hop
            for block in range(LINE - 1, hop, -1) if way == 1 else range(0, LINE - 1 - hop):
                yield way, block, source

    def start(self, hop):
        z = self.wires.z
        for way, block, source in self._moves(hop):

            @pl.when(z == source)
            def _():
                self._copy(way, hop, block, z + way).start()

    def add(self, hop):
        z, rows = self.wires.z, self.rows
        for way, block, source in self._moves(hop):

            @pl.when(z == source + way)
            def _():
                self._copy(way, hop, block, z).wait_recv()
                place = ((0 if way == 1 else 1) * LINE + block) * rows
                add_rows(
                    self.part, block * rows, self.part, block * rows, self.landing, place, rows
                )

    def finish(self, out):
        z, rows = self.wires.z, self.rows

        @pl.loop(0, rows // 16)
        def _(step):
            row = pl.multiple_of(z * rows + step * 16, 16)
            out[pl.ds(pl.multiple_of(step * 16, 16), 16), :] = self.part[pl.ds(row, 16), :].astype(
                out.dtype
            )

        for hop in range(LINE - 1):
            for way, block, source in self._moves(hop):

                @pl.when(z == source)
                def _():
                    self._copy(way, hop, block, z + way).wait_send()

    @staticmethod
    def scratch(rows, columns):
        return pltpu.VMEM((2 * LINE * rows, columns), jnp.bfloat16)


def sems(count):
    return [pltpu.SemaphoreType.DMA((count,)), pltpu.SemaphoreType.DMA((count,))]


def kernel_params(collective_id, mib):
    return pltpu.CompilerParams(
        collective_id=collective_id, has_side_effects=True, vmem_limit_bytes=mib * MIB
    )


def gather_inputs(w_in, w_out, cotangent, gates):
    rows, tokens = w_in.shape[0], cotangent.shape[0]
    planes = 8
    group = LINE * rows

    def kernel(in_ref, out_ref, cot_ref, gate_ref, all_in, all_out, all_cot, all_gate, here, send, recv):
        wires = Wires(send, recv)
        dp, z = wires.dp, wires.z
        own = pl.ds(pl.multiple_of((dp * LINE + z) * rows, 16), rows)
        locals_ = [
            pltpu.make_async_copy(in_ref, all_in.at[own], here.at[0]),
            pltpu.make_async_copy(out_ref, all_out.at[own], here.at[1]),
            pltpu.make_async_copy(
                cot_ref, all_cot.at[pl.ds(pl.multiple_of(dp * tokens, 16), tokens)], here.at[2]
            ),
            pltpu.make_async_copy(gate_ref, all_gate.at[pl.ds(pl.multiple_of(dp * 8, 8), 8)], here.at[3]),
        ]
        for one in locals_:
            one.start()
        greet(wires, range(1, planes), True)
        for one in locals_:
            one.wait()

        def block_rows(block):
            return pl.ds(pl.multiple_of((dp * LINE + block) * rows, 16), rows)

        lines = [LineGather(wires, all_in, block_rows), LineGather(wires, all_out, block_rows)]
        spreads = [
            PlaneGather(wires, all_in, group),
            PlaneGather(wires, all_out, group),
            PlaneGather(wires, all_cot, tokens),
        ]
        first = wires.take(planes - 1)

        def gate_copy(mask, owner):
            part = all_gate.at[pl.ds(pl.multiple_of(owner * 8, 8), 8)]
            return wires.copy(part, part, first + mask - 1, dp=masked(dp, mask))

        for mask in range(1, planes):
            gate_copy(mask, dp).start()
        for step in range(LINE - 1):
            lines[0].start(step)
            lines[0].wait(step)
        spreads[0].start(0)
        for step in range(LINE - 1):
            lines[1].start(step)
            lines[1].wait(step)
        spreads[0].wait(0)
        spreads[0].start(1)
        spreads[1].start(0)
        spreads[2].start(0)
        spreads[0].wait(1)
        spreads[0].start(2)
        spreads[1].wait(0)
        spreads[1].start(1)
        spreads[2].wait(0)
        spreads[2].start(1)
        spreads[1].wait(1)
        spreads[1].start(2)
        spreads[2].wait(1)
        spreads[2].start(2)
        for one in lines + spreads:
            one.finish()
        for mask in range(1, planes):
            gate_copy(mask, masked(dp, mask)).wait_recv()
        for mask in range(1, planes):
            gate_copy(mask, dp).wait_send()

    copies = 2 * LineGather.COPIES + 3 * PlaneGather.COPIES + planes - 1
    return pl.pallas_call(
        kernel,
        out_shape=(
            jax.ShapeDtypeStruct((planes * group, w_in.shape[1]), jnp.bfloat16),
            jax.ShapeDtypeStruct((planes * group, w_out.shape[1]), jnp.bfloat16),
            jax.ShapeDtypeStruct((planes * tokens, cotangent.shape[1]), jnp.bfloat16),
            jax.ShapeDtypeStruct((planes * 8, tokens), jnp.float32),
        ),
        in_specs=[ANY] * 4,
        out_specs=(ANY,) * 4,
        scratch_shapes=[pltpu.SemaphoreType.DMA((4,))] + sems(copies),
        compiler_params=kernel_params(0, 60),
        name="gather_inputs",
    )(w_in, w_out, cotangent, gates)


def gather_line(block):
    rows, columns = block.shape

    def kernel(block_ref, all_ref, here, send, recv):
        wires = Wires(send, recv)
        own = pltpu.make_async_copy(
            block_ref, all_ref.at[pl.ds(pl.multiple_of(wires.z * rows, 16), rows)], here.at[0]
        )
        own.start()
        greet(wires, (), True)
        own.wait()
        line = LineGather(wires, all_ref, lambda b: pl.ds(pl.multiple_of(b * rows, 16), rows))
        for step in range(LINE - 1):
            line.start(step)
            line.wait(step)
        line.finish()

    return pl.pallas_call(
        kernel,
        out_shape=jax.ShapeDtypeStruct((LINE * rows, columns), block.dtype),
        in_specs=[VMEM],
        out_specs=VMEM,
        scratch_shapes=[pltpu.SemaphoreType.DMA((1,))] + sems(LineGather.COPIES),
        compiler_params=kernel_params(1, 60),
        name="gather_line",
    )(block)


def gather_plane(block):
    rows, columns = block.shape

    def kernel(block_ref, all_ref, here, send, recv):
        wires = Wires(send, recv)
        own = pltpu.make_async_copy(
            block_ref, all_ref.at[pl.ds(pl.multiple_of(wires.dp * rows, 16), rows)], here.at[0]
        )
        own.start()
        greet(wires, (1, 2, 4), False)
        own.wait()
        spread = PlaneGather(wires, all_ref, rows)
        spread.start(0)
        spread.wait(0)
        spread.start(1)
        spread.wait(1)
        spread.start(2)
        spread.finish()

    return pl.pallas_call(
        kernel,
        out_shape=jax.ShapeDtypeStruct((8 * rows, columns), block.dtype),
        in_specs=[VMEM],
        out_specs=VMEM,
        scratch_shapes=[pltpu.SemaphoreType.DMA((1,))] + sems(PlaneGather.COPIES),
        compiler_params=kernel_params(2, 60),
        name="gather_plane",
    )(block)


class LineSum:
    def __init__(self, wires, own, out, landing, rows, chunks):
        self.wires, self.own, self.out, self.landing = wires, own, out, landing
        self.rows, self.chunks, self.now = rows, chunks, 0
        self.first = wires.take(3 * chunks)
        z = wires.z
        self.inner = (z == 1) | (z == 2)
        self.outer = (z == 0) | (z == 3)
        self.end = 3 * (z - 1)
        self.near = 1 + z // 3
        self.peer = 3 - z

    def _cut(self, ref, chunk):
        return ref.at[pl.ds(pl.multiple_of(chunk * self.rows, 16), self.rows)]

    def _in(self, chunk):
        return self.wires.copy(
            self._cut(self.own, chunk), self._cut(self.out, chunk), self.first + chunk, z=self.near
        )

    def _across(self, chunk):
        number = self.first + self.chunks + chunk
        return self.wires.copy(
            self._cut(self.own, chunk), self._cut(self.landing, chunk), number, z=self.peer
        )

    def _back(self, chunk):
        number = self.first + 2 * self.chunks + chunk
        return self.wires.copy(
            self._cut(self.out, chunk), self._cut(self.out, chunk), number, z=self.end
        )

    def begin(self):
        @pl.when(self.outer)
        def _():
            for chunk in range(min(2, self.chunks)):
                self._in(chunk).start()

    def tick(self, count=1):
        for _ in range(count):
            if self.now <= self.chunks:
                self._tick(self.now)
            self.now += 1

    def _tick(self, chunk):
        if chunk < self.chunks:

            @pl.when(self.outer)
            def _():
                self._in(chunk).wait_send()
                if chunk + 2 < self.chunks:
                    self._in(chunk + 2).start()

        @pl.when(self.inner)
        def _():
            if chunk < self.chunks:
                row = chunk * self.rows
                self._in(chunk).wait_recv()
                add_rows(self.own, row, self.own, row, self.out, row, self.rows)
                self._across(chunk).start()
            if chunk >= 1:
                row = (chunk - 1) * self.rows
                self._across(chunk - 1).wait_recv()
                add_rows(self.out, row, self.own, row, self.landing, row, self.rows)
                self._back(chunk - 1).start()

    def finish(self):
        self.tick(max(0, self.chunks + 1 - self.now))

        @pl.when(self.outer)
        def _():
            @pl.loop(0, self.chunks)
            def _(chunk):
                self._back(chunk).wait_recv()

        @pl.when(self.inner)
        def _():
            @pl.loop(0, self.chunks)
            def _(chunk):
                self._across(chunk).wait_send()
                self._back(chunk).wait_send()


def dot(left, right, left_dim, right_dim):
    return lax.dot_general(
        left, right, (((left_dim,), (right_dim,)), ((), ())), preferred_element_type=jnp.float32
    )


def norm_back(values, gain, grad):
    scale = lax.rsqrt(jnp.mean(values * values, axis=-1, keepdims=True) + epsilon)
    normal = values * scale
    inner = grad * gain
    to_values = scale * (inner - normal * jnp.mean(inner * normal, axis=-1, keepdims=True))
    return to_values, grad * normal


def turned(values, cosine, sine):
    return values * cosine + pltpu.roll(values, HD // 2, 1) * sine


CHUNK = 192
SPLIT = 11


def back_attention(
    sums_in,
    grad_sent,
    full_o,
    middle,
    cotangent,
    gain_moe,
    mixed,
    query,
    all_kv,
    lse,
    starts,
    cosine,
    sine,
):
    tok_rows, width = middle.shape
    keys, kv_width = all_kv.shape
    w_rows = width
    group = w_rows // 8
    chunks = SPLIT

    def kernel(
        sums_ref, sent_ref, full_o_ref, middle_ref, cot_ref, gain_ref, mixed_ref, query_ref, kv_ref, lse_ref,
        starts_ref, cos_ref, sin_ref,
        total_ref, grad_mid_ref, grad_pre_ref, gain_row_ref, w_out_ref,
        sums_own, sums_land, own, core_in, first_in, second_in, routed_grad, attn_low, mixed_grad, part_o, o_core,
        o_first, o_second, bias, key_t, kv_grad, kv_part, kv_land, kv_out, here, send, recv,
    ):
        wires = Wires(send, recv)
        dp, z = wires.dp, wires.z
        loads = [pltpu.make_async_copy(sums_ref.at[pl.ds(0, chunks * CHUNK)], sums_own, here.at[0])]
        for slot in range(4):
            row = pl.multiple_of(masked(dp, 2 * slot) * tok_rows, 16)
            loads.append(
                pltpu.make_async_copy(
                    sent_ref.at[pl.ds(row, tok_rows)],
                    own.at[pl.ds(slot * tok_rows, tok_rows)],
                    here.at[1 + slot],
                )
            )
        for one in loads:
            one.start()
        greet(wires, (1, 2, 4), True)
        summed = LineSum(wires, sums_own, total_ref, sums_land, CHUNK, chunks)
        plane = PlaneReduce(
            wires, sent_ref, tok_rows, own, lambda slot: slot * tok_rows, core_in, first_in, second_in,
            routed_grad,
        )
        dense = PlaneReduce(
            wires, part_o, group, part_o, lambda slot: pl.multiple_of(masked(dp, 2 * slot) * group, 16),
            o_core, o_first, o_second, w_out_ref,
        )
        line = LineReduce(wires, kv_part, tok_rows, kv_land)
        plane.step(0)
        loads[0].wait()
        summed.begin()
        key_place = lax.broadcasted_iota(jnp.int32, (keys, tok_rows), 0)
        query_place = lax.broadcasted_iota(jnp.int32, (keys, tok_rows), 1) + z * tok_rows
        allowed = (key_place >= starts_ref[0:1, :]) & (key_place <= query_place)
        bias[...] = jnp.where(allowed, 0.0, masked_score)
        key_t[...] = kv_ref[:, : kv_width // 2].astype(jnp.float32).T.astype(jnp.bfloat16)
        kv_grad[...] = jnp.zeros_like(kv_grad)
        for one in loads[1:]:
            one.wait()
        plane.step(1)
        plane.step(2)
        summed.tick()
        summed.tick()
        plane.step(3)
        summed.tick()
        plane.step(4)
        summed.tick()
        plane.step(5)

        tile = 32
        gain_row_ref[...] = jnp.zeros_like(gain_row_ref)

        @pl.loop(0, tok_rows // tile)
        def _(step):
            cut = pl.ds(pl.multiple_of(step * tile, tile), tile)
            to_middle, terms = norm_back(middle_ref[cut, :], gain_ref[1:2, :], routed_grad[cut, :])
            to_middle = cot_ref[cut, :].astype(jnp.float32) + to_middle
            grad_mid_ref[cut, :] = to_middle
            attn_low[cut, :] = to_middle.astype(jnp.bfloat16)
            gain_row_ref[0:1, :] += jnp.sum(terms, axis=0, keepdims=True)

        wide = 512

        @pl.loop(0, width // wide)
        def _(step):
            cut = pl.ds(pl.multiple_of(step * wide, wide), wide)
            mixed_grad[:, cut] = dot(attn_low[...], full_o_ref[cut, :], 1, 1).astype(jnp.bfloat16)

        @pl.loop(0, width // 256)
        def _(step):
            cut = pl.ds(pl.multiple_of(step * 256, 256), 256)
            part_o[cut, :] = dot(mixed_ref[:, cut], attn_low[...], 0, 0).astype(jnp.bfloat16)

        dense.step(0)
        summed.tick()
        score_scale = HD ** (-0.5)
        per_group = HEADS // KVH

        def heads(first, last):
            @pl.loop(first, last)
            def _(head):
                own_cut = pl.ds(pl.multiple_of(head * HD, HD), HD)
                pair = head // per_group
                key_cut = pl.ds(pl.multiple_of(pair * HD, HD), HD)
                value_cut = pl.ds(pl.multiple_of((KVH + pair) * HD, HD), HD)
                q, do = query_ref[:, own_cut], mixed_grad[:, own_cut]
                k, v = kv_ref[:, key_cut], kv_ref[:, value_cut]
                scores = dot(k, q, 1, 1) * score_scale + bias[...]
                probs = jnp.exp(scores - lse_ref[pl.ds(head, 1), :])
                grad_probs = dot(v, do, 1, 1)
                inner = jnp.sum(probs * grad_probs, axis=0, keepdims=True)
                grad_raw = (probs * (grad_probs - inner) * score_scale).astype(jnp.bfloat16)
                kv_grad[:, value_cut] += dot(probs.astype(jnp.bfloat16), do, 1, 0)
                kv_grad[:, key_cut] += dot(grad_raw, q, 1, 0)
                to_query = dot(key_t[key_cut, :], grad_raw, 1, 0).T
                grad_pre_ref[:, own_cut] = turned(to_query, cos_ref[...], -sin_ref[...]).astype(
                    jnp.bfloat16
                )

        heads(0, 3)
        dense.step(1)
        dense.step(2)
        summed.tick()
        heads(3, 6)
        dense.step(3)
        summed.tick()
        heads(6, 9)
        dense.step(4)
        summed.tick()
        heads(9, 12)
        kv_part[...] = kv_grad[...].astype(jnp.bfloat16)
        line.start(0)
        dense.step(5)
        summed.tick()
        line.add(0)
        line.start(1)
        summed.tick()
        line.add(1)
        line.start(2)
        summed.tick()
        line.add(2)
        line.finish(kv_out)
        q_width = HEADS * HD
        for pair in range(KVH):
            cut = slice(pair * HD, (pair + 1) * HD)
            grad_pre_ref[:, q_width + pair * HD : q_width + (pair + 1) * HD] = turned(
                kv_out[:, cut], cos_ref[...], -sin_ref[...]
            ).astype(jnp.bfloat16)
        grad_pre_ref[:, q_width + kv_width // 2 :] = kv_out[:, kv_width // 2 :].astype(jnp.bfloat16)
        summed.finish()

    f32, low = jnp.float32, jnp.bfloat16
    return pl.pallas_call(
        kernel,
        out_shape=(
            jax.ShapeDtypeStruct((chunks * CHUNK, sums_in.shape[1]), low),
            jax.ShapeDtypeStruct((tok_rows, width), f32),
            jax.ShapeDtypeStruct((tok_rows, width + kv_width), low),
            jax.ShapeDtypeStruct((8, width), f32),
            jax.ShapeDtypeStruct((group, width), low),
        ),
        in_specs=[ANY, ANY] + [VMEM] * 11,
        out_specs=(VMEM,) * 5,
        scratch_shapes=[
            pltpu.VMEM((chunks * CHUNK, sums_in.shape[1]), low),
            pltpu.VMEM((chunks * CHUNK, sums_in.shape[1]), low),
            pltpu.VMEM((4 * tok_rows, width), low),
        ]
        + PlaneReduce.scratch(tok_rows, width)
        + [
            pltpu.VMEM((tok_rows, width), f32),
            pltpu.VMEM((tok_rows, width), low),
            pltpu.VMEM((tok_rows, width), low),
            pltpu.VMEM((w_rows, width), low),
        ]
        + PlaneReduce.scratch(group, width)
        + [
            pltpu.VMEM((keys, tok_rows), f32),
            pltpu.VMEM((kv_width // 2, keys), low),
            pltpu.VMEM((keys, kv_width), f32),
            pltpu.VMEM((keys, kv_width), low),
            LineReduce.scratch(tok_rows, kv_width),
            pltpu.VMEM((tok_rows, kv_width), f32),
            pltpu.SemaphoreType.DMA((5,)),
        ]
        + sems(3 * chunks + 2 * PlaneReduce.COPIES + LineReduce.COPIES),
        compiler_params=kernel_params(3, 63),
        name="back_attention",
    )(
        sums_in, grad_sent, full_o, middle, cotangent, gain_moe, mixed, query, all_kv, lse, starts, cosine, sine
    )


def back_dense(sums_in, produced, full_in, normed, grad_pre, tokens, gains, grad_mid, gain_row, w_out_part, middle):
    tok_rows, width = middle.shape
    in_width = full_in.shape[1]
    pre_width = in_width - LANES
    w_rows = width
    group, rows = w_rows // 8, w_rows // (8 * LINE)
    chunks = sums_in.shape[0] // CHUNK - SPLIT

    def kernel(
        sums_ref, prod_ref, full_ref, normed_ref, pre_ref, tok_ref, gain_ref, mid_grad_ref, gain_row_ref, o_part_ref,
        middle_ref,
        total_ref, layer_ref, tok_grad_ref, in_ref, out_ref,
        sums_own, sums_land, own, core_in, first_in, second_in, moe, part, d_core, d_first, d_second, in_sums,
        in_land, o_sums, o_land, normed_grad, gain_rows, here, send, recv,
    ):
        wires = Wires(send, recv)
        dp, z = wires.dp, wires.z
        loads = [
            pltpu.make_async_copy(
                sums_ref.at[pl.ds(SPLIT * CHUNK, chunks * CHUNK)], sums_own, here.at[0]
            )
        ]
        for slot in range(4):
            row = pl.multiple_of(masked(dp, 2 * slot) * tok_rows, 16)
            loads.append(
                pltpu.make_async_copy(
                    prod_ref.at[pl.ds(row, tok_rows)],
                    own.at[pl.ds(slot * tok_rows, tok_rows)],
                    here.at[1 + slot],
                )
            )
        for one in loads:
            one.start()
        greet(wires, (1, 2, 4), True)
        summed = LineSum(wires, sums_own, total_ref, sums_land, CHUNK, chunks)
        dense = PlaneReduce(
            wires, part, group, part, lambda slot: pl.multiple_of(masked(dp, 2 * slot) * group, 16),
            d_core, d_first, d_second, in_sums,
        )
        plane = PlaneReduce(
            wires, prod_ref, tok_rows, own, lambda slot: slot * tok_rows, core_in, first_in, second_in, moe
        )
        o_line = LineReduce(wires, o_sums, rows, o_land)
        in_line = LineReduce(wires, in_sums, rows, in_land)
        loads[0].wait()
        summed.begin()
        o_sums[...] = o_part_ref[...]
        wide = 512

        @pl.loop(0, width // wide)
        def _(step):
            cut = pl.ds(pl.multiple_of(step * wide, wide), wide)
            normed_grad[:, cut] = dot(pre_ref[...], full_ref[cut, :pre_width], 1, 1)

        gain_rows[...] = jnp.zeros_like(gain_rows)
        gain_rows[1:2, :] = gain_row_ref[0:1, :]
        tile = 32

        @pl.loop(0, tok_rows // tile)
        def _(step):
            cut = pl.ds(pl.multiple_of(step * tile, tile), tile)
            to_tokens, terms = norm_back(
                tok_ref[cut, :].astype(jnp.float32), gain_ref[0:1, :], normed_grad[cut, :]
            )
            tok_grad_ref[cut, :] = mid_grad_ref[cut, :] + to_tokens
            gain_rows[0:1, :] += jnp.sum(terms, axis=0, keepdims=True)

        part[:, pre_width:] = gain_rows[...].T.astype(jnp.bfloat16)

        @pl.loop(0, w_rows // 256)
        def _(step):
            cut = pl.ds(pl.multiple_of(step * 256, 256), 256)
            part[cut, :pre_width] = dot(normed_ref[:, cut], pre_ref[...], 0, 0).astype(jnp.bfloat16)

        dense.step(0)
        summed.tick()
        dense.step(1)
        dense.step(2)
        summed.tick()
        for one in loads[1:]:
            one.wait()
        summed.tick()
        dense.step(3)
        plane.step(0)
        summed.tick()
        dense.step(4)
        o_line.start(0)
        summed.tick()
        dense.step(5)
        in_line.start(0)
        plane.step(1)
        plane.step(2)
        o_line.add(0)
        o_line.start(1)
        summed.tick()
        in_line.add(0)
        in_line.start(1)
        plane.step(3)
        summed.tick()
        o_line.add(1)
        o_line.start(2)
        summed.tick()
        in_line.add(1)
        in_line.start(2)
        plane.step(4)
        summed.tick()
        o_line.add(2)
        in_line.add(2)
        plane.step(5)

        @pl.loop(0, tok_rows // tile)
        def _(step):
            cut = pl.ds(pl.multiple_of(step * tile, tile), tile)
            layer_ref[cut, :] = (middle_ref[cut, :] + moe[cut, :]).astype(jnp.bfloat16)

        o_line.finish(out_ref)
        in_line.finish(in_ref)
        summed.finish()

    f32, low = jnp.float32, jnp.bfloat16
    return pl.pallas_call(
        kernel,
        out_shape=(
            jax.ShapeDtypeStruct((chunks * CHUNK, sums_in.shape[1]), low),
            jax.ShapeDtypeStruct((tok_rows, width), low),
            jax.ShapeDtypeStruct((tok_rows, width), f32),
            jax.ShapeDtypeStruct((rows, in_width), f32),
            jax.ShapeDtypeStruct((rows, width), f32),
        ),
        in_specs=[ANY, ANY] + [VMEM] * 9,
        out_specs=(VMEM,) * 5,
        scratch_shapes=[
            pltpu.VMEM((chunks * CHUNK, sums_in.shape[1]), low),
            pltpu.VMEM((chunks * CHUNK, sums_in.shape[1]), low),
            pltpu.VMEM((4 * tok_rows, width), low),
        ]
        + PlaneReduce.scratch(tok_rows, width)
        + [pltpu.VMEM((tok_rows, width), f32), pltpu.VMEM((w_rows, in_width), low)]
        + PlaneReduce.scratch(group, in_width)
        + [
            pltpu.VMEM((group, in_width), low),
            LineReduce.scratch(rows, in_width),
            pltpu.VMEM((group, width), low),
            LineReduce.scratch(rows, width),
            pltpu.VMEM((tok_rows, width), f32),
            pltpu.VMEM((LANES, width), f32),
            pltpu.SemaphoreType.DMA((5,)),
        ]
        + sems(3 * chunks + 2 * PlaneReduce.COPIES + 2 * LineReduce.COPIES),
        compiler_params=kernel_params(4, 63),
        name="back_dense",
    )(
        sums_in, produced, full_in, normed, grad_pre, tokens, gains, grad_mid, gain_row, w_out_part, middle
    )


def on_plane_device(
    tokens,
    norm_attn,
    w_query,
    w_key,
    w_value,
    w_out,
    norm_moe,
    w_gate,
    w_up,
    w_down,
    routes,
    gate_values,
    lengths,
    cotangent,
):
    tok_rows = tokens.shape[0]
    ctx_size = lax.axis_size("ctx")
    ctx_place = lax.axis_index("ctx")
    group_rows = tok_rows * ctx_size
    group_places = jnp.arange(group_rows, dtype=jnp.int32)
    seg_all, within_all = seq_tables(lengths[0], group_places)
    offset = ctx_place * tok_rows
    own_places = offset + jnp.arange(tok_rows, dtype=jnp.int32)
    seg_own = lax.dynamic_slice_in_dim(seg_all, offset, tok_rows)
    within_own = lax.dynamic_slice_in_dim(within_all, offset, tok_rows)
    allowed = (seg_own[:, None] == seg_all[None, :]) & (
        group_places[None, :] <= own_places[:, None]
    )
    kv_columns = KVH * HD
    q_columns = HEADS * HD
    gains = jnp.pad(jnp.stack([norm_attn, norm_moe], axis=1), ((0, 0), (0, LANES - 2)))
    w_in = jnp.concatenate([w_query, w_key, w_value, gains], axis=1)
    experts = jnp.arange(8, dtype=jnp.int32)
    gates = jnp.sum(
        jnp.where(routes[None, :, :] == experts[:, None, None], gate_values[None], 0.0), axis=2
    )
    full_in, full_o, cot_all, gates_all = gather_inputs(w_in, w_out, cotangent, gates)
    full_q = full_in[:, :q_columns]
    full_k = full_in[:, q_columns : q_columns + kv_columns]
    full_v = full_in[:, q_columns + kv_columns : q_columns + 2 * kv_columns]
    both_gains = full_in[:, q_columns + 2 * kv_columns :][:, :2].astype(jnp.float32).T
    gain_attn_f, gain_moe_f = both_gains[0], both_gains[1]
    inputs = tokens.astype(jnp.float32)
    normed_low = rms_norm(inputs, gain_attn_f).astype(jnp.bfloat16)
    pre = jnp.dot(
        normed_low, full_in[:, : q_columns + 2 * kv_columns], preferred_element_type=jnp.float32
    )
    query_pre = pre[:, :q_columns]
    key_pre = pre[:, q_columns : q_columns + kv_columns]
    value_pre = pre[:, q_columns + kv_columns :]
    query = rotate(query_pre.reshape(tok_rows, HEADS, HD), within_own, 1.0).astype(jnp.bfloat16)
    key_low = rotate(key_pre.reshape(tok_rows, KVH, HD), within_own, 1.0).astype(jnp.bfloat16)
    key_low = key_low.reshape(tok_rows, kv_columns)
    all_kv = gather_line(jnp.concatenate([key_low, value_pre.astype(jnp.bfloat16)], axis=1))
    all_keys, all_values = all_kv[:, :kv_columns], all_kv[:, kv_columns:]
    per_group = HEADS // KVH
    score_scale = HD ** (-0.5)
    query_groups = query.reshape(tok_rows, KVH, per_group, HD)

    def softmax_weights(group_number):
        keys_part = all_keys[:, group_number * HD : (group_number + 1) * HD]
        raw = jnp.einsum(
            "qjd,kd->jqk",
            query_groups[:, group_number],
            keys_part,
            preferred_element_type=jnp.float32,
        )
        scores = jnp.where(allowed[None], raw * score_scale, masked_score)
        row_top = jnp.max(scores, axis=-1, keepdims=True)
        expo = jnp.exp(scores - row_top)
        row_sum = jnp.sum(expo, axis=-1, keepdims=True)
        return expo / row_sum, (row_top + jnp.log(row_sum))[:, :, 0]

    mixed_parts = []
    lse_parts = []
    for group_number in range(KVH):
        probs, lse_part = softmax_weights(group_number)
        lse_parts.append(lse_part)
        values_part = all_values[:, group_number * HD : (group_number + 1) * HD]
        mixed_group = jnp.einsum(
            "jqk,kd->qjd",
            probs.astype(jnp.bfloat16),
            values_part,
            preferred_element_type=jnp.float32,
        )
        mixed_parts.append(mixed_group.reshape(tok_rows, per_group * HD))
    mixed_low = jnp.concatenate(mixed_parts, axis=1).astype(jnp.bfloat16)
    lse = jnp.pad(jnp.concatenate(lse_parts, axis=0), ((0, 16 - HEADS), (0, 0)))
    half_size = HD // 2
    frequency = rope_base ** (-jnp.arange(half_size, dtype=jnp.float32) / half_size)
    angles = within_own.astype(jnp.float32)[:, None] * frequency[None, :]
    cosine = jnp.concatenate([jnp.cos(angles), jnp.cos(angles)], axis=1)
    sine = jnp.concatenate([-jnp.sin(angles), jnp.sin(angles)], axis=1)
    starts = jnp.broadcast_to((own_places - within_own)[None, :], (8, tok_rows))
    gain_rows = jnp.pad(both_gains, ((0, 6), (0, 0)))
    middle = inputs + jnp.dot(mixed_low, full_o, preferred_element_type=jnp.float32)
    routed_low = rms_norm(middle, gain_moe_f).astype(jnp.bfloat16)

    routed_all = gather_plane(routed_low)
    my_expert = lax.axis_index("dp")
    gate_mine = lax.dynamic_index_in_dim(
        gates_all.reshape(8, 8, tok_rows), my_expert, axis=1, keepdims=False
    ).reshape(8 * tok_rows, 1)
    w_gate_e, w_up_e, w_down_e = w_gate[0], w_up[0], w_down[0]
    gate_act = jnp.dot(routed_all, w_gate_e, preferred_element_type=jnp.float32)
    up_act = jnp.dot(routed_all, w_up_e, preferred_element_type=jnp.float32)
    hidden_low = (jax.nn.silu(gate_act) * up_act).astype(jnp.bfloat16)
    grad_arrived = (cot_all.astype(jnp.float32) * gate_mine).astype(jnp.bfloat16)
    grad_hidden = jnp.einsum(
        "cd,fd->cf", grad_arrived, w_down_e, preferred_element_type=jnp.float32
    )
    grad_w_down = jnp.einsum(
        "cf,cd->fd", hidden_low, grad_arrived, preferred_element_type=jnp.float32
    )
    glu_value, glu_pull = jax.vjp(
        lambda gate_in, up_in: jax.nn.silu(gate_in) * up_in, gate_act, up_act
    )
    grad_gate, grad_up = glu_pull(grad_hidden)
    grad_gate_low = grad_gate.astype(jnp.bfloat16)
    grad_up_low = grad_up.astype(jnp.bfloat16)
    grad_w_gate = jnp.einsum(
        "cd,cf->df", routed_all, grad_gate_low, preferred_element_type=jnp.float32
    )
    grad_w_up = jnp.einsum(
        "cd,cf->df", routed_all, grad_up_low, preferred_element_type=jnp.float32
    )
    half = grad_w_down.shape[1] // 2
    partial_sums = jnp.concatenate(
        [grad_w_gate, grad_w_up, grad_w_down[:, :half], grad_w_down[:, half:]], axis=0
    ).astype(jnp.bfloat16)
    grad_sent = (
        jnp.einsum("cf,df->cd", grad_gate_low, w_gate_e, preferred_element_type=jnp.float32)
        + jnp.einsum("cf,df->cd", grad_up_low, w_up_e, preferred_element_type=jnp.float32)
    ).astype(jnp.bfloat16)
    produced = jnp.dot(hidden_low, w_down_e, preferred_element_type=jnp.float32)
    produced = produced.astype(jnp.bfloat16).astype(jnp.float32) * gate_mine
    produced = produced.astype(jnp.bfloat16)
    sums_head, grad_mid, grad_pre, gain_row, w_out_part = back_attention(
        partial_sums,
        grad_sent,
        full_o,
        middle,
        cotangent,
        gain_rows,
        mixed_low,
        query.reshape(tok_rows, q_columns),
        all_kv,
        lse,
        starts,
        cosine,
        sine,
    )
    sums_tail, layer_out, grad_tokens, in_sums, out_sums = back_dense(
        partial_sums,
        produced,
        full_in,
        normed_low,
        grad_pre,
        tokens,
        gain_rows,
        grad_mid,
        gain_row,
        w_out_part,
        middle,
    )
    expert_sums = jnp.concatenate([sums_head, sums_tail], axis=0).astype(jnp.float32)
    width = D
    edge = q_columns + 2 * kv_columns
    return (
        layer_out,
        grad_tokens,
        in_sums[:, edge],
        in_sums[:, :q_columns],
        in_sums[:, q_columns : q_columns + kv_columns],
        in_sums[:, q_columns + kv_columns : edge],
        out_sums,
        in_sums[:, edge + 1],
        expert_sums[None, :width],
        expert_sums[None, width : 2 * width],
        jnp.concatenate(
            [expert_sums[None, 2 * width : 2 * width + half], expert_sums[None, 2 * width + half :]], axis=2
        ),
    )


def solution(mesh):
    on_plane = mesh.shape["dp"] == 8 and mesh.shape["ctx"] == LINE
    return jax.shard_map(
        on_plane_device if on_plane else on_device,
        mesh=mesh,
        in_specs=(
            P(("dp", "ctx"), None),
            P(("dp", "ctx")),
            P(("dp", "ctx"), None),
            P(("dp", "ctx"), None),
            P(("dp", "ctx"), None),
            P(("dp", "ctx"), None),
            P(("dp", "ctx")),
            P("dp", None, None),
            P("dp", None, None),
            P("dp", None, None),
            P(("dp", "ctx"), None),
            P(("dp", "ctx"), None),
            P("dp", None),
            P(("dp", "ctx"), None),
        ),
        out_specs=(
            P(("dp", "ctx"), None),
            P(("dp", "ctx"), None),
            P(("dp", "ctx")),
            P(("dp", "ctx"), None),
            P(("dp", "ctx"), None),
            P(("dp", "ctx"), None),
            P(("dp", "ctx"), None),
            P(("dp", "ctx")),
            P("dp", None, None),
            P("dp", None, None),
            P("dp", None, None),
        ),
        check_vma=False,
    )
```

```python
import functools

import jax
import jax.numpy as jnp
from jax import lax
from jax.experimental import pallas as pl
from jax.experimental.pallas import tpu as pltpu
from jax.sharding import PartitionSpec as P

D = 1536
HEADS = 12
KVH = 2
HD = 128
TOP = 4
EXP_DEV = 1


epsilon = 1e-06
rope_base = 1000000.0
masked_score = -1e30


def rms_norm(values, gain):
    return values * lax.rsqrt(jnp.mean(values * values, axis=-1, keepdims=True) + epsilon) * gain


def rotate(values, within, direction):
    half_size = values.shape[-1] // 2
    frequency = rope_base ** (-jnp.arange(half_size, dtype=jnp.float32) / half_size)
    angles = direction * within.astype(jnp.float32)[:, None] * frequency[None, :]
    cosine = jnp.cos(angles)[:, None, :]
    sine = jnp.sin(angles)[:, None, :]
    first_half = values[..., :half_size]
    second = values[..., half_size:]
    return jnp.concatenate(
        [first_half * cosine - second * sine, second * cosine + first_half * sine], axis=-1
    )


def seq_tables(length_row, places):
    seq_ends = jnp.cumsum(length_row)
    passed = places[:, None] >= seq_ends[None, :]
    segment = jnp.sum(passed.astype(jnp.int32), axis=1)
    within = places - jnp.sum(jnp.where(passed, length_row[None, :], 0), axis=1)
    return (segment, within)


def collect_weights(gain_attn, w_query, w_key, w_value, w_out, gain_moe):
    return (
        lax.all_gather(gain_attn, ("dp", "ctx"), axis=0, tiled=True),
        lax.all_gather(w_query, ("dp", "ctx"), axis=0, tiled=True),
        lax.all_gather(w_key, ("dp", "ctx"), axis=0, tiled=True),
        lax.all_gather(w_value, ("dp", "ctx"), axis=0, tiled=True),
        lax.all_gather(w_out, ("dp", "ctx"), axis=0, tiled=True),
        lax.all_gather(gain_moe, ("dp", "ctx"), axis=0, tiled=True),
    )


def spread_grads(grad_gain_attn, grad_query, grad_key, grad_value, grad_outp, grad_gain_moe):
    return (
        lax.psum_scatter(grad_gain_attn, ("dp", "ctx"), scatter_dimension=0, tiled=True),
        lax.psum_scatter(grad_query, ("dp", "ctx"), scatter_dimension=0, tiled=True),
        lax.psum_scatter(grad_key, ("dp", "ctx"), scatter_dimension=0, tiled=True),
        lax.psum_scatter(grad_value, ("dp", "ctx"), scatter_dimension=0, tiled=True),
        lax.psum_scatter(grad_outp, ("dp", "ctx"), scatter_dimension=0, tiled=True),
        lax.psum_scatter(grad_gain_moe, ("dp", "ctx"), scatter_dimension=0, tiled=True),
    )


def on_device(
    tokens,
    norm_attn,
    w_query,
    w_key,
    w_value,
    w_out,
    norm_moe,
    w_gate,
    w_up,
    w_down,
    routes,
    gate_values,
    lengths,
    cotangent,
):
    tok_rows = tokens.shape[0]
    ctx_size = lax.axis_size("ctx")
    dp_size = lax.axis_size("dp")
    ctx_place = lax.axis_index("ctx")
    group_rows = tok_rows * ctx_size
    group_places = jnp.arange(group_rows, dtype=jnp.int32)
    seg_all, within_all = seq_tables(lengths[0], group_places)
    offset = ctx_place * tok_rows
    own_places = offset + jnp.arange(tok_rows, dtype=jnp.int32)
    seg_own = lax.dynamic_slice_in_dim(seg_all, offset, tok_rows)
    within_own = lax.dynamic_slice_in_dim(within_all, offset, tok_rows)
    allowed = (seg_own[:, None] == seg_all[None, :]) & (
        group_places[None, :] <= own_places[:, None]
    )
    gain_attn, full_q, full_k, full_v, full_o, gain_moe = collect_weights(
        norm_attn, w_query, w_key, w_value, w_out, norm_moe
    )
    gain_attn_f = gain_attn.astype(jnp.float32)
    gain_moe_f = gain_moe.astype(jnp.float32)
    inputs = tokens.astype(jnp.float32)
    normed_low = rms_norm(inputs, gain_attn_f).astype(jnp.bfloat16)
    query_pre = jnp.dot(normed_low, full_q, preferred_element_type=jnp.float32)
    key_pre = jnp.dot(normed_low, full_k, preferred_element_type=jnp.float32)
    value_pre = jnp.dot(normed_low, full_v, preferred_element_type=jnp.float32)
    query = rotate(query_pre.reshape(tok_rows, HEADS, HD), within_own, 1.0).astype(jnp.bfloat16)
    key_low = rotate(key_pre.reshape(tok_rows, KVH, HD), within_own, 1.0).astype(jnp.bfloat16)
    key_low = key_low.reshape(tok_rows, KVH * HD)
    value_low = value_pre.astype(jnp.bfloat16)
    all_keys, all_values = (
        lax.all_gather(key_low, "ctx", axis=0, tiled=True),
        lax.all_gather(value_low, "ctx", axis=0, tiled=True),
    )
    per_group = HEADS // KVH
    score_scale = HD ** (-0.5)
    query_groups = query.reshape(tok_rows, KVH, per_group, HD)

    def softmax_weights(group_number):
        keys_part = all_keys[:, group_number * HD : (group_number + 1) * HD]
        raw = jnp.einsum(
            "qjd,kd->jqk",
            query_groups[:, group_number],
            keys_part,
            preferred_element_type=jnp.float32,
        )
        scores = jnp.where(allowed[None], raw * score_scale, masked_score)
        row_top = jnp.max(scores, axis=-1, keepdims=True)
        expo = jnp.exp(scores - row_top)
        return expo / jnp.sum(expo, axis=-1, keepdims=True)

    mixed_parts = []
    for group_number in range(KVH):
        probs = softmax_weights(group_number)
        values_part = all_values[:, group_number * HD : (group_number + 1) * HD]
        mixed_group = jnp.einsum(
            "jqk,kd->qjd",
            probs.astype(jnp.bfloat16),
            values_part,
            preferred_element_type=jnp.float32,
        )
        mixed_parts.append(mixed_group.reshape(tok_rows, per_group * HD))
    mixed_low = jnp.concatenate(mixed_parts, axis=1).astype(jnp.bfloat16)
    middle = inputs + jnp.dot(mixed_low, full_o, preferred_element_type=jnp.float32)
    routed_low = rms_norm(middle, gain_moe_f).astype(jnp.bfloat16)
    experts_total = EXP_DEV * dp_size
    capacity = 3 * TOP * tok_rows // (2 * experts_total)
    assign_count = tok_rows * TOP
    flat_ids = routes.reshape(assign_count)
    onehot = (flat_ids[:, None] == jnp.arange(experts_total, dtype=jnp.int32)[None, :]).astype(
        jnp.int32
    )
    earlier = jnp.sum((jnp.cumsum(onehot, axis=0) - onehot) * onehot, axis=1)
    slot_index = flat_ids * capacity + earlier
    owner = (
        jnp.full((experts_total * capacity,), assign_count, jnp.int32)
        .at[slot_index]
        .set(jnp.arange(assign_count, dtype=jnp.int32))
    )
    padded = jnp.concatenate([routed_low, jnp.zeros((1, D), jnp.bfloat16)], axis=0)
    outgoing = padded[owner // TOP].reshape(experts_total, capacity, D)
    arrived = lax.all_to_all(outgoing, "dp", split_axis=0, concat_axis=0, tiled=True)
    arrived_sets = arrived.reshape(dp_size, EXP_DEV, capacity, D)
    gate_act = jnp.einsum(
        "secd,edf->secf", arrived_sets, w_gate, preferred_element_type=jnp.float32
    )
    up_act = jnp.einsum("secd,edf->secf", arrived_sets, w_up, preferred_element_type=jnp.float32)
    hidden_low = (jax.nn.silu(gate_act) * up_act).astype(jnp.bfloat16)
    produced = jnp.einsum("secf,efd->secd", hidden_low, w_down, preferred_element_type=jnp.float32)
    produced = produced.astype(jnp.bfloat16).reshape(experts_total, capacity, D)
    returned = lax.all_to_all(produced, "dp", split_axis=0, concat_axis=0, tiled=True)
    picked = returned.reshape(experts_total * capacity, D)[slot_index].reshape(tok_rows, TOP, D)
    moe_out = jnp.sum(picked.astype(jnp.float32) * gate_values[:, :, None], axis=1)
    layer_out = (middle + moe_out).astype(jnp.bfloat16)
    grad_out = cotangent.astype(jnp.float32)
    grad_assign = (grad_out[:, None, :] * gate_values[:, :, None]).astype(jnp.bfloat16)
    grad_padded = jnp.concatenate(
        [grad_assign.reshape(assign_count, D), jnp.zeros((1, D), jnp.bfloat16)], axis=0
    )
    grad_slots = grad_padded[owner].reshape(experts_total, capacity, D)
    grad_arrived = lax.all_to_all(grad_slots, "dp", split_axis=0, concat_axis=0, tiled=True)
    grad_arrived = grad_arrived.reshape(dp_size, EXP_DEV, capacity, D)
    grad_hidden = jnp.einsum(
        "secd,efd->secf", grad_arrived, w_down, preferred_element_type=jnp.float32
    )
    grad_w_down = jnp.einsum(
        "secf,secd->efd", hidden_low, grad_arrived, preferred_element_type=jnp.float32
    )
    glu_value, glu_pull = jax.vjp(
        lambda gate_in, up_in: jax.nn.silu(gate_in) * up_in, gate_act, up_act
    )
    grad_gate, grad_up = glu_pull(grad_hidden)
    grad_gate_low = grad_gate.astype(jnp.bfloat16)
    grad_up_low = grad_up.astype(jnp.bfloat16)
    grad_w_gate = jnp.einsum(
        "secd,secf->edf", arrived_sets, grad_gate_low, preferred_element_type=jnp.float32
    )
    grad_w_up = jnp.einsum(
        "secd,secf->edf", arrived_sets, grad_up_low, preferred_element_type=jnp.float32
    )
    grad_sent = jnp.einsum(
        "secf,edf->secd", grad_gate_low, w_gate, preferred_element_type=jnp.float32
    ) + jnp.einsum("secf,edf->secd", grad_up_low, w_up, preferred_element_type=jnp.float32)
    grad_sent = grad_sent.astype(jnp.bfloat16).reshape(experts_total, capacity, D)
    grad_back = lax.all_to_all(grad_sent, "dp", split_axis=0, concat_axis=0, tiled=True)
    grad_picked = grad_back.reshape(experts_total * capacity, D)[slot_index].reshape(
        tok_rows, TOP, D
    )
    grad_routed = jnp.sum(grad_picked.astype(jnp.float32), axis=1)
    expert_sums = (
        lax.psum(grad_w_gate.astype(jnp.bfloat16), "ctx").astype(jnp.float32),
        lax.psum(grad_w_up.astype(jnp.bfloat16), "ctx").astype(jnp.float32),
        lax.psum(grad_w_down.astype(jnp.bfloat16), "ctx").astype(jnp.float32),
    )
    norm_value, moe_pull = jax.vjp(rms_norm, middle, gain_moe_f)
    grad_mid_norm, grad_gain_moe = moe_pull(grad_routed)
    grad_middle = grad_out + grad_mid_norm
    grad_attn_low = grad_middle.astype(jnp.bfloat16)
    grad_w_out = jnp.einsum(
        "th,td->hd", mixed_low, grad_attn_low, preferred_element_type=jnp.float32
    )
    grad_mixed_low = jnp.einsum(
        "td,hd->th", grad_attn_low, full_o, preferred_element_type=jnp.float32
    ).astype(jnp.bfloat16)
    grad_mixed_groups = grad_mixed_low.reshape(tok_rows, KVH, per_group, HD)
    grad_query_parts = []
    prob_parts = []
    score_parts = []
    for group_number in range(KVH):
        probs = softmax_weights(group_number)
        keys_part = all_keys[:, group_number * HD : (group_number + 1) * HD]
        values_part = all_values[:, group_number * HD : (group_number + 1) * HD]
        grad_probs = jnp.einsum(
            "qjd,kd->jqk",
            grad_mixed_groups[:, group_number],
            values_part,
            preferred_element_type=jnp.float32,
        )
        grad_scores = probs * (grad_probs - jnp.sum(probs * grad_probs, axis=-1, keepdims=True))
        grad_raw_low = (grad_scores * score_scale).astype(jnp.bfloat16)
        grad_query_parts.append(
            jnp.einsum("jqk,kd->qjd", grad_raw_low, keys_part, preferred_element_type=jnp.float32)
        )
        prob_parts.append(probs.astype(jnp.bfloat16))
        score_parts.append(grad_raw_low)
    grad_query_rot = jnp.stack(grad_query_parts, axis=1).reshape(tok_rows, HEADS, HD)
    key_pieces = []
    value_pieces = []
    for group_number in range(KVH):
        score_piece = score_parts[group_number]
        prob_piece = prob_parts[group_number]
        key_pieces.append(
            jnp.einsum(
                "jqk,qjd->kd",
                score_piece,
                query_groups[:, group_number],
                preferred_element_type=jnp.float32,
            )
        )
        value_pieces.append(
            jnp.einsum(
                "jqk,qjd->kd",
                prob_piece,
                grad_mixed_groups[:, group_number],
                preferred_element_type=jnp.float32,
            )
        )
    key_value_grads = lax.psum_scatter(
        jnp.concatenate(key_pieces + value_pieces, axis=1).astype(jnp.bfloat16),
        "ctx",
        scatter_dimension=0,
        tiled=True,
    ).astype(jnp.float32)
    grad_query_low = (
        rotate(grad_query_rot, within_own, -1.0).astype(jnp.bfloat16).reshape(tok_rows, HEADS * HD)
    )
    grad_key_rot = key_value_grads[:, : KVH * HD].reshape(tok_rows, KVH, HD)
    grad_key_low = (
        rotate(grad_key_rot, within_own, -1.0).astype(jnp.bfloat16).reshape(tok_rows, KVH * HD)
    )
    grad_value_low = key_value_grads[:, KVH * HD :].astype(jnp.bfloat16)
    grad_w_query = jnp.einsum(
        "td,th->dh", normed_low, grad_query_low, preferred_element_type=jnp.float32
    )
    grad_w_key = jnp.einsum(
        "td,th->dh", normed_low, grad_key_low, preferred_element_type=jnp.float32
    )
    grad_w_value = jnp.einsum(
        "td,th->dh", normed_low, grad_value_low, preferred_element_type=jnp.float32
    )
    grad_normed = (
        jnp.einsum("th,dh->td", grad_query_low, full_q, preferred_element_type=jnp.float32)
        + jnp.einsum("th,dh->td", grad_key_low, full_k, preferred_element_type=jnp.float32)
        + jnp.einsum("th,dh->td", grad_value_low, full_v, preferred_element_type=jnp.float32)
    )
    first_value, attn_pull = jax.vjp(rms_norm, inputs, gain_attn_f)
    grad_inputs, grad_gain_attn = attn_pull(grad_normed)
    grad_tokens = grad_middle + grad_inputs
    dense_sums = spread_grads(
        grad_gain_attn, grad_w_query, grad_w_key, grad_w_value, grad_w_out, grad_gain_moe
    )
    return (
        layer_out,
        grad_tokens,
        dense_sums[0],
        dense_sums[1],
        dense_sums[2],
        dense_sums[3],
        dense_sums[4],
        dense_sums[5],
        expert_sums[0],
        expert_sums[1],
        expert_sums[2],
    )


MESH = pl.DeviceIdType.MESH
LANES = 128
MIB = 2**20
ANY = pl.BlockSpec(memory_space=pl.ANY)
VMEM = pl.BlockSpec(memory_space=pltpu.VMEM)


def flip(index, bit):
    return index + bit - 2 * bit * ((index // bit) % 2)


def masked(index, mask):
    for bit in (1, 2, 4):
        if mask & bit:
            index = flip(index, bit)
    return index


class Wires:
    def __init__(self, send, recv):
        self.send, self.recv, self.used = send, recv, 0
        self.dp, self.z = lax.axis_index("dp"), lax.axis_index("ctx")

    def take(self, count):
        first = self.used
        self.used += count
        return first

    def copy(self, src, dst, number, dp=None, z=None):
        return pltpu.make_async_remote_copy(
            src_ref=src,
            dst_ref=dst,
            send_sem=self.send.at[number],
            recv_sem=self.recv.at[number],
            device_id=(self.dp if dp is None else dp, self.z if z is None else z),
            device_id_type=MESH,
        )


def greet(wires, masks, line):
    barrier = pltpu.get_barrier_semaphore()
    dp, z = wires.dp, wires.z
    for mask in masks:
        pl.semaphore_signal(barrier, inc=1, device_id=(masked(dp, mask), z), device_id_type=MESH)
    for step in range(1, LINE) if line else ():
        pl.semaphore_signal(
            barrier, inc=1, device_id=(dp, lax.rem(z + step, LINE)), device_id_type=MESH
        )
    pl.semaphore_wait(barrier, len(masks) + (LINE - 1 if line else 0))


LINE = 4


class LineGather:
    COPIES = 2 * (LINE - 1)

    def __init__(self, wires, ref, rows_of):
        self.wires, self.ref, self.rows_of = wires, ref, rows_of
        self.first = wires.take(self.COPIES)

    def _copy(self, block, number, z):
        part = self.ref.at[self.rows_of(block)]
        return self.wires.copy(part, part, self.first + number, z=z)

    def start(self, step):
        z = self.wires.z

        @pl.when((z >= step) & (z < LINE - 1))
        def _():
            self._copy(z - step, step, z + 1).start()

        @pl.when((z + step < LINE) & (z > 0))
        def _():
            self._copy(z + step, LINE - 1 + step, z - 1).start()

    def wait(self, step):
        z = self.wires.z

        @pl.when(z - 1 - step >= 0)
        def _():
            self._copy(z - 1 - step, step, z).wait_recv()

        @pl.when(z + 1 + step < LINE)
        def _():
            self._copy(z + 1 + step, LINE - 1 + step, z).wait_recv()

    def finish(self):
        z = self.wires.z
        for step in range(LINE - 1):

            @pl.when((z >= step) & (z < LINE - 1))
            def _():
                self._copy(z - step, step, z + 1).wait_send()

            @pl.when((z + step < LINE) & (z > 0))
            def _():
                self._copy(z + step, LINE - 1 + step, z - 1).wait_send()


class PlaneGather:
    CHIP = (
        ((2, 0, 0), (4, 0, 1)),
        ((4, 0, 0), (4, 2, 0), (2, 0, 1), (2, 4, 1)),
    )
    CORE = (
        ((1, 0, 2),),
        ((1, 2, 0), (1, 4, 1)),
        ((1, 4, 0), (1, 6, 0), (1, 2, 1), (1, 6, 1)),
    )
    COPIES = 13

    def __init__(self, wires, ref, group):
        self.wires, self.ref, self.group = wires, ref, group
        first = wires.take(self.COPIES)
        self.number = {}
        for stage in self.CHIP + self.CORE:
            for one in stage:
                self.number[one] = first + len(self.number)

    def _copy(self, one, from_me):
        to, whose, half = one
        dp = self.wires.dp
        sender = dp if from_me else masked(dp, to)
        owner = masked(sender, whose)
        size = self.group if half == 2 else self.group // 2
        begin = owner * self.group + (self.group // 2 if half == 1 else 0)
        part = self.ref.at[pl.ds(pl.multiple_of(begin, 16), size)]
        return self.wires.copy(part, part, self.number[one], dp=masked(dp, to))

    def start(self, stage):
        for one in (self.CHIP[stage] if stage < 2 else ()) + self.CORE[stage]:
            self._copy(one, True).start()

    def wait(self, stage):
        for one in self.CHIP[stage]:
            self._copy(one, False).wait_recv()

    def finish(self):
        for stage in self.CORE:
            for one in stage:
                self._copy(one, False).wait_recv()
        for one in self.number:
            self._copy(one, True).wait_send()


def add_rows(out, out_row, left, left_row, right, right_row, rows):
    @pl.loop(0, rows // 16)
    def _(step):
        def cut(row):
            return pl.ds(pl.multiple_of(row + step * 16, 16), 16)

        out[cut(out_row), :] = (
            left[cut(left_row), :].astype(jnp.float32) + right[cut(right_row), :].astype(jnp.float32)
        ).astype(out.dtype)


class PlaneReduce:
    COPIES = 10
    STEPS = 6

    def __init__(self, wires, part, group, own, own_row, core_in, first_in, second_in, out):
        self.wires, self.part, self.group, self.half = wires, part, group, group // 2
        self.own, self.own_row, self.out = own, own_row, out
        self.core_in, self.first_in, self.second_in = core_in, first_in, second_in
        self.first = wires.take(self.COPIES)

    def _send(self, src, src_row, dst, dst_row, rows, number, to):
        return self.wires.copy(
            src.at[pl.ds(src_row, rows)],
            dst.at[pl.ds(dst_row, rows)],
            self.first + number,
            dp=masked(self.wires.dp, to),
        )

    def _core(self, slot):
        row = pl.multiple_of(masked(self.wires.dp, 1 + 2 * slot) * self.group, 16)
        return self._send(self.part, row, self.core_in, slot * self.group, self.group, slot, 1)

    def _far(self, number):
        g, h = self.group, self.half
        src_row, dst, dst_row, to = (
            (3 * g, self.first_in, h, 4),
            (3 * g + h, self.first_in, 3 * h, 2),
            (2 * g, self.first_in, 0, 4),
            (1 * g + h, self.first_in, 2 * h, 2),
            (1 * g, self.second_in, 0, 2),
            (2 * g + h, self.second_in, h, 4),
        )[number]
        return self._send(self.core_in, src_row, dst, dst_row, h, 4 + number, to)

    def _sum_core(self, slot):
        self._core(slot).wait()
        row = slot * self.group
        add_rows(self.core_in, row, self.own, self.own_row(slot), self.core_in, row, self.group)

    def _sum_far(self, number, row, in_row):
        self._far(number).wait()
        add_rows(self.core_in, row, self.core_in, row, self.first_in, in_row, self.half)

    def step(self, number):
        g, h = self.group, self.half
        if number == 0:
            for slot in (3, 2, 1, 0):
                self._core(slot).start()
        elif number == 1:
            self._sum_core(3)
            self._far(0).start()
            self._far(1).start()
        elif number == 2:
            self._sum_core(2)
            self._far(2).start()
            self._sum_core(1)
            self._far(3).start()
            self._sum_core(0)
        elif number == 3:
            self._sum_far(0, 1 * g, h)
            self._far(4).start()
            self._sum_far(1, 2 * g + h, 3 * h)
            self._far(5).start()
        elif number == 4:
            self._sum_far(2, 0, 0)
            self._sum_far(3, h, 2 * h)
        else:
            self._far(4).wait()
            add_rows(self.out, 0, self.core_in, 0, self.second_in, 0, h)
            self._far(5).wait()
            add_rows(self.out, h, self.core_in, h, self.second_in, h, h)

    @staticmethod
    def scratch(group, columns):
        return [
            pltpu.VMEM((4 * group, columns), jnp.bfloat16),
            pltpu.VMEM((2 * group, columns), jnp.bfloat16),
            pltpu.VMEM((group, columns), jnp.bfloat16),
        ]


class LineReduce:
    COPIES = 2 * (LINE - 1) * LINE

    def __init__(self, wires, part, rows, landing):
        self.wires, self.part, self.rows, self.landing = wires, part, rows, landing
        self.first = wires.take(self.COPIES)

    def _copy(self, way, hop, block, z):
        number = ((0 if way == 1 else 1) * (LINE - 1) + hop) * LINE + block
        return self.wires.copy(
            self.part.at[pl.ds(block * self.rows, self.rows)],
            self.landing.at[pl.ds(((0 if way == 1 else 1) * LINE + block) * self.rows, self.rows)],
            self.first + number,
            z=z,
        )

    def _moves(self, hop):
        for way in (1, -1):
            source = hop if way == 1 else LINE - 1 - hop
            for block in range(LINE - 1, hop, -1) if way == 1 else range(0, LINE - 1 - hop):
                yield way, block, source

    def start(self, hop):
        z = self.wires.z
        for way, block, source in self._moves(hop):

            @pl.when(z == source)
            def _():
                self._copy(way, hop, block, z + way).start()

    def add(self, hop):
        z, rows = self.wires.z, self.rows
        for way, block, source in self._moves(hop):

            @pl.when(z == source + way)
            def _():
                self._copy(way, hop, block, z).wait_recv()
                place = ((0 if way == 1 else 1) * LINE + block) * rows
                add_rows(
                    self.part, block * rows, self.part, block * rows, self.landing, place, rows
                )

    def finish(self, outs):
        z, rows = self.wires.z, self.rows

        @pl.loop(0, rows // 16)
        def _(step):
            row = pl.multiple_of(z * rows + step * 16, 16)
            begin = 0
            for out in outs:
                out[pl.ds(pl.multiple_of(step * 16, 16), 16), :] = self.part[
                    pl.ds(row, 16), begin : begin + out.shape[1]
                ].astype(out.dtype)
                begin += out.shape[1]

        for hop in range(LINE - 1):
            for way, block, source in self._moves(hop):

                @pl.when(z == source)
                def _():
                    self._copy(way, hop, block, z + way).wait_send()

    @staticmethod
    def scratch(rows, columns):
        return pltpu.VMEM((2 * LINE * rows, columns), jnp.bfloat16)


def sems(count):
    return [pltpu.SemaphoreType.DMA((count,)), pltpu.SemaphoreType.DMA((count,))]


def kernel_params(collective_id, mib):
    return pltpu.CompilerParams(
        collective_id=collective_id, has_side_effects=True, vmem_limit_bytes=mib * MIB
    )


def dot(left, right, left_dim, right_dim):
    return lax.dot_general(
        left, right, (((left_dim,), (right_dim,)), ((), ())), preferred_element_type=jnp.float32
    )


def rows_at(begin, size):
    return pl.ds(pl.multiple_of(begin, 16), size)


def front(w_query, w_key, w_value, gains, w_out, cotangent, gates, tokens, starts, cosine, sine):
    rows, width = w_query.shape
    kv_width = w_key.shape[1] + w_value.shape[1]
    key_width = w_key.shape[1]
    tok_rows = tokens.shape[0]
    keys = LINE * tok_rows
    planes = 8
    group = LINE * rows
    w_rows = planes * group
    score_scale = HD ** (-0.5)
    per_group = HEADS // KVH

    def kernel(
        wq_ref, wk_ref, wv_ref, gains_ref, wo_ref, cot_ref, gate_ref, tok_ref, starts_ref, cos_ref, sin_ref,
        out_q, out_kv, out_o, out_cot, all_gate, query_ref, all_kv, lse_ref, mixed_ref, middle_ref, normed_ref,
        routed_ref, gain_rows_ref,
        full_q, full_kv, full_o, all_cot, bias, value_t, here, there, send, recv,
    ):
        wires = Wires(send, recv)
        dp, z = wires.dp, wires.z
        own = rows_at((dp * LINE + z) * rows, rows)
        locals_ = [
            (wk_ref, full_kv.at[own, pl.ds(0, key_width)]),
            (wv_ref, full_kv.at[own, pl.ds(key_width, kv_width - key_width)]),
            (gains_ref, full_kv.at[own, pl.ds(kv_width, LANES)]),
            (wq_ref, full_q.at[own]),
            (wo_ref, full_o.at[own]),
            (cot_ref, all_cot.at[rows_at(dp * tok_rows, tok_rows)]),
            (gate_ref, all_gate.at[pl.ds(pl.multiple_of(dp * 8, 8), 8)]),
        ]
        locals_ = [pltpu.make_async_copy(a, b, here.at[i]) for i, (a, b) in enumerate(locals_)]
        for one in locals_:
            one.start()
        greet(wires, range(1, planes), True)
        for one in locals_:
            one.wait()

        def block_rows(block):
            return rows_at((dp * LINE + block) * rows, rows)

        line_kv, line_q, line_o = [LineGather(wires, r, block_rows) for r in (full_kv, full_q, full_o)]
        plane_kv, plane_q, plane_o = [PlaneGather(wires, r, group) for r in (full_kv, full_q, full_o)]
        plane_cot = PlaneGather(wires, all_cot, tok_rows)
        line_keys = LineGather(wires, all_kv, lambda block: rows_at(block * tok_rows, tok_rows))
        first = wires.take(planes - 1)

        def gate_copy(mask, owner):
            part = all_gate.at[pl.ds(pl.multiple_of(owner * 8, 8), 8)]
            return wires.copy(part, part, first + mask - 1, dp=masked(dp, mask))

        for step in range(LINE - 1):
            line_kv.start(step)
            line_q.start(step)
            if step == 0:
                for mask in range(1, planes):
                    gate_copy(mask, dp).start()
                key_place = lax.broadcasted_iota(jnp.int32, (keys, tok_rows), 0)
                query_place = lax.broadcasted_iota(jnp.int32, (keys, tok_rows), 1) + z * tok_rows
                allowed = (key_place >= starts_ref[0:1, :]) & (key_place <= query_place)
                bias[...] = jnp.where(allowed, 0.0, masked_score)
            line_kv.wait(step)
            if step == LINE - 2:
                plane_kv.start(0)
            line_q.wait(step)
        plane_q.start(0)
        plane_kv.wait(0)
        plane_kv.start(1)
        line_o.start(0)
        plane_kv.wait(1)
        plane_kv.start(2)
        plane_q.wait(0)
        plane_q.start(1)
        line_o.wait(0)
        line_o.start(1)
        plane_kv.finish()

        gain_rows_ref[...] = full_kv[:, kv_width:].astype(jnp.float32).T[:8, :]
        tile = 32

        @pl.loop(0, tok_rows // tile)
        def _(step):
            cut = pl.ds(pl.multiple_of(step * tile, tile), tile)
            normed_ref[cut, :] = rms_norm(
                tok_ref[cut, :].astype(jnp.float32), gain_rows_ref[0:1, :]
            ).astype(jnp.bfloat16)

        own_keys = rows_at(z * tok_rows, tok_rows)
        pre = dot(normed_ref[...], full_kv[:, :kv_width], 1, 0)
        for pair in range(KVH):
            cut = slice(pair * HD, (pair + 1) * HD)
            all_kv[own_keys, cut] = turned(pre[:, cut], cos_ref[...], sin_ref[...]).astype(jnp.bfloat16)
        all_kv[own_keys, key_width:] = pre[:, key_width:].astype(jnp.bfloat16)
        line_keys.start(0)
        line_o.wait(1)
        line_o.start(2)
        line_keys.wait(0)
        line_keys.start(1)
        line_o.wait(2)
        plane_o.start(0)
        plane_cot.start(0)
        plane_q.wait(1)
        plane_q.start(2)
        plane_o.wait(0)
        plane_o.start(1)
        plane_cot.wait(0)
        plane_cot.start(1)
        plane_q.finish()
        saves = [pltpu.make_async_copy(full_q, out_q, there.at[0])]
        saves.append(pltpu.make_async_copy(full_kv, out_kv, there.at[1]))
        saves[0].start()
        saves[1].start()

        @pl.loop(0, HEADS // 2)
        def _(step):
            wide = pl.ds(pl.multiple_of(step * 2 * HD, 2 * HD), 2 * HD)
            pre_q = dot(normed_ref[...], full_q[:, wide], 1, 0)
            for one in range(2):
                query_ref[:, pl.ds(pl.multiple_of((2 * step + one) * HD, HD), HD)] = turned(
                    pre_q[:, one * HD : (one + 1) * HD], cos_ref[...], sin_ref[...]
                ).astype(jnp.bfloat16)

        line_keys.wait(1)
        line_keys.start(2)
        line_keys.wait(2)
        value_t[...] = all_kv[:, key_width:].astype(jnp.float32).T.astype(jnp.bfloat16)
        lse_ref[...] = jnp.zeros_like(lse_ref)

        @pl.loop(0, HEADS)
        def _(head):
            own_cut = pl.ds(pl.multiple_of(head * HD, HD), HD)
            key_cut = pl.ds(pl.multiple_of((head // per_group) * HD, HD), HD)
            scores = dot(all_kv[:, key_cut], query_ref[:, own_cut], 1, 1) * score_scale + bias[...]
            top = jnp.max(scores, axis=0, keepdims=True)
            expo = jnp.exp(scores - top)
            total = jnp.sum(expo, axis=0, keepdims=True)
            lse_ref[pl.ds(head, 1), :] = top + jnp.log(total)
            probs = (expo * (1.0 / total)).astype(jnp.bfloat16)
            mixed_ref[:, own_cut] = dot(value_t[key_cut, :], probs, 1, 0).T.astype(jnp.bfloat16)

        plane_o.wait(1)
        plane_o.start(2)
        plane_o.finish()
        saves.append(pltpu.make_async_copy(full_o, out_o, there.at[2]))
        saves[2].start()

        @pl.loop(0, width // 512)
        def _(step):
            cut = pl.ds(pl.multiple_of(step * 512, 512), 512)
            middle_ref[:, cut] = tok_ref[:, cut].astype(jnp.float32) + dot(
                mixed_ref[...], full_o[:, cut], 1, 0
            )

        @pl.loop(0, tok_rows // tile)
        def _(step):
            cut = pl.ds(pl.multiple_of(step * tile, tile), tile)
            routed_ref[cut, :] = rms_norm(middle_ref[cut, :], gain_rows_ref[1:2, :]).astype(jnp.bfloat16)

        plane_cot.wait(1)
        plane_cot.start(2)
        plane_cot.finish()
        saves.append(pltpu.make_async_copy(all_cot, out_cot, there.at[3]))
        saves[3].start()
        for mask in range(1, planes):
            gate_copy(mask, masked(dp, mask)).wait_recv()
        for mask in range(1, planes):
            gate_copy(mask, dp).wait_send()
        for one in (line_kv, line_q, line_o, line_keys):
            one.finish()
        for one in saves:
            one.wait()

    f32, low = jnp.float32, jnp.bfloat16
    copies = 4 * LineGather.COPIES + 4 * PlaneGather.COPIES + planes - 1
    return pl.pallas_call(
        kernel,
        out_shape=(
            jax.ShapeDtypeStruct((w_rows, width), low),
            jax.ShapeDtypeStruct((w_rows, kv_width + LANES), low),
            jax.ShapeDtypeStruct((w_rows, width), low),
            jax.ShapeDtypeStruct((planes * tok_rows, width), low),
            jax.ShapeDtypeStruct((planes * 8, tok_rows), f32),
            jax.ShapeDtypeStruct((tok_rows, width), low),
            jax.ShapeDtypeStruct((keys, kv_width), low),
            jax.ShapeDtypeStruct((16, tok_rows), f32),
            jax.ShapeDtypeStruct((tok_rows, width), low),
            jax.ShapeDtypeStruct((tok_rows, width), f32),
            jax.ShapeDtypeStruct((tok_rows, width), low),
            jax.ShapeDtypeStruct((tok_rows, width), low),
            jax.ShapeDtypeStruct((8, width), f32),
        ),
        in_specs=[VMEM] * 11,
        out_specs=(ANY,) * 4 + (VMEM,) * 9,
        scratch_shapes=[
            pltpu.VMEM((w_rows, width), low),
            pltpu.VMEM((w_rows, kv_width + LANES), low),
            pltpu.VMEM((w_rows, width), low),
            pltpu.VMEM((planes * tok_rows, width), low),
            pltpu.VMEM((keys, tok_rows), f32),
            pltpu.VMEM((kv_width - key_width, keys), low),
            pltpu.SemaphoreType.DMA((7,)),
            pltpu.SemaphoreType.DMA((4,)),
        ]
        + sems(copies),
        compiler_params=kernel_params(0, 63),
        name="front",
    )(w_query, w_key, w_value, gains, w_out, cotangent, gates, tokens, starts, cosine, sine)


def experts(routed, all_cot, all_gate, w_gate, w_up, w_down):
    tok_rows, width = routed.shape
    hidden_width = w_gate.shape[1]
    total_rows = 8 * tok_rows

    def kernel(
        routed_ref, cot_ref, gate_ref, wg_ref, wu_ref, wd_ref,
        sums_ref, sent_ref, prod_ref,
        w_in, w_down, x_all, y_all, hidden, grad_hidden, grad_in, sums, gate_t, stage, here, there, send, recv,
    ):
        wires = Wires(send, recv)
        dp = wires.dp
        own = pltpu.make_async_copy(routed_ref, x_all.at[rows_at(dp * tok_rows, tok_rows)], here.at[0])
        loads = [
            pltpu.make_async_copy(cot_ref, y_all, here.at[1]),
            pltpu.make_async_copy(wd_ref, w_down, here.at[2]),
            pltpu.make_async_copy(wg_ref, w_in.at[:, pl.ds(0, hidden_width)], here.at[3]),
            pltpu.make_async_copy(wu_ref, w_in.at[:, pl.ds(hidden_width, hidden_width)], here.at[4]),
        ]
        own.start()
        for one in loads:
            one.start()
        greet(wires, (1, 2, 4), False)
        own.wait()
        spread = PlaneGather(wires, x_all, tok_rows)
        spread.start(0)
        gate_t[...] = gate_ref[...].T
        for one in loads:
            one.wait()

        def gate_of(block):
            lane = lax.broadcasted_iota(jnp.int32, gate_t.shape, 1)
            return jnp.sum(jnp.where(lane == block * 8 + dp, gate_t[...], 0.0), axis=1, keepdims=True)

        def back_hidden(block):
            cut = rows_at(block * tok_rows, tok_rows)
            y_all[cut, :] = (y_all[cut, :].astype(jnp.float32) * gate_of(block)).astype(jnp.bfloat16)
            grad_hidden[cut, :] = dot(y_all[cut, :], w_down[...], 1, 1)

        def through(block):
            cut = rows_at(block * tok_rows, tok_rows)
            acts = dot(x_all[cut, :], w_in[...], 1, 0)
            gate_act, up_act = acts[:, :hidden_width], acts[:, hidden_width:]
            share = jax.nn.sigmoid(gate_act)
            silu = gate_act * share
            hidden[cut, :] = (silu * up_act).astype(jnp.bfloat16)
            grad = grad_hidden[cut, :]
            grad_in[cut, :hidden_width] = (
                grad * up_act * share * (1.0 + gate_act * (1.0 - share))
            ).astype(jnp.bfloat16)
            grad_in[cut, hidden_width:] = (grad * silu).astype(jnp.bfloat16)

        pl.loop(0, 4)(back_hidden)
        spread.wait(0)
        spread.start(1)
        pl.loop(4, 8)(back_hidden)
        through(dp)
        spread.wait(1)
        spread.start(2)
        spread.finish()
        for mask in range(1, 8):
            through(masked(dp, mask))

        @pl.loop(0, width // 256)
        def _(step):
            cut = rows_at(step * 256, 256)
            sums[cut, :] = dot(x_all[:, cut], grad_in[...], 0, 0).astype(jnp.bfloat16)

        @pl.loop(0, hidden_width // 256)
        def _(step):
            cut = rows_at(step * 256, 256)
            out = rows_at(width + step * 256, 256)
            sums[out, :] = dot(hidden[:, cut], y_all[...], 0, 0).astype(jnp.bfloat16)

        save = pltpu.make_async_copy(sums, sums_ref, there.at[0])
        save.start()

        def stage_copy(slot, ref, block):
            return pltpu.make_async_copy(
                stage.at[slot], ref.at[rows_at(block * tok_rows, tok_rows)], there.at[1 + slot]
            )

        for block in range(8):
            slot = block % 2
            cut = rows_at(block * tok_rows, tok_rows)
            if block >= 2:
                stage_copy(slot, sent_ref, block - 2).wait()
            stage[slot] = dot(grad_in[cut, :], w_in[...], 1, 1).astype(jnp.bfloat16)
            stage_copy(slot, sent_ref, block).start()
        for block in range(8):
            slot = block % 2
            cut = rows_at(block * tok_rows, tok_rows)
            stage_copy(slot, sent_ref if block < 2 else prod_ref, (block - 2) % 8).wait()
            made = dot(hidden[cut, :], w_down[...], 1, 0).astype(jnp.bfloat16).astype(jnp.float32)
            stage[slot] = (made * gate_of(block)).astype(jnp.bfloat16)
            stage_copy(slot, prod_ref, block).start()
        stage_copy(0, prod_ref, 6).wait()
        stage_copy(1, prod_ref, 7).wait()
        save.wait()

    f32, low = jnp.float32, jnp.bfloat16
    return pl.pallas_call(
        kernel,
        out_shape=(
            jax.ShapeDtypeStruct((width + hidden_width, width), low),
            jax.ShapeDtypeStruct((total_rows, width), low),
            jax.ShapeDtypeStruct((total_rows, width), low),
        ),
        in_specs=[VMEM, ANY, VMEM, ANY, ANY, ANY],
        out_specs=(ANY,) * 3,
        scratch_shapes=[
            pltpu.VMEM((width, 2 * hidden_width), low),
            pltpu.VMEM((hidden_width, width), low),
            pltpu.VMEM((total_rows, width), low),
            pltpu.VMEM((total_rows, width), low),
            pltpu.VMEM((total_rows, hidden_width), low),
            pltpu.VMEM((total_rows, hidden_width), f32),
            pltpu.VMEM((total_rows, 2 * hidden_width), low),
            pltpu.VMEM((width + hidden_width, width), low),
            pltpu.VMEM((tok_rows, 64), f32),
            pltpu.VMEM((2, tok_rows, width), low),
            pltpu.SemaphoreType.DMA((5,)),
            pltpu.SemaphoreType.DMA((3,)),
        ]
        + sems(PlaneGather.COPIES),
        compiler_params=kernel_params(1, 63),
        name="experts",
    )(routed, all_cot, all_gate, w_gate, w_up, w_down)


class LineSum:
    def __init__(self, wires, own, out, landing, rows, chunks):
        self.wires, self.own, self.out, self.landing = wires, own, out, landing
        self.rows, self.chunks, self.now = rows, chunks, 0
        self.first = wires.take(3 * chunks)
        z = wires.z
        self.inner = (z == 1) | (z == 2)
        self.outer = (z == 0) | (z == 3)
        self.end = 3 * (z - 1)
        self.near = 1 + z // 3
        self.peer = 3 - z

    def _cut(self, ref, chunk):
        return ref.at[pl.ds(pl.multiple_of(chunk * self.rows, 16), self.rows)]

    def _in(self, chunk):
        return self.wires.copy(
            self._cut(self.own, chunk), self._cut(self.out, chunk), self.first + chunk, z=self.near
        )

    def _across(self, chunk):
        number = self.first + self.chunks + chunk
        return self.wires.copy(
            self._cut(self.own, chunk), self._cut(self.landing, chunk), number, z=self.peer
        )

    def _back(self, chunk):
        number = self.first + 2 * self.chunks + chunk
        return self.wires.copy(
            self._cut(self.out, chunk), self._cut(self.out, chunk), number, z=self.end
        )

    def begin(self):
        @pl.when(self.outer)
        def _():
            for chunk in range(min(2, self.chunks)):
                self._in(chunk).start()

    def tick(self, count=1):
        for _ in range(count):
            if self.now <= self.chunks:
                self._tick(self.now)
            self.now += 1

    def _tick(self, chunk):
        if chunk < self.chunks:

            @pl.when(self.outer)
            def _():
                self._in(chunk).wait_send()
                if chunk + 2 < self.chunks:
                    self._in(chunk + 2).start()

        @pl.when(self.inner)
        def _():
            if chunk < self.chunks:
                row = chunk * self.rows
                self._in(chunk).wait_recv()
                add_rows(self.own, row, self.own, row, self.out, row, self.rows)
                self._across(chunk).start()
            if chunk >= 1:
                row = (chunk - 1) * self.rows
                self._across(chunk - 1).wait_recv()
                add_rows(self.out, row, self.own, row, self.landing, row, self.rows)
                self._back(chunk - 1).start()

    def finish(self):
        self.tick(max(0, self.chunks + 1 - self.now))

        @pl.when(self.outer)
        def _():
            @pl.loop(0, self.chunks)
            def _(chunk):
                self._back(chunk).wait_recv()

        @pl.when(self.inner)
        def _():
            @pl.loop(0, self.chunks)
            def _(chunk):
                self._across(chunk).wait_send()
                self._back(chunk).wait_send()


def norm_back(values, gain, grad):
    scale = lax.rsqrt(jnp.mean(values * values, axis=-1, keepdims=True) + epsilon)
    normal = values * scale
    inner = grad * gain
    to_values = scale * (inner - normal * jnp.mean(inner * normal, axis=-1, keepdims=True))
    return to_values, grad * normal


def turned(values, cosine, sine):
    return values * cosine + pltpu.roll(values, HD // 2, 1) * sine


CHUNK = 96
SPLIT = 11


def back_attention(
    sums_in,
    grad_sent,
    full_o,
    middle,
    cotangent,
    gain_moe,
    mixed,
    query,
    all_kv,
    lse,
    starts,
    cosine,
    sine,
):
    tok_rows, width = middle.shape
    keys, kv_width = all_kv.shape
    w_rows = width
    group = w_rows // 8
    chunks = SPLIT

    def kernel(
        sums_ref, sent_ref, full_o_ref, middle_ref, cot_ref, gain_ref, mixed_ref, query_ref, kv_ref, lse_ref,
        starts_ref, cos_ref, sin_ref,
        total_ref, grad_mid_ref, grad_pre_ref, gain_row_ref, w_out_ref,
        sums_own, sums_land, own, core_in, first_in, second_in, routed_grad, attn_low, mixed_grad, part_o, o_core,
        o_first, o_second, bias, key_t, kv_grad, kv_part, kv_land, kv_out, here, send, recv,
    ):
        wires = Wires(send, recv)
        dp, z = wires.dp, wires.z
        loads = [pltpu.make_async_copy(sums_ref.at[pl.ds(0, chunks * CHUNK)], sums_own, here.at[0])]
        for slot in range(4):
            row = pl.multiple_of(masked(dp, 2 * slot) * tok_rows, 16)
            loads.append(
                pltpu.make_async_copy(
                    sent_ref.at[pl.ds(row, tok_rows)],
                    own.at[pl.ds(slot * tok_rows, tok_rows)],
                    here.at[1 + slot],
                )
            )
        for one in loads:
            one.start()
        greet(wires, (1, 2, 4), True)
        summed = LineSum(wires, sums_own, total_ref, sums_land, CHUNK, chunks)
        plane = PlaneReduce(
            wires, sent_ref, tok_rows, own, lambda slot: slot * tok_rows, core_in, first_in, second_in,
            routed_grad,
        )
        dense = PlaneReduce(
            wires, part_o, group, part_o, lambda slot: pl.multiple_of(masked(dp, 2 * slot) * group, 16),
            o_core, o_first, o_second, w_out_ref,
        )
        line = LineReduce(wires, kv_part, tok_rows, kv_land)
        plane.step(0)
        loads[0].wait()
        summed.begin()
        key_place = lax.broadcasted_iota(jnp.int32, (keys, tok_rows), 0)
        query_place = lax.broadcasted_iota(jnp.int32, (keys, tok_rows), 1) + z * tok_rows
        allowed = (key_place >= starts_ref[0:1, :]) & (key_place <= query_place)
        bias[...] = jnp.where(allowed, 0.0, masked_score)
        key_t[...] = kv_ref[:, : kv_width // 2].astype(jnp.float32).T.astype(jnp.bfloat16)
        kv_grad[...] = jnp.zeros_like(kv_grad)
        for one in loads[1:]:
            one.wait()
        plane.step(1)
        plane.step(2)
        summed.tick()
        summed.tick()
        plane.step(3)
        summed.tick()
        plane.step(4)
        summed.tick()
        plane.step(5)

        tile = 32
        gain_row_ref[...] = jnp.zeros_like(gain_row_ref)

        @pl.loop(0, tok_rows // tile)
        def _(step):
            cut = pl.ds(pl.multiple_of(step * tile, tile), tile)
            to_middle, terms = norm_back(middle_ref[cut, :], gain_ref[1:2, :], routed_grad[cut, :])
            to_middle = cot_ref[cut, :].astype(jnp.float32) + to_middle
            grad_mid_ref[cut, :] = to_middle
            attn_low[cut, :] = to_middle.astype(jnp.bfloat16)
            gain_row_ref[0:1, :] += jnp.sum(terms, axis=0, keepdims=True)

        wide = 512

        @pl.loop(0, width // wide)
        def _(step):
            cut = pl.ds(pl.multiple_of(step * wide, wide), wide)
            mixed_grad[:, cut] = dot(attn_low[...], full_o_ref[cut, :], 1, 1).astype(jnp.bfloat16)

        @pl.loop(0, width // 256)
        def _(step):
            cut = pl.ds(pl.multiple_of(step * 256, 256), 256)
            part_o[cut, :] = dot(mixed_ref[:, cut], attn_low[...], 0, 0).astype(jnp.bfloat16)

        dense.step(0)
        summed.tick()
        score_scale = HD ** (-0.5)
        per_group = HEADS // KVH

        def heads(first, last):
            @pl.loop(first, last)
            def _(head):
                own_cut = pl.ds(pl.multiple_of(head * HD, HD), HD)
                pair = head // per_group
                key_cut = pl.ds(pl.multiple_of(pair * HD, HD), HD)
                value_cut = pl.ds(pl.multiple_of((KVH + pair) * HD, HD), HD)
                q, do = query_ref[:, own_cut], mixed_grad[:, own_cut]
                k, v = kv_ref[:, key_cut], kv_ref[:, value_cut]
                scores = dot(k, q, 1, 1) * score_scale + bias[...]
                probs = jnp.exp(scores - lse_ref[pl.ds(head, 1), :])
                grad_probs = dot(v, do, 1, 1)
                inner = jnp.sum(probs * grad_probs, axis=0, keepdims=True)
                grad_raw = (probs * (grad_probs - inner) * score_scale).astype(jnp.bfloat16)
                kv_grad[:, value_cut] += dot(probs.astype(jnp.bfloat16), do, 1, 0)
                kv_grad[:, key_cut] += dot(grad_raw, q, 1, 0)
                to_query = dot(key_t[key_cut, :], grad_raw, 1, 0).T
                grad_pre_ref[:, own_cut] = turned(to_query, cos_ref[...], -sin_ref[...]).astype(
                    jnp.bfloat16
                )

        heads(0, 3)
        dense.step(1)
        dense.step(2)
        summed.tick()
        heads(3, 6)
        dense.step(3)
        summed.tick()
        heads(6, 9)
        dense.step(4)
        summed.tick()
        heads(9, 12)
        kv_part[...] = kv_grad[...].astype(jnp.bfloat16)
        line.start(0)
        dense.step(5)
        summed.tick()
        line.add(0)
        line.start(1)
        summed.tick()
        line.add(1)
        line.start(2)
        summed.tick()
        line.add(2)
        line.finish((kv_out,))
        q_width = HEADS * HD
        for pair in range(KVH):
            cut = slice(pair * HD, (pair + 1) * HD)
            grad_pre_ref[:, q_width + pair * HD : q_width + (pair + 1) * HD] = turned(
                kv_out[:, cut], cos_ref[...], -sin_ref[...]
            ).astype(jnp.bfloat16)
        grad_pre_ref[:, q_width + kv_width // 2 :] = kv_out[:, kv_width // 2 :].astype(jnp.bfloat16)
        summed.finish()

    f32, low = jnp.float32, jnp.bfloat16
    return pl.pallas_call(
        kernel,
        out_shape=(
            jax.ShapeDtypeStruct((chunks * CHUNK, sums_in.shape[1]), low),
            jax.ShapeDtypeStruct((tok_rows, width), f32),
            jax.ShapeDtypeStruct((tok_rows, width + kv_width), low),
            jax.ShapeDtypeStruct((8, width), f32),
            jax.ShapeDtypeStruct((group, width), low),
        ),
        in_specs=[ANY, ANY] + [VMEM] * 11,
        out_specs=(VMEM,) * 5,
        scratch_shapes=[
            pltpu.VMEM((chunks * CHUNK, sums_in.shape[1]), low),
            pltpu.VMEM((chunks * CHUNK, sums_in.shape[1]), low),
            pltpu.VMEM((4 * tok_rows, width), low),
        ]
        + PlaneReduce.scratch(tok_rows, width)
        + [
            pltpu.VMEM((tok_rows, width), f32),
            pltpu.VMEM((tok_rows, width), low),
            pltpu.VMEM((tok_rows, width), low),
            pltpu.VMEM((w_rows, width), low),
        ]
        + PlaneReduce.scratch(group, width)
        + [
            pltpu.VMEM((keys, tok_rows), f32),
            pltpu.VMEM((kv_width // 2, keys), low),
            pltpu.VMEM((keys, kv_width), f32),
            pltpu.VMEM((keys, kv_width), low),
            LineReduce.scratch(tok_rows, kv_width),
            pltpu.VMEM((tok_rows, kv_width), f32),
            pltpu.SemaphoreType.DMA((5,)),
        ]
        + sems(3 * chunks + 2 * PlaneReduce.COPIES + LineReduce.COPIES),
        compiler_params=kernel_params(3, 63),
        name="back_attention",
    )(
        sums_in, grad_sent, full_o, middle, cotangent, gain_moe, mixed, query, all_kv, lse, starts, cosine, sine
    )


def back_dense(sums_in, produced, full_q, full_kv, normed, grad_pre, tokens, gains, grad_mid, gain_row, w_out_part, middle):
    tok_rows, width = middle.shape
    q_width = full_q.shape[1]
    in_width = q_width + full_kv.shape[1]
    pre_width = in_width - LANES
    w_rows = width
    group, rows = w_rows // 8, w_rows // (8 * LINE)
    chunks = sums_in.shape[0] // CHUNK - SPLIT

    def kernel(
        sums_ref, prod_ref, full_q_ref, full_kv_ref, normed_ref, pre_ref, tok_ref, gain_ref, mid_grad_ref, gain_row_ref, o_part_ref,
        middle_ref,
        total_ref, layer_ref, tok_grad_ref, wq_ref, wk_ref, wv_ref, gains_ref, out_ref,
        sums_own, sums_land, own, core_in, first_in, second_in, moe, part, d_core, d_first, d_second, in_sums,
        in_land, o_sums, o_land, normed_grad, gain_rows, here, send, recv,
    ):
        wires = Wires(send, recv)
        dp, z = wires.dp, wires.z
        loads = [
            pltpu.make_async_copy(
                sums_ref.at[pl.ds(SPLIT * CHUNK, chunks * CHUNK)], sums_own, here.at[0]
            )
        ]
        for slot in range(4):
            row = pl.multiple_of(masked(dp, 2 * slot) * tok_rows, 16)
            loads.append(
                pltpu.make_async_copy(
                    prod_ref.at[pl.ds(row, tok_rows)],
                    own.at[pl.ds(slot * tok_rows, tok_rows)],
                    here.at[1 + slot],
                )
            )
        for one in loads:
            one.start()
        greet(wires, (1, 2, 4), True)
        summed = LineSum(wires, sums_own, total_ref, sums_land, CHUNK, chunks)
        dense = PlaneReduce(
            wires, part, group, part, lambda slot: pl.multiple_of(masked(dp, 2 * slot) * group, 16),
            d_core, d_first, d_second, in_sums,
        )
        plane = PlaneReduce(
            wires, prod_ref, tok_rows, own, lambda slot: slot * tok_rows, core_in, first_in, second_in, moe
        )
        o_line = LineReduce(wires, o_sums, rows, o_land)
        in_line = LineReduce(wires, in_sums, rows, in_land)
        loads[0].wait()
        summed.begin()
        o_sums[...] = o_part_ref[...]
        wide = 512

        @pl.loop(0, width // wide)
        def _(step):
            cut = pl.ds(pl.multiple_of(step * wide, wide), wide)
            normed_grad[:, cut] = dot(pre_ref[:, :q_width], full_q_ref[cut, :], 1, 1) + dot(
                pre_ref[:, q_width:], full_kv_ref[cut, : pre_width - q_width], 1, 1
            )

        gain_rows[...] = jnp.zeros_like(gain_rows)
        gain_rows[1:2, :] = gain_row_ref[0:1, :]
        tile = 32

        @pl.loop(0, tok_rows // tile)
        def _(step):
            cut = pl.ds(pl.multiple_of(step * tile, tile), tile)
            to_tokens, terms = norm_back(
                tok_ref[cut, :].astype(jnp.float32), gain_ref[0:1, :], normed_grad[cut, :]
            )
            tok_grad_ref[cut, :] = mid_grad_ref[cut, :] + to_tokens
            gain_rows[0:1, :] += jnp.sum(terms, axis=0, keepdims=True)

        part[:, pre_width:] = gain_rows[...].T.astype(jnp.bfloat16)

        @pl.loop(0, w_rows // 256)
        def _(step):
            cut = pl.ds(pl.multiple_of(step * 256, 256), 256)
            part[cut, :pre_width] = dot(normed_ref[:, cut], pre_ref[...], 0, 0).astype(jnp.bfloat16)

        dense.step(0)
        summed.tick()
        dense.step(1)
        dense.step(2)
        summed.tick()
        for one in loads[1:]:
            one.wait()
        summed.tick()
        dense.step(3)
        plane.step(0)
        summed.tick()
        dense.step(4)
        o_line.start(0)
        summed.tick()
        dense.step(5)
        in_line.start(0)
        plane.step(1)
        plane.step(2)
        o_line.add(0)
        o_line.start(1)
        summed.tick()
        in_line.add(0)
        in_line.start(1)
        plane.step(3)
        summed.tick()
        o_line.add(1)
        o_line.start(2)
        summed.tick()
        in_line.add(1)
        in_line.start(2)
        plane.step(4)
        summed.tick()
        o_line.add(2)
        in_line.add(2)
        plane.step(5)

        @pl.loop(0, tok_rows // tile)
        def _(step):
            cut = pl.ds(pl.multiple_of(step * tile, tile), tile)
            layer_ref[cut, :] = (middle_ref[cut, :] + moe[cut, :]).astype(jnp.bfloat16)

        o_line.finish((out_ref,))
        in_line.finish((wq_ref, wk_ref, wv_ref, gains_ref))
        summed.finish()

    f32, low = jnp.float32, jnp.bfloat16
    return pl.pallas_call(
        kernel,
        out_shape=(
            jax.ShapeDtypeStruct((chunks * CHUNK, sums_in.shape[1]), low),
            jax.ShapeDtypeStruct((tok_rows, width), low),
            jax.ShapeDtypeStruct((tok_rows, width), f32),
            jax.ShapeDtypeStruct((rows, q_width), f32),
            jax.ShapeDtypeStruct((rows, (pre_width - q_width) // 2), f32),
            jax.ShapeDtypeStruct((rows, (pre_width - q_width) // 2), f32),
            jax.ShapeDtypeStruct((rows, LANES), f32),
            jax.ShapeDtypeStruct((rows, width), f32),
        ),
        in_specs=[ANY, ANY] + [VMEM] * 10,
        out_specs=(VMEM,) * 8,
        scratch_shapes=[
            pltpu.VMEM((chunks * CHUNK, sums_in.shape[1]), low),
            pltpu.VMEM((chunks * CHUNK, sums_in.shape[1]), low),
            pltpu.VMEM((4 * tok_rows, width), low),
        ]
        + PlaneReduce.scratch(tok_rows, width)
        + [pltpu.VMEM((tok_rows, width), f32), pltpu.VMEM((w_rows, in_width), low)]
        + PlaneReduce.scratch(group, in_width)
        + [
            pltpu.VMEM((group, in_width), low),
            LineReduce.scratch(rows, in_width),
            pltpu.VMEM((group, width), low),
            LineReduce.scratch(rows, width),
            pltpu.VMEM((tok_rows, width), f32),
            pltpu.VMEM((LANES, width), f32),
            pltpu.SemaphoreType.DMA((5,)),
        ]
        + sems(3 * chunks + 2 * PlaneReduce.COPIES + 2 * LineReduce.COPIES),
        compiler_params=kernel_params(4, 63),
        name="back_dense",
    )(
        sums_in, produced, full_q, full_kv, normed, grad_pre, tokens, gains, grad_mid, gain_row, w_out_part, middle
    )


def on_plane_device(
    tokens,
    norm_attn,
    w_query,
    w_key,
    w_value,
    w_out,
    norm_moe,
    w_gate,
    w_up,
    w_down,
    routes,
    gate_values,
    lengths,
    cotangent,
):
    tok_rows = tokens.shape[0]
    ctx_size = lax.axis_size("ctx")
    ctx_place = lax.axis_index("ctx")
    group_places = jnp.arange(tok_rows * ctx_size, dtype=jnp.int32)
    seg_all, within_all = seq_tables(lengths[0], group_places)
    offset = ctx_place * tok_rows
    own_places = offset + jnp.arange(tok_rows, dtype=jnp.int32)
    within_own = lax.dynamic_slice_in_dim(within_all, offset, tok_rows)
    kv_columns = KVH * HD
    q_columns = HEADS * HD
    gains = jnp.pad(jnp.stack([norm_attn, norm_moe], axis=1), ((0, 0), (0, LANES - 2)))
    numbers = jnp.arange(8, dtype=jnp.int32)
    gates = jnp.sum(
        jnp.where(routes[None, :, :] == numbers[:, None, None], gate_values[None], 0.0), axis=2
    )
    half_size = HD // 2
    frequency = rope_base ** (-jnp.arange(half_size, dtype=jnp.float32) / half_size)
    angles = within_own.astype(jnp.float32)[:, None] * frequency[None, :]
    cosine = jnp.concatenate([jnp.cos(angles), jnp.cos(angles)], axis=1)
    sine = jnp.concatenate([-jnp.sin(angles), jnp.sin(angles)], axis=1)
    starts = jnp.broadcast_to((own_places - within_own)[None, :], (8, tok_rows))
    (
        full_q, full_kv, full_o, all_cot, all_gate, query, all_kv, lse, mixed_low, middle, normed_low, routed_low,
        gain_rows,
    ) = front(
        w_query, w_key, w_value, gains, w_out, cotangent, gates, tokens, starts, cosine, sine
    )
    partial_sums, grad_sent, produced = experts(
        routed_low, all_cot, all_gate, w_gate[0], w_up[0], w_down[0]
    )
    half = w_gate.shape[2]
    sums_head, grad_mid, grad_pre, gain_row, w_out_part = back_attention(
        partial_sums,
        grad_sent,
        full_o,
        middle,
        cotangent,
        gain_rows,
        mixed_low,
        query,
        all_kv,
        lse,
        starts,
        cosine,
        sine,
    )
    sums_tail, layer_out, grad_tokens, sum_q, sum_k, sum_v, sum_gains, sum_o = back_dense(
        partial_sums,
        produced,
        full_q,
        full_kv,
        normed_low,
        grad_pre,
        tokens,
        gain_rows,
        grad_mid,
        gain_row,
        w_out_part,
        middle,
    )
    in_tail = D - sums_head.shape[0]

    def whole(columns):
        return jnp.concatenate([sums_head[:, columns], sums_tail[:in_tail, columns]], axis=0)

    return (
        layer_out,
        grad_tokens,
        sum_gains[:, 0],
        sum_q,
        sum_k,
        sum_v,
        sum_o,
        sum_gains[:, 1],
        whole(slice(0, half)).astype(jnp.float32)[None],
        whole(slice(half, 2 * half)).astype(jnp.float32)[None],
        sums_tail[in_tail:].astype(jnp.float32)[None],
    )


def solution(mesh):
    on_plane = mesh.shape["dp"] == 8 and mesh.shape["ctx"] == LINE
    return jax.shard_map(
        on_plane_device if on_plane else on_device,
        mesh=mesh,
        in_specs=(
            P(("dp", "ctx"), None),
            P(("dp", "ctx")),
            P(("dp", "ctx"), None),
            P(("dp", "ctx"), None),
            P(("dp", "ctx"), None),
            P(("dp", "ctx"), None),
            P(("dp", "ctx")),
            P("dp", None, None),
            P("dp", None, None),
            P("dp", None, None),
            P(("dp", "ctx"), None),
            P(("dp", "ctx"), None),
            P("dp", None),
            P(("dp", "ctx"), None),
        ),
        out_specs=(
            P(("dp", "ctx"), None),
            P(("dp", "ctx"), None),
            P(("dp", "ctx")),
            P(("dp", "ctx"), None),
            P(("dp", "ctx"), None),
            P(("dp", "ctx"), None),
            P(("dp", "ctx"), None),
            P(("dp", "ctx")),
            P("dp", None, None),
            P("dp", None, None),
            P("dp", None, None),
        ),
        check_vma=False,
    )
```

```python
import functools

import jax
import jax.numpy as jnp
from jax import lax
from jax.experimental import pallas as pl
from jax.experimental.pallas import tpu as pltpu
from jax.sharding import PartitionSpec as P

D = 1536
HEADS = 12
KVH = 2
HD = 128
TOP = 4
EXP_DEV = 1


epsilon = 1e-06
rope_base = 1000000.0
masked_score = -1e30


def rms_norm(values, gain):
    return values * lax.rsqrt(jnp.mean(values * values, axis=-1, keepdims=True) + epsilon) * gain


def rotate(values, within, direction):
    half_size = values.shape[-1] // 2
    frequency = rope_base ** (-jnp.arange(half_size, dtype=jnp.float32) / half_size)
    angles = direction * within.astype(jnp.float32)[:, None] * frequency[None, :]
    cosine = jnp.cos(angles)[:, None, :]
    sine = jnp.sin(angles)[:, None, :]
    first_half = values[..., :half_size]
    second = values[..., half_size:]
    return jnp.concatenate(
        [first_half * cosine - second * sine, second * cosine + first_half * sine], axis=-1
    )


def seq_tables(length_row, places):
    seq_ends = jnp.cumsum(length_row)
    passed = places[:, None] >= seq_ends[None, :]
    segment = jnp.sum(passed.astype(jnp.int32), axis=1)
    within = places - jnp.sum(jnp.where(passed, length_row[None, :], 0), axis=1)
    return (segment, within)


def collect_weights(gain_attn, w_query, w_key, w_value, w_out, gain_moe):
    return (
        lax.all_gather(gain_attn, ("dp", "ctx"), axis=0, tiled=True),
        lax.all_gather(w_query, ("dp", "ctx"), axis=0, tiled=True),
        lax.all_gather(w_key, ("dp", "ctx"), axis=0, tiled=True),
        lax.all_gather(w_value, ("dp", "ctx"), axis=0, tiled=True),
        lax.all_gather(w_out, ("dp", "ctx"), axis=0, tiled=True),
        lax.all_gather(gain_moe, ("dp", "ctx"), axis=0, tiled=True),
    )


def spread_grads(grad_gain_attn, grad_query, grad_key, grad_value, grad_outp, grad_gain_moe):
    return (
        lax.psum_scatter(grad_gain_attn, ("dp", "ctx"), scatter_dimension=0, tiled=True),
        lax.psum_scatter(grad_query, ("dp", "ctx"), scatter_dimension=0, tiled=True),
        lax.psum_scatter(grad_key, ("dp", "ctx"), scatter_dimension=0, tiled=True),
        lax.psum_scatter(grad_value, ("dp", "ctx"), scatter_dimension=0, tiled=True),
        lax.psum_scatter(grad_outp, ("dp", "ctx"), scatter_dimension=0, tiled=True),
        lax.psum_scatter(grad_gain_moe, ("dp", "ctx"), scatter_dimension=0, tiled=True),
    )


def on_device(
    tokens,
    norm_attn,
    w_query,
    w_key,
    w_value,
    w_out,
    norm_moe,
    w_gate,
    w_up,
    w_down,
    routes,
    gate_values,
    lengths,
    cotangent,
):
    tok_rows = tokens.shape[0]
    ctx_size = lax.axis_size("ctx")
    dp_size = lax.axis_size("dp")
    ctx_place = lax.axis_index("ctx")
    group_rows = tok_rows * ctx_size
    group_places = jnp.arange(group_rows, dtype=jnp.int32)
    seg_all, within_all = seq_tables(lengths[0], group_places)
    offset = ctx_place * tok_rows
    own_places = offset + jnp.arange(tok_rows, dtype=jnp.int32)
    seg_own = lax.dynamic_slice_in_dim(seg_all, offset, tok_rows)
    within_own = lax.dynamic_slice_in_dim(within_all, offset, tok_rows)
    allowed = (seg_own[:, None] == seg_all[None, :]) & (
        group_places[None, :] <= own_places[:, None]
    )
    gain_attn, full_q, full_k, full_v, full_o, gain_moe = collect_weights(
        norm_attn, w_query, w_key, w_value, w_out, norm_moe
    )
    gain_attn_f = gain_attn.astype(jnp.float32)
    gain_moe_f = gain_moe.astype(jnp.float32)
    inputs = tokens.astype(jnp.float32)
    normed_low = rms_norm(inputs, gain_attn_f).astype(jnp.bfloat16)
    query_pre = jnp.dot(normed_low, full_q, preferred_element_type=jnp.float32)
    key_pre = jnp.dot(normed_low, full_k, preferred_element_type=jnp.float32)
    value_pre = jnp.dot(normed_low, full_v, preferred_element_type=jnp.float32)
    query = rotate(query_pre.reshape(tok_rows, HEADS, HD), within_own, 1.0).astype(jnp.bfloat16)
    key_low = rotate(key_pre.reshape(tok_rows, KVH, HD), within_own, 1.0).astype(jnp.bfloat16)
    key_low = key_low.reshape(tok_rows, KVH * HD)
    value_low = value_pre.astype(jnp.bfloat16)
    all_keys, all_values = (
        lax.all_gather(key_low, "ctx", axis=0, tiled=True),
        lax.all_gather(value_low, "ctx", axis=0, tiled=True),
    )
    per_group = HEADS // KVH
    score_scale = HD ** (-0.5)
    query_groups = query.reshape(tok_rows, KVH, per_group, HD)

    def softmax_weights(group_number):
        keys_part = all_keys[:, group_number * HD : (group_number + 1) * HD]
        raw = jnp.einsum(
            "qjd,kd->jqk",
            query_groups[:, group_number],
            keys_part,
            preferred_element_type=jnp.float32,
        )
        scores = jnp.where(allowed[None], raw * score_scale, masked_score)
        row_top = jnp.max(scores, axis=-1, keepdims=True)
        expo = jnp.exp(scores - row_top)
        return expo / jnp.sum(expo, axis=-1, keepdims=True)

    mixed_parts = []
    for group_number in range(KVH):
        probs = softmax_weights(group_number)
        values_part = all_values[:, group_number * HD : (group_number + 1) * HD]
        mixed_group = jnp.einsum(
            "jqk,kd->qjd",
            probs.astype(jnp.bfloat16),
            values_part,
            preferred_element_type=jnp.float32,
        )
        mixed_parts.append(mixed_group.reshape(tok_rows, per_group * HD))
    mixed_low = jnp.concatenate(mixed_parts, axis=1).astype(jnp.bfloat16)
    middle = inputs + jnp.dot(mixed_low, full_o, preferred_element_type=jnp.float32)
    routed_low = rms_norm(middle, gain_moe_f).astype(jnp.bfloat16)
    experts_total = EXP_DEV * dp_size
    capacity = 3 * TOP * tok_rows // (2 * experts_total)
    assign_count = tok_rows * TOP
    flat_ids = routes.reshape(assign_count)
    onehot = (flat_ids[:, None] == jnp.arange(experts_total, dtype=jnp.int32)[None, :]).astype(
        jnp.int32
    )
    earlier = jnp.sum((jnp.cumsum(onehot, axis=0) - onehot) * onehot, axis=1)
    slot_index = flat_ids * capacity + earlier
    owner = (
        jnp.full((experts_total * capacity,), assign_count, jnp.int32)
        .at[slot_index]
        .set(jnp.arange(assign_count, dtype=jnp.int32))
    )
    padded = jnp.concatenate([routed_low, jnp.zeros((1, D), jnp.bfloat16)], axis=0)
    outgoing = padded[owner // TOP].reshape(experts_total, capacity, D)
    arrived = lax.all_to_all(outgoing, "dp", split_axis=0, concat_axis=0, tiled=True)
    arrived_sets = arrived.reshape(dp_size, EXP_DEV, capacity, D)
    gate_act = jnp.einsum(
        "secd,edf->secf", arrived_sets, w_gate, preferred_element_type=jnp.float32
    )
    up_act = jnp.einsum("secd,edf->secf", arrived_sets, w_up, preferred_element_type=jnp.float32)
    hidden_low = (jax.nn.silu(gate_act) * up_act).astype(jnp.bfloat16)
    produced = jnp.einsum("secf,efd->secd", hidden_low, w_down, preferred_element_type=jnp.float32)
    produced = produced.astype(jnp.bfloat16).reshape(experts_total, capacity, D)
    returned = lax.all_to_all(produced, "dp", split_axis=0, concat_axis=0, tiled=True)
    picked = returned.reshape(experts_total * capacity, D)[slot_index].reshape(tok_rows, TOP, D)
    moe_out = jnp.sum(picked.astype(jnp.float32) * gate_values[:, :, None], axis=1)
    layer_out = (middle + moe_out).astype(jnp.bfloat16)
    grad_out = cotangent.astype(jnp.float32)
    grad_assign = (grad_out[:, None, :] * gate_values[:, :, None]).astype(jnp.bfloat16)
    grad_padded = jnp.concatenate(
        [grad_assign.reshape(assign_count, D), jnp.zeros((1, D), jnp.bfloat16)], axis=0
    )
    grad_slots = grad_padded[owner].reshape(experts_total, capacity, D)
    grad_arrived = lax.all_to_all(grad_slots, "dp", split_axis=0, concat_axis=0, tiled=True)
    grad_arrived = grad_arrived.reshape(dp_size, EXP_DEV, capacity, D)
    grad_hidden = jnp.einsum(
        "secd,efd->secf", grad_arrived, w_down, preferred_element_type=jnp.float32
    )
    grad_w_down = jnp.einsum(
        "secf,secd->efd", hidden_low, grad_arrived, preferred_element_type=jnp.float32
    )
    glu_value, glu_pull = jax.vjp(
        lambda gate_in, up_in: jax.nn.silu(gate_in) * up_in, gate_act, up_act
    )
    grad_gate, grad_up = glu_pull(grad_hidden)
    grad_gate_low = grad_gate.astype(jnp.bfloat16)
    grad_up_low = grad_up.astype(jnp.bfloat16)
    grad_w_gate = jnp.einsum(
        "secd,secf->edf", arrived_sets, grad_gate_low, preferred_element_type=jnp.float32
    )
    grad_w_up = jnp.einsum(
        "secd,secf->edf", arrived_sets, grad_up_low, preferred_element_type=jnp.float32
    )
    grad_sent = jnp.einsum(
        "secf,edf->secd", grad_gate_low, w_gate, preferred_element_type=jnp.float32
    ) + jnp.einsum("secf,edf->secd", grad_up_low, w_up, preferred_element_type=jnp.float32)
    grad_sent = grad_sent.astype(jnp.bfloat16).reshape(experts_total, capacity, D)
    grad_back = lax.all_to_all(grad_sent, "dp", split_axis=0, concat_axis=0, tiled=True)
    grad_picked = grad_back.reshape(experts_total * capacity, D)[slot_index].reshape(
        tok_rows, TOP, D
    )
    grad_routed = jnp.sum(grad_picked.astype(jnp.float32), axis=1)
    expert_sums = (
        lax.psum(grad_w_gate.astype(jnp.bfloat16), "ctx").astype(jnp.float32),
        lax.psum(grad_w_up.astype(jnp.bfloat16), "ctx").astype(jnp.float32),
        lax.psum(grad_w_down.astype(jnp.bfloat16), "ctx").astype(jnp.float32),
    )
    norm_value, moe_pull = jax.vjp(rms_norm, middle, gain_moe_f)
    grad_mid_norm, grad_gain_moe = moe_pull(grad_routed)
    grad_middle = grad_out + grad_mid_norm
    grad_attn_low = grad_middle.astype(jnp.bfloat16)
    grad_w_out = jnp.einsum(
        "th,td->hd", mixed_low, grad_attn_low, preferred_element_type=jnp.float32
    )
    grad_mixed_low = jnp.einsum(
        "td,hd->th", grad_attn_low, full_o, preferred_element_type=jnp.float32
    ).astype(jnp.bfloat16)
    grad_mixed_groups = grad_mixed_low.reshape(tok_rows, KVH, per_group, HD)
    grad_query_parts = []
    prob_parts = []
    score_parts = []
    for group_number in range(KVH):
        probs = softmax_weights(group_number)
        keys_part = all_keys[:, group_number * HD : (group_number + 1) * HD]
        values_part = all_values[:, group_number * HD : (group_number + 1) * HD]
        grad_probs = jnp.einsum(
            "qjd,kd->jqk",
            grad_mixed_groups[:, group_number],
            values_part,
            preferred_element_type=jnp.float32,
        )
        grad_scores = probs * (grad_probs - jnp.sum(probs * grad_probs, axis=-1, keepdims=True))
        grad_raw_low = (grad_scores * score_scale).astype(jnp.bfloat16)
        grad_query_parts.append(
            jnp.einsum("jqk,kd->qjd", grad_raw_low, keys_part, preferred_element_type=jnp.float32)
        )
        prob_parts.append(probs.astype(jnp.bfloat16))
        score_parts.append(grad_raw_low)
    grad_query_rot = jnp.stack(grad_query_parts, axis=1).reshape(tok_rows, HEADS, HD)
    key_pieces = []
    value_pieces = []
    for group_number in range(KVH):
        score_piece = score_parts[group_number]
        prob_piece = prob_parts[group_number]
        key_pieces.append(
            jnp.einsum(
                "jqk,qjd->kd",
                score_piece,
                query_groups[:, group_number],
                preferred_element_type=jnp.float32,
            )
        )
        value_pieces.append(
            jnp.einsum(
                "jqk,qjd->kd",
                prob_piece,
                grad_mixed_groups[:, group_number],
                preferred_element_type=jnp.float32,
            )
        )
    key_value_grads = lax.psum_scatter(
        jnp.concatenate(key_pieces + value_pieces, axis=1).astype(jnp.bfloat16),
        "ctx",
        scatter_dimension=0,
        tiled=True,
    ).astype(jnp.float32)
    grad_query_low = (
        rotate(grad_query_rot, within_own, -1.0).astype(jnp.bfloat16).reshape(tok_rows, HEADS * HD)
    )
    grad_key_rot = key_value_grads[:, : KVH * HD].reshape(tok_rows, KVH, HD)
    grad_key_low = (
        rotate(grad_key_rot, within_own, -1.0).astype(jnp.bfloat16).reshape(tok_rows, KVH * HD)
    )
    grad_value_low = key_value_grads[:, KVH * HD :].astype(jnp.bfloat16)
    grad_w_query = jnp.einsum(
        "td,th->dh", normed_low, grad_query_low, preferred_element_type=jnp.float32
    )
    grad_w_key = jnp.einsum(
        "td,th->dh", normed_low, grad_key_low, preferred_element_type=jnp.float32
    )
    grad_w_value = jnp.einsum(
        "td,th->dh", normed_low, grad_value_low, preferred_element_type=jnp.float32
    )
    grad_normed = (
        jnp.einsum("th,dh->td", grad_query_low, full_q, preferred_element_type=jnp.float32)
        + jnp.einsum("th,dh->td", grad_key_low, full_k, preferred_element_type=jnp.float32)
        + jnp.einsum("th,dh->td", grad_value_low, full_v, preferred_element_type=jnp.float32)
    )
    first_value, attn_pull = jax.vjp(rms_norm, inputs, gain_attn_f)
    grad_inputs, grad_gain_attn = attn_pull(grad_normed)
    grad_tokens = grad_middle + grad_inputs
    dense_sums = spread_grads(
        grad_gain_attn, grad_w_query, grad_w_key, grad_w_value, grad_w_out, grad_gain_moe
    )
    return (
        layer_out,
        grad_tokens,
        dense_sums[0],
        dense_sums[1],
        dense_sums[2],
        dense_sums[3],
        dense_sums[4],
        dense_sums[5],
        expert_sums[0],
        expert_sums[1],
        expert_sums[2],
    )


MESH = pl.DeviceIdType.MESH
LANES = 128
MIB = 2**20
ANY = pl.BlockSpec(memory_space=pl.ANY)
VMEM = pl.BlockSpec(memory_space=pltpu.VMEM)


def flip(index, bit):
    return index + bit - 2 * bit * ((index // bit) % 2)


def masked(index, mask):
    for bit in (1, 2, 4):
        if mask & bit:
            index = flip(index, bit)
    return index


class Wires:
    def __init__(self, send, recv):
        self.send, self.recv, self.used = send, recv, 0
        self.dp, self.z = lax.axis_index("dp"), lax.axis_index("ctx")

    def take(self, count):
        first = self.used
        self.used += count
        return first

    def copy(self, src, dst, number, dp=None, z=None):
        return pltpu.make_async_remote_copy(
            src_ref=src,
            dst_ref=dst,
            send_sem=self.send.at[number],
            recv_sem=self.recv.at[number],
            device_id=(self.dp if dp is None else dp, self.z if z is None else z),
            device_id_type=MESH,
        )


def greet(wires, masks, line):
    barrier = pltpu.get_barrier_semaphore()
    dp, z = wires.dp, wires.z
    for mask in masks:
        pl.semaphore_signal(barrier, inc=1, device_id=(masked(dp, mask), z), device_id_type=MESH)
    for step in range(1, LINE) if line else ():
        pl.semaphore_signal(
            barrier, inc=1, device_id=(dp, lax.rem(z + step, LINE)), device_id_type=MESH
        )
    pl.semaphore_wait(barrier, len(masks) + (LINE - 1 if line else 0))


LINE = 4


class LineGather:
    COPIES = 2 * (LINE - 1)

    def __init__(self, wires, ref, rows_of):
        self.wires, self.ref, self.rows_of = wires, ref, rows_of
        self.first = wires.take(self.COPIES)

    def _copy(self, block, number, z):
        part = self.ref.at[self.rows_of(block)]
        return self.wires.copy(part, part, self.first + number, z=z)

    def start(self, step):
        z = self.wires.z

        @pl.when((z >= step) & (z < LINE - 1))
        def _():
            self._copy(z - step, step, z + 1).start()

        @pl.when((z + step < LINE) & (z > 0))
        def _():
            self._copy(z + step, LINE - 1 + step, z - 1).start()

    def wait(self, step):
        z = self.wires.z

        @pl.when(z - 1 - step >= 0)
        def _():
            self._copy(z - 1 - step, step, z).wait_recv()

        @pl.when(z + 1 + step < LINE)
        def _():
            self._copy(z + 1 + step, LINE - 1 + step, z).wait_recv()

    def finish(self):
        z = self.wires.z
        for step in range(LINE - 1):

            @pl.when((z >= step) & (z < LINE - 1))
            def _():
                self._copy(z - step, step, z + 1).wait_send()

            @pl.when((z + step < LINE) & (z > 0))
            def _():
                self._copy(z + step, LINE - 1 + step, z - 1).wait_send()


class PlaneGather:
    CHIP = (((2, 0, 0), (4, 0, 1)), ((4, 0, 0), (2, 0, 1)), ((4, 2, 0), (2, 4, 1)))
    CORE = (
        ((1, 0, 2),),
        ((1, 2, 0), (1, 4, 1)),
        ((1, 4, 0), (1, 2, 1)),
        ((1, 6, 0), (1, 6, 1)),
    )
    COPIES = 13

    def __init__(self, wires, ref, group):
        self.wires, self.ref, self.group = wires, ref, group
        first = wires.take(self.COPIES)
        self.number = {}
        for stage in self.CHIP + self.CORE:
            for one in stage:
                self.number[one] = first + len(self.number)
        self.core_left = [0, 1, 2, 3]

    def _copy(self, one, from_me):
        to, whose, half = one
        dp = self.wires.dp
        sender = dp if from_me else masked(dp, to)
        owner = masked(sender, whose)
        size = self.group if half == 2 else self.group // 2
        begin = owner * self.group + (self.group // 2 if half == 1 else 0)
        part = self.ref.at[pl.ds(pl.multiple_of(begin, 16), size)]
        return self.wires.copy(part, part, self.number[one], dp=masked(dp, to))

    def start(self, stage, far=True):
        for one in (self.CHIP[stage] if stage < 2 else ()) + self.CORE[stage]:
            self._copy(one, True).start()
        if stage == 1 and far:
            self.start_far()

    def start_far(self):
        for one in self.CHIP[2]:
            self._copy(one, True).start()

    def wait(self, stage):
        for one in self.CHIP[stage]:
            self._copy(one, False).wait_recv()

    def wait_core(self, stage):
        self.core_left.remove(stage)
        for one in self.CORE[stage]:
            self._copy(one, False).wait_recv()

    def finish(self):
        for stage in list(self.core_left):
            self.wait_core(stage)
        for one in self.number:
            self._copy(one, True).wait_send()


def add_rows(out, out_row, left, left_row, right, right_row, rows):
    @pl.loop(0, rows // 16)
    def _(step):
        def cut(row):
            return pl.ds(pl.multiple_of(row + step * 16, 16), 16)

        out[cut(out_row), :] = (
            left[cut(left_row), :].astype(jnp.float32) + right[cut(right_row), :].astype(jnp.float32)
        ).astype(out.dtype)


class PlaneReduce:
    COPIES = 10
    STEPS = 6

    def __init__(self, wires, part, group, own, own_row, core_in, first_in, second_in, out):
        self.wires, self.part, self.group, self.half = wires, part, group, group // 2
        self.own, self.own_row, self.out = own, own_row, out
        self.core_in, self.first_in, self.second_in = core_in, first_in, second_in
        self.first = wires.take(self.COPIES)

    def _send(self, src, src_row, dst, dst_row, rows, number, to):
        return self.wires.copy(
            src.at[pl.ds(src_row, rows)],
            dst.at[pl.ds(dst_row, rows)],
            self.first + number,
            dp=masked(self.wires.dp, to),
        )

    def _core(self, slot):
        row = pl.multiple_of(masked(self.wires.dp, 1 + 2 * slot) * self.group, 16)
        return self._send(self.part, row, self.core_in, slot * self.group, self.group, slot, 1)

    def _far(self, number):
        g, h = self.group, self.half
        src_row, dst, dst_row, to = (
            (3 * g, self.first_in, h, 4),
            (3 * g + h, self.first_in, 3 * h, 2),
            (2 * g, self.first_in, 0, 4),
            (1 * g + h, self.first_in, 2 * h, 2),
            (1 * g, self.second_in, 0, 2),
            (2 * g + h, self.second_in, h, 4),
        )[number]
        return self._send(self.core_in, src_row, dst, dst_row, h, 4 + number, to)

    def _sum_core(self, slot):
        self._core(slot).wait()
        row = slot * self.group
        add_rows(self.core_in, row, self.own, self.own_row(slot), self.core_in, row, self.group)

    def _sum_far(self, number, row, in_row):
        self._far(number).wait()
        add_rows(self.core_in, row, self.core_in, row, self.first_in, in_row, self.half)

    def start_core(self, slot):
        self._core(slot).start()

    def step(self, number):
        g, h = self.group, self.half
        if number == 0:
            for slot in (3, 2, 1, 0):
                self.start_core(slot)
        elif number == 1:
            self._sum_core(3)
            self._far(0).start()
            self._far(1).start()
        elif number == 2:
            self._sum_core(2)
            self._far(2).start()
            self._sum_core(1)
            self._far(3).start()
            self._sum_core(0)
        elif number == 3:
            self._sum_far(0, 1 * g, h)
            self._far(4).start()
            self._sum_far(1, 2 * g + h, 3 * h)
            self._far(5).start()
        elif number == 4:
            self._sum_far(2, 0, 0)
            self._sum_far(3, h, 2 * h)
        else:
            self._far(4).wait()
            add_rows(self.out, 0, self.core_in, 0, self.second_in, 0, h)
            self._far(5).wait()
            add_rows(self.out, h, self.core_in, h, self.second_in, h, h)

    @staticmethod
    def scratch(group, columns):
        return [
            pltpu.VMEM((4 * group, columns), jnp.bfloat16),
            pltpu.VMEM((2 * group, columns), jnp.bfloat16),
            pltpu.VMEM((group, columns), jnp.bfloat16),
        ]


class LineReduce:
    COPIES = 2 * (LINE - 1) * LINE
    EVENTS = ((0, 0), (0, 1), (1, 0), (0, 2), (1, 1), (2, 0))

    def __init__(self, wires, part, rows, landing, ways=(1, -1)):
        self.wires, self.part, self.rows, self.landing, self.ways = wires, part, rows, landing, ways
        self.first = wires.take(self.COPIES)

    def _place(self, way, hop, nearer):
        return (LINE - 1 - nearer, hop) if way == 1 else (nearer, LINE - 1 - hop)

    def _copy(self, way, hop, nearer, z):
        side = self.ways.index(way)
        block, _ = self._place(way, hop, nearer)
        return self.wires.copy(
            self.part.at[pl.ds(block * self.rows, self.rows)],
            self.landing.at[pl.ds((side * LINE + block) * self.rows, self.rows)],
            self.first + (side * (LINE - 1) + hop) * LINE + nearer,
            z=z,
        )

    def _send(self, way, hop, nearer):
        z = self.wires.z

        @pl.when(z == self._place(way, hop, nearer)[1])
        def _():
            self._copy(way, hop, nearer, z + way).start()

    def begin(self):
        for nearer in range(LINE - 1):
            for way in self.ways:
                self._send(way, 0, nearer)

    def event(self, number):
        hop, nearer = self.EVENTS[number]
        z, rows = self.wires.z, self.rows
        for way in self.ways:
            block, source = self._place(way, hop, nearer)

            @pl.when(z == source + way)
            def _():
                self._copy(way, hop, nearer, z).wait_recv()
                landed = (self.ways.index(way) * LINE + block) * rows
                add_rows(
                    self.part, block * rows, self.part, block * rows, self.landing, landed, rows
                )
                if nearer < LINE - 2 - hop:
                    self._copy(way, hop + 1, nearer, z + way).start()

    def finish(self, outs):
        z, rows = self.wires.z, self.rows

        @pl.loop(0, rows // 16)
        def _(step):
            row = pl.multiple_of(z * rows + step * 16, 16)
            begin = 0
            for out in outs:
                out[pl.ds(pl.multiple_of(step * 16, 16), 16), :] = self.part[
                    pl.ds(row, 16), begin : begin + out.shape[1]
                ].astype(out.dtype)
                begin += out.shape[1]

        for hop, nearer in self.EVENTS:
            for way in self.ways:

                @pl.when(z == self._place(way, hop, nearer)[1])
                def _():
                    self._copy(way, hop, nearer, z + way).wait_send()

    @staticmethod
    def scratch(rows, columns, ways=2):
        return pltpu.VMEM((ways * LINE * rows, columns), jnp.bfloat16)


def sems(count):
    return [pltpu.SemaphoreType.DMA((count,)), pltpu.SemaphoreType.DMA((count,))]


def kernel_params(collective_id, mib):
    return pltpu.CompilerParams(
        collective_id=collective_id, has_side_effects=True, vmem_limit_bytes=mib * MIB
    )


def dot(left, right, left_dim, right_dim):
    return lax.dot_general(
        left, right, (((left_dim,), (right_dim,)), ((), ())), preferred_element_type=jnp.float32
    )


def rows_at(begin, size):
    return pl.ds(pl.multiple_of(begin, 16), size)


def front(w_query, w_key, w_value, gains, w_out, cotangent, gates, tokens, starts, cosine, sine):
    rows, width = w_query.shape
    kv_width = w_key.shape[1] + w_value.shape[1]
    key_width = w_key.shape[1]
    tok_rows = tokens.shape[0]
    keys = LINE * tok_rows
    planes = 8
    group = LINE * rows
    w_rows = planes * group
    score_scale = HD ** (-0.5)
    per_group = HEADS // KVH

    def kernel(
        wq_ref, wk_ref, wv_ref, gains_ref, wo_ref, cot_ref, gate_ref, tok_ref, starts_ref, cos_ref, sin_ref,
        out_q, out_kv, out_o, out_cot, all_gate, query_ref, all_kv, lse_ref, mixed_ref, middle_ref, normed_ref,
        routed_ref, gain_rows_ref,
        full_q, full_kv, full_o, all_cot, bias, value_t, here, there, send, recv,
    ):
        wires = Wires(send, recv)
        dp, z = wires.dp, wires.z
        own = rows_at((dp * LINE + z) * rows, rows)
        locals_ = [
            (wk_ref, full_kv.at[own, pl.ds(0, key_width)]),
            (wv_ref, full_kv.at[own, pl.ds(key_width, kv_width - key_width)]),
            (gains_ref, full_kv.at[own, pl.ds(kv_width, LANES)]),
            (wq_ref, full_q.at[own]),
            (wo_ref, full_o.at[own]),
            (cot_ref, all_cot.at[rows_at(dp * tok_rows, tok_rows)]),
            (gate_ref, all_gate.at[pl.ds(pl.multiple_of(dp * 8, 8), 8)]),
        ]
        locals_ = [pltpu.make_async_copy(a, b, here.at[i]) for i, (a, b) in enumerate(locals_)]
        for one in locals_:
            one.start()
        greet(wires, range(1, planes), True)
        for one in locals_:
            one.wait()

        def block_rows(block):
            return rows_at((dp * LINE + block) * rows, rows)

        line_kv, line_q, line_o = [LineGather(wires, r, block_rows) for r in (full_kv, full_q, full_o)]
        plane_kv, plane_q, plane_o = [PlaneGather(wires, r, group) for r in (full_kv, full_q, full_o)]
        plane_cot = PlaneGather(wires, all_cot, tok_rows)
        line_keys = LineGather(wires, all_kv, lambda block: rows_at(block * tok_rows, tok_rows))
        first = wires.take(planes - 1)

        def gate_copy(mask, owner):
            part = all_gate.at[pl.ds(pl.multiple_of(owner * 8, 8), 8)]
            return wires.copy(part, part, first + mask - 1, dp=masked(dp, mask))

        line_kv.start(0)
        line_q.start(0)
        plane_cot.start(0)
        for mask in range(1, planes):
            gate_copy(mask, dp).start()
        key_place = lax.broadcasted_iota(jnp.int32, (keys, tok_rows), 0)
        query_place = lax.broadcasted_iota(jnp.int32, (keys, tok_rows), 1) + z * tok_rows
        allowed = (key_place >= starts_ref[0:1, :]) & (key_place <= query_place)
        bias[...] = jnp.where(allowed, 0.0, masked_score)
        line_kv.wait(0)
        line_kv.start(1)
        line_q.wait(0)
        line_q.start(1)
        plane_cot.wait(0)
        plane_cot.start(1, far=False)
        line_kv.wait(1)
        line_kv.start(2)
        line_q.wait(1)
        line_q.start(2)
        line_kv.wait(2)
        plane_kv.start(0)
        line_q.wait(2)
        plane_q.start(0)
        line_o.start(0)
        plane_cot.wait(1)
        plane_cot.start(2)
        plane_kv.wait(0)
        plane_kv.start(1)
        plane_q.wait(0)
        plane_q.start(1)
        line_o.wait(0)
        line_o.start(1)
        plane_kv.wait(1)
        plane_kv.start(2)
        plane_kv.wait(2)
        plane_kv.start(3)
        plane_kv.finish()

        gain_rows_ref[...] = full_kv[:, kv_width:].astype(jnp.float32).T[:8, :]
        tile = 32

        @pl.loop(0, tok_rows // tile)
        def _(step):
            cut = pl.ds(pl.multiple_of(step * tile, tile), tile)
            normed_ref[cut, :] = rms_norm(
                tok_ref[cut, :].astype(jnp.float32), gain_rows_ref[0:1, :]
            ).astype(jnp.bfloat16)

        own_keys = rows_at(z * tok_rows, tok_rows)
        pre = dot(normed_ref[...], full_kv[:, :kv_width], 1, 0)
        for pair in range(KVH):
            cut = slice(pair * HD, (pair + 1) * HD)
            all_kv[own_keys, cut] = turned(pre[:, cut], cos_ref[...], sin_ref[...]).astype(jnp.bfloat16)
        all_kv[own_keys, key_width:] = pre[:, key_width:].astype(jnp.bfloat16)
        line_keys.start(0)
        line_o.wait(1)
        line_o.start(2)
        line_keys.wait(0)
        line_keys.start(1)
        line_o.wait(2)
        plane_o.start(0)
        plane_q.wait(1)
        plane_q.start(2)
        line_keys.wait(1)
        line_keys.start(2)
        plane_q.wait(2)
        plane_q.start(3)
        plane_q.finish()
        saves = [pltpu.make_async_copy(full_q, out_q, there.at[0])]
        saves.append(pltpu.make_async_copy(full_kv, out_kv, there.at[1]))
        saves[0].start()
        saves[1].start()

        @pl.loop(0, HEADS // 2)
        def _(step):
            wide = pl.ds(pl.multiple_of(step * 2 * HD, 2 * HD), 2 * HD)
            pre_q = dot(normed_ref[...], full_q[:, wide], 1, 0)
            for one in range(2):
                query_ref[:, pl.ds(pl.multiple_of((2 * step + one) * HD, HD), HD)] = turned(
                    pre_q[:, one * HD : (one + 1) * HD], cos_ref[...], sin_ref[...]
                ).astype(jnp.bfloat16)

        line_keys.wait(2)
        value_t[...] = all_kv[:, key_width:].astype(jnp.float32).T.astype(jnp.bfloat16)
        lse_ref[...] = jnp.zeros_like(lse_ref)

        def attend(head):
            own_cut = pl.ds(pl.multiple_of(head * HD, HD), HD)
            key_cut = pl.ds(pl.multiple_of((head // per_group) * HD, HD), HD)
            scores = dot(all_kv[:, key_cut], query_ref[:, own_cut], 1, 1) * score_scale + bias[...]
            top = jnp.max(scores, axis=0, keepdims=True)
            expo = jnp.exp(scores - top)
            total = jnp.sum(expo, axis=0, keepdims=True)
            lse_ref[pl.ds(head, 1), :] = top + jnp.log(total)
            probs = (expo * (1.0 / total)).astype(jnp.bfloat16)
            mixed_ref[:, own_cut] = dot(value_t[key_cut, :], probs, 1, 0).T.astype(jnp.bfloat16)

        pl.loop(0, 2)(attend)
        plane_o.wait(0)
        plane_o.start(1)
        plane_cot.start_far()
        pl.loop(2, HEADS)(attend)
        plane_o.wait(1)
        plane_o.start(2)
        plane_o.wait(2)
        plane_o.start(3)
        plane_o.finish()
        saves.append(pltpu.make_async_copy(full_o, out_o, there.at[2]))
        saves[2].start()

        @pl.loop(0, width // 512)
        def _(step):
            cut = pl.ds(pl.multiple_of(step * 512, 512), 512)
            middle_ref[:, cut] = tok_ref[:, cut].astype(jnp.float32) + dot(
                mixed_ref[...], full_o[:, cut], 1, 0
            )

        @pl.loop(0, tok_rows // tile)
        def _(step):
            cut = pl.ds(pl.multiple_of(step * tile, tile), tile)
            routed_ref[cut, :] = rms_norm(middle_ref[cut, :], gain_rows_ref[1:2, :]).astype(jnp.bfloat16)

        plane_cot.wait(2)
        plane_cot.start(3)
        plane_cot.finish()
        saves.append(pltpu.make_async_copy(all_cot, out_cot, there.at[3]))
        saves[3].start()
        for mask in range(1, planes):
            gate_copy(mask, masked(dp, mask)).wait_recv()
        for mask in range(1, planes):
            gate_copy(mask, dp).wait_send()
        for one in (line_kv, line_q, line_o, line_keys):
            one.finish()
        for one in saves:
            one.wait()

    f32, low = jnp.float32, jnp.bfloat16
    copies = 4 * LineGather.COPIES + 4 * PlaneGather.COPIES + planes - 1
    return pl.pallas_call(
        kernel,
        out_shape=(
            jax.ShapeDtypeStruct((w_rows, width), low),
            jax.ShapeDtypeStruct((w_rows, kv_width + LANES), low),
            jax.ShapeDtypeStruct((w_rows, width), low),
            jax.ShapeDtypeStruct((planes * tok_rows, width), low),
            jax.ShapeDtypeStruct((planes * 8, tok_rows), f32),
            jax.ShapeDtypeStruct((tok_rows, width), low),
            jax.ShapeDtypeStruct((keys, kv_width), low),
            jax.ShapeDtypeStruct((16, tok_rows), f32),
            jax.ShapeDtypeStruct((tok_rows, width), low),
            jax.ShapeDtypeStruct((tok_rows, width), f32),
            jax.ShapeDtypeStruct((tok_rows, width), low),
            jax.ShapeDtypeStruct((tok_rows, width), low),
            jax.ShapeDtypeStruct((8, width), f32),
        ),
        in_specs=[VMEM] * 11,
        out_specs=(ANY,) * 4 + (VMEM,) * 9,
        scratch_shapes=[
            pltpu.VMEM((w_rows, width), low),
            pltpu.VMEM((w_rows, kv_width + LANES), low),
            pltpu.VMEM((w_rows, width), low),
            pltpu.VMEM((planes * tok_rows, width), low),
            pltpu.VMEM((keys, tok_rows), f32),
            pltpu.VMEM((kv_width - key_width, keys), low),
            pltpu.SemaphoreType.DMA((7,)),
            pltpu.SemaphoreType.DMA((4,)),
        ]
        + sems(copies),
        compiler_params=kernel_params(0, 63),
        name="front",
    )(w_query, w_key, w_value, gains, w_out, cotangent, gates, tokens, starts, cosine, sine)


def experts(routed, all_cot, all_gate, w_gate, w_up, w_down):
    tok_rows, width = routed.shape
    hidden_width = w_gate.shape[1]
    total_rows = 8 * tok_rows

    sum_rows = width + hidden_width
    chunks = WITH_EXPERTS

    def kernel(
        routed_ref, cot_ref, gate_ref, wg_ref, wu_ref, wd_ref,
        sums_ref, prod_ref, total_ref, routed_grad_ref,
        w_in, w_down, x_all, y_all, hidden, grad_hidden, grad_in, sums, sums_land, gate_t, core_in, first_in,
        second_in, here, there, send, recv,
    ):
        wires = Wires(send, recv)
        dp = wires.dp
        own = pltpu.make_async_copy(routed_ref, x_all.at[rows_at(dp * tok_rows, tok_rows)], here.at[0])
        loads = [
            pltpu.make_async_copy(wd_ref, w_down, here.at[1]),
            pltpu.make_async_copy(cot_ref, y_all, here.at[2]),
            pltpu.make_async_copy(wg_ref, w_in.at[:, pl.ds(0, hidden_width)], here.at[3]),
            pltpu.make_async_copy(wu_ref, w_in.at[:, pl.ds(hidden_width, hidden_width)], here.at[4]),
        ]
        own.start()
        for one in loads:
            one.start()
        greet(wires, (1, 2, 4), True)
        own.wait()
        spread = PlaneGather(wires, x_all, tok_rows)
        plane = PlaneReduce(
            wires, x_all, tok_rows, x_all, lambda slot: rows_begin(masked(dp, 2 * slot)), core_in, first_in, second_in,
            routed_grad_ref,
        )
        summed = LineSum(wires, sums, total_ref, sums_land, CHUNK, chunks)
        spread.start(0)
        gate_t[...] = gate_ref[...].T

        def rows_begin(block):
            return pl.multiple_of(block * tok_rows, 16)

        def cut_of(block):
            return pl.ds(rows_begin(block), tok_rows)

        def gate_of(block):
            lane = lax.broadcasted_iota(jnp.int32, gate_t.shape, 1)
            return jnp.sum(jnp.where(lane == block * 8 + dp, gate_t[...], 0.0), axis=1, keepdims=True)

        def back_hidden(block):
            cut = cut_of(block)
            y_all[cut, :] = (y_all[cut, :].astype(jnp.float32) * gate_of(block)).astype(jnp.bfloat16)
            grad_hidden[cut, :] = dot(y_all[cut, :], w_down[...], 1, 1)

        def through(mask):
            cut = cut_of(masked(dp, mask))
            acts = dot(x_all[cut, :], w_in[...], 1, 0)
            gate_act, up_act = acts[:, :hidden_width], acts[:, hidden_width:]
            share = jax.nn.sigmoid(gate_act)
            silu = gate_act * share
            hidden[cut, :] = (silu * up_act).astype(jnp.bfloat16)
            grad = grad_hidden[cut, :]
            grad_in[cut, :hidden_width] = (
                grad * up_act * share * (1.0 + gate_act * (1.0 - share))
            ).astype(jnp.bfloat16)
            grad_in[cut, hidden_width:] = (grad * silu).astype(jnp.bfloat16)

        loads[0].wait()
        loads[1].wait()
        pl.loop(0, 4)(back_hidden)
        spread.wait(0)
        spread.start(1)
        pl.loop(4, 8)(back_hidden)
        loads[2].wait()
        loads[3].wait()
        through(0)
        spread.wait_core(0)
        through(1)
        spread.wait(1)
        spread.start(2)
        through(2)
        through(4)
        spread.wait_core(1)
        spread.wait_core(2)
        through(3)
        through(5)
        spread.wait(2)
        spread.start(3)
        through(6)
        spread.wait_core(3)
        through(7)
        spread.finish()

        def weights_in(step):
            cut = rows_at(step * 256, 256)
            sums[cut, :] = dot(x_all[:, cut], grad_in[...], 0, 0).astype(jnp.bfloat16)

        def weights_down(step):
            cut = rows_at(step * 256, 256)
            out = rows_at(width + step * 256, 256)
            sums[out, :] = dot(hidden[:, cut], y_all[...], 0, 0).astype(jnp.bfloat16)

        def save_sums(begin, end, number):
            rows = pl.ds(begin, end - begin)
            return pltpu.make_async_copy(sums.at[rows], sums_ref.at[rows], there.at[number])

        pl.loop(0, 2)(weights_in)
        summed.begin()
        pl.loop(2, 4)(weights_in)
        pl.loop(4, 6)(weights_in)
        summed.tick()
        pl.loop(0, 3)(weights_down)
        summed.tick()
        save = save_sums(chunks * CHUNK, sum_rows, 0)
        save.start()

        def input_grads(side):
            for slot in (3, 2, 1, 0):
                cut = cut_of(masked(dp, 2 * slot + side))
                x_all[cut, :] = dot(grad_in[cut, :], w_in[...], 1, 1).astype(jnp.bfloat16)
                if side:
                    plane.start_core(slot)

        input_grads(1)
        summed.tick()
        input_grads(0)
        summed.tick()
        plane.step(1)
        plane.step(2)
        summed.tick()

        def save_made(block):
            return pltpu.make_async_copy(
                y_all.at[cut_of(block)], prod_ref.at[cut_of(block)], there.at[1 + block]
            )

        def make(block):
            made = dot(hidden[cut_of(block), :], w_down[...], 1, 0).astype(jnp.bfloat16).astype(jnp.float32)
            y_all[cut_of(block), :] = (made * gate_of(block)).astype(jnp.bfloat16)
            save_made(block).start()

        pl.loop(0, 4)(make)
        summed.tick()
        pl.loop(4, 8)(make)
        plane.step(3)
        summed.tick(2)
        plane.step(4)
        summed.tick(2)
        plane.step(5)
        summed.finish()
        for block in range(8):
            save_made(block).wait()
        save.wait()

    f32, low = jnp.float32, jnp.bfloat16
    return pl.pallas_call(
        kernel,
        out_shape=(
            jax.ShapeDtypeStruct((sum_rows, width), low),
            jax.ShapeDtypeStruct((total_rows, width), low),
            jax.ShapeDtypeStruct((chunks * CHUNK, width), low),
            jax.ShapeDtypeStruct((tok_rows, width), f32),
        ),
        in_specs=[VMEM, ANY, VMEM, ANY, ANY, ANY],
        out_specs=(ANY, ANY, VMEM, VMEM),
        scratch_shapes=[
            pltpu.VMEM((width, 2 * hidden_width), low),
            pltpu.VMEM((hidden_width, width), low),
            pltpu.VMEM((total_rows, width), low),
            pltpu.VMEM((total_rows, width), low),
            pltpu.VMEM((total_rows, hidden_width), low),
            pltpu.VMEM((total_rows, hidden_width), f32),
            pltpu.VMEM((total_rows, 2 * hidden_width), low),
            pltpu.VMEM((sum_rows, width), low),
            pltpu.VMEM((chunks * CHUNK, width), low),
            pltpu.VMEM((tok_rows, 64), f32),
        ]
        + PlaneReduce.scratch(tok_rows, width)
        + [pltpu.SemaphoreType.DMA((5,)), pltpu.SemaphoreType.DMA((9,))]
        + sems(PlaneGather.COPIES + PlaneReduce.COPIES + 3 * chunks),
        compiler_params=kernel_params(1, 63),
        name="experts",
    )(routed, all_cot, all_gate, w_gate, w_up, w_down)


CHUNK = 64
AHEAD = 4
WITH_EXPERTS = 9
WITH_ATTENTION = 7


class LineSum:
    def __init__(self, wires, own, out, landing, rows, chunks):
        self.wires, self.own, self.out, self.landing = wires, own, out, landing
        self.rows, self.chunks, self.now = rows, chunks, 0
        self.first = wires.take(3 * chunks)
        z = wires.z
        self.inner = (z == 1) | (z == 2)
        self.outer = (z == 0) | (z == 3)
        self.end = 3 * (z - 1)
        self.near = 1 + z // 3
        self.peer = 3 - z

    def _cut(self, ref, chunk):
        return ref.at[pl.ds(pl.multiple_of(chunk * self.rows, 16), self.rows)]

    def _in(self, chunk):
        return self.wires.copy(
            self._cut(self.own, chunk), self._cut(self.out, chunk), self.first + chunk, z=self.near
        )

    def _across(self, chunk):
        number = self.first + self.chunks + chunk
        return self.wires.copy(
            self._cut(self.own, chunk), self._cut(self.landing, chunk), number, z=self.peer
        )

    def _back(self, chunk):
        number = self.first + 2 * self.chunks + chunk
        return self.wires.copy(
            self._cut(self.out, chunk), self._cut(self.out, chunk), number, z=self.end
        )

    def begin(self):
        @pl.when(self.outer)
        def _():
            for chunk in range(min(AHEAD, self.chunks)):
                self._in(chunk).start()

    def tick(self, count=1):
        for _ in range(count):
            if self.now <= self.chunks:
                self._tick(self.now)
            self.now += 1

    def _tick(self, chunk):
        if chunk < self.chunks:

            @pl.when(self.outer)
            def _():
                self._in(chunk).wait_send()
                if chunk + AHEAD < self.chunks:
                    self._in(chunk + AHEAD).start()

        @pl.when(self.inner)
        def _():
            if chunk < self.chunks:
                row = chunk * self.rows
                self._in(chunk).wait_recv()
                add_rows(self.own, row, self.own, row, self.out, row, self.rows)
                self._across(chunk).start()
            if chunk >= 1:
                row = (chunk - 1) * self.rows
                self._across(chunk - 1).wait_recv()
                add_rows(self.out, row, self.own, row, self.landing, row, self.rows)
                self._back(chunk - 1).start()

    def finish(self):
        self.tick(max(0, self.chunks + 1 - self.now))

        @pl.when(self.outer)
        def _():
            @pl.loop(0, self.chunks)
            def _(chunk):
                self._back(chunk).wait_recv()

        @pl.when(self.inner)
        def _():
            @pl.loop(0, self.chunks)
            def _(chunk):
                self._across(chunk).wait_send()
                self._back(chunk).wait_send()


def norm_back(values, gain, grad):
    scale = lax.rsqrt(jnp.mean(values * values, axis=-1, keepdims=True) + epsilon)
    normal = values * scale
    inner = grad * gain
    to_values = scale * (inner - normal * jnp.mean(inner * normal, axis=-1, keepdims=True))
    return to_values, grad * normal


def turned(values, cosine, sine):
    return values * cosine + pltpu.roll(values, HD // 2, 1) * sine


def back_attention(
    sums_in,
    full_o,
    routed_grad,
    middle,
    cotangent,
    gain_moe,
    mixed,
    query,
    all_kv,
    lse,
    starts,
    cosine,
    sine,
):
    tok_rows, width = middle.shape
    keys, kv_width = all_kv.shape
    w_rows = width
    group = w_rows // 8
    skipped, chunks = WITH_EXPERTS, WITH_ATTENTION

    def kernel(
        sums_ref, full_o_hbm, routed_grad_ref, middle_ref, cot_ref, gain_ref, mixed_ref, query_ref, kv_ref, lse_ref,
        starts_ref, cos_ref, sin_ref,
        total_ref, grad_mid_ref, grad_pre_ref, gain_row_ref, w_out_ref,
        sums_own, sums_land, full_o_ref, attn_low, mixed_grad, part_o, o_core,
        o_first, o_second, bias, key_t, kv_grad, kv_part, kv_land, kv_out, here, send, recv,
    ):
        wires = Wires(send, recv)
        dp, z = wires.dp, wires.z
        loads = [
            pltpu.make_async_copy(sums_ref.at[pl.ds(skipped * CHUNK, chunks * CHUNK)], sums_own, here.at[0]),
            pltpu.make_async_copy(full_o_hbm, full_o_ref, here.at[1]),
        ]
        for one in loads:
            one.start()
        greet(wires, (1, 2, 4), True)
        summed = LineSum(wires, sums_own, total_ref, sums_land, CHUNK, chunks)
        dense = PlaneReduce(
            wires, part_o, group, part_o, lambda slot: pl.multiple_of(masked(dp, 2 * slot) * group, 16),
            o_core, o_first, o_second, w_out_ref,
        )
        line = LineReduce(wires, kv_part, tok_rows, kv_land, ways=(-1,))
        loads[0].wait()
        summed.begin()
        key_place = lax.broadcasted_iota(jnp.int32, (keys, tok_rows), 0)
        query_place = lax.broadcasted_iota(jnp.int32, (keys, tok_rows), 1) + z * tok_rows
        allowed = (key_place >= starts_ref[0:1, :]) & (key_place <= query_place)
        bias[...] = jnp.where(allowed, 0.0, masked_score)
        key_t[...] = kv_ref[:, : kv_width // 2].astype(jnp.float32).T.astype(jnp.bfloat16)
        kv_grad[...] = jnp.zeros_like(kv_grad)

        tile = 32
        gain_row_ref[...] = jnp.zeros_like(gain_row_ref)

        @pl.loop(0, tok_rows // tile)
        def _(step):
            cut = pl.ds(pl.multiple_of(step * tile, tile), tile)
            to_middle, terms = norm_back(middle_ref[cut, :], gain_ref[1:2, :], routed_grad_ref[cut, :])
            to_middle = cot_ref[cut, :].astype(jnp.float32) + to_middle
            grad_mid_ref[cut, :] = to_middle
            attn_low[cut, :] = to_middle.astype(jnp.bfloat16)
            gain_row_ref[0:1, :] += jnp.sum(terms, axis=0, keepdims=True)

        summed.tick()
        loads[1].wait()
        wide = 512

        @pl.loop(0, width // wide)
        def _(step):
            cut = pl.ds(pl.multiple_of(step * wide, wide), wide)
            mixed_grad[:, cut] = dot(attn_low[...], full_o_ref[cut, :], 1, 1).astype(jnp.bfloat16)

        @pl.loop(0, width // 256)
        def _(step):
            cut = pl.ds(pl.multiple_of(step * 256, 256), 256)
            part_o[cut, :] = dot(mixed_ref[:, cut], attn_low[...], 0, 0).astype(jnp.bfloat16)

        dense.step(0)
        summed.tick()
        score_scale = HD ** (-0.5)
        per_group = HEADS // KVH

        def heads(first, last):
            @pl.loop(first, last)
            def _(head):
                own_cut = pl.ds(pl.multiple_of(head * HD, HD), HD)
                pair = head // per_group
                key_cut = pl.ds(pl.multiple_of(pair * HD, HD), HD)
                value_cut = pl.ds(pl.multiple_of((KVH + pair) * HD, HD), HD)
                q, do = query_ref[:, own_cut], mixed_grad[:, own_cut]
                k, v = kv_ref[:, key_cut], kv_ref[:, value_cut]
                scores = dot(k, q, 1, 1) * score_scale + bias[...]
                probs = jnp.exp(scores - lse_ref[pl.ds(head, 1), :])
                grad_probs = dot(v, do, 1, 1)
                inner = jnp.sum(probs * grad_probs, axis=0, keepdims=True)
                grad_raw = (probs * (grad_probs - inner) * score_scale).astype(jnp.bfloat16)
                kv_grad[:, value_cut] += dot(probs.astype(jnp.bfloat16), do, 1, 0)
                kv_grad[:, key_cut] += dot(grad_raw, q, 1, 0)
                to_query = dot(key_t[key_cut, :], grad_raw, 1, 0).T
                grad_pre_ref[:, own_cut] = turned(to_query, cos_ref[...], -sin_ref[...]).astype(
                    jnp.bfloat16
                )

        heads(0, 3)
        summed.tick()
        dense.step(1)
        dense.step(2)
        heads(3, 6)
        summed.tick()
        heads(6, 9)
        summed.tick()
        heads(9, 12)
        kv_part[...] = kv_grad[...].astype(jnp.bfloat16)
        line.begin()
        summed.tick()
        dense.step(3)
        summed.tick()
        line.event(0)
        summed.tick()
        dense.step(4)
        line.event(1)
        line.event(2)
        line.event(3)
        line.event(4)
        dense.step(5)
        line.event(5)
        line.finish((kv_out,))
        q_width = HEADS * HD
        for pair in range(KVH):
            cut = slice(pair * HD, (pair + 1) * HD)
            grad_pre_ref[:, q_width + pair * HD : q_width + (pair + 1) * HD] = turned(
                kv_out[:, cut], cos_ref[...], -sin_ref[...]
            ).astype(jnp.bfloat16)
        grad_pre_ref[:, q_width + kv_width // 2 :] = kv_out[:, kv_width // 2 :].astype(jnp.bfloat16)
        summed.finish()

    f32, low = jnp.float32, jnp.bfloat16
    return pl.pallas_call(
        kernel,
        out_shape=(
            jax.ShapeDtypeStruct((chunks * CHUNK, sums_in.shape[1]), low),
            jax.ShapeDtypeStruct((tok_rows, width), f32),
            jax.ShapeDtypeStruct((tok_rows, width + kv_width), low),
            jax.ShapeDtypeStruct((8, width), f32),
            jax.ShapeDtypeStruct((group, width), low),
        ),
        in_specs=[ANY, ANY] + [VMEM] * 11,
        out_specs=(VMEM,) * 5,
        scratch_shapes=[
            pltpu.VMEM((chunks * CHUNK, sums_in.shape[1]), low),
            pltpu.VMEM((chunks * CHUNK, sums_in.shape[1]), low),
            pltpu.VMEM((w_rows, width), low),
            pltpu.VMEM((tok_rows, width), low),
            pltpu.VMEM((tok_rows, width), low),
            pltpu.VMEM((w_rows, width), low),
        ]
        + PlaneReduce.scratch(group, width)
        + [
            pltpu.VMEM((keys, tok_rows), f32),
            pltpu.VMEM((kv_width // 2, keys), low),
            pltpu.VMEM((keys, kv_width), f32),
            pltpu.VMEM((keys, kv_width), low),
            LineReduce.scratch(tok_rows, kv_width, 1),
            pltpu.VMEM((tok_rows, kv_width), f32),
            pltpu.SemaphoreType.DMA((2,)),
        ]
        + sems(3 * chunks + PlaneReduce.COPIES + LineReduce.COPIES),
        compiler_params=kernel_params(3, 63),
        name="back_attention",
    )(
        sums_in, full_o, routed_grad, middle, cotangent, gain_moe, mixed, query, all_kv, lse, starts, cosine, sine
    )


def back_dense(sums_in, produced, full_q, full_kv, normed, grad_pre, tokens, gains, grad_mid, gain_row, w_out_part, middle):
    tok_rows, width = middle.shape
    q_width = full_q.shape[1]
    in_width = q_width + full_kv.shape[1]
    pre_width = in_width - LANES
    w_rows = width
    group, rows = w_rows // 8, w_rows // (8 * LINE)
    skipped = WITH_EXPERTS + WITH_ATTENTION
    chunks = sums_in.shape[0] // CHUNK - skipped

    def kernel(
        sums_ref, prod_ref, full_q_ref, full_kv_ref, normed_ref, pre_ref, tok_ref, gain_ref, mid_grad_ref, gain_row_ref, o_part_ref,
        middle_ref,
        total_ref, layer_ref, tok_grad_ref, wq_ref, wk_ref, wv_ref, gains_ref, out_ref,
        sums_own, sums_land, own, core_in, first_in, second_in, moe, part, d_core, d_first, d_second, in_sums,
        in_land, o_sums, o_land, normed_grad, gain_rows, here, send, recv,
    ):
        wires = Wires(send, recv)
        dp, z = wires.dp, wires.z
        loads = [
            pltpu.make_async_copy(
                sums_ref.at[pl.ds(skipped * CHUNK, chunks * CHUNK)], sums_own, here.at[0]
            )
        ]
        for slot in range(4):
            row = pl.multiple_of(masked(dp, 2 * slot) * tok_rows, 16)
            loads.append(
                pltpu.make_async_copy(
                    prod_ref.at[pl.ds(row, tok_rows)],
                    own.at[pl.ds(slot * tok_rows, tok_rows)],
                    here.at[1 + slot],
                )
            )
        for one in loads:
            one.start()
        greet(wires, (1, 2, 4), True)
        summed = LineSum(wires, sums_own, total_ref, sums_land, CHUNK, chunks)
        dense = PlaneReduce(
            wires, part, group, part, lambda slot: pl.multiple_of(masked(dp, 2 * slot) * group, 16),
            d_core, d_first, d_second, in_sums,
        )
        plane = PlaneReduce(
            wires, prod_ref, tok_rows, own, lambda slot: slot * tok_rows, core_in, first_in, second_in, moe
        )
        o_line = LineReduce(wires, o_sums, rows, o_land)
        in_line = LineReduce(wires, in_sums, rows, in_land)
        o_sums[...] = o_part_ref[...]
        o_line.begin()
        loads[0].wait()
        summed.begin()
        wide = 512

        @pl.loop(0, width // wide)
        def _(step):
            cut = pl.ds(pl.multiple_of(step * wide, wide), wide)
            normed_grad[:, cut] = dot(pre_ref[:, :q_width], full_q_ref[cut, :], 1, 1) + dot(
                pre_ref[:, q_width:], full_kv_ref[cut, : pre_width - q_width], 1, 1
            )

        summed.tick()
        gain_rows[...] = jnp.zeros_like(gain_rows)
        gain_rows[1:2, :] = gain_row_ref[0:1, :]
        tile = 32

        @pl.loop(0, tok_rows // tile)
        def _(step):
            cut = pl.ds(pl.multiple_of(step * tile, tile), tile)
            to_tokens, terms = norm_back(
                tok_ref[cut, :].astype(jnp.float32), gain_ref[0:1, :], normed_grad[cut, :]
            )
            tok_grad_ref[cut, :] = mid_grad_ref[cut, :] + to_tokens
            gain_rows[0:1, :] += jnp.sum(terms, axis=0, keepdims=True)

        summed.tick()
        o_line.event(0)
        part[:, pre_width:] = gain_rows[...].T.astype(jnp.bfloat16)

        @pl.loop(0, w_rows // 256)
        def _(step):
            cut = pl.ds(pl.multiple_of(step * 256, 256), 256)
            part[cut, :pre_width] = dot(normed_ref[:, cut], pre_ref[...], 0, 0).astype(jnp.bfloat16)

        dense.step(0)
        o_line.event(1)
        o_line.event(2)
        summed.tick(2)
        dense.step(1)
        o_line.event(3)
        summed.tick()
        dense.step(2)
        o_line.event(4)
        summed.tick()
        o_line.event(5)
        for one in loads[1:]:
            one.wait()
        plane.step(0)
        summed.tick(2)
        plane.step(1)
        summed.tick()
        dense.step(3)
        plane.step(2)
        summed.tick(2)
        dense.step(4)
        dense.step(5)
        in_line.begin()
        summed.tick()
        in_line.event(0)
        summed.tick()
        plane.step(3)
        in_line.event(1)
        in_line.event(2)
        summed.tick(2)
        in_line.event(3)
        in_line.event(4)
        plane.step(4)
        summed.tick(2)
        in_line.event(5)
        plane.step(5)
        summed.tick(2)

        @pl.loop(0, tok_rows // tile)
        def _(step):
            cut = pl.ds(pl.multiple_of(step * tile, tile), tile)
            layer_ref[cut, :] = (middle_ref[cut, :] + moe[cut, :]).astype(jnp.bfloat16)

        o_line.finish((out_ref,))
        in_line.finish((wq_ref, wk_ref, wv_ref, gains_ref))
        summed.finish()

    f32, low = jnp.float32, jnp.bfloat16
    return pl.pallas_call(
        kernel,
        out_shape=(
            jax.ShapeDtypeStruct((chunks * CHUNK, sums_in.shape[1]), low),
            jax.ShapeDtypeStruct((tok_rows, width), low),
            jax.ShapeDtypeStruct((tok_rows, width), f32),
            jax.ShapeDtypeStruct((rows, q_width), f32),
            jax.ShapeDtypeStruct((rows, (pre_width - q_width) // 2), f32),
            jax.ShapeDtypeStruct((rows, (pre_width - q_width) // 2), f32),
            jax.ShapeDtypeStruct((rows, LANES), f32),
            jax.ShapeDtypeStruct((rows, width), f32),
        ),
        in_specs=[ANY, ANY] + [VMEM] * 10,
        out_specs=(VMEM,) * 8,
        scratch_shapes=[
            pltpu.VMEM((chunks * CHUNK, sums_in.shape[1]), low),
            pltpu.VMEM((chunks * CHUNK, sums_in.shape[1]), low),
            pltpu.VMEM((4 * tok_rows, width), low),
        ]
        + PlaneReduce.scratch(tok_rows, width)
        + [pltpu.VMEM((tok_rows, width), f32), pltpu.VMEM((w_rows, in_width), low)]
        + PlaneReduce.scratch(group, in_width)
        + [
            pltpu.VMEM((group, in_width), low),
            LineReduce.scratch(rows, in_width),
            pltpu.VMEM((group, width), low),
            LineReduce.scratch(rows, width),
            pltpu.VMEM((tok_rows, width), f32),
            pltpu.VMEM((LANES, width), f32),
            pltpu.SemaphoreType.DMA((5,)),
        ]
        + sems(3 * chunks + 2 * PlaneReduce.COPIES + 2 * LineReduce.COPIES),
        compiler_params=kernel_params(4, 63),
        name="back_dense",
    )(
        sums_in, produced, full_q, full_kv, normed, grad_pre, tokens, gains, grad_mid, gain_row, w_out_part, middle
    )


def on_plane_device(
    tokens,
    norm_attn,
    w_query,
    w_key,
    w_value,
    w_out,
    norm_moe,
    w_gate,
    w_up,
    w_down,
    routes,
    gate_values,
    lengths,
    cotangent,
):
    tok_rows = tokens.shape[0]
    ctx_size = lax.axis_size("ctx")
    ctx_place = lax.axis_index("ctx")
    group_places = jnp.arange(tok_rows * ctx_size, dtype=jnp.int32)
    seg_all, within_all = seq_tables(lengths[0], group_places)
    offset = ctx_place * tok_rows
    own_places = offset + jnp.arange(tok_rows, dtype=jnp.int32)
    within_own = lax.dynamic_slice_in_dim(within_all, offset, tok_rows)
    kv_columns = KVH * HD
    q_columns = HEADS * HD
    gains = jnp.pad(jnp.stack([norm_attn, norm_moe], axis=1), ((0, 0), (0, LANES - 2)))
    numbers = jnp.arange(8, dtype=jnp.int32)
    gates = jnp.sum(
        jnp.where(routes[None, :, :] == numbers[:, None, None], gate_values[None], 0.0), axis=2
    )
    half_size = HD // 2
    frequency = rope_base ** (-jnp.arange(half_size, dtype=jnp.float32) / half_size)
    angles = within_own.astype(jnp.float32)[:, None] * frequency[None, :]
    cosine = jnp.concatenate([jnp.cos(angles), jnp.cos(angles)], axis=1)
    sine = jnp.concatenate([-jnp.sin(angles), jnp.sin(angles)], axis=1)
    starts = jnp.broadcast_to((own_places - within_own)[None, :], (8, tok_rows))
    (
        full_q, full_kv, full_o, all_cot, all_gate, query, all_kv, lse, mixed_low, middle, normed_low, routed_low,
        gain_rows,
    ) = front(
        w_query, w_key, w_value, gains, w_out, cotangent, gates, tokens, starts, cosine, sine
    )
    partial_sums, produced, sums_first, routed_grad = experts(
        routed_low, all_cot, all_gate, w_gate[0], w_up[0], w_down[0]
    )
    half = w_gate.shape[2]
    sums_second, grad_mid, grad_pre, gain_row, w_out_part = back_attention(
        partial_sums,
        full_o,
        routed_grad,
        middle,
        cotangent,
        gain_rows,
        mixed_low,
        query,
        all_kv,
        lse,
        starts,
        cosine,
        sine,
    )
    sums_tail, layer_out, grad_tokens, sum_q, sum_k, sum_v, sum_gains, sum_o = back_dense(
        partial_sums,
        produced,
        full_q,
        full_kv,
        normed_low,
        grad_pre,
        tokens,
        gain_rows,
        grad_mid,
        gain_row,
        w_out_part,
        middle,
    )
    in_tail = D - sums_first.shape[0] - sums_second.shape[0]

    def whole(columns):
        return jnp.concatenate(
            [sums_first[:, columns], sums_second[:, columns], sums_tail[:in_tail, columns]], axis=0
        )

    return (
        layer_out,
        grad_tokens,
        sum_gains[:, 0],
        sum_q,
        sum_k,
        sum_v,
        sum_o,
        sum_gains[:, 1],
        whole(slice(0, half)).astype(jnp.float32)[None],
        whole(slice(half, 2 * half)).astype(jnp.float32)[None],
        sums_tail[in_tail:].astype(jnp.float32)[None],
    )


def solution(mesh):
    on_plane = mesh.shape["dp"] == 8 and mesh.shape["ctx"] == LINE
    return jax.shard_map(
        on_plane_device if on_plane else on_device,
        mesh=mesh,
        in_specs=(
            P(("dp", "ctx"), None),
            P(("dp", "ctx")),
            P(("dp", "ctx"), None),
            P(("dp", "ctx"), None),
            P(("dp", "ctx"), None),
            P(("dp", "ctx"), None),
            P(("dp", "ctx")),
            P("dp", None, None),
            P("dp", None, None),
            P("dp", None, None),
            P(("dp", "ctx"), None),
            P(("dp", "ctx"), None),
            P("dp", None),
            P(("dp", "ctx"), None),
        ),
        out_specs=(
            P(("dp", "ctx"), None),
            P(("dp", "ctx"), None),
            P(("dp", "ctx")),
            P(("dp", "ctx"), None),
            P(("dp", "ctx"), None),
            P(("dp", "ctx"), None),
            P(("dp", "ctx"), None),
            P(("dp", "ctx")),
            P("dp", None, None),
            P("dp", None, None),
            P("dp", None, None),
        ),
        check_vma=False,
    )
```

```python
import functools

import jax
import jax.numpy as jnp
from jax import lax
from jax.experimental import pallas as pl
from jax.experimental.pallas import tpu as pltpu
from jax.sharding import PartitionSpec as P

D = 1536
HEADS = 12
KVH = 2
HD = 128
TOP = 4
EXP_DEV = 1


epsilon = 1e-06
rope_base = 1000000.0
masked_score = -1e30


def rms_norm(values, gain):
    return values * lax.rsqrt(jnp.mean(values * values, axis=-1, keepdims=True) + epsilon) * gain


def rotate(values, within, direction):
    half_size = values.shape[-1] // 2
    frequency = rope_base ** (-jnp.arange(half_size, dtype=jnp.float32) / half_size)
    angles = direction * within.astype(jnp.float32)[:, None] * frequency[None, :]
    cosine = jnp.cos(angles)[:, None, :]
    sine = jnp.sin(angles)[:, None, :]
    first_half = values[..., :half_size]
    second = values[..., half_size:]
    return jnp.concatenate(
        [first_half * cosine - second * sine, second * cosine + first_half * sine], axis=-1
    )


def seq_tables(length_row, places):
    seq_ends = jnp.cumsum(length_row)
    passed = places[:, None] >= seq_ends[None, :]
    segment = jnp.sum(passed.astype(jnp.int32), axis=1)
    within = places - jnp.sum(jnp.where(passed, length_row[None, :], 0), axis=1)
    return (segment, within)


def collect_weights(gain_attn, w_query, w_key, w_value, w_out, gain_moe):
    return (
        lax.all_gather(gain_attn, ("dp", "ctx"), axis=0, tiled=True),
        lax.all_gather(w_query, ("dp", "ctx"), axis=0, tiled=True),
        lax.all_gather(w_key, ("dp", "ctx"), axis=0, tiled=True),
        lax.all_gather(w_value, ("dp", "ctx"), axis=0, tiled=True),
        lax.all_gather(w_out, ("dp", "ctx"), axis=0, tiled=True),
        lax.all_gather(gain_moe, ("dp", "ctx"), axis=0, tiled=True),
    )


def spread_grads(grad_gain_attn, grad_query, grad_key, grad_value, grad_outp, grad_gain_moe):
    return (
        lax.psum_scatter(grad_gain_attn, ("dp", "ctx"), scatter_dimension=0, tiled=True),
        lax.psum_scatter(grad_query, ("dp", "ctx"), scatter_dimension=0, tiled=True),
        lax.psum_scatter(grad_key, ("dp", "ctx"), scatter_dimension=0, tiled=True),
        lax.psum_scatter(grad_value, ("dp", "ctx"), scatter_dimension=0, tiled=True),
        lax.psum_scatter(grad_outp, ("dp", "ctx"), scatter_dimension=0, tiled=True),
        lax.psum_scatter(grad_gain_moe, ("dp", "ctx"), scatter_dimension=0, tiled=True),
    )


def on_device(
    tokens,
    norm_attn,
    w_query,
    w_key,
    w_value,
    w_out,
    norm_moe,
    w_gate,
    w_up,
    w_down,
    routes,
    gate_values,
    lengths,
    cotangent,
):
    tok_rows = tokens.shape[0]
    ctx_size = lax.axis_size("ctx")
    dp_size = lax.axis_size("dp")
    ctx_place = lax.axis_index("ctx")
    group_rows = tok_rows * ctx_size
    group_places = jnp.arange(group_rows, dtype=jnp.int32)
    seg_all, within_all = seq_tables(lengths[0], group_places)
    offset = ctx_place * tok_rows
    own_places = offset + jnp.arange(tok_rows, dtype=jnp.int32)
    seg_own = lax.dynamic_slice_in_dim(seg_all, offset, tok_rows)
    within_own = lax.dynamic_slice_in_dim(within_all, offset, tok_rows)
    allowed = (seg_own[:, None] == seg_all[None, :]) & (
        group_places[None, :] <= own_places[:, None]
    )
    gain_attn, full_q, full_k, full_v, full_o, gain_moe = collect_weights(
        norm_attn, w_query, w_key, w_value, w_out, norm_moe
    )
    gain_attn_f = gain_attn.astype(jnp.float32)
    gain_moe_f = gain_moe.astype(jnp.float32)
    inputs = tokens.astype(jnp.float32)
    normed_low = rms_norm(inputs, gain_attn_f).astype(jnp.bfloat16)
    query_pre = jnp.dot(normed_low, full_q, preferred_element_type=jnp.float32)
    key_pre = jnp.dot(normed_low, full_k, preferred_element_type=jnp.float32)
    value_pre = jnp.dot(normed_low, full_v, preferred_element_type=jnp.float32)
    query = rotate(query_pre.reshape(tok_rows, HEADS, HD), within_own, 1.0).astype(jnp.bfloat16)
    key_low = rotate(key_pre.reshape(tok_rows, KVH, HD), within_own, 1.0).astype(jnp.bfloat16)
    key_low = key_low.reshape(tok_rows, KVH * HD)
    value_low = value_pre.astype(jnp.bfloat16)
    all_keys, all_values = (
        lax.all_gather(key_low, "ctx", axis=0, tiled=True),
        lax.all_gather(value_low, "ctx", axis=0, tiled=True),
    )
    per_group = HEADS // KVH
    score_scale = HD ** (-0.5)
    query_groups = query.reshape(tok_rows, KVH, per_group, HD)

    def softmax_weights(group_number):
        keys_part = all_keys[:, group_number * HD : (group_number + 1) * HD]
        raw = jnp.einsum(
            "qjd,kd->jqk",
            query_groups[:, group_number],
            keys_part,
            preferred_element_type=jnp.float32,
        )
        scores = jnp.where(allowed[None], raw * score_scale, masked_score)
        row_top = jnp.max(scores, axis=-1, keepdims=True)
        expo = jnp.exp(scores - row_top)
        return expo / jnp.sum(expo, axis=-1, keepdims=True)

    mixed_parts = []
    for group_number in range(KVH):
        probs = softmax_weights(group_number)
        values_part = all_values[:, group_number * HD : (group_number + 1) * HD]
        mixed_group = jnp.einsum(
            "jqk,kd->qjd",
            probs.astype(jnp.bfloat16),
            values_part,
            preferred_element_type=jnp.float32,
        )
        mixed_parts.append(mixed_group.reshape(tok_rows, per_group * HD))
    mixed_low = jnp.concatenate(mixed_parts, axis=1).astype(jnp.bfloat16)
    middle = inputs + jnp.dot(mixed_low, full_o, preferred_element_type=jnp.float32)
    routed_low = rms_norm(middle, gain_moe_f).astype(jnp.bfloat16)
    experts_total = EXP_DEV * dp_size
    capacity = 3 * TOP * tok_rows // (2 * experts_total)
    assign_count = tok_rows * TOP
    flat_ids = routes.reshape(assign_count)
    onehot = (flat_ids[:, None] == jnp.arange(experts_total, dtype=jnp.int32)[None, :]).astype(
        jnp.int32
    )
    earlier = jnp.sum((jnp.cumsum(onehot, axis=0) - onehot) * onehot, axis=1)
    slot_index = flat_ids * capacity + earlier
    owner = (
        jnp.full((experts_total * capacity,), assign_count, jnp.int32)
        .at[slot_index]
        .set(jnp.arange(assign_count, dtype=jnp.int32))
    )
    padded = jnp.concatenate([routed_low, jnp.zeros((1, D), jnp.bfloat16)], axis=0)
    outgoing = padded[owner // TOP].reshape(experts_total, capacity, D)
    arrived = lax.all_to_all(outgoing, "dp", split_axis=0, concat_axis=0, tiled=True)
    arrived_sets = arrived.reshape(dp_size, EXP_DEV, capacity, D)
    gate_act = jnp.einsum(
        "secd,edf->secf", arrived_sets, w_gate, preferred_element_type=jnp.float32
    )
    up_act = jnp.einsum("secd,edf->secf", arrived_sets, w_up, preferred_element_type=jnp.float32)
    hidden_low = (jax.nn.silu(gate_act) * up_act).astype(jnp.bfloat16)
    produced = jnp.einsum("secf,efd->secd", hidden_low, w_down, preferred_element_type=jnp.float32)
    produced = produced.astype(jnp.bfloat16).reshape(experts_total, capacity, D)
    returned = lax.all_to_all(produced, "dp", split_axis=0, concat_axis=0, tiled=True)
    picked = returned.reshape(experts_total * capacity, D)[slot_index].reshape(tok_rows, TOP, D)
    moe_out = jnp.sum(picked.astype(jnp.float32) * gate_values[:, :, None], axis=1)
    layer_out = (middle + moe_out).astype(jnp.bfloat16)
    grad_out = cotangent.astype(jnp.float32)
    grad_assign = (grad_out[:, None, :] * gate_values[:, :, None]).astype(jnp.bfloat16)
    grad_padded = jnp.concatenate(
        [grad_assign.reshape(assign_count, D), jnp.zeros((1, D), jnp.bfloat16)], axis=0
    )
    grad_slots = grad_padded[owner].reshape(experts_total, capacity, D)
    grad_arrived = lax.all_to_all(grad_slots, "dp", split_axis=0, concat_axis=0, tiled=True)
    grad_arrived = grad_arrived.reshape(dp_size, EXP_DEV, capacity, D)
    grad_hidden = jnp.einsum(
        "secd,efd->secf", grad_arrived, w_down, preferred_element_type=jnp.float32
    )
    grad_w_down = jnp.einsum(
        "secf,secd->efd", hidden_low, grad_arrived, preferred_element_type=jnp.float32
    )
    glu_value, glu_pull = jax.vjp(
        lambda gate_in, up_in: jax.nn.silu(gate_in) * up_in, gate_act, up_act
    )
    grad_gate, grad_up = glu_pull(grad_hidden)
    grad_gate_low = grad_gate.astype(jnp.bfloat16)
    grad_up_low = grad_up.astype(jnp.bfloat16)
    grad_w_gate = jnp.einsum(
        "secd,secf->edf", arrived_sets, grad_gate_low, preferred_element_type=jnp.float32
    )
    grad_w_up = jnp.einsum(
        "secd,secf->edf", arrived_sets, grad_up_low, preferred_element_type=jnp.float32
    )
    grad_sent = jnp.einsum(
        "secf,edf->secd", grad_gate_low, w_gate, preferred_element_type=jnp.float32
    ) + jnp.einsum("secf,edf->secd", grad_up_low, w_up, preferred_element_type=jnp.float32)
    grad_sent = grad_sent.astype(jnp.bfloat16).reshape(experts_total, capacity, D)
    grad_back = lax.all_to_all(grad_sent, "dp", split_axis=0, concat_axis=0, tiled=True)
    grad_picked = grad_back.reshape(experts_total * capacity, D)[slot_index].reshape(
        tok_rows, TOP, D
    )
    grad_routed = jnp.sum(grad_picked.astype(jnp.float32), axis=1)
    expert_sums = (
        lax.psum(grad_w_gate.astype(jnp.bfloat16), "ctx").astype(jnp.float32),
        lax.psum(grad_w_up.astype(jnp.bfloat16), "ctx").astype(jnp.float32),
        lax.psum(grad_w_down.astype(jnp.bfloat16), "ctx").astype(jnp.float32),
    )
    norm_value, moe_pull = jax.vjp(rms_norm, middle, gain_moe_f)
    grad_mid_norm, grad_gain_moe = moe_pull(grad_routed)
    grad_middle = grad_out + grad_mid_norm
    grad_attn_low = grad_middle.astype(jnp.bfloat16)
    grad_w_out = jnp.einsum(
        "th,td->hd", mixed_low, grad_attn_low, preferred_element_type=jnp.float32
    )
    grad_mixed_low = jnp.einsum(
        "td,hd->th", grad_attn_low, full_o, preferred_element_type=jnp.float32
    ).astype(jnp.bfloat16)
    grad_mixed_groups = grad_mixed_low.reshape(tok_rows, KVH, per_group, HD)
    grad_query_parts = []
    prob_parts = []
    score_parts = []
    for group_number in range(KVH):
        probs = softmax_weights(group_number)
        keys_part = all_keys[:, group_number * HD : (group_number + 1) * HD]
        values_part = all_values[:, group_number * HD : (group_number + 1) * HD]
        grad_probs = jnp.einsum(
            "qjd,kd->jqk",
            grad_mixed_groups[:, group_number],
            values_part,
            preferred_element_type=jnp.float32,
        )
        grad_scores = probs * (grad_probs - jnp.sum(probs * grad_probs, axis=-1, keepdims=True))
        grad_raw_low = (grad_scores * score_scale).astype(jnp.bfloat16)
        grad_query_parts.append(
            jnp.einsum("jqk,kd->qjd", grad_raw_low, keys_part, preferred_element_type=jnp.float32)
        )
        prob_parts.append(probs.astype(jnp.bfloat16))
        score_parts.append(grad_raw_low)
    grad_query_rot = jnp.stack(grad_query_parts, axis=1).reshape(tok_rows, HEADS, HD)
    key_pieces = []
    value_pieces = []
    for group_number in range(KVH):
        score_piece = score_parts[group_number]
        prob_piece = prob_parts[group_number]
        key_pieces.append(
            jnp.einsum(
                "jqk,qjd->kd",
                score_piece,
                query_groups[:, group_number],
                preferred_element_type=jnp.float32,
            )
        )
        value_pieces.append(
            jnp.einsum(
                "jqk,qjd->kd",
                prob_piece,
                grad_mixed_groups[:, group_number],
                preferred_element_type=jnp.float32,
            )
        )
    key_value_grads = lax.psum_scatter(
        jnp.concatenate(key_pieces + value_pieces, axis=1).astype(jnp.bfloat16),
        "ctx",
        scatter_dimension=0,
        tiled=True,
    ).astype(jnp.float32)
    grad_query_low = (
        rotate(grad_query_rot, within_own, -1.0).astype(jnp.bfloat16).reshape(tok_rows, HEADS * HD)
    )
    grad_key_rot = key_value_grads[:, : KVH * HD].reshape(tok_rows, KVH, HD)
    grad_key_low = (
        rotate(grad_key_rot, within_own, -1.0).astype(jnp.bfloat16).reshape(tok_rows, KVH * HD)
    )
    grad_value_low = key_value_grads[:, KVH * HD :].astype(jnp.bfloat16)
    grad_w_query = jnp.einsum(
        "td,th->dh", normed_low, grad_query_low, preferred_element_type=jnp.float32
    )
    grad_w_key = jnp.einsum(
        "td,th->dh", normed_low, grad_key_low, preferred_element_type=jnp.float32
    )
    grad_w_value = jnp.einsum(
        "td,th->dh", normed_low, grad_value_low, preferred_element_type=jnp.float32
    )
    grad_normed = (
        jnp.einsum("th,dh->td", grad_query_low, full_q, preferred_element_type=jnp.float32)
        + jnp.einsum("th,dh->td", grad_key_low, full_k, preferred_element_type=jnp.float32)
        + jnp.einsum("th,dh->td", grad_value_low, full_v, preferred_element_type=jnp.float32)
    )
    first_value, attn_pull = jax.vjp(rms_norm, inputs, gain_attn_f)
    grad_inputs, grad_gain_attn = attn_pull(grad_normed)
    grad_tokens = grad_middle + grad_inputs
    dense_sums = spread_grads(
        grad_gain_attn, grad_w_query, grad_w_key, grad_w_value, grad_w_out, grad_gain_moe
    )
    return (
        layer_out,
        grad_tokens,
        dense_sums[0],
        dense_sums[1],
        dense_sums[2],
        dense_sums[3],
        dense_sums[4],
        dense_sums[5],
        expert_sums[0],
        expert_sums[1],
        expert_sums[2],
    )


MESH = pl.DeviceIdType.MESH
LANES = 128
MIB = 2**20
ANY = pl.BlockSpec(memory_space=pl.ANY)
VMEM = pl.BlockSpec(memory_space=pltpu.VMEM)


def flip(index, bit):
    return index + bit - 2 * bit * ((index // bit) % 2)


def masked(index, mask):
    for bit in (1, 2, 4):
        if mask & bit:
            index = flip(index, bit)
    return index


class Wires:
    def __init__(self, send, recv):
        self.send, self.recv, self.used = send, recv, 0
        self.dp, self.z = lax.axis_index("dp"), lax.axis_index("ctx")

    def take(self, count):
        first = self.used
        self.used += count
        return first

    def copy(self, src, dst, number, dp=None, z=None):
        return pltpu.make_async_remote_copy(
            src_ref=src,
            dst_ref=dst,
            send_sem=self.send.at[number],
            recv_sem=self.recv.at[number],
            device_id=(self.dp if dp is None else dp, self.z if z is None else z),
            device_id_type=MESH,
        )


def greet(wires, masks, line):
    barrier = pltpu.get_barrier_semaphore()
    dp, z = wires.dp, wires.z
    for mask in masks:
        pl.semaphore_signal(barrier, inc=1, device_id=(masked(dp, mask), z), device_id_type=MESH)
    for step in range(1, LINE) if line else ():
        pl.semaphore_signal(
            barrier, inc=1, device_id=(dp, lax.rem(z + step, LINE)), device_id_type=MESH
        )
    pl.semaphore_wait(barrier, len(masks) + (LINE - 1 if line else 0))


LINE = 4


class LineGather:
    COPIES = 2 * (LINE - 1)

    def __init__(self, wires, ref, rows_of):
        self.wires, self.ref, self.rows_of = wires, ref, rows_of
        self.first = wires.take(self.COPIES)

    def _copy(self, block, number, z):
        part = self.ref.at[self.rows_of(block)]
        return self.wires.copy(part, part, self.first + number, z=z)

    def start(self, step):
        z = self.wires.z

        @pl.when((z >= step) & (z < LINE - 1))
        def _():
            self._copy(z - step, step, z + 1).start()

        @pl.when((z + step < LINE) & (z > 0))
        def _():
            self._copy(z + step, LINE - 1 + step, z - 1).start()

    def wait(self, step):
        z = self.wires.z

        @pl.when(z - 1 - step >= 0)
        def _():
            self._copy(z - 1 - step, step, z).wait_recv()

        @pl.when(z + 1 + step < LINE)
        def _():
            self._copy(z + 1 + step, LINE - 1 + step, z).wait_recv()

    def finish(self):
        z = self.wires.z
        for step in range(LINE - 1):

            @pl.when((z >= step) & (z < LINE - 1))
            def _():
                self._copy(z - step, step, z + 1).wait_send()

            @pl.when((z + step < LINE) & (z > 0))
            def _():
                self._copy(z + step, LINE - 1 + step, z - 1).wait_send()


class PlaneGather:
    CHIP = (((2, 0, 0), (4, 0, 1)), ((4, 0, 0), (2, 0, 1)), ((4, 2, 0), (2, 4, 1)))
    CORE = (
        ((1, 0, 2),),
        ((1, 2, 0), (1, 4, 1)),
        ((1, 4, 0), (1, 2, 1)),
        ((1, 6, 0), (1, 6, 1)),
    )
    COPIES = 13

    def __init__(self, wires, ref, group):
        self.wires, self.ref, self.group = wires, ref, group
        first = wires.take(self.COPIES)
        self.number = {}
        for stage in self.CHIP + self.CORE:
            for one in stage:
                self.number[one] = first + len(self.number)
        self.core_left = [0, 1, 2, 3]

    def _copy(self, one, from_me):
        to, whose, half = one
        dp = self.wires.dp
        sender = dp if from_me else masked(dp, to)
        owner = masked(sender, whose)
        size = self.group if half == 2 else self.group // 2
        begin = owner * self.group + (self.group // 2 if half == 1 else 0)
        part = self.ref.at[pl.ds(pl.multiple_of(begin, 16), size)]
        return self.wires.copy(part, part, self.number[one], dp=masked(dp, to))

    def start(self, stage, far=True):
        for one in (self.CHIP[stage] if stage < 2 else ()) + self.CORE[stage]:
            self._copy(one, True).start()
        if stage == 1 and far:
            self.start_far()

    def start_far(self):
        for one in self.CHIP[2]:
            self._copy(one, True).start()

    def wait(self, stage):
        for one in self.CHIP[stage]:
            self._copy(one, False).wait_recv()

    def wait_core(self, stage):
        self.core_left.remove(stage)
        for one in self.CORE[stage]:
            self._copy(one, False).wait_recv()

    def finish(self):
        for stage in list(self.core_left):
            self.wait_core(stage)
        for one in self.number:
            self._copy(one, True).wait_send()


def add_rows(out, out_row, left, left_row, right, right_row, rows):
    @pl.loop(0, rows // 16)
    def _(step):
        def cut(row):
            return pl.ds(pl.multiple_of(row + step * 16, 16), 16)

        out[cut(out_row), :] = (
            left[cut(left_row), :].astype(jnp.float32) + right[cut(right_row), :].astype(jnp.float32)
        ).astype(out.dtype)


class PlaneReduce:
    COPIES = 10
    STEPS = 6

    def __init__(self, wires, part, group, own, own_row, core_in, first_in, second_in, out):
        self.wires, self.part, self.group, self.half = wires, part, group, group // 2
        self.own, self.own_row, self.out = own, own_row, out
        self.core_in, self.first_in, self.second_in = core_in, first_in, second_in
        self.first = wires.take(self.COPIES)

    def _send(self, src, src_row, dst, dst_row, rows, number, to):
        return self.wires.copy(
            src.at[pl.ds(src_row, rows)],
            dst.at[pl.ds(dst_row, rows)],
            self.first + number,
            dp=masked(self.wires.dp, to),
        )

    def _core(self, slot):
        row = pl.multiple_of(masked(self.wires.dp, 1 + 2 * slot) * self.group, 16)
        return self._send(self.part, row, self.core_in, slot * self.group, self.group, slot, 1)

    def _far(self, number):
        g, h = self.group, self.half
        src_row, dst, dst_row, to = (
            (3 * g, self.first_in, h, 4),
            (3 * g + h, self.first_in, 3 * h, 2),
            (2 * g, self.first_in, 0, 4),
            (1 * g + h, self.first_in, 2 * h, 2),
            (1 * g, self.second_in, 0, 2),
            (2 * g + h, self.second_in, h, 4),
        )[number]
        return self._send(self.core_in, src_row, dst, dst_row, h, 4 + number, to)

    def _sum_core(self, slot):
        self._core(slot).wait()
        row = slot * self.group
        add_rows(self.core_in, row, self.own, self.own_row(slot), self.core_in, row, self.group)

    def _sum_far(self, number, row, in_row):
        self._far(number).wait()
        add_rows(self.core_in, row, self.core_in, row, self.first_in, in_row, self.half)

    def start_core(self, slot):
        self._core(slot).start()

    def step(self, number):
        g, h = self.group, self.half
        if number == 0:
            for slot in (3, 2, 1, 0):
                self.start_core(slot)
        elif number == 1:
            self._sum_core(3)
            self._far(0).start()
            self._far(1).start()
        elif number == 2:
            self._sum_core(2)
            self._far(2).start()
            self._sum_core(1)
            self._far(3).start()
            self._sum_core(0)
        elif number == 3:
            self._sum_far(0, 1 * g, h)
            self._far(4).start()
            self._sum_far(1, 2 * g + h, 3 * h)
            self._far(5).start()
        elif number == 4:
            self._sum_far(2, 0, 0)
            self._sum_far(3, h, 2 * h)
        else:
            self._far(4).wait()
            add_rows(self.out, 0, self.core_in, 0, self.second_in, 0, h)
            self._far(5).wait()
            add_rows(self.out, h, self.core_in, h, self.second_in, h, h)

    @staticmethod
    def scratch(group, columns):
        return [
            pltpu.VMEM((4 * group, columns), jnp.bfloat16),
            pltpu.VMEM((2 * group, columns), jnp.bfloat16),
            pltpu.VMEM((group, columns), jnp.bfloat16),
        ]


class LineReduce:
    COPIES = 2 * (LINE - 1) * LINE
    EVENTS = ((0, 0), (0, 1), (1, 0), (0, 2), (1, 1), (2, 0))

    def __init__(self, wires, part, rows, landing, ways=(1, -1)):
        self.wires, self.part, self.rows, self.landing, self.ways = wires, part, rows, landing, ways
        self.first = wires.take(self.COPIES)

    def _place(self, way, hop, nearer):
        return (LINE - 1 - nearer, hop) if way == 1 else (nearer, LINE - 1 - hop)

    def _copy(self, way, hop, nearer, z):
        side = self.ways.index(way)
        block, _ = self._place(way, hop, nearer)
        return self.wires.copy(
            self.part.at[pl.ds(block * self.rows, self.rows)],
            self.landing.at[pl.ds((side * LINE + block) * self.rows, self.rows)],
            self.first + (side * (LINE - 1) + hop) * LINE + nearer,
            z=z,
        )

    def _send(self, way, hop, nearer):
        z = self.wires.z

        @pl.when(z == self._place(way, hop, nearer)[1])
        def _():
            self._copy(way, hop, nearer, z + way).start()

    def begin(self):
        for nearer in range(LINE - 1):
            for way in self.ways:
                self._send(way, 0, nearer)

    def event(self, number):
        hop, nearer = self.EVENTS[number]
        z, rows = self.wires.z, self.rows
        for way in self.ways:
            block, source = self._place(way, hop, nearer)

            @pl.when(z == source + way)
            def _():
                self._copy(way, hop, nearer, z).wait_recv()
                landed = (self.ways.index(way) * LINE + block) * rows
                add_rows(
                    self.part, block * rows, self.part, block * rows, self.landing, landed, rows
                )
                if nearer < LINE - 2 - hop:
                    self._copy(way, hop + 1, nearer, z + way).start()

    def finish(self, outs):
        z, rows = self.wires.z, self.rows

        @pl.loop(0, rows // 16)
        def _(step):
            row = pl.multiple_of(z * rows + step * 16, 16)
            begin = 0
            for out in outs:
                out[pl.ds(pl.multiple_of(step * 16, 16), 16), :] = self.part[
                    pl.ds(row, 16), begin : begin + out.shape[1]
                ].astype(out.dtype)
                begin += out.shape[1]

        for hop, nearer in self.EVENTS:
            for way in self.ways:

                @pl.when(z == self._place(way, hop, nearer)[1])
                def _():
                    self._copy(way, hop, nearer, z + way).wait_send()

    @staticmethod
    def scratch(rows, columns, ways=2):
        return pltpu.VMEM((ways * LINE * rows, columns), jnp.bfloat16)


def sems(count):
    return [pltpu.SemaphoreType.DMA((count,)), pltpu.SemaphoreType.DMA((count,))]


def kernel_params(collective_id, mib):
    return pltpu.CompilerParams(
        collective_id=collective_id, has_side_effects=True, vmem_limit_bytes=mib * MIB
    )


def dot(left, right, left_dim, right_dim):
    return lax.dot_general(
        left, right, (((left_dim,), (right_dim,)), ((), ())), preferred_element_type=jnp.float32
    )


def rows_at(begin, size):
    return pl.ds(pl.multiple_of(begin, 16), size)


def front(w_query, w_key, w_value, gains, w_out, cotangent, gates, tokens, starts, cosine, sine):
    rows, width = w_query.shape
    kv_width = w_key.shape[1] + w_value.shape[1]
    key_width = w_key.shape[1]
    tok_rows = tokens.shape[0]
    keys = LINE * tok_rows
    planes = 8
    group = LINE * rows
    w_rows = planes * group
    score_scale = HD ** (-0.5)
    per_group = HEADS // KVH

    def kernel(
        wq_ref, wk_ref, wv_ref, gains_ref, wo_ref, cot_ref, gate_ref, tok_ref, starts_ref, cos_ref, sin_ref,
        out_q, out_kv, out_o, out_cot, all_gate, query_ref, all_kv, lse_ref, mixed_ref, middle_ref, normed_ref,
        routed_ref, gain_rows_ref,
        full_q, full_kv, full_o, all_cot, bias, value_t, here, there, send, recv,
    ):
        wires = Wires(send, recv)
        dp, z = wires.dp, wires.z
        own = rows_at((dp * LINE + z) * rows, rows)
        locals_ = [
            (wk_ref, full_kv.at[own, pl.ds(0, key_width)]),
            (wv_ref, full_kv.at[own, pl.ds(key_width, kv_width - key_width)]),
            (gains_ref, full_kv.at[own, pl.ds(kv_width, LANES)]),
            (wq_ref, full_q.at[own]),
            (wo_ref, full_o.at[own]),
            (cot_ref, all_cot.at[rows_at(dp * tok_rows, tok_rows)]),
            (gate_ref, all_gate.at[pl.ds(pl.multiple_of(dp * 8, 8), 8)]),
        ]
        locals_ = [pltpu.make_async_copy(a, b, here.at[i]) for i, (a, b) in enumerate(locals_)]
        for one in locals_:
            one.start()
        greet(wires, range(1, planes), True)
        for one in locals_:
            one.wait()

        def block_rows(block):
            return rows_at((dp * LINE + block) * rows, rows)

        line_kv, line_q, line_o = [LineGather(wires, r, block_rows) for r in (full_kv, full_q, full_o)]
        plane_kv, plane_q, plane_o = [PlaneGather(wires, r, group) for r in (full_kv, full_q, full_o)]
        plane_cot = PlaneGather(wires, all_cot, tok_rows)
        line_keys = LineGather(wires, all_kv, lambda block: rows_at(block * tok_rows, tok_rows))
        first = wires.take(planes - 1)

        def gate_copy(mask, owner):
            part = all_gate.at[pl.ds(pl.multiple_of(owner * 8, 8), 8)]
            return wires.copy(part, part, first + mask - 1, dp=masked(dp, mask))

        line_kv.start(0)
        plane_cot.start(0)
        for mask in range(1, planes):
            gate_copy(mask, dp).start()
        line_kv.wait(0)
        line_kv.start(1)
        key_place = lax.broadcasted_iota(jnp.int32, (keys, tok_rows), 0)
        query_place = lax.broadcasted_iota(jnp.int32, (keys, tok_rows), 1) + z * tok_rows
        allowed = (key_place >= starts_ref[0:1, :]) & (key_place <= query_place)
        bias[...] = jnp.where(allowed, 0.0, masked_score)
        line_kv.wait(1)
        line_kv.start(2)
        line_q.start(0)
        line_kv.wait(2)
        plane_kv.start(0)
        plane_cot.wait(0)
        line_q.wait(0)
        line_q.start(1)
        plane_kv.wait(0)
        plane_kv.start(1)
        plane_cot.start(1, far=False)
        line_q.wait(1)
        line_q.start(2)
        line_o.start(0)
        plane_kv.wait(1)
        plane_kv.start(2)
        plane_kv.wait(2)
        plane_kv.start(3)
        plane_kv.finish()
        line_q.wait(2)
        plane_q.start(0)

        gain_rows_ref[...] = full_kv[:, kv_width:].astype(jnp.float32).T[:8, :]
        tile = 32

        @pl.loop(0, tok_rows // tile)
        def _(step):
            cut = pl.ds(pl.multiple_of(step * tile, tile), tile)
            normed_ref[cut, :] = rms_norm(
                tok_ref[cut, :].astype(jnp.float32), gain_rows_ref[0:1, :]
            ).astype(jnp.bfloat16)

        own_keys = rows_at(z * tok_rows, tok_rows)
        pre = dot(normed_ref[...], full_kv[:, :kv_width], 1, 0)
        for pair in range(KVH):
            cut = slice(pair * HD, (pair + 1) * HD)
            all_kv[own_keys, cut] = turned(pre[:, cut], cos_ref[...], sin_ref[...]).astype(jnp.bfloat16)
        all_kv[own_keys, key_width:] = pre[:, key_width:].astype(jnp.bfloat16)
        line_keys.start(0)
        line_o.wait(0)
        line_o.start(1)
        plane_q.wait(0)
        plane_q.start(1)
        plane_cot.wait(1)
        plane_cot.start(2)
        line_keys.wait(0)
        line_keys.start(1)
        line_o.wait(1)
        line_o.start(2)
        line_keys.wait(1)
        line_keys.start(2)
        line_o.wait(2)
        plane_o.start(0)
        plane_q.wait(1)
        plane_q.start(2)
        plane_q.wait(2)
        plane_q.start(3)
        plane_q.finish()
        saves = [pltpu.make_async_copy(full_q, out_q, there.at[0])]
        saves.append(pltpu.make_async_copy(full_kv, out_kv, there.at[1]))
        saves[0].start()
        saves[1].start()

        @pl.loop(0, HEADS // 2)
        def _(step):
            wide = pl.ds(pl.multiple_of(step * 2 * HD, 2 * HD), 2 * HD)
            pre_q = dot(normed_ref[...], full_q[:, wide], 1, 0)
            for one in range(2):
                query_ref[:, pl.ds(pl.multiple_of((2 * step + one) * HD, HD), HD)] = turned(
                    pre_q[:, one * HD : (one + 1) * HD], cos_ref[...], sin_ref[...]
                ).astype(jnp.bfloat16)

        plane_o.wait(0)
        plane_o.start(1)
        plane_cot.start_far()
        line_keys.wait(2)
        value_t[...] = all_kv[:, key_width:].astype(jnp.float32).T.astype(jnp.bfloat16)
        lse_ref[...] = jnp.zeros_like(lse_ref)

        def attend(head):
            own_cut = pl.ds(pl.multiple_of(head * HD, HD), HD)
            key_cut = pl.ds(pl.multiple_of((head // per_group) * HD, HD), HD)
            scores = dot(all_kv[:, key_cut], query_ref[:, own_cut], 1, 1) * score_scale + bias[...]
            top = jnp.max(scores, axis=0, keepdims=True)
            expo = jnp.exp(scores - top)
            total = jnp.sum(expo, axis=0, keepdims=True)
            lse_ref[pl.ds(head, 1), :] = top + jnp.log(total)
            probs = (expo * (1.0 / total)).astype(jnp.bfloat16)
            mixed_ref[:, own_cut] = dot(value_t[key_cut, :], probs, 1, 0).T.astype(jnp.bfloat16)

        pl.loop(0, HEADS)(attend)
        plane_o.wait(1)
        plane_o.start(2)
        plane_o.wait(2)
        plane_o.start(3)
        plane_o.finish()
        saves.append(pltpu.make_async_copy(full_o, out_o, there.at[2]))
        saves[2].start()

        @pl.loop(0, width // 512)
        def _(step):
            cut = pl.ds(pl.multiple_of(step * 512, 512), 512)
            middle_ref[:, cut] = tok_ref[:, cut].astype(jnp.float32) + dot(
                mixed_ref[...], full_o[:, cut], 1, 0
            )

        @pl.loop(0, tok_rows // tile)
        def _(step):
            cut = pl.ds(pl.multiple_of(step * tile, tile), tile)
            routed_ref[cut, :] = rms_norm(middle_ref[cut, :], gain_rows_ref[1:2, :]).astype(jnp.bfloat16)

        plane_cot.wait(2)
        plane_cot.start(3)
        plane_cot.finish()
        saves.append(pltpu.make_async_copy(all_cot, out_cot, there.at[3]))
        saves[3].start()
        for mask in range(1, planes):
            gate_copy(mask, masked(dp, mask)).wait_recv()
        for mask in range(1, planes):
            gate_copy(mask, dp).wait_send()
        for one in (line_kv, line_q, line_o, line_keys):
            one.finish()
        for one in saves:
            one.wait()

    f32, low = jnp.float32, jnp.bfloat16
    copies = 4 * LineGather.COPIES + 4 * PlaneGather.COPIES + planes - 1
    return pl.pallas_call(
        kernel,
        out_shape=(
            jax.ShapeDtypeStruct((w_rows, width), low),
            jax.ShapeDtypeStruct((w_rows, kv_width + LANES), low),
            jax.ShapeDtypeStruct((w_rows, width), low),
            jax.ShapeDtypeStruct((planes * tok_rows, width), low),
            jax.ShapeDtypeStruct((planes * 8, tok_rows), f32),
            jax.ShapeDtypeStruct((tok_rows, width), low),
            jax.ShapeDtypeStruct((keys, kv_width), low),
            jax.ShapeDtypeStruct((16, tok_rows), f32),
            jax.ShapeDtypeStruct((tok_rows, width), low),
            jax.ShapeDtypeStruct((tok_rows, width), f32),
            jax.ShapeDtypeStruct((tok_rows, width), low),
            jax.ShapeDtypeStruct((tok_rows, width), low),
            jax.ShapeDtypeStruct((8, width), f32),
        ),
        in_specs=[VMEM] * 11,
        out_specs=(ANY,) * 4 + (VMEM,) * 9,
        scratch_shapes=[
            pltpu.VMEM((w_rows, width), low),
            pltpu.VMEM((w_rows, kv_width + LANES), low),
            pltpu.VMEM((w_rows, width), low),
            pltpu.VMEM((planes * tok_rows, width), low),
            pltpu.VMEM((keys, tok_rows), f32),
            pltpu.VMEM((kv_width - key_width, keys), low),
            pltpu.SemaphoreType.DMA((7,)),
            pltpu.SemaphoreType.DMA((4,)),
        ]
        + sems(copies),
        compiler_params=kernel_params(0, 63),
        name="front",
    )(w_query, w_key, w_value, gains, w_out, cotangent, gates, tokens, starts, cosine, sine)


CHUNK = 64
AHEAD = 4
CARRIED = 2
RING = 4
BEFORE_DENSE = 16


class LineSum:
    def __init__(self, wires, own, out, landing, rows, chunks, came=False, goes_on=False):
        self.wires, self.own, self.out, self.landing = wires, own, out, landing
        self.rows, self.chunks, self.came, self.goes_on = rows, chunks, came, goes_on
        self.all = chunks + (CARRIED if goes_on else 0)
        self.begun = CARRIED if came else 0
        self.now = self.begun
        self.first = wires.take(3 * self.all)
        z = wires.z
        self.inner = (z == 1) | (z == 2)
        self.outer = (z == 0) | (z == 3)
        self.end = 3 * (z - 1)
        self.near = 1 + z // 3
        self.peer = 3 - z

    def _cut(self, ref, chunk):
        return ref.at[pl.ds(pl.multiple_of(chunk * self.rows, 16), self.rows)]

    def _in(self, chunk):
        return self.wires.copy(
            self._cut(self.own, chunk), self._cut(self.out, chunk), self.first + chunk, z=self.near
        )

    def _across(self, chunk):
        number = self.first + self.all + chunk
        return self.wires.copy(
            self._cut(self.own, chunk), self._cut(self.landing, lax.rem(chunk, RING)), number, z=self.peer
        )

    def _back(self, chunk, ref=None):
        number = self.first + 2 * self.all + chunk
        return self.wires.copy(
            self._cut(self.out if ref is None else ref, chunk), self._cut(self.out, chunk), number, z=self.end
        )

    def begin(self):
        @pl.when(self.outer)
        def _():
            for chunk in range(self.begun, min(self.begun + AHEAD, self.all)):
                self._in(chunk).start()

        if self.came:

            @pl.when(self.inner)
            def _():
                self._across(1).start()
                self._back(0, self.own).start()
                self.out[pl.ds(0, self.rows), :] = self.own[pl.ds(0, self.rows), :]

    def tick(self, count=1):
        for _ in range(count):
            if self.now < self.all + (0 if self.goes_on else 1):
                self._tick(self.now)
            self.now += 1

    def _tick(self, chunk):
        if chunk < self.all:

            @pl.when(self.outer)
            def _():
                self._in(chunk).wait_send()
                if chunk + AHEAD < self.all:
                    self._in(chunk + AHEAD).start()

        @pl.when(self.inner)
        def _():
            if chunk < self.all:
                row = chunk * self.rows
                self._in(chunk).wait_recv()
                add_rows(self.own, row, self.own, row, self.out, row, self.rows)
                if chunk <= self.chunks:
                    self._across(chunk).start()
            if chunk >= 1:
                row = (chunk - 1) * self.rows
                landed = (chunk - 1) % RING * self.rows
                self._across(chunk - 1).wait_recv()
                if chunk - 1 < self.chunks:
                    add_rows(self.out, row, self.own, row, self.landing, landed, self.rows)
                    self._back(chunk - 1).start()
                else:
                    self._across(chunk - 1).wait_send()
                    add_rows(self.own, row, self.own, row, self.landing, landed, self.rows)

    def finish(self):
        self.tick(max(0, self.all + (0 if self.goes_on else 1) - self.now))

        @pl.when(self.outer)
        def _():
            @pl.loop(0, self.chunks)
            def _(chunk):
                self._back(chunk).wait_recv()

        @pl.when(self.inner)
        def _():
            @pl.loop(1 if self.came else 0, self.chunks)
            def _(chunk):
                self._across(chunk).wait_send()

            @pl.loop(0, self.chunks)
            def _(chunk):
                self._back(chunk).wait_send()


def norm_back(values, gain, grad):
    scale = lax.rsqrt(jnp.mean(values * values, axis=-1, keepdims=True) + epsilon)
    normal = values * scale
    inner = grad * gain
    to_values = scale * (inner - normal * jnp.mean(inner * normal, axis=-1, keepdims=True))
    return to_values, grad * normal


def turned(values, cosine, sine):
    return values * cosine + pltpu.roll(values, HD // 2, 1) * sine


def experts_attention(
    routed,
    all_cot,
    all_gate,
    w_gate,
    w_up,
    w_down,
    full_o,
    middle,
    cotangent,
    gain_rows,
    mixed,
    query,
    all_kv,
    lse,
    starts,
    cosine,
    sine,
):
    tok_rows, width = routed.shape
    hidden_width = w_gate.shape[1]
    keys, kv_width = all_kv.shape
    total_rows = 8 * tok_rows
    sum_rows = width + hidden_width
    group = width // 8
    chunks = BEFORE_DENSE
    score_scale = HD ** (-0.5)
    per_group = HEADS // KVH
    q_width = HEADS * HD

    def kernel(
        routed_ref, all_cot_ref, gate_ref, wg_ref, wu_ref, wd_ref, full_o_hbm, middle_hbm, cot_hbm, gain_ref, mixed_hbm,
        query_hbm, kv_hbm, lse_ref, starts_ref, cos_ref, sin_ref,
        sums_ref, prod_ref, total_ref, grad_mid_hbm, grad_pre_ref, gain_row_ref, w_out_ref,
        w_in, w_down, x_all, y_all, hidden, grad_hidden, grad_in, sums, sums_land, gate_t, core_in, first_in, second_in,
        routed_grad, middle_ref, key_t, kv_land, here, there, freed, send, recv,
    ):
        wires = Wires(send, recv)
        dp, z = wires.dp, wires.z

        def rows_begin(block):
            return pl.multiple_of(block * tok_rows, 16)

        def cut_of(block):
            return pl.ds(rows_begin(block), tok_rows)

        full_o_ref = w_in
        part_o = y_all.at[pl.ds(0, width)]
        query_ref, mixed_ref, cot_ref, attn_low, mixed_grad = [grad_in.at[pl.ds(i * tok_rows, tok_rows)] for i in range(5)]
        kv_ref = hidden.at[pl.ds(0, keys), pl.ds(0, kv_width)]
        kv_part = hidden.at[pl.ds(keys, keys), pl.ds(0, kv_width)]
        kv_grad = grad_hidden.at[pl.ds(0, keys), pl.ds(0, kv_width)]
        bias = grad_hidden.at[pl.ds(keys, keys), pl.ds(0, tok_rows)]
        kv_out = grad_hidden.at[pl.ds(keys, tok_rows), pl.ds(tok_rows, kv_width)]

        loads = [
            (routed_ref, x_all.at[cut_of(dp)]),
            (wd_ref, w_down),
            (all_cot_ref, y_all),
            (wg_ref, w_in.at[:, pl.ds(0, hidden_width)]),
            (wu_ref, w_in.at[:, pl.ds(hidden_width, hidden_width)]),
            (middle_hbm, middle_ref),
        ]
        later = [(full_o_hbm, full_o_ref), (query_hbm, query_ref), (mixed_hbm, mixed_ref), (cot_hbm, cot_ref), (kv_hbm, kv_ref)]
        loads = [pltpu.make_async_copy(a, b, here.at[i]) for i, (a, b) in enumerate(loads + later)]
        loads, later = loads[: len(loads) - len(later)], loads[len(loads) - len(later) :]
        for one in loads:
            one.start()
        greet(wires, (1, 2, 4), True)
        loads[0].wait()
        spread = PlaneGather(wires, x_all, tok_rows)
        plane = PlaneReduce(
            wires, y_all, tok_rows, y_all, lambda slot: rows_begin(masked(dp, 2 * slot)), core_in, first_in, second_in,
            routed_grad,
        )
        summed = LineSum(wires, sums, total_ref, sums_land, CHUNK, chunks, goes_on=True)
        dense = PlaneReduce(
            wires, part_o, group, part_o, lambda slot: pl.multiple_of(masked(dp, 2 * slot) * group, 16),
            core_in, first_in, second_in, w_out_ref,
        )
        line = LineReduce(wires, kv_part, tok_rows, kv_land, ways=(-1,))
        spread.start(0)
        gate_t[...] = gate_ref[...].T

        def gate_of(block):
            lane = lax.broadcasted_iota(jnp.int32, gate_t.shape, 1)
            return jnp.sum(jnp.where(lane == block * 8 + dp, gate_t[...], 0.0), axis=1, keepdims=True)

        def back_hidden(block):
            cut = cut_of(block)
            y_all[cut, :] = (y_all[cut, :].astype(jnp.float32) * gate_of(block)).astype(jnp.bfloat16)
            grad_hidden[cut, :] = dot(y_all[cut, :], w_down[...], 1, 1)

        def through(mask):
            cut = cut_of(masked(dp, mask))
            acts = dot(x_all[cut, :], w_in[...], 1, 0)
            gate_act, up_act = acts[:, :hidden_width], acts[:, hidden_width:]
            share = jax.nn.sigmoid(gate_act)
            silu = gate_act * share
            hidden[cut, :] = (silu * up_act).astype(jnp.bfloat16)
            grad = grad_hidden[cut, :]
            grad_in[cut, :hidden_width] = (
                grad * up_act * share * (1.0 + gate_act * (1.0 - share))
            ).astype(jnp.bfloat16)
            grad_in[cut, hidden_width:] = (grad * silu).astype(jnp.bfloat16)

        loads[1].wait()
        loads[2].wait()
        pl.loop(0, 4)(back_hidden)
        spread.wait(0)
        spread.start(1)
        pl.loop(4, 8)(back_hidden)
        loads[3].wait()
        loads[4].wait()
        through(0)
        spread.wait_core(0)
        through(1)
        spread.wait(1)
        spread.start(2)
        through(2)
        through(4)
        spread.wait_core(1)
        spread.wait_core(2)
        through(3)
        through(5)
        spread.wait(2)
        spread.start(3)
        through(6)
        spread.wait_core(3)
        through(7)

        def weights_down(step):
            cut = rows_at(step * 256, 256)
            sums[cut, :] = dot(hidden[:, cut], y_all[...], 0, 0).astype(jnp.bfloat16)

        def weights_in(step):
            cut = rows_at(step * 256, 256)
            out = rows_at(hidden_width + step * 256, 256)
            sums[out, :] = dot(x_all[:, cut], grad_in[...], 0, 0).astype(jnp.bfloat16)

        def save_sums(begin, end, number):
            rows = pl.ds(begin, end - begin)
            return pltpu.make_async_copy(sums.at[rows], sums_ref.at[rows], there.at[number])

        pl.loop(0, 1)(weights_down)
        summed.begin()
        pl.loop(1, 3)(weights_down)
        spread.finish()

        def input_grads(side):
            for slot in (3, 2, 1, 0):
                cut = cut_of(masked(dp, 2 * slot + side))
                y_all[cut, :] = dot(grad_in[cut, :], w_in[...], 1, 1).astype(jnp.bfloat16)
                if side:
                    plane.start_core(slot)

        input_grads(1)
        summed.tick()
        input_grads(0)
        summed.tick()
        later[0].start()
        plane.step(1)
        plane.step(2)
        summed.tick()
        pl.loop(0, 2)(weights_in)
        summed.tick()
        pl.loop(2, 4)(weights_in)
        summed.tick()
        plane.step(3)
        pl.loop(4, 6)(weights_in)
        summed.tick()
        for one in later[1:4]:
            one.start()
        saved = (chunks + CARRIED) * CHUNK
        save = save_sums(saved, sum_rows, 0)
        save.start()

        def save_made(block):
            return pltpu.make_async_copy(
                x_all.at[cut_of(block)], prod_ref.at[cut_of(block)], there.at[3 + block]
            )

        def make(block):
            made = dot(hidden[cut_of(block), :], w_down[...], 1, 0).astype(jnp.bfloat16).astype(jnp.float32)
            x_all[cut_of(block), :] = (made * gate_of(block)).astype(jnp.bfloat16)
            save_made(block).start()

        pl.loop(0, 4)(make)
        summed.tick()
        pl.loop(4, 8)(make)
        later[4].start()
        plane.step(4)
        summed.tick()
        key_place = lax.broadcasted_iota(jnp.int32, (keys, tok_rows), 0)
        query_place = lax.broadcasted_iota(jnp.int32, (keys, tok_rows), 1) + z * tok_rows
        allowed = (key_place >= starts_ref[0:1, :]) & (key_place <= query_place)
        bias[...] = jnp.where(allowed, 0.0, masked_score)
        kv_grad[...] = jnp.zeros_like(kv_grad)
        gain_row_ref[...] = jnp.zeros_like(gain_row_ref)
        loads[5].wait()
        for one in later:
            one.wait()
        key_t[...] = kv_ref[:, : kv_width // 2].astype(jnp.float32).T.astype(jnp.bfloat16)
        summed.tick()
        plane.step(5)
        for mask in (1, 2, 4):
            pl.semaphore_signal(freed, inc=1, device_id=(masked(dp, mask), z), device_id_type=MESH)

        tile = 32

        @pl.loop(0, tok_rows // tile)
        def _(step):
            cut = pl.ds(pl.multiple_of(step * tile, tile), tile)
            to_middle, terms = norm_back(middle_ref[cut, :], gain_ref[1:2, :], routed_grad[cut, :])
            to_middle = cot_ref[cut, :].astype(jnp.float32) + to_middle
            middle_ref[cut, :] = to_middle
            attn_low[cut, :] = to_middle.astype(jnp.bfloat16)
            gain_row_ref[0:1, :] += jnp.sum(terms, axis=0, keepdims=True)

        save_mid = pltpu.make_async_copy(middle_ref, grad_mid_hbm, there.at[1])
        save_mid.start()
        summed.tick()
        wide = 512

        @pl.loop(0, width // wide)
        def _(step):
            cut = pl.ds(pl.multiple_of(step * wide, wide), wide)
            mixed_grad[:, cut] = dot(attn_low[...], full_o_ref[cut, :], 1, 1).astype(jnp.bfloat16)

        @pl.loop(0, width // 256)
        def _(step):
            cut = pl.ds(pl.multiple_of(step * 256, 256), 256)
            part_o[cut, :] = dot(mixed_ref[:, cut], attn_low[...], 0, 0).astype(jnp.bfloat16)

        pl.semaphore_wait(freed, 3)
        dense.step(0)
        summed.tick()

        def heads(first, last):
            @pl.loop(first, last)
            def _(head):
                own_cut = pl.ds(pl.multiple_of(head * HD, HD), HD)
                pair = head // per_group
                key_cut = pl.ds(pl.multiple_of(pair * HD, HD), HD)
                value_cut = pl.ds(pl.multiple_of((KVH + pair) * HD, HD), HD)
                q, do = query_ref[:, own_cut], mixed_grad[:, own_cut]
                k, v = kv_ref[:, key_cut], kv_ref[:, value_cut]
                scores = dot(k, q, 1, 1) * score_scale + bias[...]
                probs = jnp.exp(scores - lse_ref[pl.ds(head, 1), :])
                grad_probs = dot(v, do, 1, 1)
                inner = jnp.sum(probs * grad_probs, axis=0, keepdims=True)
                grad_raw = (probs * (grad_probs - inner) * score_scale).astype(jnp.bfloat16)
                kv_grad[:, value_cut] += dot(probs.astype(jnp.bfloat16), do, 1, 0)
                kv_grad[:, key_cut] += dot(grad_raw, q, 1, 0)
                to_query = dot(key_t[key_cut, :], grad_raw, 1, 0).T
                grad_pre_ref[:, own_cut] = turned(to_query, cos_ref[...], -sin_ref[...]).astype(
                    jnp.bfloat16
                )

        heads(0, 3)
        summed.tick()
        dense.step(1)
        dense.step(2)
        heads(3, 6)
        summed.tick()
        heads(6, 9)
        summed.tick()
        heads(9, 12)
        kv_part[...] = kv_grad[...].astype(jnp.bfloat16)
        line.begin()
        summed.tick()
        dense.step(3)
        summed.tick()
        line.event(0)
        summed.tick()
        dense.step(4)
        line.event(1)
        line.event(2)
        summed.tick()
        line.event(3)
        line.event(4)
        dense.step(5)
        summed.tick(max(0, summed.all - summed.now))
        save_last = save_sums(chunks * CHUNK, saved, 2)
        save_last.start()
        line.event(5)
        line.finish((kv_out,))
        for pair in range(KVH):
            cut = slice(pair * HD, (pair + 1) * HD)
            grad_pre_ref[:, q_width + pair * HD : q_width + (pair + 1) * HD] = turned(
                kv_out[:, cut], cos_ref[...], -sin_ref[...]
            ).astype(jnp.bfloat16)
        grad_pre_ref[:, q_width + kv_width // 2 :] = kv_out[:, kv_width // 2 :].astype(jnp.bfloat16)
        summed.finish()
        for block in range(8):
            save_made(block).wait()
        for one in (save, save_mid, save_last):
            one.wait()

    f32, low = jnp.float32, jnp.bfloat16
    return pl.pallas_call(
        kernel,
        out_shape=(
            jax.ShapeDtypeStruct((sum_rows, width), low),
            jax.ShapeDtypeStruct((total_rows, width), low),
            jax.ShapeDtypeStruct(((chunks + CARRIED) * CHUNK, width), low),
            jax.ShapeDtypeStruct((tok_rows, width), f32),
            jax.ShapeDtypeStruct((tok_rows, width + kv_width), low),
            jax.ShapeDtypeStruct((8, width), f32),
            jax.ShapeDtypeStruct((group, width), low),
        ),
        in_specs=[ANY, ANY, VMEM] + [ANY] * 6 + [VMEM] + [ANY] * 3 + [VMEM] * 4,
        out_specs=(ANY, ANY, VMEM, ANY, VMEM, VMEM, VMEM),
        scratch_shapes=[
            pltpu.VMEM((width, 2 * hidden_width), low),
            pltpu.VMEM((hidden_width, width), low),
            pltpu.VMEM((total_rows, width), low),
            pltpu.VMEM((total_rows, width), low),
            pltpu.VMEM((total_rows, hidden_width), low),
            pltpu.VMEM((total_rows, hidden_width), f32),
            pltpu.VMEM((total_rows, 2 * hidden_width), low),
            pltpu.VMEM((sum_rows, width), low),
            pltpu.VMEM((RING * CHUNK, width), low),
            pltpu.VMEM((tok_rows, 64), f32),
        ]
        + PlaneReduce.scratch(tok_rows, width)
        + [
            pltpu.VMEM((tok_rows, width), f32),
            pltpu.VMEM((tok_rows, width), f32),
            pltpu.VMEM((kv_width // 2, keys), low),
            LineReduce.scratch(tok_rows, kv_width, 1),
            pltpu.SemaphoreType.DMA((11,)),
            pltpu.SemaphoreType.DMA((11,)),
            pltpu.SemaphoreType.REGULAR,
        ]
        + sems(
            PlaneGather.COPIES + 2 * PlaneReduce.COPIES + 3 * (chunks + CARRIED) + LineReduce.COPIES
        ),
        compiler_params=kernel_params(1, 63),
        name="experts_attention",
    )(
        routed, all_cot, all_gate, w_gate, w_up, w_down, full_o, middle, cotangent, gain_rows, mixed, query, all_kv,
        lse, starts, cosine, sine,
    )


def back_dense(sums_in, produced, full_q, full_kv, normed, grad_pre, tokens, gains, grad_mid, gain_row, w_out_part, middle):
    tok_rows, width = middle.shape
    q_width = full_q.shape[1]
    in_width = q_width + full_kv.shape[1]
    pre_width = in_width - LANES
    w_rows = width
    group, rows = w_rows // 8, w_rows // (8 * LINE)
    skipped = BEFORE_DENSE
    chunks = sums_in.shape[0] // CHUNK - skipped

    def kernel(
        sums_ref, prod_ref, full_q_hbm, full_kv_hbm, normed_hbm, pre_hbm, tok_hbm, gain_ref, mid_grad_hbm,
        gain_row_ref, o_part_hbm, middle_hbm,
        total_ref, layer_ref, tok_grad_ref, wq_ref, wk_ref, wv_ref, gains_ref, out_ref,
        sums_own, sums_land, full_q_ref, full_kv_ref, normed_ref, pre_ref, tok_ref, mid_grad_ref, middle_ref, own, core_in, first_in, second_in, moe, part, d_core, d_first, d_second, in_sums,
        in_land, o_sums, o_land, normed_grad, gain_rows, here, send, recv,
    ):
        wires = Wires(send, recv)
        dp, z = wires.dp, wires.z
        early = (CARRIED + AHEAD) * CHUNK
        begin = skipped * CHUNK
        loads = [
            pltpu.make_async_copy(sums_ref.at[pl.ds(begin, early)], sums_own.at[pl.ds(0, early)], here.at[0]),
            pltpu.make_async_copy(
                sums_ref.at[pl.ds(begin + early, chunks * CHUNK - early)],
                sums_own.at[pl.ds(early, chunks * CHUNK - early)],
                here.at[1],
            ),
            pltpu.make_async_copy(o_part_hbm, o_sums, here.at[2]),
            pltpu.make_async_copy(pre_hbm, pre_ref, here.at[3]),
            pltpu.make_async_copy(full_q_hbm, full_q_ref, here.at[4]),
            pltpu.make_async_copy(full_kv_hbm, full_kv_ref, here.at[5]),
            pltpu.make_async_copy(tok_hbm, tok_ref, here.at[6]),
            pltpu.make_async_copy(mid_grad_hbm, mid_grad_ref, here.at[7]),
            pltpu.make_async_copy(normed_hbm, normed_ref, here.at[8]),
            pltpu.make_async_copy(middle_hbm, middle_ref, here.at[9]),
        ]
        first_loads = len(loads)
        for slot in range(4):
            row = pl.multiple_of(masked(dp, 2 * slot) * tok_rows, 16)
            loads.append(
                pltpu.make_async_copy(
                    prod_ref.at[pl.ds(row, tok_rows)],
                    own.at[pl.ds(slot * tok_rows, tok_rows)],
                    here.at[first_loads + slot],
                )
            )
        for one in loads:
            one.start()
        greet(wires, (1, 2, 4), True)
        summed = LineSum(wires, sums_own, total_ref, sums_land, CHUNK, chunks, came=True)
        dense = PlaneReduce(
            wires, part, group, part, lambda slot: pl.multiple_of(masked(dp, 2 * slot) * group, 16),
            d_core, d_first, d_second, in_sums,
        )
        plane = PlaneReduce(
            wires, prod_ref, tok_rows, own, lambda slot: slot * tok_rows, core_in, first_in, second_in, moe
        )
        o_line = LineReduce(wires, o_sums, rows, o_land)
        in_line = LineReduce(wires, in_sums, rows, in_land)
        loads[0].wait()
        summed.begin()
        loads[1].wait()
        loads[2].wait()
        o_line.begin()
        for one in loads[3:first_loads]:
            one.wait()
        wide = 512

        @pl.loop(0, width // wide)
        def _(step):
            cut = pl.ds(pl.multiple_of(step * wide, wide), wide)
            normed_grad[:, cut] = dot(pre_ref[:, :q_width], full_q_ref[cut, :], 1, 1) + dot(
                pre_ref[:, q_width:], full_kv_ref[cut, : pre_width - q_width], 1, 1
            )

        summed.tick()
        gain_rows[...] = jnp.zeros_like(gain_rows)
        gain_rows[1:2, :] = gain_row_ref[0:1, :]
        tile = 32

        @pl.loop(0, tok_rows // tile)
        def _(step):
            cut = pl.ds(pl.multiple_of(step * tile, tile), tile)
            to_tokens, terms = norm_back(
                tok_ref[cut, :].astype(jnp.float32), gain_ref[0:1, :], normed_grad[cut, :]
            )
            tok_grad_ref[cut, :] = mid_grad_ref[cut, :] + to_tokens
            gain_rows[0:1, :] += jnp.sum(terms, axis=0, keepdims=True)

        summed.tick()
        o_line.event(0)
        part[:, pre_width:] = gain_rows[...].T.astype(jnp.bfloat16)

        @pl.loop(0, w_rows // 256)
        def _(step):
            cut = pl.ds(pl.multiple_of(step * 256, 256), 256)
            part[cut, :pre_width] = dot(normed_ref[:, cut], pre_ref[...], 0, 0).astype(jnp.bfloat16)

        dense.step(0)
        o_line.event(1)
        o_line.event(2)
        summed.tick(2)
        dense.step(1)
        o_line.event(3)
        summed.tick()
        dense.step(2)
        o_line.event(4)
        summed.tick()
        o_line.event(5)
        for one in loads[first_loads:]:
            one.wait()
        plane.step(0)
        summed.tick(2)
        plane.step(1)
        summed.tick()
        dense.step(3)
        plane.step(2)
        summed.tick(2)
        dense.step(4)
        dense.step(5)
        in_line.begin()
        summed.tick()
        in_line.event(0)
        summed.tick()
        plane.step(3)
        in_line.event(1)
        in_line.event(2)
        summed.tick(2)
        in_line.event(3)
        in_line.event(4)
        plane.step(4)
        summed.tick(2)
        in_line.event(5)
        plane.step(5)
        summed.tick(2)

        @pl.loop(0, tok_rows // tile)
        def _(step):
            cut = pl.ds(pl.multiple_of(step * tile, tile), tile)
            layer_ref[cut, :] = (middle_ref[cut, :] + moe[cut, :]).astype(jnp.bfloat16)

        o_line.finish((out_ref,))
        in_line.finish((wq_ref, wk_ref, wv_ref, gains_ref))
        summed.finish()

    f32, low = jnp.float32, jnp.bfloat16
    return pl.pallas_call(
        kernel,
        out_shape=(
            jax.ShapeDtypeStruct((chunks * CHUNK, sums_in.shape[1]), low),
            jax.ShapeDtypeStruct((tok_rows, width), low),
            jax.ShapeDtypeStruct((tok_rows, width), f32),
            jax.ShapeDtypeStruct((rows, q_width), f32),
            jax.ShapeDtypeStruct((rows, (pre_width - q_width) // 2), f32),
            jax.ShapeDtypeStruct((rows, (pre_width - q_width) // 2), f32),
            jax.ShapeDtypeStruct((rows, LANES), f32),
            jax.ShapeDtypeStruct((rows, width), f32),
        ),
        in_specs=[ANY] * 7 + [VMEM, ANY, VMEM, ANY, ANY],
        out_specs=(VMEM,) * 8,
        scratch_shapes=[
            pltpu.VMEM((chunks * CHUNK, width), low),
            pltpu.VMEM((RING * CHUNK, width), low),
            pltpu.VMEM(full_q.shape, low),
            pltpu.VMEM(full_kv.shape, low),
            pltpu.VMEM((tok_rows, width), low),
            pltpu.VMEM((tok_rows, pre_width), low),
            pltpu.VMEM((tok_rows, width), low),
            pltpu.VMEM((tok_rows, width), f32),
            pltpu.VMEM((tok_rows, width), f32),
            pltpu.VMEM((4 * tok_rows, width), low),
        ]
        + PlaneReduce.scratch(tok_rows, width)
        + [pltpu.VMEM((tok_rows, width), f32), pltpu.VMEM((w_rows, in_width), low)]
        + PlaneReduce.scratch(group, in_width)
        + [
            pltpu.VMEM((group, in_width), low),
            LineReduce.scratch(rows, in_width),
            pltpu.VMEM((group, width), low),
            LineReduce.scratch(rows, width),
            pltpu.VMEM((tok_rows, width), f32),
            pltpu.VMEM((LANES, width), f32),
            pltpu.SemaphoreType.DMA((14,)),
        ]
        + sems(3 * chunks + 2 * PlaneReduce.COPIES + 2 * LineReduce.COPIES),
        compiler_params=kernel_params(4, 63),
        name="back_dense",
    )(
        sums_in, produced, full_q, full_kv, normed, grad_pre, tokens, gains, grad_mid, gain_row, w_out_part, middle
    )


def on_plane_device(
    tokens,
    norm_attn,
    w_query,
    w_key,
    w_value,
    w_out,
    norm_moe,
    w_gate,
    w_up,
    w_down,
    routes,
    gate_values,
    lengths,
    cotangent,
):
    tok_rows = tokens.shape[0]
    ctx_size = lax.axis_size("ctx")
    ctx_place = lax.axis_index("ctx")
    group_places = jnp.arange(tok_rows * ctx_size, dtype=jnp.int32)
    seg_all, within_all = seq_tables(lengths[0], group_places)
    offset = ctx_place * tok_rows
    own_places = offset + jnp.arange(tok_rows, dtype=jnp.int32)
    within_own = lax.dynamic_slice_in_dim(within_all, offset, tok_rows)
    kv_columns = KVH * HD
    q_columns = HEADS * HD
    gains = jnp.pad(jnp.stack([norm_attn, norm_moe], axis=1), ((0, 0), (0, LANES - 2)))
    numbers = jnp.arange(8, dtype=jnp.int32)
    gates = jnp.sum(
        jnp.where(routes[None, :, :] == numbers[:, None, None], gate_values[None], 0.0), axis=2
    )
    half_size = HD // 2
    frequency = rope_base ** (-jnp.arange(half_size, dtype=jnp.float32) / half_size)
    angles = within_own.astype(jnp.float32)[:, None] * frequency[None, :]
    cosine = jnp.concatenate([jnp.cos(angles), jnp.cos(angles)], axis=1)
    sine = jnp.concatenate([-jnp.sin(angles), jnp.sin(angles)], axis=1)
    starts = jnp.broadcast_to((own_places - within_own)[None, :], (8, tok_rows))
    (
        full_q, full_kv, full_o, all_cot, all_gate, query, all_kv, lse, mixed_low, middle, normed_low, routed_low,
        gain_rows,
    ) = front(
        w_query, w_key, w_value, gains, w_out, cotangent, gates, tokens, starts, cosine, sine
    )
    partial_sums, produced, sums_head, grad_mid, grad_pre, gain_row, w_out_part = experts_attention(
        routed_low,
        all_cot,
        all_gate,
        w_gate[0],
        w_up[0],
        w_down[0],
        full_o,
        middle,
        cotangent,
        gain_rows,
        mixed_low,
        query,
        all_kv,
        lse,
        starts,
        cosine,
        sine,
    )
    half = w_gate.shape[2]
    sums_tail, layer_out, grad_tokens, sum_q, sum_k, sum_v, sum_gains, sum_o = back_dense(
        partial_sums,
        produced,
        full_q,
        full_kv,
        normed_low,
        grad_pre,
        tokens,
        gain_rows,
        grad_mid,
        gain_row,
        w_out_part,
        middle,
    )
    head = BEFORE_DENSE * CHUNK

    def whole(columns):
        return jnp.concatenate([sums_head[half:head, columns], sums_tail[:, columns]], axis=0)

    return (
        layer_out,
        grad_tokens,
        sum_gains[:, 0],
        sum_q,
        sum_k,
        sum_v,
        sum_o,
        sum_gains[:, 1],
        whole(slice(0, half)).astype(jnp.float32)[None],
        whole(slice(half, 2 * half)).astype(jnp.float32)[None],
        sums_head[:half].astype(jnp.float32)[None],
    )


def solution(mesh):
    on_plane = mesh.shape["dp"] == 8 and mesh.shape["ctx"] == LINE
    return jax.shard_map(
        on_plane_device if on_plane else on_device,
        mesh=mesh,
        in_specs=(
            P(("dp", "ctx"), None),
            P(("dp", "ctx")),
            P(("dp", "ctx"), None),
            P(("dp", "ctx"), None),
            P(("dp", "ctx"), None),
            P(("dp", "ctx"), None),
            P(("dp", "ctx")),
            P("dp", None, None),
            P("dp", None, None),
            P("dp", None, None),
            P(("dp", "ctx"), None),
            P(("dp", "ctx"), None),
            P("dp", None),
            P(("dp", "ctx"), None),
        ),
        out_specs=(
            P(("dp", "ctx"), None),
            P(("dp", "ctx"), None),
            P(("dp", "ctx")),
            P(("dp", "ctx"), None),
            P(("dp", "ctx"), None),
            P(("dp", "ctx"), None),
            P(("dp", "ctx"), None),
            P(("dp", "ctx")),
            P("dp", None, None),
            P("dp", None, None),
            P("dp", None, None),
        ),
        check_vma=False,
    )
```

```python
import functools

import jax
import jax.numpy as jnp
from jax import lax
from jax.experimental import pallas as pl
from jax.experimental.pallas import tpu as pltpu
from jax.sharding import PartitionSpec as P

D = 1536
HEADS = 12
KVH = 2
HD = 128
TOP = 4
EXP_DEV = 1


epsilon = 1e-06
rope_base = 1000000.0
masked_score = -1e30


def rms_norm(values, gain):
    return values * lax.rsqrt(jnp.mean(values * values, axis=-1, keepdims=True) + epsilon) * gain


def rotate(values, within, direction):
    half_size = values.shape[-1] // 2
    frequency = rope_base ** (-jnp.arange(half_size, dtype=jnp.float32) / half_size)
    angles = direction * within.astype(jnp.float32)[:, None] * frequency[None, :]
    cosine = jnp.cos(angles)[:, None, :]
    sine = jnp.sin(angles)[:, None, :]
    first_half = values[..., :half_size]
    second = values[..., half_size:]
    return jnp.concatenate(
        [first_half * cosine - second * sine, second * cosine + first_half * sine], axis=-1
    )


def seq_tables(length_row, places):
    seq_ends = jnp.cumsum(length_row)
    passed = places[:, None] >= seq_ends[None, :]
    segment = jnp.sum(passed.astype(jnp.int32), axis=1)
    within = places - jnp.sum(jnp.where(passed, length_row[None, :], 0), axis=1)
    return (segment, within)


def collect_weights(gain_attn, w_query, w_key, w_value, w_out, gain_moe):
    return (
        lax.all_gather(gain_attn, ("dp", "ctx"), axis=0, tiled=True),
        lax.all_gather(w_query, ("dp", "ctx"), axis=0, tiled=True),
        lax.all_gather(w_key, ("dp", "ctx"), axis=0, tiled=True),
        lax.all_gather(w_value, ("dp", "ctx"), axis=0, tiled=True),
        lax.all_gather(w_out, ("dp", "ctx"), axis=0, tiled=True),
        lax.all_gather(gain_moe, ("dp", "ctx"), axis=0, tiled=True),
    )


def spread_grads(grad_gain_attn, grad_query, grad_key, grad_value, grad_outp, grad_gain_moe):
    return (
        lax.psum_scatter(grad_gain_attn, ("dp", "ctx"), scatter_dimension=0, tiled=True),
        lax.psum_scatter(grad_query, ("dp", "ctx"), scatter_dimension=0, tiled=True),
        lax.psum_scatter(grad_key, ("dp", "ctx"), scatter_dimension=0, tiled=True),
        lax.psum_scatter(grad_value, ("dp", "ctx"), scatter_dimension=0, tiled=True),
        lax.psum_scatter(grad_outp, ("dp", "ctx"), scatter_dimension=0, tiled=True),
        lax.psum_scatter(grad_gain_moe, ("dp", "ctx"), scatter_dimension=0, tiled=True),
    )


def on_device(
    tokens,
    norm_attn,
    w_query,
    w_key,
    w_value,
    w_out,
    norm_moe,
    w_gate,
    w_up,
    w_down,
    routes,
    gate_values,
    lengths,
    cotangent,
):
    tok_rows = tokens.shape[0]
    ctx_size = lax.axis_size("ctx")
    dp_size = lax.axis_size("dp")
    ctx_place = lax.axis_index("ctx")
    group_rows = tok_rows * ctx_size
    group_places = jnp.arange(group_rows, dtype=jnp.int32)
    seg_all, within_all = seq_tables(lengths[0], group_places)
    offset = ctx_place * tok_rows
    own_places = offset + jnp.arange(tok_rows, dtype=jnp.int32)
    seg_own = lax.dynamic_slice_in_dim(seg_all, offset, tok_rows)
    within_own = lax.dynamic_slice_in_dim(within_all, offset, tok_rows)
    allowed = (seg_own[:, None] == seg_all[None, :]) & (
        group_places[None, :] <= own_places[:, None]
    )
    gain_attn, full_q, full_k, full_v, full_o, gain_moe = collect_weights(
        norm_attn, w_query, w_key, w_value, w_out, norm_moe
    )
    gain_attn_f = gain_attn.astype(jnp.float32)
    gain_moe_f = gain_moe.astype(jnp.float32)
    inputs = tokens.astype(jnp.float32)
    normed_low = rms_norm(inputs, gain_attn_f).astype(jnp.bfloat16)
    query_pre = jnp.dot(normed_low, full_q, preferred_element_type=jnp.float32)
    key_pre = jnp.dot(normed_low, full_k, preferred_element_type=jnp.float32)
    value_pre = jnp.dot(normed_low, full_v, preferred_element_type=jnp.float32)
    query = rotate(query_pre.reshape(tok_rows, HEADS, HD), within_own, 1.0).astype(jnp.bfloat16)
    key_low = rotate(key_pre.reshape(tok_rows, KVH, HD), within_own, 1.0).astype(jnp.bfloat16)
    key_low = key_low.reshape(tok_rows, KVH * HD)
    value_low = value_pre.astype(jnp.bfloat16)
    all_keys, all_values = (
        lax.all_gather(key_low, "ctx", axis=0, tiled=True),
        lax.all_gather(value_low, "ctx", axis=0, tiled=True),
    )
    per_group = HEADS // KVH
    score_scale = HD ** (-0.5)
    query_groups = query.reshape(tok_rows, KVH, per_group, HD)

    def softmax_weights(group_number):
        keys_part = all_keys[:, group_number * HD : (group_number + 1) * HD]
        raw = jnp.einsum(
            "qjd,kd->jqk",
            query_groups[:, group_number],
            keys_part,
            preferred_element_type=jnp.float32,
        )
        scores = jnp.where(allowed[None], raw * score_scale, masked_score)
        row_top = jnp.max(scores, axis=-1, keepdims=True)
        expo = jnp.exp(scores - row_top)
        return expo / jnp.sum(expo, axis=-1, keepdims=True)

    mixed_parts = []
    for group_number in range(KVH):
        probs = softmax_weights(group_number)
        values_part = all_values[:, group_number * HD : (group_number + 1) * HD]
        mixed_group = jnp.einsum(
            "jqk,kd->qjd",
            probs.astype(jnp.bfloat16),
            values_part,
            preferred_element_type=jnp.float32,
        )
        mixed_parts.append(mixed_group.reshape(tok_rows, per_group * HD))
    mixed_low = jnp.concatenate(mixed_parts, axis=1).astype(jnp.bfloat16)
    middle = inputs + jnp.dot(mixed_low, full_o, preferred_element_type=jnp.float32)
    routed_low = rms_norm(middle, gain_moe_f).astype(jnp.bfloat16)
    experts_total = EXP_DEV * dp_size
    capacity = 3 * TOP * tok_rows // (2 * experts_total)
    assign_count = tok_rows * TOP
    flat_ids = routes.reshape(assign_count)
    onehot = (flat_ids[:, None] == jnp.arange(experts_total, dtype=jnp.int32)[None, :]).astype(
        jnp.int32
    )
    earlier = jnp.sum((jnp.cumsum(onehot, axis=0) - onehot) * onehot, axis=1)
    slot_index = flat_ids * capacity + earlier
    owner = (
        jnp.full((experts_total * capacity,), assign_count, jnp.int32)
        .at[slot_index]
        .set(jnp.arange(assign_count, dtype=jnp.int32))
    )
    padded = jnp.concatenate([routed_low, jnp.zeros((1, D), jnp.bfloat16)], axis=0)
    outgoing = padded[owner // TOP].reshape(experts_total, capacity, D)
    arrived = lax.all_to_all(outgoing, "dp", split_axis=0, concat_axis=0, tiled=True)
    arrived_sets = arrived.reshape(dp_size, EXP_DEV, capacity, D)
    gate_act = jnp.einsum(
        "secd,edf->secf", arrived_sets, w_gate, preferred_element_type=jnp.float32
    )
    up_act = jnp.einsum("secd,edf->secf", arrived_sets, w_up, preferred_element_type=jnp.float32)
    hidden_low = (jax.nn.silu(gate_act) * up_act).astype(jnp.bfloat16)
    produced = jnp.einsum("secf,efd->secd", hidden_low, w_down, preferred_element_type=jnp.float32)
    produced = produced.astype(jnp.bfloat16).reshape(experts_total, capacity, D)
    returned = lax.all_to_all(produced, "dp", split_axis=0, concat_axis=0, tiled=True)
    picked = returned.reshape(experts_total * capacity, D)[slot_index].reshape(tok_rows, TOP, D)
    moe_out = jnp.sum(picked.astype(jnp.float32) * gate_values[:, :, None], axis=1)
    layer_out = (middle + moe_out).astype(jnp.bfloat16)
    grad_out = cotangent.astype(jnp.float32)
    grad_assign = (grad_out[:, None, :] * gate_values[:, :, None]).astype(jnp.bfloat16)
    grad_padded = jnp.concatenate(
        [grad_assign.reshape(assign_count, D), jnp.zeros((1, D), jnp.bfloat16)], axis=0
    )
    grad_slots = grad_padded[owner].reshape(experts_total, capacity, D)
    grad_arrived = lax.all_to_all(grad_slots, "dp", split_axis=0, concat_axis=0, tiled=True)
    grad_arrived = grad_arrived.reshape(dp_size, EXP_DEV, capacity, D)
    grad_hidden = jnp.einsum(
        "secd,efd->secf", grad_arrived, w_down, preferred_element_type=jnp.float32
    )
    grad_w_down = jnp.einsum(
        "secf,secd->efd", hidden_low, grad_arrived, preferred_element_type=jnp.float32
    )
    glu_value, glu_pull = jax.vjp(
        lambda gate_in, up_in: jax.nn.silu(gate_in) * up_in, gate_act, up_act
    )
    grad_gate, grad_up = glu_pull(grad_hidden)
    grad_gate_low = grad_gate.astype(jnp.bfloat16)
    grad_up_low = grad_up.astype(jnp.bfloat16)
    grad_w_gate = jnp.einsum(
        "secd,secf->edf", arrived_sets, grad_gate_low, preferred_element_type=jnp.float32
    )
    grad_w_up = jnp.einsum(
        "secd,secf->edf", arrived_sets, grad_up_low, preferred_element_type=jnp.float32
    )
    grad_sent = jnp.einsum(
        "secf,edf->secd", grad_gate_low, w_gate, preferred_element_type=jnp.float32
    ) + jnp.einsum("secf,edf->secd", grad_up_low, w_up, preferred_element_type=jnp.float32)
    grad_sent = grad_sent.astype(jnp.bfloat16).reshape(experts_total, capacity, D)
    grad_back = lax.all_to_all(grad_sent, "dp", split_axis=0, concat_axis=0, tiled=True)
    grad_picked = grad_back.reshape(experts_total * capacity, D)[slot_index].reshape(
        tok_rows, TOP, D
    )
    grad_routed = jnp.sum(grad_picked.astype(jnp.float32), axis=1)
    expert_sums = (
        lax.psum(grad_w_gate.astype(jnp.bfloat16), "ctx").astype(jnp.float32),
        lax.psum(grad_w_up.astype(jnp.bfloat16), "ctx").astype(jnp.float32),
        lax.psum(grad_w_down.astype(jnp.bfloat16), "ctx").astype(jnp.float32),
    )
    norm_value, moe_pull = jax.vjp(rms_norm, middle, gain_moe_f)
    grad_mid_norm, grad_gain_moe = moe_pull(grad_routed)
    grad_middle = grad_out + grad_mid_norm
    grad_attn_low = grad_middle.astype(jnp.bfloat16)
    grad_w_out = jnp.einsum(
        "th,td->hd", mixed_low, grad_attn_low, preferred_element_type=jnp.float32
    )
    grad_mixed_low = jnp.einsum(
        "td,hd->th", grad_attn_low, full_o, preferred_element_type=jnp.float32
    ).astype(jnp.bfloat16)
    grad_mixed_groups = grad_mixed_low.reshape(tok_rows, KVH, per_group, HD)
    grad_query_parts = []
    prob_parts = []
    score_parts = []
    for group_number in range(KVH):
        probs = softmax_weights(group_number)
        keys_part = all_keys[:, group_number * HD : (group_number + 1) * HD]
        values_part = all_values[:, group_number * HD : (group_number + 1) * HD]
        grad_probs = jnp.einsum(
            "qjd,kd->jqk",
            grad_mixed_groups[:, group_number],
            values_part,
            preferred_element_type=jnp.float32,
        )
        grad_scores = probs * (grad_probs - jnp.sum(probs * grad_probs, axis=-1, keepdims=True))
        grad_raw_low = (grad_scores * score_scale).astype(jnp.bfloat16)
        grad_query_parts.append(
            jnp.einsum("jqk,kd->qjd", grad_raw_low, keys_part, preferred_element_type=jnp.float32)
        )
        prob_parts.append(probs.astype(jnp.bfloat16))
        score_parts.append(grad_raw_low)
    grad_query_rot = jnp.stack(grad_query_parts, axis=1).reshape(tok_rows, HEADS, HD)
    key_pieces = []
    value_pieces = []
    for group_number in range(KVH):
        score_piece = score_parts[group_number]
        prob_piece = prob_parts[group_number]
        key_pieces.append(
            jnp.einsum(
                "jqk,qjd->kd",
                score_piece,
                query_groups[:, group_number],
                preferred_element_type=jnp.float32,
            )
        )
        value_pieces.append(
            jnp.einsum(
                "jqk,qjd->kd",
                prob_piece,
                grad_mixed_groups[:, group_number],
                preferred_element_type=jnp.float32,
            )
        )
    key_value_grads = lax.psum_scatter(
        jnp.concatenate(key_pieces + value_pieces, axis=1).astype(jnp.bfloat16),
        "ctx",
        scatter_dimension=0,
        tiled=True,
    ).astype(jnp.float32)
    grad_query_low = (
        rotate(grad_query_rot, within_own, -1.0).astype(jnp.bfloat16).reshape(tok_rows, HEADS * HD)
    )
    grad_key_rot = key_value_grads[:, : KVH * HD].reshape(tok_rows, KVH, HD)
    grad_key_low = (
        rotate(grad_key_rot, within_own, -1.0).astype(jnp.bfloat16).reshape(tok_rows, KVH * HD)
    )
    grad_value_low = key_value_grads[:, KVH * HD :].astype(jnp.bfloat16)
    grad_w_query = jnp.einsum(
        "td,th->dh", normed_low, grad_query_low, preferred_element_type=jnp.float32
    )
    grad_w_key = jnp.einsum(
        "td,th->dh", normed_low, grad_key_low, preferred_element_type=jnp.float32
    )
    grad_w_value = jnp.einsum(
        "td,th->dh", normed_low, grad_value_low, preferred_element_type=jnp.float32
    )
    grad_normed = (
        jnp.einsum("th,dh->td", grad_query_low, full_q, preferred_element_type=jnp.float32)
        + jnp.einsum("th,dh->td", grad_key_low, full_k, preferred_element_type=jnp.float32)
        + jnp.einsum("th,dh->td", grad_value_low, full_v, preferred_element_type=jnp.float32)
    )
    first_value, attn_pull = jax.vjp(rms_norm, inputs, gain_attn_f)
    grad_inputs, grad_gain_attn = attn_pull(grad_normed)
    grad_tokens = grad_middle + grad_inputs
    dense_sums = spread_grads(
        grad_gain_attn, grad_w_query, grad_w_key, grad_w_value, grad_w_out, grad_gain_moe
    )
    return (
        layer_out,
        grad_tokens,
        dense_sums[0],
        dense_sums[1],
        dense_sums[2],
        dense_sums[3],
        dense_sums[4],
        dense_sums[5],
        expert_sums[0],
        expert_sums[1],
        expert_sums[2],
    )


MESH = pl.DeviceIdType.MESH
LANES = 128
MIB = 2**20
ANY = pl.BlockSpec(memory_space=pl.ANY)
VMEM = pl.BlockSpec(memory_space=pltpu.VMEM)


def flip(index, bit):
    return index + bit - 2 * bit * ((index // bit) % 2)


def masked(index, mask):
    for bit in (1, 2, 4):
        if mask & bit:
            index = flip(index, bit)
    return index


class Wires:
    def __init__(self, send, recv):
        self.send, self.recv, self.used = send, recv, 0
        self.dp, self.z = lax.axis_index("dp"), lax.axis_index("ctx")

    def take(self, count):
        first = self.used
        self.used += count
        return first

    def copy(self, src, dst, number, dp=None, z=None):
        return pltpu.make_async_remote_copy(
            src_ref=src,
            dst_ref=dst,
            send_sem=self.send.at[number],
            recv_sem=self.recv.at[number],
            device_id=(self.dp if dp is None else dp, self.z if z is None else z),
            device_id_type=MESH,
        )


def greet(wires, masks, line):
    barrier = pltpu.get_barrier_semaphore()
    dp, z = wires.dp, wires.z
    for mask in masks:
        pl.semaphore_signal(barrier, inc=1, device_id=(masked(dp, mask), z), device_id_type=MESH)
    for step in range(1, LINE) if line else ():
        pl.semaphore_signal(
            barrier, inc=1, device_id=(dp, lax.rem(z + step, LINE)), device_id_type=MESH
        )
    pl.semaphore_wait(barrier, len(masks) + (LINE - 1 if line else 0))


LINE = 4


class LineGather:
    COPIES = 2 * (LINE - 1)

    def __init__(self, wires, ref, rows_of):
        self.wires, self.ref, self.rows_of = wires, ref, rows_of
        self.first = wires.take(self.COPIES)

    def _copy(self, block, number, z):
        part = self.ref.at[self.rows_of(block)]
        return self.wires.copy(part, part, self.first + number, z=z)

    def start(self, step):
        z = self.wires.z

        @pl.when((z >= step) & (z < LINE - 1))
        def _():
            self._copy(z - step, step, z + 1).start()

        @pl.when((z + step < LINE) & (z > 0))
        def _():
            self._copy(z + step, LINE - 1 + step, z - 1).start()

    def wait(self, step):
        z = self.wires.z

        @pl.when(z - 1 - step >= 0)
        def _():
            self._copy(z - 1 - step, step, z).wait_recv()

        @pl.when(z + 1 + step < LINE)
        def _():
            self._copy(z + 1 + step, LINE - 1 + step, z).wait_recv()

    def finish(self):
        z = self.wires.z
        for step in range(LINE - 1):

            @pl.when((z >= step) & (z < LINE - 1))
            def _():
                self._copy(z - step, step, z + 1).wait_send()

            @pl.when((z + step < LINE) & (z > 0))
            def _():
                self._copy(z + step, LINE - 1 + step, z - 1).wait_send()


class PlaneGather:
    CHIP = (((2, 0, 0), (4, 0, 1)), ((4, 0, 0), (2, 0, 1)), ((4, 2, 0), (2, 4, 1)))
    CORE = (
        ((1, 0, 2),),
        ((1, 2, 0), (1, 4, 1)),
        ((1, 4, 0), (1, 2, 1)),
        ((1, 6, 0), (1, 6, 1)),
    )
    COPIES = 13

    def __init__(self, wires, ref, group):
        self.wires, self.ref, self.group = wires, ref, group
        first = wires.take(self.COPIES)
        self.number = {}
        for stage in self.CHIP + self.CORE:
            for one in stage:
                self.number[one] = first + len(self.number)
        self.core_left = [0, 1, 2, 3]

    def _copy(self, one, from_me):
        to, whose, half = one
        dp = self.wires.dp
        sender = dp if from_me else masked(dp, to)
        owner = masked(sender, whose)
        size = self.group if half == 2 else self.group // 2
        begin = owner * self.group + (self.group // 2 if half == 1 else 0)
        part = self.ref.at[pl.ds(pl.multiple_of(begin, 16), size)]
        return self.wires.copy(part, part, self.number[one], dp=masked(dp, to))

    def start(self, stage, far=True):
        for one in (self.CHIP[stage] if stage < 2 else ()) + self.CORE[stage]:
            self._copy(one, True).start()
        if stage == 1 and far:
            self.start_far()

    def start_one(self, number):
        self._copy((self.CHIP[0] + self.CORE[0])[number], True).start()

    def start_far(self):
        for one in self.CHIP[2]:
            self._copy(one, True).start()

    def wait(self, stage):
        for one in self.CHIP[stage]:
            self._copy(one, False).wait_recv()

    def wait_core(self, stage):
        self.core_left.remove(stage)
        for one in self.CORE[stage]:
            self._copy(one, False).wait_recv()

    def finish(self):
        for stage in list(self.core_left):
            self.wait_core(stage)
        for one in self.number:
            self._copy(one, True).wait_send()


def add_rows(out, out_row, left, left_row, right, right_row, rows):
    @pl.loop(0, rows // 16)
    def _(step):
        def cut(row):
            return pl.ds(pl.multiple_of(row + step * 16, 16), 16)

        out[cut(out_row), :] = (
            left[cut(left_row), :].astype(jnp.float32) + right[cut(right_row), :].astype(jnp.float32)
        ).astype(out.dtype)


class PlaneReduce:
    COPIES = 10
    STEPS = 6

    def __init__(self, wires, part, group, own, own_row, core_in, first_in, second_in, out):
        self.wires, self.part, self.group, self.half = wires, part, group, group // 2
        self.own, self.own_row, self.out = own, own_row, out
        self.core_in, self.first_in, self.second_in = core_in, first_in, second_in
        self.first = wires.take(self.COPIES)

    def _send(self, src, src_row, dst, dst_row, rows, number, to):
        return self.wires.copy(
            src.at[pl.ds(src_row, rows)],
            dst.at[pl.ds(dst_row, rows)],
            self.first + number,
            dp=masked(self.wires.dp, to),
        )

    def _core(self, slot):
        row = pl.multiple_of(masked(self.wires.dp, 1 + 2 * slot) * self.group, 16)
        return self._send(self.part, row, self.core_in, slot * self.group, self.group, slot, 1)

    def _far(self, number):
        g, h = self.group, self.half
        src_row, dst, dst_row, to = (
            (3 * g, self.first_in, h, 4),
            (3 * g + h, self.first_in, 3 * h, 2),
            (2 * g, self.first_in, 0, 4),
            (1 * g + h, self.first_in, 2 * h, 2),
            (1 * g, self.second_in, 0, 2),
            (2 * g + h, self.second_in, h, 4),
        )[number]
        return self._send(self.core_in, src_row, dst, dst_row, h, 4 + number, to)

    def _sum_core(self, slot):
        self._core(slot).wait()
        row = slot * self.group
        add_rows(self.core_in, row, self.own, self.own_row(slot), self.core_in, row, self.group)

    def _sum_far(self, number, row, in_row):
        self._far(number).wait()
        add_rows(self.core_in, row, self.core_in, row, self.first_in, in_row, self.half)

    def start_core(self, slot):
        self._core(slot).start()

    def step(self, number):
        g, h = self.group, self.half
        if number == 0:
            for slot in (3, 2, 1, 0):
                self.start_core(slot)
        elif number == 1:
            self._sum_core(3)
            self._far(0).start()
            self._far(1).start()
        elif number == 2:
            self._sum_core(2)
            self._far(2).start()
            self._sum_core(1)
            self._far(3).start()
            self._sum_core(0)
        elif number == 3:
            self._sum_far(0, 1 * g, h)
            self._far(4).start()
            self._sum_far(1, 2 * g + h, 3 * h)
            self._far(5).start()
        elif number == 4:
            self._sum_far(2, 0, 0)
            self._sum_far(3, h, 2 * h)
        elif self.out is None:
            self._far(4).wait()
            self._far(5).wait()
        else:
            self._far(4).wait()
            add_rows(self.out, 0, self.core_in, 0, self.second_in, 0, h)
            self._far(5).wait()
            add_rows(self.out, h, self.core_in, h, self.second_in, h, h)

    @staticmethod
    def scratch(group, columns):
        return [
            pltpu.VMEM((4 * group, columns), jnp.bfloat16),
            pltpu.VMEM((2 * group, columns), jnp.bfloat16),
            pltpu.VMEM((group, columns), jnp.bfloat16),
        ]


class LineReduce:
    COPIES = 2 * (LINE - 1) * LINE
    EVENTS = ((0, 0), (0, 1), (1, 0), (0, 2), (1, 1), (2, 0))

    def __init__(self, wires, part, rows, landing, ways=(1, -1)):
        self.wires, self.part, self.rows, self.landing, self.ways = wires, part, rows, landing, ways
        self.first = wires.take(self.COPIES)

    def _place(self, way, hop, nearer):
        return (LINE - 1 - nearer, hop) if way == 1 else (nearer, LINE - 1 - hop)

    def _copy(self, way, hop, nearer, z):
        side = self.ways.index(way)
        block, _ = self._place(way, hop, nearer)
        return self.wires.copy(
            self.part.at[pl.ds(block * self.rows, self.rows)],
            self.landing.at[pl.ds((side * LINE + block) * self.rows, self.rows)],
            self.first + (side * (LINE - 1) + hop) * LINE + nearer,
            z=z,
        )

    def _send(self, way, hop, nearer):
        z = self.wires.z

        @pl.when(z == self._place(way, hop, nearer)[1])
        def _():
            self._copy(way, hop, nearer, z + way).start()

    def begin(self):
        for nearer in range(LINE - 1):
            for way in self.ways:
                self._send(way, 0, nearer)

    def event(self, number):
        hop, nearer = self.EVENTS[number]
        z, rows = self.wires.z, self.rows
        for way in self.ways:
            block, source = self._place(way, hop, nearer)

            @pl.when(z == source + way)
            def _():
                self._copy(way, hop, nearer, z).wait_recv()
                landed = (self.ways.index(way) * LINE + block) * rows
                add_rows(
                    self.part, block * rows, self.part, block * rows, self.landing, landed, rows
                )
                if nearer < LINE - 2 - hop:
                    self._copy(way, hop + 1, nearer, z + way).start()

    def finish(self, outs):
        z, rows = self.wires.z, self.rows

        @pl.loop(0, rows // 16)
        def _(step):
            row = pl.multiple_of(z * rows + step * 16, 16)
            begin = 0
            for out in outs:
                out[pl.ds(pl.multiple_of(step * 16, 16), 16), :] = self.part[
                    pl.ds(row, 16), begin : begin + out.shape[1]
                ].astype(out.dtype)
                begin += out.shape[1]

        for hop, nearer in self.EVENTS:
            for way in self.ways:

                @pl.when(z == self._place(way, hop, nearer)[1])
                def _():
                    self._copy(way, hop, nearer, z + way).wait_send()

    @staticmethod
    def scratch(rows, columns, ways=2):
        return pltpu.VMEM(((ways * LINE - 1) * rows, columns), jnp.bfloat16)


def sems(count):
    return [pltpu.SemaphoreType.DMA((count,)), pltpu.SemaphoreType.DMA((count,))]


def kernel_params(collective_id, mib):
    return pltpu.CompilerParams(
        collective_id=collective_id, has_side_effects=True, vmem_limit_bytes=mib * MIB
    )


def dot(left, right, left_dim, right_dim):
    return lax.dot_general(
        left, right, (((left_dim,), (right_dim,)), ((), ())), preferred_element_type=jnp.float32
    )


def rows_at(begin, size):
    return pl.ds(pl.multiple_of(begin, 16), size)


CHUNK = 64
AHEAD = 4
CARRIED = 2
RING = 4
BEFORE_DENSE = 16


class LineSum:
    def __init__(self, wires, own, out, landing, rows, chunks, came=False, goes_on=False):
        self.wires, self.own, self.out, self.landing = wires, own, out, landing
        self.rows, self.chunks, self.came, self.goes_on = rows, chunks, came, goes_on
        self.all = chunks + (CARRIED if goes_on else 0)
        self.begun = CARRIED if came else 0
        self.now = self.begun
        self.first = wires.take(3 * self.all)
        z = wires.z
        self.inner = (z == 1) | (z == 2)
        self.outer = (z == 0) | (z == 3)
        self.end = 3 * (z - 1)
        self.near = 1 + z // 3
        self.peer = 3 - z

    def _cut(self, ref, chunk):
        return ref.at[pl.ds(pl.multiple_of(chunk * self.rows, 16), self.rows)]

    def _in(self, chunk):
        return self.wires.copy(
            self._cut(self.own, chunk), self._cut(self.out, chunk), self.first + chunk, z=self.near
        )

    def _across(self, chunk):
        number = self.first + self.all + chunk
        return self.wires.copy(
            self._cut(self.own, chunk), self._cut(self.landing, lax.rem(chunk, RING)), number, z=self.peer
        )

    def _back(self, chunk, ref=None):
        number = self.first + 2 * self.all + chunk
        return self.wires.copy(
            self._cut(self.out if ref is None else ref, chunk), self._cut(self.out, chunk), number, z=self.end
        )

    def begin(self):
        @pl.when(self.outer)
        def _():
            for chunk in range(self.begun, min(self.begun + AHEAD, self.all)):
                self._in(chunk).start()

        if self.came:

            @pl.when(self.inner)
            def _():
                self._across(1).start()
                self._back(0, self.own).start()
                self.out[pl.ds(0, self.rows), :] = self.own[pl.ds(0, self.rows), :]

    def tick(self, count=1):
        for _ in range(count):
            if self.now < self.all + (0 if self.goes_on else 1):
                self._tick(self.now)
            self.now += 1

    def _tick(self, chunk):
        if chunk < self.all:

            @pl.when(self.outer)
            def _():
                self._in(chunk).wait_send()
                if chunk + AHEAD < self.all:
                    self._in(chunk + AHEAD).start()

        @pl.when(self.inner)
        def _():
            if chunk < self.all:
                row = chunk * self.rows
                self._in(chunk).wait_recv()
                add_rows(self.own, row, self.own, row, self.out, row, self.rows)
                if chunk <= self.chunks:
                    self._across(chunk).start()
            if chunk >= 1:
                row = (chunk - 1) * self.rows
                landed = (chunk - 1) % RING * self.rows
                self._across(chunk - 1).wait_recv()
                if chunk - 1 < self.chunks:
                    add_rows(self.out, row, self.own, row, self.landing, landed, self.rows)
                    self._back(chunk - 1).start()
                else:
                    self._across(chunk - 1).wait_send()
                    add_rows(self.own, row, self.own, row, self.landing, landed, self.rows)

    def finish(self):
        self.tick(max(0, self.all + (0 if self.goes_on else 1) - self.now))

        @pl.when(self.outer)
        def _():
            @pl.loop(0, self.chunks)
            def _(chunk):
                self._back(chunk).wait_recv()

        @pl.when(self.inner)
        def _():
            @pl.loop(1 if self.came else 0, self.chunks)
            def _(chunk):
                self._across(chunk).wait_send()

            @pl.loop(0, self.chunks)
            def _(chunk):
                self._back(chunk).wait_send()


def norm_back(values, gain, grad):
    scale = lax.rsqrt(jnp.mean(values * values, axis=-1, keepdims=True) + epsilon)
    normal = values * scale
    inner = grad * gain
    to_values = scale * (inner - normal * jnp.mean(inner * normal, axis=-1, keepdims=True))
    return to_values, grad * normal


def turned(values, cosine, sine):
    return values * cosine + pltpu.roll(values, HD // 2, 1) * sine


def up_to_attention_back(
    w_query, w_key, w_value, gains, w_out, tokens, cotangent, gates, w_gate, w_up, w_down, starts, cosine, sine
):
    rows, width = w_query.shape
    key_width = w_key.shape[1]
    kv_width = key_width + w_value.shape[1]
    tok_rows = tokens.shape[0]
    keys = LINE * tok_rows
    planes = 8
    group = LINE * rows
    hidden_width = w_gate.shape[1]
    total_rows = planes * tok_rows
    sum_rows = width + hidden_width
    chunks = BEFORE_DENSE
    score_scale = HD ** (-0.5)
    per_group = HEADS // KVH
    q_width = HEADS * HD

    def kernel(
        wq_ref, wk_ref, wv_ref, gains_ref, wo_ref, tok_hbm, cot_hbm, gate_ref, wg_ref, wu_ref, wd_ref, starts_ref, cos_ref,
        sin_ref,
        out_q, out_kv, out_o, query_hbm, mixed_hbm, normed_hbm, middle_hbm, gain_rows_ref, sums_ref, prod_ref, total_ref,
        grad_mid_hbm, grad_pre_ref, gain_row_ref, w_out_ref,
        w_in, w_down, x_all, y_all, hidden, grad_hidden, grad_in, sums, sums_land, all_gate, gate_t, all_kv, lse_ref,
        core_in, first_in, second_in, middle_ref, kv_land, here, there, freed, send, recv,
    ):
        wires = Wires(send, recv)
        dp, z = wires.dp, wires.z

        def rows_begin(block):
            return pl.multiple_of(block * tok_rows, 16)

        def cut_of(block):
            return pl.ds(rows_begin(block), tok_rows)

        def gate_rows(block):
            return pl.ds(pl.multiple_of(block * planes, planes), planes)

        full_q = w_in
        full_kv = hidden.at[pl.ds(0, width), pl.ds(0, kv_width + LANES)]
        full_o = sums.at[pl.ds(0, width)]
        all_cot = y_all
        query_ref, mixed_ref, tok_ref, normed_ref, cot_ref = [
            grad_in.at[pl.ds(i * tok_rows, tok_rows)] for i in range(5)
        ]
        value_t = key_t = grad_in.at[pl.ds(5 * tok_rows, kv_width // 2), pl.ds(0, keys)]
        bias = grad_hidden.at[pl.ds(keys, keys), pl.ds(0, tok_rows)]
        full_o_ref = w_in
        part_o = y_all.at[pl.ds(0, width)]
        attn_low, mixed_grad = tok_ref, normed_ref
        kv_part = hidden.at[pl.ds(keys, keys), pl.ds(0, kv_width)]
        kv_grad = grad_hidden.at[pl.ds(0, keys), pl.ds(0, kv_width)]
        kv_out = grad_hidden.at[pl.ds(keys, tok_rows), pl.ds(tok_rows, kv_width)]

        own = rows_at((dp * LINE + z) * rows, rows)
        moves = [
            (wk_ref, full_kv.at[own, pl.ds(0, key_width)]),
            (wv_ref, full_kv.at[own, pl.ds(key_width, kv_width - key_width)]),
            (gains_ref, full_kv.at[own, pl.ds(kv_width, LANES)]),
            (cot_hbm, all_cot.at[cut_of(dp)]),
            (gate_ref, all_gate.at[gate_rows(dp)]),
            (wq_ref, full_q.at[own]),
            (wo_ref, full_o.at[own]),
            (tok_hbm, tok_ref),
            (wd_ref, w_down),
            (wg_ref, w_in.at[:, pl.ds(0, hidden_width)]),
            (wu_ref, w_in.at[:, pl.ds(hidden_width, hidden_width)]),
            (out_o, full_o_ref),
            (query_hbm, query_ref),
            (mixed_hbm, mixed_ref),
            (cot_hbm, cot_ref),
        ]
        moves = [pltpu.make_async_copy(a, b, here.at[i]) for i, (a, b) in enumerate(moves)]
        locals_, load_down, load_in, later = moves[:8], moves[8], moves[9:11], moves[11:]
        for one in locals_:
            one.start()
        load_down.start()
        greet(wires, range(1, planes), True)
        for one in locals_:
            one.wait()

        def block_rows(block):
            return rows_at((dp * LINE + block) * rows, rows)

        line_kv, line_q, line_o = [LineGather(wires, r, block_rows) for r in (full_kv, full_q, full_o)]
        plane_kv, plane_q, plane_o = [PlaneGather(wires, r, group) for r in (full_kv, full_q, full_o)]
        plane_cot = PlaneGather(wires, all_cot, tok_rows)
        line_keys = LineGather(wires, all_kv, lambda block: rows_at(block * tok_rows, tok_rows))
        spread = PlaneGather(wires, x_all, tok_rows)
        plane = PlaneReduce(
            wires, y_all, tok_rows, y_all, lambda slot: rows_begin(masked(dp, 2 * slot)), core_in, first_in, second_in,
            None,
        )
        summed = LineSum(wires, sums, total_ref, sums_land, CHUNK, chunks, goes_on=True)
        dense = PlaneReduce(
            wires, part_o, group, part_o, lambda slot: pl.multiple_of(masked(dp, 2 * slot) * group, 16),
            core_in, first_in, second_in, w_out_ref,
        )
        line = LineReduce(wires, kv_part, tok_rows, kv_land, ways=(-1,))
        first = wires.take(planes - 1)

        def gate_copy(mask, owner):
            part = all_gate.at[gate_rows(owner)]
            return wires.copy(part, part, first + mask - 1, dp=masked(dp, mask))

        def set_bias():
            key_place = lax.broadcasted_iota(jnp.int32, (keys, tok_rows), 0)
            query_place = lax.broadcasted_iota(jnp.int32, (keys, tok_rows), 1) + z * tok_rows
            allowed = (key_place >= starts_ref[0:1, :]) & (key_place <= query_place)
            bias[...] = jnp.where(allowed, 0.0, masked_score)

        line_kv.start(0)
        plane_cot.start(0)
        for mask in range(1, planes):
            gate_copy(mask, dp).start()
        line_kv.wait(0)
        line_kv.start(1)
        set_bias()
        line_kv.wait(1)
        line_kv.start(2)
        line_q.start(0)
        line_kv.wait(2)
        plane_kv.start(0)
        plane_cot.wait(0)
        line_q.wait(0)
        line_q.start(1)
        plane_kv.wait(0)
        plane_kv.start(1)
        plane_cot.start(1, far=False)
        line_q.wait(1)
        line_q.start(2)
        line_o.start(0)
        plane_kv.wait(1)
        plane_kv.start(2)
        plane_kv.wait(2)
        plane_kv.start(3)
        plane_kv.finish()
        line_q.wait(2)
        plane_q.start(0)

        gain_rows_ref[...] = full_kv[:, kv_width:].astype(jnp.float32).T[:8, :]
        tile = 32

        @pl.loop(0, tok_rows // tile)
        def _(step):
            cut = pl.ds(pl.multiple_of(step * tile, tile), tile)
            normed_ref[cut, :] = rms_norm(
                tok_ref[cut, :].astype(jnp.float32), gain_rows_ref[0:1, :]
            ).astype(jnp.bfloat16)

        own_keys = rows_at(z * tok_rows, tok_rows)
        pre = dot(normed_ref[...], full_kv[:, :kv_width], 1, 0)
        for pair in range(KVH):
            cut = slice(pair * HD, (pair + 1) * HD)
            all_kv[own_keys, cut] = turned(pre[:, cut], cos_ref[...], sin_ref[...]).astype(jnp.bfloat16)
        all_kv[own_keys, key_width:] = pre[:, key_width:].astype(jnp.bfloat16)
        line_keys.start(0)
        line_o.wait(0)
        line_o.start(1)
        plane_q.wait(0)
        plane_q.start(1)
        plane_cot.wait(1)
        plane_cot.start(2)
        line_keys.wait(0)
        line_keys.start(1)
        line_o.wait(1)
        line_o.start(2)
        line_keys.wait(1)
        line_keys.start(2)
        line_o.wait(2)
        plane_o.start(0)
        plane_q.wait(1)
        plane_q.start(2)
        plane_q.wait(2)
        plane_q.start(3)
        plane_q.finish()
        line_kv.finish()
        line_q.finish()
        saves = [
            (full_q, out_q),
            (full_kv, out_kv),
            (normed_ref, normed_hbm),
            (query_ref, query_hbm),
            (full_o, out_o),
            (mixed_ref, mixed_hbm),
            (middle_ref, middle_hbm),
        ]
        saves = [pltpu.make_async_copy(a, b, there.at[11 + i]) for i, (a, b) in enumerate(saves)]
        save_q, saves = saves[0], saves[1:]
        save_q.start()
        saves[0].start()
        saves[1].start()

        @pl.loop(0, HEADS // 2)
        def _(step):
            wide = pl.ds(pl.multiple_of(step * 2 * HD, 2 * HD), 2 * HD)
            pre_q = dot(normed_ref[...], full_q[:, wide], 1, 0)
            for one in range(2):
                query_ref[:, pl.ds(pl.multiple_of((2 * step + one) * HD, HD), HD)] = turned(
                    pre_q[:, one * HD : (one + 1) * HD], cos_ref[...], sin_ref[...]
                ).astype(jnp.bfloat16)

        saves[2].start()
        plane_o.wait(0)
        plane_o.start(1)
        save_q.wait()
        for one in load_in:
            one.start()
        line_keys.wait(2)
        value_t[...] = all_kv[:, key_width:].astype(jnp.float32).T.astype(jnp.bfloat16)
        lse_ref[...] = jnp.zeros_like(lse_ref)

        def attend(head):
            own_cut = pl.ds(pl.multiple_of(head * HD, HD), HD)
            key_cut = pl.ds(pl.multiple_of((head // per_group) * HD, HD), HD)
            scores = dot(all_kv[:, key_cut], query_ref[:, own_cut], 1, 1) * score_scale + bias[...]
            top = jnp.max(scores, axis=0, keepdims=True)
            expo = jnp.exp(scores - top)
            total = jnp.sum(expo, axis=0, keepdims=True)
            lse_ref[pl.ds(head, 1), :] = top + jnp.log(total)
            probs = (expo * (1.0 / total)).astype(jnp.bfloat16)
            mixed_ref[:, own_cut] = dot(value_t[key_cut, :], probs, 1, 0).T.astype(jnp.bfloat16)

        pl.loop(0, HEADS // 2)(attend)
        plane_cot.start_far()
        pl.loop(HEADS // 2, HEADS)(attend)
        plane_o.wait(1)
        plane_o.start(2)
        plane_o.wait(2)
        plane_o.start(3)
        plane_o.finish()
        line_o.finish()
        saves[3].start()
        saves[4].start()

        half_rows = tok_rows // 2
        for half in range(2):
            half_cut = pl.ds(half * half_rows, half_rows)

            @pl.loop(0, width // 512)
            def _(step):
                cut = pl.ds(pl.multiple_of(step * 512, 512), 512)
                middle_ref[half_cut, cut] = tok_ref[half_cut, cut].astype(jnp.float32) + dot(
                    mixed_ref[half_cut, :], full_o[:, cut], 1, 0
                )

            @pl.loop(0, half_rows // tile)
            def _(step):
                begin = half * half_rows + step * tile
                cut = pl.ds(pl.multiple_of(begin, tile), tile)
                x_all[pl.ds(pl.multiple_of(dp * tok_rows + begin, tile), tile), :] = rms_norm(
                    middle_ref[cut, :], gain_rows_ref[1:2, :]
                ).astype(jnp.bfloat16)

            spread.start_one(half)
        spread.start_one(2)
        saves[5].start()
        plane_cot.wait(2)
        plane_cot.start(3)
        plane_cot.finish()
        for mask in range(1, planes):
            gate_copy(mask, masked(dp, mask)).wait_recv()
        gate_t[...] = all_gate[...].T

        def gate_of(block):
            lane = lax.broadcasted_iota(jnp.int32, gate_t.shape, 1)
            return jnp.sum(jnp.where(lane == block * 8 + dp, gate_t[...], 0.0), axis=1, keepdims=True)

        def back_hidden(block):
            cut = cut_of(block)
            y_all[cut, :] = (y_all[cut, :].astype(jnp.float32) * gate_of(block)).astype(jnp.bfloat16)
            grad_hidden[cut, :] = dot(y_all[cut, :], w_down[...], 1, 1)

        def through(mask):
            cut = cut_of(masked(dp, mask))
            acts = dot(x_all[cut, :], w_in[...], 1, 0)
            gate_act, up_act = acts[:, :hidden_width], acts[:, hidden_width:]
            share = jax.nn.sigmoid(gate_act)
            silu = gate_act * share
            hidden[cut, :] = (silu * up_act).astype(jnp.bfloat16)
            grad = grad_hidden[cut, :]
            grad_in[cut, :hidden_width] = (
                grad * up_act * share * (1.0 + gate_act * (1.0 - share))
            ).astype(jnp.bfloat16)
            grad_in[cut, hidden_width:] = (grad * silu).astype(jnp.bfloat16)

        load_down.wait()
        pl.loop(0, 4)(back_hidden)
        spread.wait(0)
        spread.start(1)
        pl.loop(4, 8)(back_hidden)
        for one in load_in + saves:
            one.wait()
        through(0)
        spread.wait_core(0)
        through(1)
        spread.wait(1)
        spread.start(2)
        through(2)
        through(4)
        spread.wait_core(1)
        spread.wait_core(2)
        through(3)
        through(5)
        spread.wait(2)
        spread.start(3)
        through(6)
        spread.wait_core(3)
        through(7)

        def weights_down(step):
            cut = rows_at(step * 256, 256)
            sums[cut, :] = dot(hidden[:, cut], y_all[...], 0, 0).astype(jnp.bfloat16)

        def weights_in(step):
            cut = rows_at(step * 256, 256)
            out = rows_at(hidden_width + step * 256, 256)
            sums[out, :] = dot(x_all[:, cut], grad_in[...], 0, 0).astype(jnp.bfloat16)

        def save_sums(begin, end, number):
            rows = pl.ds(begin, end - begin)
            return pltpu.make_async_copy(sums.at[rows], sums_ref.at[rows], there.at[number])

        pl.loop(0, 1)(weights_down)
        summed.begin()
        pl.loop(1, 3)(weights_down)
        spread.finish()

        def input_grads(side):
            for slot in (3, 2, 1, 0):
                cut = cut_of(masked(dp, 2 * slot + side))
                y_all[cut, :] = dot(grad_in[cut, :], w_in[...], 1, 1).astype(jnp.bfloat16)
                if side:
                    plane.start_core(slot)

        input_grads(1)
        summed.tick()
        input_grads(0)
        summed.tick()
        later[0].start()
        plane.step(1)
        plane.step(2)
        summed.tick()
        pl.loop(0, 2)(weights_in)
        summed.tick()
        pl.loop(2, 4)(weights_in)
        summed.tick()
        plane.step(3)
        pl.loop(4, 6)(weights_in)
        summed.tick()
        for one in later[1:]:
            one.start()
        saved = (chunks + CARRIED) * CHUNK
        save = save_sums(saved, sum_rows, 0)
        save.start()

        def save_made(block):
            return pltpu.make_async_copy(
                x_all.at[cut_of(block)], prod_ref.at[cut_of(block)], there.at[3 + block]
            )

        def make(block):
            made = dot(hidden[cut_of(block), :], w_down[...], 1, 0).astype(jnp.bfloat16).astype(jnp.float32)
            x_all[cut_of(block), :] = (made * gate_of(block)).astype(jnp.bfloat16)
            save_made(block).start()

        pl.loop(0, 4)(make)
        summed.tick()
        pl.loop(4, 8)(make)
        plane.step(4)
        summed.tick()
        set_bias()
        kv_grad[...] = jnp.zeros_like(kv_grad)
        gain_row_ref[...] = jnp.zeros_like(gain_row_ref)
        for one in later:
            one.wait()
        key_t[...] = all_kv[:, : kv_width // 2].astype(jnp.float32).T.astype(jnp.bfloat16)
        summed.tick()
        plane.step(5)

        tile = 32

        @pl.loop(0, tok_rows // tile)
        def _(step):
            cut = pl.ds(pl.multiple_of(step * tile, tile), tile)
            routed_grad = core_in[cut, :].astype(jnp.float32) + second_in[cut, :].astype(jnp.float32)
            to_middle, terms = norm_back(middle_ref[cut, :], gain_rows_ref[1:2, :], routed_grad)
            to_middle = cot_ref[cut, :].astype(jnp.float32) + to_middle
            middle_ref[cut, :] = to_middle
            attn_low[cut, :] = to_middle.astype(jnp.bfloat16)
            gain_row_ref[0:1, :] += jnp.sum(terms, axis=0, keepdims=True)

        for mask in (1, 2, 4):
            pl.semaphore_signal(freed, inc=1, device_id=(masked(dp, mask), z), device_id_type=MESH)
        save_mid = pltpu.make_async_copy(middle_ref, grad_mid_hbm, there.at[1])
        save_mid.start()
        summed.tick()
        wide = 512

        @pl.loop(0, width // wide)
        def _(step):
            cut = pl.ds(pl.multiple_of(step * wide, wide), wide)
            mixed_grad[:, cut] = dot(attn_low[...], full_o_ref[cut, :], 1, 1).astype(jnp.bfloat16)

        @pl.loop(0, width // 256)
        def _(step):
            cut = pl.ds(pl.multiple_of(step * 256, 256), 256)
            part_o[cut, :] = dot(mixed_ref[:, cut], attn_low[...], 0, 0).astype(jnp.bfloat16)

        pl.semaphore_wait(freed, 3)
        dense.step(0)
        summed.tick()

        def heads(first, last):
            @pl.loop(first, last)
            def _(head):
                own_cut = pl.ds(pl.multiple_of(head * HD, HD), HD)
                pair = head // per_group
                key_cut = pl.ds(pl.multiple_of(pair * HD, HD), HD)
                value_cut = pl.ds(pl.multiple_of((KVH + pair) * HD, HD), HD)
                q, do = query_ref[:, own_cut], mixed_grad[:, own_cut]
                k, v = all_kv[:, key_cut], all_kv[:, value_cut]
                scores = dot(k, q, 1, 1) * score_scale + bias[...]
                probs = jnp.exp(scores - lse_ref[pl.ds(head, 1), :])
                grad_probs = dot(v, do, 1, 1)
                inner = jnp.sum(probs * grad_probs, axis=0, keepdims=True)
                grad_raw = (probs * (grad_probs - inner) * score_scale).astype(jnp.bfloat16)
                kv_grad[:, value_cut] += dot(probs.astype(jnp.bfloat16), do, 1, 0)
                kv_grad[:, key_cut] += dot(grad_raw, q, 1, 0)
                to_query = dot(key_t[key_cut, :], grad_raw, 1, 0).T
                grad_pre_ref[:, own_cut] = turned(to_query, cos_ref[...], -sin_ref[...]).astype(
                    jnp.bfloat16
                )

        heads(0, 3)
        summed.tick()
        dense.step(1)
        dense.step(2)
        heads(3, 6)
        summed.tick()
        heads(6, 9)
        summed.tick()
        heads(9, 12)
        kv_part[...] = kv_grad[...].astype(jnp.bfloat16)
        line.begin()
        summed.tick()
        dense.step(3)
        summed.tick()
        line.event(0)
        summed.tick()
        dense.step(4)
        line.event(1)
        line.event(2)
        summed.tick()
        line.event(3)
        line.event(4)
        dense.step(5)
        summed.tick(max(0, summed.all - summed.now))
        save_last = save_sums(chunks * CHUNK, saved, 2)
        save_last.start()
        line.event(5)
        line.finish((kv_out,))
        for pair in range(KVH):
            cut = slice(pair * HD, (pair + 1) * HD)
            grad_pre_ref[:, q_width + pair * HD : q_width + (pair + 1) * HD] = turned(
                kv_out[:, cut], cos_ref[...], -sin_ref[...]
            ).astype(jnp.bfloat16)
        grad_pre_ref[:, q_width + kv_width // 2 :] = kv_out[:, kv_width // 2 :].astype(jnp.bfloat16)
        summed.finish()
        for block in range(8):
            save_made(block).wait()
        for one in (save, save_mid, save_last):
            one.wait()
        line_keys.finish()
        for mask in range(1, planes):
            gate_copy(mask, dp).wait_send()

    f32, low = jnp.float32, jnp.bfloat16
    copies = 4 * LineGather.COPIES + 5 * PlaneGather.COPIES + planes - 1
    copies += 2 * PlaneReduce.COPIES + 3 * (chunks + CARRIED) + LineReduce.COPIES
    return pl.pallas_call(
        kernel,
        out_shape=(
            jax.ShapeDtypeStruct((width, width), low),
            jax.ShapeDtypeStruct((width, kv_width + LANES), low),
            jax.ShapeDtypeStruct((width, width), low),
            jax.ShapeDtypeStruct((tok_rows, width), low),
            jax.ShapeDtypeStruct((tok_rows, width), low),
            jax.ShapeDtypeStruct((tok_rows, width), low),
            jax.ShapeDtypeStruct((tok_rows, width), f32),
            jax.ShapeDtypeStruct((8, width), f32),
            jax.ShapeDtypeStruct((sum_rows, width), low),
            jax.ShapeDtypeStruct((total_rows, width), low),
            jax.ShapeDtypeStruct(((chunks + CARRIED) * CHUNK, width), low),
            jax.ShapeDtypeStruct((tok_rows, width), f32),
            jax.ShapeDtypeStruct((tok_rows, width + kv_width), low),
            jax.ShapeDtypeStruct((8, width), f32),
            jax.ShapeDtypeStruct((group, width), low),
        ),
        in_specs=[ANY] * 11 + [VMEM] * 3,
        out_specs=(ANY,) * 7 + (VMEM, ANY, ANY, VMEM, ANY, VMEM, VMEM, VMEM),
        scratch_shapes=[
            pltpu.VMEM((width, 2 * hidden_width), low),
            pltpu.VMEM((hidden_width, width), low),
            pltpu.VMEM((total_rows, width), low),
            pltpu.VMEM((total_rows, width), low),
            pltpu.VMEM((total_rows, hidden_width), low),
            pltpu.VMEM((total_rows, hidden_width), f32),
            pltpu.VMEM((total_rows, 2 * hidden_width), low),
            pltpu.VMEM((sum_rows, width), low),
            pltpu.VMEM((RING * CHUNK, width), low),
            pltpu.VMEM((planes * planes, tok_rows), f32),
            pltpu.VMEM((tok_rows, planes * planes), f32),
            pltpu.VMEM((keys, kv_width), low),
            pltpu.VMEM((16, tok_rows), f32),
        ]
        + PlaneReduce.scratch(tok_rows, width)
        + [
            pltpu.VMEM((tok_rows, width), f32),
            LineReduce.scratch(tok_rows, kv_width, 1),
            pltpu.SemaphoreType.DMA((15,)),
            pltpu.SemaphoreType.DMA((18,)),
            pltpu.SemaphoreType.REGULAR,
        ]
        + sems(copies),
        compiler_params=kernel_params(1, 63),
        name="up_to_attention_back",
    )(
        w_query, w_key, w_value, gains, w_out, tokens, cotangent, gates, w_gate, w_up, w_down, starts, cosine, sine
    )


def back_dense(sums_in, produced, full_q, full_kv, normed, grad_pre, tokens, gains, grad_mid, gain_row, w_out_part, middle):
    tok_rows, width = middle.shape
    q_width = full_q.shape[1]
    in_width = q_width + full_kv.shape[1]
    pre_width = in_width - LANES
    w_rows = width
    group, rows = w_rows // 8, w_rows // (8 * LINE)
    skipped = BEFORE_DENSE
    chunks = sums_in.shape[0] // CHUNK - skipped

    def kernel(
        sums_ref, prod_ref, full_q_hbm, full_kv_hbm, normed_hbm, pre_hbm, tok_hbm, gain_ref, mid_grad_hbm,
        gain_row_ref, o_part_hbm, middle_hbm,
        total_ref, layer_ref, tok_grad_ref, wq_ref, wk_ref, wv_ref, gains_ref, out_ref,
        sums_own, sums_land, full_q_ref, full_kv_ref, normed_ref, pre_ref, tok_ref, mid_grad_ref, middle_ref, own, core_in, first_in, second_in, moe, part, d_core, d_first, d_second, in_sums,
        in_land, o_sums, o_land, normed_grad, gain_rows, here, send, recv,
    ):
        wires = Wires(send, recv)
        dp, z = wires.dp, wires.z
        early = (CARRIED + AHEAD) * CHUNK
        begin = skipped * CHUNK
        loads = [
            pltpu.make_async_copy(sums_ref.at[pl.ds(begin, early)], sums_own.at[pl.ds(0, early)], here.at[0]),
            pltpu.make_async_copy(
                sums_ref.at[pl.ds(begin + early, chunks * CHUNK - early)],
                sums_own.at[pl.ds(early, chunks * CHUNK - early)],
                here.at[1],
            ),
            pltpu.make_async_copy(o_part_hbm, o_sums, here.at[2]),
            pltpu.make_async_copy(pre_hbm, pre_ref, here.at[3]),
            pltpu.make_async_copy(full_q_hbm, full_q_ref, here.at[4]),
            pltpu.make_async_copy(full_kv_hbm, full_kv_ref, here.at[5]),
            pltpu.make_async_copy(tok_hbm, tok_ref, here.at[6]),
            pltpu.make_async_copy(mid_grad_hbm, mid_grad_ref, here.at[7]),
            pltpu.make_async_copy(normed_hbm, normed_ref, here.at[8]),
            pltpu.make_async_copy(middle_hbm, middle_ref, here.at[9]),
        ]
        first_loads = len(loads)
        for slot in range(4):
            row = pl.multiple_of(masked(dp, 2 * slot) * tok_rows, 16)
            loads.append(
                pltpu.make_async_copy(
                    prod_ref.at[pl.ds(row, tok_rows)],
                    own.at[pl.ds(slot * tok_rows, tok_rows)],
                    here.at[first_loads + slot],
                )
            )
        for one in loads:
            one.start()
        greet(wires, (1, 2, 4), True)
        summed = LineSum(wires, sums_own, total_ref, sums_land, CHUNK, chunks, came=True)
        dense = PlaneReduce(
            wires, part, group, part, lambda slot: pl.multiple_of(masked(dp, 2 * slot) * group, 16),
            d_core, d_first, d_second, in_sums,
        )
        plane = PlaneReduce(
            wires, prod_ref, tok_rows, own, lambda slot: slot * tok_rows, core_in, first_in, second_in, moe
        )
        o_line = LineReduce(wires, o_sums, rows, o_land)
        in_line = LineReduce(wires, in_sums, rows, in_land)
        loads[0].wait()
        summed.begin()
        loads[1].wait()
        loads[2].wait()
        o_line.begin()
        for one in loads[3:first_loads]:
            one.wait()
        wide = 512

        @pl.loop(0, width // wide)
        def _(step):
            cut = pl.ds(pl.multiple_of(step * wide, wide), wide)
            normed_grad[:, cut] = dot(pre_ref[:, :q_width], full_q_ref[cut, :], 1, 1) + dot(
                pre_ref[:, q_width:], full_kv_ref[cut, : pre_width - q_width], 1, 1
            )

        summed.tick()
        gain_rows[...] = jnp.zeros_like(gain_rows)
        gain_rows[1:2, :] = gain_row_ref[0:1, :]
        tile = 32

        @pl.loop(0, tok_rows // tile)
        def _(step):
            cut = pl.ds(pl.multiple_of(step * tile, tile), tile)
            to_tokens, terms = norm_back(
                tok_ref[cut, :].astype(jnp.float32), gain_ref[0:1, :], normed_grad[cut, :]
            )
            tok_grad_ref[cut, :] = mid_grad_ref[cut, :] + to_tokens
            gain_rows[0:1, :] += jnp.sum(terms, axis=0, keepdims=True)

        summed.tick()
        o_line.event(0)
        part[:, pre_width:] = gain_rows[...].T.astype(jnp.bfloat16)

        @pl.loop(0, w_rows // 256)
        def _(step):
            cut = pl.ds(pl.multiple_of(step * 256, 256), 256)
            part[cut, :pre_width] = dot(normed_ref[:, cut], pre_ref[...], 0, 0).astype(jnp.bfloat16)

        dense.step(0)
        o_line.event(1)
        o_line.event(2)
        summed.tick(2)
        dense.step(1)
        o_line.event(3)
        summed.tick()
        dense.step(2)
        o_line.event(4)
        summed.tick()
        o_line.event(5)
        for one in loads[first_loads:]:
            one.wait()
        plane.step(0)
        summed.tick(2)
        plane.step(1)
        summed.tick()
        dense.step(3)
        plane.step(2)
        summed.tick(2)
        dense.step(4)
        dense.step(5)
        in_line.begin()
        summed.tick()
        in_line.event(0)
        summed.tick()
        plane.step(3)
        in_line.event(1)
        in_line.event(2)
        summed.tick(2)
        in_line.event(3)
        in_line.event(4)
        plane.step(4)
        summed.tick(2)
        in_line.event(5)
        plane.step(5)
        summed.tick(2)

        @pl.loop(0, tok_rows // tile)
        def _(step):
            cut = pl.ds(pl.multiple_of(step * tile, tile), tile)
            layer_ref[cut, :] = (middle_ref[cut, :] + moe[cut, :]).astype(jnp.bfloat16)

        o_line.finish((out_ref,))
        in_line.finish((wq_ref, wk_ref, wv_ref, gains_ref))
        summed.finish()

    f32, low = jnp.float32, jnp.bfloat16
    return pl.pallas_call(
        kernel,
        out_shape=(
            jax.ShapeDtypeStruct((chunks * CHUNK, sums_in.shape[1]), low),
            jax.ShapeDtypeStruct((tok_rows, width), low),
            jax.ShapeDtypeStruct((tok_rows, width), f32),
            jax.ShapeDtypeStruct((rows, q_width), f32),
            jax.ShapeDtypeStruct((rows, (pre_width - q_width) // 2), f32),
            jax.ShapeDtypeStruct((rows, (pre_width - q_width) // 2), f32),
            jax.ShapeDtypeStruct((rows, LANES), f32),
            jax.ShapeDtypeStruct((rows, width), f32),
        ),
        in_specs=[ANY] * 7 + [VMEM, ANY, VMEM, ANY, ANY],
        out_specs=(VMEM,) * 8,
        scratch_shapes=[
            pltpu.VMEM((chunks * CHUNK, width), low),
            pltpu.VMEM((RING * CHUNK, width), low),
            pltpu.VMEM(full_q.shape, low),
            pltpu.VMEM(full_kv.shape, low),
            pltpu.VMEM((tok_rows, width), low),
            pltpu.VMEM((tok_rows, pre_width), low),
            pltpu.VMEM((tok_rows, width), low),
            pltpu.VMEM((tok_rows, width), f32),
            pltpu.VMEM((tok_rows, width), f32),
            pltpu.VMEM((4 * tok_rows, width), low),
        ]
        + PlaneReduce.scratch(tok_rows, width)
        + [pltpu.VMEM((tok_rows, width), f32), pltpu.VMEM((w_rows, in_width), low)]
        + PlaneReduce.scratch(group, in_width)
        + [
            pltpu.VMEM((group, in_width), low),
            LineReduce.scratch(rows, in_width),
            pltpu.VMEM((group, width), low),
            LineReduce.scratch(rows, width),
            pltpu.VMEM((tok_rows, width), f32),
            pltpu.VMEM((LANES, width), f32),
            pltpu.SemaphoreType.DMA((14,)),
        ]
        + sems(3 * chunks + 2 * PlaneReduce.COPIES + 2 * LineReduce.COPIES),
        compiler_params=kernel_params(4, 63),
        name="back_dense",
    )(
        sums_in, produced, full_q, full_kv, normed, grad_pre, tokens, gains, grad_mid, gain_row, w_out_part, middle
    )


def on_plane_device(
    tokens,
    norm_attn,
    w_query,
    w_key,
    w_value,
    w_out,
    norm_moe,
    w_gate,
    w_up,
    w_down,
    routes,
    gate_values,
    lengths,
    cotangent,
):
    tok_rows = tokens.shape[0]
    ctx_size = lax.axis_size("ctx")
    ctx_place = lax.axis_index("ctx")
    group_places = jnp.arange(tok_rows * ctx_size, dtype=jnp.int32)
    seg_all, within_all = seq_tables(lengths[0], group_places)
    offset = ctx_place * tok_rows
    own_places = offset + jnp.arange(tok_rows, dtype=jnp.int32)
    within_own = lax.dynamic_slice_in_dim(within_all, offset, tok_rows)
    kv_columns = KVH * HD
    q_columns = HEADS * HD
    gains = jnp.pad(jnp.stack([norm_attn, norm_moe], axis=1), ((0, 0), (0, LANES - 2)))
    numbers = jnp.arange(8, dtype=jnp.int32)
    gates = jnp.sum(
        jnp.where(routes[None, :, :] == numbers[:, None, None], gate_values[None], 0.0), axis=2
    )
    half_size = HD // 2
    frequency = rope_base ** (-jnp.arange(half_size, dtype=jnp.float32) / half_size)
    angles = within_own.astype(jnp.float32)[:, None] * frequency[None, :]
    cosine = jnp.concatenate([jnp.cos(angles), jnp.cos(angles)], axis=1)
    sine = jnp.concatenate([-jnp.sin(angles), jnp.sin(angles)], axis=1)
    starts = jnp.broadcast_to((own_places - within_own)[None, :], (8, tok_rows))
    (
        full_q, full_kv, _, _, _, normed_low, middle, gain_rows, partial_sums, produced, sums_head, grad_mid, grad_pre,
        gain_row, w_out_part,
    ) = up_to_attention_back(
        w_query, w_key, w_value, gains, w_out, tokens, cotangent, gates, w_gate[0], w_up[0], w_down[0], starts, cosine,
        sine,
    )
    half = w_gate.shape[2]
    sums_tail, layer_out, grad_tokens, sum_q, sum_k, sum_v, sum_gains, sum_o = back_dense(
        partial_sums,
        produced,
        full_q,
        full_kv,
        normed_low,
        grad_pre,
        tokens,
        gain_rows,
        grad_mid,
        gain_row,
        w_out_part,
        middle,
    )
    head = BEFORE_DENSE * CHUNK

    def whole(columns):
        return jnp.concatenate([sums_head[half:head, columns], sums_tail[:, columns]], axis=0)

    return (
        layer_out,
        grad_tokens,
        sum_gains[:, 0],
        sum_q,
        sum_k,
        sum_v,
        sum_o,
        sum_gains[:, 1],
        whole(slice(0, half)).astype(jnp.float32)[None],
        whole(slice(half, 2 * half)).astype(jnp.float32)[None],
        sums_head[:half].astype(jnp.float32)[None],
    )


def solution(mesh):
    on_plane = mesh.shape["dp"] == 8 and mesh.shape["ctx"] == LINE
    return jax.shard_map(
        on_plane_device if on_plane else on_device,
        mesh=mesh,
        in_specs=(
            P(("dp", "ctx"), None),
            P(("dp", "ctx")),
            P(("dp", "ctx"), None),
            P(("dp", "ctx"), None),
            P(("dp", "ctx"), None),
            P(("dp", "ctx"), None),
            P(("dp", "ctx")),
            P("dp", None, None),
            P("dp", None, None),
            P("dp", None, None),
            P(("dp", "ctx"), None),
            P(("dp", "ctx"), None),
            P("dp", None),
            P(("dp", "ctx"), None),
        ),
        out_specs=(
            P(("dp", "ctx"), None),
            P(("dp", "ctx"), None),
            P(("dp", "ctx")),
            P(("dp", "ctx"), None),
            P(("dp", "ctx"), None),
            P(("dp", "ctx"), None),
            P(("dp", "ctx"), None),
            P(("dp", "ctx")),
            P("dp", None, None),
            P("dp", None, None),
            P("dp", None, None),
        ),
        check_vma=False,
    )
```

```python
import functools

import jax
import jax.numpy as jnp
from jax import lax
from jax.experimental import pallas as pl
from jax.experimental.pallas import tpu as pltpu
from jax.sharding import PartitionSpec as P

D = 1536
HEADS = 12
KVH = 2
HD = 128
TOP = 4
EXP_DEV = 1


epsilon = 1e-06
rope_base = 1000000.0
masked_score = -1e30


def rms_norm(values, gain):
    return values * lax.rsqrt(jnp.mean(values * values, axis=-1, keepdims=True) + epsilon) * gain


def rotate(values, within, direction):
    half_size = values.shape[-1] // 2
    frequency = rope_base ** (-jnp.arange(half_size, dtype=jnp.float32) / half_size)
    angles = direction * within.astype(jnp.float32)[:, None] * frequency[None, :]
    cosine = jnp.cos(angles)[:, None, :]
    sine = jnp.sin(angles)[:, None, :]
    first_half = values[..., :half_size]
    second = values[..., half_size:]
    return jnp.concatenate(
        [first_half * cosine - second * sine, second * cosine + first_half * sine], axis=-1
    )


def seq_tables(length_row, places):
    seq_ends = jnp.cumsum(length_row)
    passed = places[:, None] >= seq_ends[None, :]
    segment = jnp.sum(passed.astype(jnp.int32), axis=1)
    within = places - jnp.sum(jnp.where(passed, length_row[None, :], 0), axis=1)
    return (segment, within)


def collect_weights(gain_attn, w_query, w_key, w_value, w_out, gain_moe):
    return (
        lax.all_gather(gain_attn, ("dp", "ctx"), axis=0, tiled=True),
        lax.all_gather(w_query, ("dp", "ctx"), axis=0, tiled=True),
        lax.all_gather(w_key, ("dp", "ctx"), axis=0, tiled=True),
        lax.all_gather(w_value, ("dp", "ctx"), axis=0, tiled=True),
        lax.all_gather(w_out, ("dp", "ctx"), axis=0, tiled=True),
        lax.all_gather(gain_moe, ("dp", "ctx"), axis=0, tiled=True),
    )


def spread_grads(grad_gain_attn, grad_query, grad_key, grad_value, grad_outp, grad_gain_moe):
    return (
        lax.psum_scatter(grad_gain_attn, ("dp", "ctx"), scatter_dimension=0, tiled=True),
        lax.psum_scatter(grad_query, ("dp", "ctx"), scatter_dimension=0, tiled=True),
        lax.psum_scatter(grad_key, ("dp", "ctx"), scatter_dimension=0, tiled=True),
        lax.psum_scatter(grad_value, ("dp", "ctx"), scatter_dimension=0, tiled=True),
        lax.psum_scatter(grad_outp, ("dp", "ctx"), scatter_dimension=0, tiled=True),
        lax.psum_scatter(grad_gain_moe, ("dp", "ctx"), scatter_dimension=0, tiled=True),
    )


def on_device(
    tokens,
    norm_attn,
    w_query,
    w_key,
    w_value,
    w_out,
    norm_moe,
    w_gate,
    w_up,
    w_down,
    routes,
    gate_values,
    lengths,
    cotangent,
):
    tok_rows = tokens.shape[0]
    ctx_size = lax.axis_size("ctx")
    dp_size = lax.axis_size("dp")
    ctx_place = lax.axis_index("ctx")
    group_rows = tok_rows * ctx_size
    group_places = jnp.arange(group_rows, dtype=jnp.int32)
    seg_all, within_all = seq_tables(lengths[0], group_places)
    offset = ctx_place * tok_rows
    own_places = offset + jnp.arange(tok_rows, dtype=jnp.int32)
    seg_own = lax.dynamic_slice_in_dim(seg_all, offset, tok_rows)
    within_own = lax.dynamic_slice_in_dim(within_all, offset, tok_rows)
    allowed = (seg_own[:, None] == seg_all[None, :]) & (
        group_places[None, :] <= own_places[:, None]
    )
    gain_attn, full_q, full_k, full_v, full_o, gain_moe = collect_weights(
        norm_attn, w_query, w_key, w_value, w_out, norm_moe
    )
    gain_attn_f = gain_attn.astype(jnp.float32)
    gain_moe_f = gain_moe.astype(jnp.float32)
    inputs = tokens.astype(jnp.float32)
    normed_low = rms_norm(inputs, gain_attn_f).astype(jnp.bfloat16)
    query_pre = jnp.dot(normed_low, full_q, preferred_element_type=jnp.float32)
    key_pre = jnp.dot(normed_low, full_k, preferred_element_type=jnp.float32)
    value_pre = jnp.dot(normed_low, full_v, preferred_element_type=jnp.float32)
    query = rotate(query_pre.reshape(tok_rows, HEADS, HD), within_own, 1.0).astype(jnp.bfloat16)
    key_low = rotate(key_pre.reshape(tok_rows, KVH, HD), within_own, 1.0).astype(jnp.bfloat16)
    key_low = key_low.reshape(tok_rows, KVH * HD)
    value_low = value_pre.astype(jnp.bfloat16)
    all_keys, all_values = (
        lax.all_gather(key_low, "ctx", axis=0, tiled=True),
        lax.all_gather(value_low, "ctx", axis=0, tiled=True),
    )
    per_group = HEADS // KVH
    score_scale = HD ** (-0.5)
    query_groups = query.reshape(tok_rows, KVH, per_group, HD)

    def softmax_weights(group_number):
        keys_part = all_keys[:, group_number * HD : (group_number + 1) * HD]
        raw = jnp.einsum(
            "qjd,kd->jqk",
            query_groups[:, group_number],
            keys_part,
            preferred_element_type=jnp.float32,
        )
        scores = jnp.where(allowed[None], raw * score_scale, masked_score)
        row_top = jnp.max(scores, axis=-1, keepdims=True)
        expo = jnp.exp(scores - row_top)
        return expo / jnp.sum(expo, axis=-1, keepdims=True)

    mixed_parts = []
    for group_number in range(KVH):
        probs = softmax_weights(group_number)
        values_part = all_values[:, group_number * HD : (group_number + 1) * HD]
        mixed_group = jnp.einsum(
            "jqk,kd->qjd",
            probs.astype(jnp.bfloat16),
            values_part,
            preferred_element_type=jnp.float32,
        )
        mixed_parts.append(mixed_group.reshape(tok_rows, per_group * HD))
    mixed_low = jnp.concatenate(mixed_parts, axis=1).astype(jnp.bfloat16)
    middle = inputs + jnp.dot(mixed_low, full_o, preferred_element_type=jnp.float32)
    routed_low = rms_norm(middle, gain_moe_f).astype(jnp.bfloat16)
    experts_total = EXP_DEV * dp_size
    capacity = 3 * TOP * tok_rows // (2 * experts_total)
    assign_count = tok_rows * TOP
    flat_ids = routes.reshape(assign_count)
    onehot = (flat_ids[:, None] == jnp.arange(experts_total, dtype=jnp.int32)[None, :]).astype(
        jnp.int32
    )
    earlier = jnp.sum((jnp.cumsum(onehot, axis=0) - onehot) * onehot, axis=1)
    slot_index = flat_ids * capacity + earlier
    owner = (
        jnp.full((experts_total * capacity,), assign_count, jnp.int32)
        .at[slot_index]
        .set(jnp.arange(assign_count, dtype=jnp.int32))
    )
    padded = jnp.concatenate([routed_low, jnp.zeros((1, D), jnp.bfloat16)], axis=0)
    outgoing = padded[owner // TOP].reshape(experts_total, capacity, D)
    arrived = lax.all_to_all(outgoing, "dp", split_axis=0, concat_axis=0, tiled=True)
    arrived_sets = arrived.reshape(dp_size, EXP_DEV, capacity, D)
    gate_act = jnp.einsum(
        "secd,edf->secf", arrived_sets, w_gate, preferred_element_type=jnp.float32
    )
    up_act = jnp.einsum("secd,edf->secf", arrived_sets, w_up, preferred_element_type=jnp.float32)
    hidden_low = (jax.nn.silu(gate_act) * up_act).astype(jnp.bfloat16)
    produced = jnp.einsum("secf,efd->secd", hidden_low, w_down, preferred_element_type=jnp.float32)
    produced = produced.astype(jnp.bfloat16).reshape(experts_total, capacity, D)
    returned = lax.all_to_all(produced, "dp", split_axis=0, concat_axis=0, tiled=True)
    picked = returned.reshape(experts_total * capacity, D)[slot_index].reshape(tok_rows, TOP, D)
    moe_out = jnp.sum(picked.astype(jnp.float32) * gate_values[:, :, None], axis=1)
    layer_out = (middle + moe_out).astype(jnp.bfloat16)
    grad_out = cotangent.astype(jnp.float32)
    grad_assign = (grad_out[:, None, :] * gate_values[:, :, None]).astype(jnp.bfloat16)
    grad_padded = jnp.concatenate(
        [grad_assign.reshape(assign_count, D), jnp.zeros((1, D), jnp.bfloat16)], axis=0
    )
    grad_slots = grad_padded[owner].reshape(experts_total, capacity, D)
    grad_arrived = lax.all_to_all(grad_slots, "dp", split_axis=0, concat_axis=0, tiled=True)
    grad_arrived = grad_arrived.reshape(dp_size, EXP_DEV, capacity, D)
    grad_hidden = jnp.einsum(
        "secd,efd->secf", grad_arrived, w_down, preferred_element_type=jnp.float32
    )
    grad_w_down = jnp.einsum(
        "secf,secd->efd", hidden_low, grad_arrived, preferred_element_type=jnp.float32
    )
    glu_value, glu_pull = jax.vjp(
        lambda gate_in, up_in: jax.nn.silu(gate_in) * up_in, gate_act, up_act
    )
    grad_gate, grad_up = glu_pull(grad_hidden)
    grad_gate_low = grad_gate.astype(jnp.bfloat16)
    grad_up_low = grad_up.astype(jnp.bfloat16)
    grad_w_gate = jnp.einsum(
        "secd,secf->edf", arrived_sets, grad_gate_low, preferred_element_type=jnp.float32
    )
    grad_w_up = jnp.einsum(
        "secd,secf->edf", arrived_sets, grad_up_low, preferred_element_type=jnp.float32
    )
    grad_sent = jnp.einsum(
        "secf,edf->secd", grad_gate_low, w_gate, preferred_element_type=jnp.float32
    ) + jnp.einsum("secf,edf->secd", grad_up_low, w_up, preferred_element_type=jnp.float32)
    grad_sent = grad_sent.astype(jnp.bfloat16).reshape(experts_total, capacity, D)
    grad_back = lax.all_to_all(grad_sent, "dp", split_axis=0, concat_axis=0, tiled=True)
    grad_picked = grad_back.reshape(experts_total * capacity, D)[slot_index].reshape(
        tok_rows, TOP, D
    )
    grad_routed = jnp.sum(grad_picked.astype(jnp.float32), axis=1)
    expert_sums = (
        lax.psum(grad_w_gate.astype(jnp.bfloat16), "ctx").astype(jnp.float32),
        lax.psum(grad_w_up.astype(jnp.bfloat16), "ctx").astype(jnp.float32),
        lax.psum(grad_w_down.astype(jnp.bfloat16), "ctx").astype(jnp.float32),
    )
    norm_value, moe_pull = jax.vjp(rms_norm, middle, gain_moe_f)
    grad_mid_norm, grad_gain_moe = moe_pull(grad_routed)
    grad_middle = grad_out + grad_mid_norm
    grad_attn_low = grad_middle.astype(jnp.bfloat16)
    grad_w_out = jnp.einsum(
        "th,td->hd", mixed_low, grad_attn_low, preferred_element_type=jnp.float32
    )
    grad_mixed_low = jnp.einsum(
        "td,hd->th", grad_attn_low, full_o, preferred_element_type=jnp.float32
    ).astype(jnp.bfloat16)
    grad_mixed_groups = grad_mixed_low.reshape(tok_rows, KVH, per_group, HD)
    grad_query_parts = []
    prob_parts = []
    score_parts = []
    for group_number in range(KVH):
        probs = softmax_weights(group_number)
        keys_part = all_keys[:, group_number * HD : (group_number + 1) * HD]
        values_part = all_values[:, group_number * HD : (group_number + 1) * HD]
        grad_probs = jnp.einsum(
            "qjd,kd->jqk",
            grad_mixed_groups[:, group_number],
            values_part,
            preferred_element_type=jnp.float32,
        )
        grad_scores = probs * (grad_probs - jnp.sum(probs * grad_probs, axis=-1, keepdims=True))
        grad_raw_low = (grad_scores * score_scale).astype(jnp.bfloat16)
        grad_query_parts.append(
            jnp.einsum("jqk,kd->qjd", grad_raw_low, keys_part, preferred_element_type=jnp.float32)
        )
        prob_parts.append(probs.astype(jnp.bfloat16))
        score_parts.append(grad_raw_low)
    grad_query_rot = jnp.stack(grad_query_parts, axis=1).reshape(tok_rows, HEADS, HD)
    key_pieces = []
    value_pieces = []
    for group_number in range(KVH):
        score_piece = score_parts[group_number]
        prob_piece = prob_parts[group_number]
        key_pieces.append(
            jnp.einsum(
                "jqk,qjd->kd",
                score_piece,
                query_groups[:, group_number],
                preferred_element_type=jnp.float32,
            )
        )
        value_pieces.append(
            jnp.einsum(
                "jqk,qjd->kd",
                prob_piece,
                grad_mixed_groups[:, group_number],
                preferred_element_type=jnp.float32,
            )
        )
    key_value_grads = lax.psum_scatter(
        jnp.concatenate(key_pieces + value_pieces, axis=1).astype(jnp.bfloat16),
        "ctx",
        scatter_dimension=0,
        tiled=True,
    ).astype(jnp.float32)
    grad_query_low = (
        rotate(grad_query_rot, within_own, -1.0).astype(jnp.bfloat16).reshape(tok_rows, HEADS * HD)
    )
    grad_key_rot = key_value_grads[:, : KVH * HD].reshape(tok_rows, KVH, HD)
    grad_key_low = (
        rotate(grad_key_rot, within_own, -1.0).astype(jnp.bfloat16).reshape(tok_rows, KVH * HD)
    )
    grad_value_low = key_value_grads[:, KVH * HD :].astype(jnp.bfloat16)
    grad_w_query = jnp.einsum(
        "td,th->dh", normed_low, grad_query_low, preferred_element_type=jnp.float32
    )
    grad_w_key = jnp.einsum(
        "td,th->dh", normed_low, grad_key_low, preferred_element_type=jnp.float32
    )
    grad_w_value = jnp.einsum(
        "td,th->dh", normed_low, grad_value_low, preferred_element_type=jnp.float32
    )
    grad_normed = (
        jnp.einsum("th,dh->td", grad_query_low, full_q, preferred_element_type=jnp.float32)
        + jnp.einsum("th,dh->td", grad_key_low, full_k, preferred_element_type=jnp.float32)
        + jnp.einsum("th,dh->td", grad_value_low, full_v, preferred_element_type=jnp.float32)
    )
    first_value, attn_pull = jax.vjp(rms_norm, inputs, gain_attn_f)
    grad_inputs, grad_gain_attn = attn_pull(grad_normed)
    grad_tokens = grad_middle + grad_inputs
    dense_sums = spread_grads(
        grad_gain_attn, grad_w_query, grad_w_key, grad_w_value, grad_w_out, grad_gain_moe
    )
    return (
        layer_out,
        grad_tokens,
        dense_sums[0],
        dense_sums[1],
        dense_sums[2],
        dense_sums[3],
        dense_sums[4],
        dense_sums[5],
        expert_sums[0],
        expert_sums[1],
        expert_sums[2],
    )


MESH = pl.DeviceIdType.MESH
LANES = 128
MIB = 2**20
ANY = pl.BlockSpec(memory_space=pl.ANY)
VMEM = pl.BlockSpec(memory_space=pltpu.VMEM)


def flip(index, bit):
    return index + bit - 2 * bit * ((index // bit) % 2)


def masked(index, mask):
    for bit in (1, 2, 4):
        if mask & bit:
            index = flip(index, bit)
    return index


class Wires:
    def __init__(self, send, recv):
        self.send, self.recv, self.used = send, recv, 0
        self.dp, self.z = lax.axis_index("dp"), lax.axis_index("ctx")

    def take(self, count):
        first = self.used
        self.used += count
        return first

    def copy(self, src, dst, number, dp=None, z=None):
        return pltpu.make_async_remote_copy(
            src_ref=src,
            dst_ref=dst,
            send_sem=self.send.at[number],
            recv_sem=self.recv.at[number],
            device_id=(self.dp if dp is None else dp, self.z if z is None else z),
            device_id_type=MESH,
        )


def greet(wires, masks, line):
    barrier = pltpu.get_barrier_semaphore()
    dp, z = wires.dp, wires.z
    for mask in masks:
        pl.semaphore_signal(barrier, inc=1, device_id=(masked(dp, mask), z), device_id_type=MESH)
    for step in range(1, LINE) if line else ():
        pl.semaphore_signal(
            barrier, inc=1, device_id=(dp, lax.rem(z + step, LINE)), device_id_type=MESH
        )
    pl.semaphore_wait(barrier, len(masks) + (LINE - 1 if line else 0))


LINE = 4


class LineGather:
    COPIES = 2 * (LINE - 1)

    def __init__(self, wires, ref, rows_of):
        self.wires, self.ref, self.rows_of = wires, ref, rows_of
        self.first = wires.take(self.COPIES)

    def _copy(self, block, number, z):
        part = self.ref.at[self.rows_of(block)]
        return self.wires.copy(part, part, self.first + number, z=z)

    def start(self, step):
        z = self.wires.z

        @pl.when((z >= step) & (z < LINE - 1))
        def _():
            self._copy(z - step, step, z + 1).start()

        @pl.when((z + step < LINE) & (z > 0))
        def _():
            self._copy(z + step, LINE - 1 + step, z - 1).start()

    def wait(self, step):
        z = self.wires.z

        @pl.when(z - 1 - step >= 0)
        def _():
            self._copy(z - 1 - step, step, z).wait_recv()

        @pl.when(z + 1 + step < LINE)
        def _():
            self._copy(z + 1 + step, LINE - 1 + step, z).wait_recv()

    def finish(self):
        z = self.wires.z
        for step in range(LINE - 1):

            @pl.when((z >= step) & (z < LINE - 1))
            def _():
                self._copy(z - step, step, z + 1).wait_send()

            @pl.when((z + step < LINE) & (z > 0))
            def _():
                self._copy(z + step, LINE - 1 + step, z - 1).wait_send()


class PlaneGather:
    CHIP = (((2, 0, 0), (4, 0, 1)), ((4, 0, 0), (2, 0, 1)), ((4, 2, 0), (2, 4, 1)))
    CORE = (
        ((1, 0, 2),),
        ((1, 2, 0), (1, 4, 1)),
        ((1, 4, 0), (1, 2, 1)),
        ((1, 6, 0), (1, 6, 1)),
    )
    COPIES = 13

    def __init__(self, wires, ref, group):
        self.wires, self.ref, self.group = wires, ref, group
        first = wires.take(self.COPIES)
        self.number = {}
        for stage in self.CHIP + self.CORE:
            for one in stage:
                self.number[one] = first + len(self.number)
        self.core_left = [0, 1, 2, 3]

    def _copy(self, one, from_me):
        to, whose, half = one
        dp = self.wires.dp
        sender = dp if from_me else masked(dp, to)
        owner = masked(sender, whose)
        size = self.group if half == 2 else self.group // 2
        begin = owner * self.group + (self.group // 2 if half == 1 else 0)
        part = self.ref.at[pl.ds(pl.multiple_of(begin, 16), size)]
        return self.wires.copy(part, part, self.number[one], dp=masked(dp, to))

    def start(self, stage, far=True):
        for one in (self.CHIP[stage] if stage < 2 else ()) + self.CORE[stage]:
            self._copy(one, True).start()
        if stage == 1 and far:
            self.start_far()

    def start_one(self, number):
        self._copy((self.CHIP[0] + self.CORE[0])[number], True).start()

    def start_far(self):
        for one in self.CHIP[2]:
            self._copy(one, True).start()

    def wait(self, stage):
        for one in self.CHIP[stage]:
            self._copy(one, False).wait_recv()

    def wait_core(self, stage):
        self.core_left.remove(stage)
        for one in self.CORE[stage]:
            self._copy(one, False).wait_recv()

    def finish(self):
        for stage in list(self.core_left):
            self.wait_core(stage)
        for one in self.number:
            self._copy(one, True).wait_send()


def add_rows(out, out_row, left, left_row, right, right_row, rows):
    @pl.loop(0, rows // 16)
    def _(step):
        def cut(row):
            return pl.ds(pl.multiple_of(row + step * 16, 16), 16)

        out[cut(out_row), :] = (
            left[cut(left_row), :].astype(jnp.float32) + right[cut(right_row), :].astype(jnp.float32)
        ).astype(out.dtype)


class PlaneReduce:
    COPIES = 10
    STEPS = 6

    def __init__(self, wires, part, group, own, own_row, core_in, first_in, second_in, out):
        self.wires, self.part, self.group, self.half = wires, part, group, group // 2
        self.own, self.own_row, self.out = own, own_row, out
        self.core_in, self.first_in, self.second_in = core_in, first_in, second_in
        self.first = wires.take(self.COPIES)

    def _send(self, src, src_row, dst, dst_row, rows, number, to):
        return self.wires.copy(
            src.at[pl.ds(src_row, rows)],
            dst.at[pl.ds(dst_row, rows)],
            self.first + number,
            dp=masked(self.wires.dp, to),
        )

    def _core(self, slot):
        row = pl.multiple_of(masked(self.wires.dp, 1 + 2 * slot) * self.group, 16)
        return self._send(self.part, row, self.core_in, slot * self.group, self.group, slot, 1)

    def _far(self, number):
        g, h = self.group, self.half
        src_row, dst, dst_row, to = (
            (3 * g, self.first_in, h, 4),
            (3 * g + h, self.first_in, 3 * h, 2),
            (2 * g, self.first_in, 0, 4),
            (1 * g + h, self.first_in, 2 * h, 2),
            (1 * g, self.second_in, 0, 2),
            (2 * g + h, self.second_in, h, 4),
        )[number]
        return self._send(self.core_in, src_row, dst, dst_row, h, 4 + number, to)

    def _sum_core(self, slot):
        self._core(slot).wait()
        row = slot * self.group
        add_rows(self.core_in, row, self.own, self.own_row(slot), self.core_in, row, self.group)

    def _sum_far(self, number, row, in_row):
        self._far(number).wait()
        add_rows(self.core_in, row, self.core_in, row, self.first_in, in_row, self.half)

    def start_core(self, slot):
        self._core(slot).start()

    def step(self, number):
        g, h = self.group, self.half
        if number == 0:
            for slot in (3, 2, 1, 0):
                self.start_core(slot)
        elif number == 1:
            self._sum_core(3)
            self._far(0).start()
            self._far(1).start()
        elif number == 2:
            self._sum_core(2)
            self._far(2).start()
            self._sum_core(1)
            self._far(3).start()
            self._sum_core(0)
        elif number == 3:
            self._sum_far(0, 1 * g, h)
            self._far(4).start()
            self._sum_far(1, 2 * g + h, 3 * h)
            self._far(5).start()
        elif number == 4:
            self._sum_far(2, 0, 0)
            self._sum_far(3, h, 2 * h)
        elif self.out is None:
            self._far(4).wait()
            self._far(5).wait()
        else:
            self._far(4).wait()
            add_rows(self.out, 0, self.core_in, 0, self.second_in, 0, h)
            self._far(5).wait()
            add_rows(self.out, h, self.core_in, h, self.second_in, h, h)

    @staticmethod
    def scratch(group, columns):
        return [
            pltpu.VMEM((4 * group, columns), jnp.bfloat16),
            pltpu.VMEM((2 * group, columns), jnp.bfloat16),
            pltpu.VMEM((group, columns), jnp.bfloat16),
        ]


class LineReduce:
    COPIES = 2 * (LINE - 1) * LINE
    EVENTS = ((0, 0), (0, 1), (1, 0), (0, 2), (1, 1), (2, 0))

    def __init__(self, wires, part, rows, landing, ways=(1, -1)):
        self.wires, self.part, self.rows, self.landing, self.ways = wires, part, rows, landing, ways
        self.first = wires.take(self.COPIES)

    def _place(self, way, hop, nearer):
        return (LINE - 1 - nearer, hop) if way == 1 else (nearer, LINE - 1 - hop)

    def _copy(self, way, hop, nearer, z):
        side = self.ways.index(way)
        block, _ = self._place(way, hop, nearer)
        return self.wires.copy(
            self.part.at[pl.ds(block * self.rows, self.rows)],
            self.landing.at[pl.ds((side * LINE + block) * self.rows, self.rows)],
            self.first + (side * (LINE - 1) + hop) * LINE + nearer,
            z=z,
        )

    def _send(self, way, hop, nearer):
        z = self.wires.z

        @pl.when(z == self._place(way, hop, nearer)[1])
        def _():
            self._copy(way, hop, nearer, z + way).start()

    def begin(self):
        for nearer in range(LINE - 1):
            for way in self.ways:
                self._send(way, 0, nearer)

    def event(self, number):
        hop, nearer = self.EVENTS[number]
        z, rows = self.wires.z, self.rows
        for way in self.ways:
            block, source = self._place(way, hop, nearer)

            @pl.when(z == source + way)
            def _():
                self._copy(way, hop, nearer, z).wait_recv()
                landed = (self.ways.index(way) * LINE + block) * rows
                add_rows(
                    self.part, block * rows, self.part, block * rows, self.landing, landed, rows
                )
                if nearer < LINE - 2 - hop:
                    self._copy(way, hop + 1, nearer, z + way).start()

    def finish(self, outs):
        z, rows = self.wires.z, self.rows

        @pl.loop(0, rows // 16)
        def _(step):
            row = pl.multiple_of(z * rows + step * 16, 16)
            begin = 0
            for out in outs:
                out[pl.ds(pl.multiple_of(step * 16, 16), 16), :] = self.part[
                    pl.ds(row, 16), begin : begin + out.shape[1]
                ].astype(out.dtype)
                begin += out.shape[1]

        for hop, nearer in self.EVENTS:
            for way in self.ways:

                @pl.when(z == self._place(way, hop, nearer)[1])
                def _():
                    self._copy(way, hop, nearer, z + way).wait_send()

    @staticmethod
    def scratch(rows, columns, ways=2):
        return pltpu.VMEM(((ways * LINE - 1) * rows, columns), jnp.bfloat16)


def sems(count):
    return [pltpu.SemaphoreType.DMA((count,)), pltpu.SemaphoreType.DMA((count,))]


def kernel_params(collective_id, mib):
    return pltpu.CompilerParams(
        collective_id=collective_id, has_side_effects=True, vmem_limit_bytes=mib * MIB
    )


def dot(left, right, left_dim, right_dim):
    return lax.dot_general(
        left, right, (((left_dim,), (right_dim,)), ((), ())), preferred_element_type=jnp.float32
    )


def rows_at(begin, size):
    return pl.ds(pl.multiple_of(begin, 16), size)


CHUNK = 64
AHEAD = 3
CARRIED = 2
RING = 4
FIRST_CHUNKS = (CHUNK,) * 22
LAST_CHUNKS = (CHUNK,) * 16


class LineSum:
    def __init__(self, wires, own, out, landing, sizes, came=False, goes_on=False):
        self.wires, self.own, self.out, self.landing = wires, own, out, landing
        self.sizes, self.came, self.goes_on = sizes, came, goes_on
        self.all = len(sizes)
        self.chunks = self.all - (CARRIED if goes_on else 0)
        self.begun = CARRIED if came else 0
        self.now = self.begun
        self.first = wires.take(3 * self.all)
        z = wires.z
        self.inner = (z == 1) | (z == 2)
        self.outer = (z == 0) | (z == 3)
        self.end = 3 * (z - 1)
        self.near = 1 + z // 3
        self.peer = 3 - z

    def _row(self, chunk):
        return sum(self.sizes[:chunk])

    def _cut(self, ref, chunk):
        return ref.at[pl.ds(self._row(chunk), self.sizes[chunk])]

    def _slot(self, chunk):
        return chunk % RING * CHUNK

    def _in(self, chunk):
        return self.wires.copy(
            self._cut(self.own, chunk), self._cut(self.out, chunk), self.first + chunk, z=self.near
        )

    def _across(self, chunk):
        landed = self.landing.at[pl.ds(self._slot(chunk), self.sizes[chunk])]
        return self.wires.copy(
            self._cut(self.own, chunk), landed, self.first + self.all + chunk, z=self.peer
        )

    def _back(self, chunk, ref=None):
        number = self.first + 2 * self.all + chunk
        return self.wires.copy(
            self._cut(self.out if ref is None else ref, chunk), self._cut(self.out, chunk), number, z=self.end
        )

    def begin(self):
        @pl.when(self.outer)
        def _():
            for chunk in range(self.begun, min(self.begun + AHEAD, self.all)):
                self._in(chunk).start()

        if self.came:

            @pl.when(self.inner)
            def _():
                self._across(1).start()
                self._back(0, self.own).start()
                self.out[pl.ds(0, self.sizes[0]), :] = self.own[pl.ds(0, self.sizes[0]), :]

    def tick(self, count=1):
        for _ in range(count):
            if self.now < self.all + (0 if self.goes_on else 1):
                self._tick(self.now)
            self.now += 1

    def _tick(self, chunk):
        if chunk < self.all:

            @pl.when(self.outer)
            def _():
                self._in(chunk).wait_send()
                if chunk + AHEAD < self.all:
                    self._in(chunk + AHEAD).start()

        @pl.when(self.inner)
        def _():
            if chunk < self.all:
                row = self._row(chunk)
                self._in(chunk).wait_recv()
                add_rows(self.own, row, self.own, row, self.out, row, self.sizes[chunk])
                if chunk <= self.chunks:
                    self._across(chunk).start()
            if chunk >= 1:
                last = chunk - 1
                row, landed, rows = self._row(last), self._slot(last), self.sizes[last]
                self._across(last).wait_recv()
                if last < self.chunks:
                    add_rows(self.out, row, self.own, row, self.landing, landed, rows)
                    self._back(last).start()
                else:
                    self._across(last).wait_send()
                    add_rows(self.own, row, self.own, row, self.landing, landed, rows)

    def finish(self):
        self.tick(max(0, self.all + (0 if self.goes_on else 1) - self.now))

        @pl.when(self.outer)
        def _():
            for chunk in range(self.chunks):
                self._back(chunk).wait_recv()

        @pl.when(self.inner)
        def _():
            for chunk in range(1 if self.came else 0, self.chunks):
                self._across(chunk).wait_send()
            for chunk in range(self.chunks):
                self._back(chunk).wait_send()


def norm_back(values, gain, grad):
    scale = lax.rsqrt(jnp.mean(values * values, axis=-1, keepdims=True) + epsilon)
    normal = values * scale
    inner = grad * gain
    to_values = scale * (inner - normal * jnp.mean(inner * normal, axis=-1, keepdims=True))
    return to_values, grad * normal


def turned(values, cosine, sine):
    return values * cosine + pltpu.roll(values, HD // 2, 1) * sine


def up_to_attention_back(
    w_query, w_key, w_value, gains, w_out, tokens, cotangent, gates, w_gate, w_up, w_down, starts, cosine, sine
):
    rows, width = w_query.shape
    key_width = w_key.shape[1]
    kv_width = key_width + w_value.shape[1]
    tok_rows = tokens.shape[0]
    keys = LINE * tok_rows
    planes = 8
    group = LINE * rows
    hidden_width = w_gate.shape[1]
    total_rows = planes * tok_rows
    sum_rows = width + hidden_width
    sent_rows, done_rows = sum(FIRST_CHUNKS), sum(FIRST_CHUNKS[:-CARRIED])
    score_scale = HD ** (-0.5)
    per_group = HEADS // KVH
    q_width = HEADS * HD

    def kernel(
        wq_ref, wk_ref, wv_ref, gains_ref, wo_ref, tok_hbm, cot_hbm, gate_ref, wg_ref, wu_ref, wd_ref, starts_ref, cos_ref,
        sin_ref,
        out_q, out_kv, out_o, query_hbm, mixed_hbm, normed_hbm, middle_hbm, gain_rows_ref, sums_ref, prod_ref, total_ref,
        grad_mid_hbm, grad_pre_ref, gain_row_ref, w_out_ref,
        w_in, w_down, x_all, y_all, hidden, grad_hidden, grad_in, sums, sums_land, all_gate, gate_t, all_kv, lse_ref,
        core_in, first_in, second_in, middle_ref, kv_land, here, there, freed, send, recv,
    ):
        wires = Wires(send, recv)
        dp, z = wires.dp, wires.z

        def rows_begin(block):
            return pl.multiple_of(block * tok_rows, 16)

        def cut_of(block):
            return pl.ds(rows_begin(block), tok_rows)

        def gate_rows(block):
            return pl.ds(pl.multiple_of(block * planes, planes), planes)

        full_q = w_in
        full_kv = hidden.at[pl.ds(0, width), pl.ds(0, kv_width + LANES)]
        full_o = sums.at[pl.ds(0, width)]
        all_cot = y_all
        query_ref, mixed_ref, tok_ref, normed_ref, cot_ref = [
            grad_in.at[pl.ds(i * tok_rows, tok_rows)] for i in range(5)
        ]
        value_t = key_t = grad_in.at[pl.ds(5 * tok_rows, kv_width // 2), pl.ds(0, keys)]
        bias = grad_hidden.at[pl.ds(keys, keys), pl.ds(0, tok_rows)]
        full_o_ref = w_in
        part_o = y_all.at[pl.ds(0, width)]
        attn_low, mixed_grad = tok_ref, normed_ref
        kv_part = hidden.at[pl.ds(keys, keys), pl.ds(0, kv_width)]
        kv_grad = grad_hidden.at[pl.ds(0, keys), pl.ds(0, kv_width)]
        kv_out = grad_hidden.at[pl.ds(keys, tok_rows), pl.ds(tok_rows, kv_width)]

        own = rows_at((dp * LINE + z) * rows, rows)
        moves = [
            (wk_ref, full_kv.at[own, pl.ds(0, key_width)]),
            (wv_ref, full_kv.at[own, pl.ds(key_width, kv_width - key_width)]),
            (gains_ref, full_kv.at[own, pl.ds(kv_width, LANES)]),
            (cot_hbm, all_cot.at[cut_of(dp)]),
            (gate_ref, all_gate.at[gate_rows(dp)]),
            (wq_ref, full_q.at[own]),
            (wo_ref, full_o.at[own]),
            (tok_hbm, tok_ref),
            (wd_ref, w_down),
            (wg_ref, w_in.at[:, pl.ds(0, hidden_width)]),
            (wu_ref, w_in.at[:, pl.ds(hidden_width, hidden_width)]),
            (out_o, full_o_ref),
            (query_hbm, query_ref),
            (mixed_hbm, mixed_ref),
            (cot_hbm, cot_ref),
        ]
        moves = [pltpu.make_async_copy(a, b, here.at[i]) for i, (a, b) in enumerate(moves)]
        locals_, load_down, load_in, later = moves[:8], moves[8], moves[9:11], moves[11:]
        for one in locals_:
            one.start()
        load_down.start()
        greet(wires, range(1, planes), True)
        for one in locals_:
            one.wait()

        def block_rows(block):
            return rows_at((dp * LINE + block) * rows, rows)

        line_kv, line_q, line_o = [LineGather(wires, r, block_rows) for r in (full_kv, full_q, full_o)]
        plane_kv, plane_q, plane_o = [PlaneGather(wires, r, group) for r in (full_kv, full_q, full_o)]
        plane_cot = PlaneGather(wires, all_cot, tok_rows)
        line_keys = LineGather(wires, all_kv, lambda block: rows_at(block * tok_rows, tok_rows))
        spread = PlaneGather(wires, x_all, tok_rows)
        plane = PlaneReduce(
            wires, y_all, tok_rows, y_all, lambda slot: rows_begin(masked(dp, 2 * slot)), core_in, first_in, second_in,
            None,
        )
        summed = LineSum(wires, sums, total_ref, sums_land, FIRST_CHUNKS, goes_on=True)
        dense = PlaneReduce(
            wires, part_o, group, part_o, lambda slot: pl.multiple_of(masked(dp, 2 * slot) * group, 16),
            core_in, first_in, second_in, w_out_ref,
        )
        line = LineReduce(wires, kv_part, tok_rows, kv_land, ways=(-1,))
        first = wires.take(planes - 1)

        def gate_copy(mask, owner):
            part = all_gate.at[gate_rows(owner)]
            return wires.copy(part, part, first + mask - 1, dp=masked(dp, mask))

        def set_bias():
            key_place = lax.broadcasted_iota(jnp.int32, (keys, tok_rows), 0)
            query_place = lax.broadcasted_iota(jnp.int32, (keys, tok_rows), 1) + z * tok_rows
            allowed = (key_place >= starts_ref[0:1, :]) & (key_place <= query_place)
            bias[...] = jnp.where(allowed, 0.0, masked_score)

        line_kv.start(0)
        plane_cot.start(0)
        for mask in range(1, planes):
            gate_copy(mask, dp).start()
        line_kv.wait(0)
        line_kv.start(1)
        set_bias()
        line_kv.wait(1)
        line_kv.start(2)
        line_q.start(0)
        line_kv.wait(2)
        plane_kv.start(0)
        plane_cot.wait(0)
        line_q.wait(0)
        line_q.start(1)
        plane_kv.wait(0)
        plane_kv.start(1)
        plane_cot.start(1, far=False)
        line_q.wait(1)
        line_q.start(2)
        line_o.start(0)
        plane_kv.wait(1)
        plane_kv.start(2)
        plane_kv.wait(2)
        plane_kv.start(3)
        plane_kv.finish()
        line_q.wait(2)
        plane_q.start(0)

        gain_rows_ref[...] = full_kv[:, kv_width:].astype(jnp.float32).T[:8, :]
        tile = 32

        @pl.loop(0, tok_rows // tile)
        def _(step):
            cut = pl.ds(pl.multiple_of(step * tile, tile), tile)
            normed_ref[cut, :] = rms_norm(
                tok_ref[cut, :].astype(jnp.float32), gain_rows_ref[0:1, :]
            ).astype(jnp.bfloat16)

        own_keys = rows_at(z * tok_rows, tok_rows)
        pre = dot(normed_ref[...], full_kv[:, :kv_width], 1, 0)
        for pair in range(KVH):
            cut = slice(pair * HD, (pair + 1) * HD)
            all_kv[own_keys, cut] = turned(pre[:, cut], cos_ref[...], sin_ref[...]).astype(jnp.bfloat16)
        all_kv[own_keys, key_width:] = pre[:, key_width:].astype(jnp.bfloat16)
        line_keys.start(0)
        line_o.wait(0)
        line_o.start(1)
        plane_q.wait(0)
        plane_q.start(1)
        plane_cot.wait(1)
        plane_cot.start(2)
        line_keys.wait(0)
        line_keys.start(1)
        line_o.wait(1)
        line_o.start(2)
        line_keys.wait(1)
        line_keys.start(2)
        line_o.wait(2)
        plane_o.start(0)
        plane_q.wait(1)
        plane_q.start(2)
        plane_q.wait(2)
        plane_q.start(3)
        plane_q.finish()
        line_kv.finish()
        line_q.finish()
        saves = [
            (full_q, out_q),
            (full_kv, out_kv),
            (normed_ref, normed_hbm),
            (query_ref, query_hbm),
            (full_o, out_o),
            (mixed_ref, mixed_hbm),
            (middle_ref, middle_hbm),
        ]
        saves = [pltpu.make_async_copy(a, b, there.at[11 + i]) for i, (a, b) in enumerate(saves)]
        save_q, saves = saves[0], saves[1:]
        save_q.start()
        saves[0].start()
        saves[1].start()

        @pl.loop(0, HEADS // 2)
        def _(step):
            wide = pl.ds(pl.multiple_of(step * 2 * HD, 2 * HD), 2 * HD)
            pre_q = dot(normed_ref[...], full_q[:, wide], 1, 0)
            for one in range(2):
                query_ref[:, pl.ds(pl.multiple_of((2 * step + one) * HD, HD), HD)] = turned(
                    pre_q[:, one * HD : (one + 1) * HD], cos_ref[...], sin_ref[...]
                ).astype(jnp.bfloat16)

        saves[2].start()
        plane_o.wait(0)
        plane_o.start(1)
        save_q.wait()
        for one in load_in:
            one.start()
        line_keys.wait(2)
        value_t[...] = all_kv[:, key_width:].astype(jnp.float32).T.astype(jnp.bfloat16)
        lse_ref[...] = jnp.zeros_like(lse_ref)

        def attend(head):
            own_cut = pl.ds(pl.multiple_of(head * HD, HD), HD)
            key_cut = pl.ds(pl.multiple_of((head // per_group) * HD, HD), HD)
            scores = dot(all_kv[:, key_cut], query_ref[:, own_cut], 1, 1) * score_scale + bias[...]
            top = jnp.max(scores, axis=0, keepdims=True)
            expo = jnp.exp(scores - top)
            total = jnp.sum(expo, axis=0, keepdims=True)
            lse_ref[pl.ds(head, 1), :] = top + jnp.log(total)
            probs = (expo * (1.0 / total)).astype(jnp.bfloat16)
            mixed_ref[:, own_cut] = dot(value_t[key_cut, :], probs, 1, 0).T.astype(jnp.bfloat16)

        pl.loop(0, HEADS // 2)(attend)
        plane_cot.start_far()
        pl.loop(HEADS // 2, HEADS)(attend)
        plane_o.wait(1)
        plane_o.start(2)
        plane_o.wait(2)
        plane_o.start(3)
        plane_o.finish()
        line_o.finish()
        saves[3].start()
        saves[4].start()

        half_rows = tok_rows // 2
        for half in range(2):
            half_cut = pl.ds(half * half_rows, half_rows)

            @pl.loop(0, width // 512)
            def _(step):
                cut = pl.ds(pl.multiple_of(step * 512, 512), 512)
                middle_ref[half_cut, cut] = tok_ref[half_cut, cut].astype(jnp.float32) + dot(
                    mixed_ref[half_cut, :], full_o[:, cut], 1, 0
                )

            @pl.loop(0, half_rows // tile)
            def _(step):
                begin = half * half_rows + step * tile
                cut = pl.ds(pl.multiple_of(begin, tile), tile)
                x_all[pl.ds(pl.multiple_of(dp * tok_rows + begin, tile), tile), :] = rms_norm(
                    middle_ref[cut, :], gain_rows_ref[1:2, :]
                ).astype(jnp.bfloat16)

            spread.start_one(half)
        spread.start_one(2)
        saves[5].start()
        plane_cot.wait(2)
        plane_cot.start(3)
        plane_cot.finish()
        for mask in range(1, planes):
            gate_copy(mask, masked(dp, mask)).wait_recv()
        gate_t[...] = all_gate[...].T

        def gate_of(block):
            lane = lax.broadcasted_iota(jnp.int32, gate_t.shape, 1)
            return jnp.sum(jnp.where(lane == block * 8 + dp, gate_t[...], 0.0), axis=1, keepdims=True)

        def back_hidden(block):
            cut = cut_of(block)
            y_all[cut, :] = (y_all[cut, :].astype(jnp.float32) * gate_of(block)).astype(jnp.bfloat16)
            grad_hidden[cut, :] = dot(y_all[cut, :], w_down[...], 1, 1)

        def through(mask):
            cut = cut_of(masked(dp, mask))
            acts = dot(x_all[cut, :], w_in[...], 1, 0)
            gate_act, up_act = acts[:, :hidden_width], acts[:, hidden_width:]
            share = jax.nn.sigmoid(gate_act)
            silu = gate_act * share
            hidden[cut, :] = (silu * up_act).astype(jnp.bfloat16)
            grad = grad_hidden[cut, :]
            grad_in[cut, :hidden_width] = (
                grad * up_act * share * (1.0 + gate_act * (1.0 - share))
            ).astype(jnp.bfloat16)
            grad_in[cut, hidden_width:] = (grad * silu).astype(jnp.bfloat16)

        load_down.wait()
        pl.loop(0, 4)(back_hidden)
        spread.wait(0)
        spread.start(1)
        pl.loop(4, 8)(back_hidden)
        for one in load_in + saves:
            one.wait()
        through(0)
        spread.wait_core(0)
        through(1)
        spread.wait(1)
        spread.start(2)
        through(2)
        through(4)
        spread.wait_core(1)
        spread.wait_core(2)
        through(3)
        through(5)
        spread.wait(2)
        spread.start(3)
        through(6)
        spread.wait_core(3)
        through(7)

        def weights_down(step):
            cut = rows_at(step * 256, 256)
            sums[cut, :] = dot(hidden[:, cut], y_all[...], 0, 0).astype(jnp.bfloat16)

        def weights_in(step):
            cut = rows_at(step * 256, 256)
            out = rows_at(hidden_width + step * 256, 256)
            sums[out, :] = dot(x_all[:, cut], grad_in[...], 0, 0).astype(jnp.bfloat16)

        def save_sums(begin, end, number):
            rows = pl.ds(begin, end - begin)
            return pltpu.make_async_copy(sums.at[rows], sums_ref.at[rows], there.at[number])

        pl.loop(0, 1)(weights_down)
        summed.begin()
        pl.loop(1, 3)(weights_down)
        spread.finish()

        def input_grads(side):
            for slot in (3, 2, 1, 0):
                cut = cut_of(masked(dp, 2 * slot + side))
                y_all[cut, :] = dot(grad_in[cut, :], w_in[...], 1, 1).astype(jnp.bfloat16)
                if side:
                    plane.start_core(slot)

        input_grads(1)
        summed.tick()
        input_grads(0)
        summed.tick()
        later[0].start()
        plane.step(1)
        plane.step(2)
        summed.tick()
        pl.loop(0, 2)(weights_in)
        summed.tick()
        pl.loop(2, 4)(weights_in)
        summed.tick()
        plane.step(3)
        pl.loop(4, 6)(weights_in)
        summed.tick()
        for one in later[1:]:
            one.start()
        save = save_sums(sent_rows, sum_rows, 0)
        save.start()

        def save_made(block):
            return pltpu.make_async_copy(
                x_all.at[cut_of(block)], prod_ref.at[cut_of(block)], there.at[3 + block]
            )

        def make(block):
            made = dot(hidden[cut_of(block), :], w_down[...], 1, 0).astype(jnp.bfloat16).astype(jnp.float32)
            x_all[cut_of(block), :] = (made * gate_of(block)).astype(jnp.bfloat16)
            save_made(block).start()

        pl.loop(0, 4)(make)
        summed.tick()
        pl.loop(4, 8)(make)
        plane.step(4)
        summed.tick()
        set_bias()
        kv_grad[...] = jnp.zeros_like(kv_grad)
        gain_row_ref[...] = jnp.zeros_like(gain_row_ref)
        for one in later:
            one.wait()
        key_t[...] = all_kv[:, : kv_width // 2].astype(jnp.float32).T.astype(jnp.bfloat16)
        summed.tick()
        plane.step(5)

        tile = 32

        @pl.loop(0, tok_rows // tile)
        def _(step):
            cut = pl.ds(pl.multiple_of(step * tile, tile), tile)
            routed_grad = core_in[cut, :].astype(jnp.float32) + second_in[cut, :].astype(jnp.float32)
            to_middle, terms = norm_back(middle_ref[cut, :], gain_rows_ref[1:2, :], routed_grad)
            to_middle = cot_ref[cut, :].astype(jnp.float32) + to_middle
            middle_ref[cut, :] = to_middle
            attn_low[cut, :] = to_middle.astype(jnp.bfloat16)
            gain_row_ref[0:1, :] += jnp.sum(terms, axis=0, keepdims=True)

        for mask in (1, 2, 4):
            pl.semaphore_signal(freed, inc=1, device_id=(masked(dp, mask), z), device_id_type=MESH)
        save_mid = pltpu.make_async_copy(middle_ref, grad_mid_hbm, there.at[1])
        save_mid.start()
        summed.tick()
        wide = 512

        @pl.loop(0, width // wide)
        def _(step):
            cut = pl.ds(pl.multiple_of(step * wide, wide), wide)
            mixed_grad[:, cut] = dot(attn_low[...], full_o_ref[cut, :], 1, 1).astype(jnp.bfloat16)

        @pl.loop(0, width // 256)
        def _(step):
            cut = pl.ds(pl.multiple_of(step * 256, 256), 256)
            part_o[cut, :] = dot(mixed_ref[:, cut], attn_low[...], 0, 0).astype(jnp.bfloat16)

        pl.semaphore_wait(freed, 3)
        dense.step(0)
        summed.tick()

        def heads(first, last):
            @pl.loop(first, last)
            def _(head):
                own_cut = pl.ds(pl.multiple_of(head * HD, HD), HD)
                pair = head // per_group
                key_cut = pl.ds(pl.multiple_of(pair * HD, HD), HD)
                value_cut = pl.ds(pl.multiple_of((KVH + pair) * HD, HD), HD)
                q, do = query_ref[:, own_cut], mixed_grad[:, own_cut]
                k, v = all_kv[:, key_cut], all_kv[:, value_cut]
                scores = dot(k, q, 1, 1) * score_scale + bias[...]
                probs = jnp.exp(scores - lse_ref[pl.ds(head, 1), :])
                grad_probs = dot(v, do, 1, 1)
                inner = jnp.sum(probs * grad_probs, axis=0, keepdims=True)
                grad_raw = (probs * (grad_probs - inner) * score_scale).astype(jnp.bfloat16)
                kv_grad[:, value_cut] += dot(probs.astype(jnp.bfloat16), do, 1, 0)
                kv_grad[:, key_cut] += dot(grad_raw, q, 1, 0)
                to_query = dot(key_t[key_cut, :], grad_raw, 1, 0).T
                grad_pre_ref[:, own_cut] = turned(to_query, cos_ref[...], -sin_ref[...]).astype(
                    jnp.bfloat16
                )

        heads(0, 3)
        summed.tick()
        dense.step(1)
        dense.step(2)
        heads(3, 6)
        summed.tick()
        heads(6, 9)
        summed.tick()
        heads(9, 12)
        kv_part[...] = kv_grad[...].astype(jnp.bfloat16)
        line.begin()
        summed.tick()
        dense.step(3)
        summed.tick()
        line.event(0)
        summed.tick()
        dense.step(4)
        line.event(1)
        line.event(2)
        summed.tick()
        line.event(3)
        line.event(4)
        dense.step(5)
        summed.tick(max(0, summed.all - summed.now))
        save_last = save_sums(done_rows, sent_rows, 2)
        save_last.start()
        line.event(5)
        line.finish((kv_out,))
        for pair in range(KVH):
            cut = slice(pair * HD, (pair + 1) * HD)
            grad_pre_ref[:, q_width + pair * HD : q_width + (pair + 1) * HD] = turned(
                kv_out[:, cut], cos_ref[...], -sin_ref[...]
            ).astype(jnp.bfloat16)
        grad_pre_ref[:, q_width + kv_width // 2 :] = kv_out[:, kv_width // 2 :].astype(jnp.bfloat16)
        summed.finish()
        for block in range(8):
            save_made(block).wait()
        for one in (save, save_mid, save_last):
            one.wait()
        line_keys.finish()
        for mask in range(1, planes):
            gate_copy(mask, dp).wait_send()

    f32, low = jnp.float32, jnp.bfloat16
    copies = 4 * LineGather.COPIES + 5 * PlaneGather.COPIES + planes - 1
    copies += 2 * PlaneReduce.COPIES + 3 * len(FIRST_CHUNKS) + LineReduce.COPIES
    return pl.pallas_call(
        kernel,
        out_shape=(
            jax.ShapeDtypeStruct((width, width), low),
            jax.ShapeDtypeStruct((width, kv_width + LANES), low),
            jax.ShapeDtypeStruct((width, width), low),
            jax.ShapeDtypeStruct((tok_rows, width), low),
            jax.ShapeDtypeStruct((tok_rows, width), low),
            jax.ShapeDtypeStruct((tok_rows, width), low),
            jax.ShapeDtypeStruct((tok_rows, width), f32),
            jax.ShapeDtypeStruct((8, width), f32),
            jax.ShapeDtypeStruct((sum_rows, width), low),
            jax.ShapeDtypeStruct((total_rows, width), low),
            jax.ShapeDtypeStruct((sent_rows, width), low),
            jax.ShapeDtypeStruct((tok_rows, width), f32),
            jax.ShapeDtypeStruct((tok_rows, width + kv_width), low),
            jax.ShapeDtypeStruct((8, width), f32),
            jax.ShapeDtypeStruct((group, width), low),
        ),
        in_specs=[ANY] * 11 + [VMEM] * 3,
        out_specs=(ANY,) * 7 + (VMEM, ANY, ANY, VMEM, ANY, VMEM, VMEM, VMEM),
        scratch_shapes=[
            pltpu.VMEM((width, 2 * hidden_width), low),
            pltpu.VMEM((hidden_width, width), low),
            pltpu.VMEM((total_rows, width), low),
            pltpu.VMEM((total_rows, width), low),
            pltpu.VMEM((total_rows, hidden_width), low),
            pltpu.VMEM((total_rows, hidden_width), f32),
            pltpu.VMEM((total_rows, 2 * hidden_width), low),
            pltpu.VMEM((sum_rows, width), low),
            pltpu.VMEM((RING * CHUNK, width), low),
            pltpu.VMEM((planes * planes, tok_rows), f32),
            pltpu.VMEM((tok_rows, planes * planes), f32),
            pltpu.VMEM((keys, kv_width), low),
            pltpu.VMEM((16, tok_rows), f32),
        ]
        + PlaneReduce.scratch(tok_rows, width)
        + [
            pltpu.VMEM((tok_rows, width), f32),
            LineReduce.scratch(tok_rows, kv_width, 1),
            pltpu.SemaphoreType.DMA((15,)),
            pltpu.SemaphoreType.DMA((18,)),
            pltpu.SemaphoreType.REGULAR,
        ]
        + sems(copies),
        compiler_params=kernel_params(1, 63),
        name="up_to_attention_back",
    )(
        w_query, w_key, w_value, gains, w_out, tokens, cotangent, gates, w_gate, w_up, w_down, starts, cosine, sine
    )


def back_dense(sums_in, produced, full_q, full_kv, normed, grad_pre, tokens, gains, grad_mid, gain_row, w_out_part, middle):
    tok_rows, width = middle.shape
    q_width = full_q.shape[1]
    in_width = q_width + full_kv.shape[1]
    pre_width = in_width - LANES
    w_rows = width
    group, rows = w_rows // 8, w_rows // (8 * LINE)
    skipped, sum_rows = sum(FIRST_CHUNKS[:-CARRIED]), sum(LAST_CHUNKS)

    def kernel(
        sums_ref, prod_ref, full_q_hbm, full_kv_hbm, normed_hbm, pre_hbm, tok_hbm, gain_ref, mid_grad_hbm,
        gain_row_ref, o_part_hbm, middle_hbm,
        total_ref, layer_ref, tok_grad_ref, wq_ref, wk_ref, wv_ref, gains_ref, out_ref,
        sums_own, sums_land, full_q_ref, full_kv_ref, normed_ref, pre_ref, tok_ref, mid_grad_ref, middle_ref, own, core_in, first_in, second_in, moe, part, d_core, d_first, d_second, in_sums,
        in_land, o_sums, o_land, normed_grad, gain_rows, here, send, recv,
    ):
        wires = Wires(send, recv)
        dp, z = wires.dp, wires.z
        early = (CARRIED + AHEAD) * CHUNK
        loads = [
            pltpu.make_async_copy(sums_ref.at[pl.ds(skipped, early)], sums_own.at[pl.ds(0, early)], here.at[0]),
            pltpu.make_async_copy(
                sums_ref.at[pl.ds(skipped + early, sum_rows - early)],
                sums_own.at[pl.ds(early, sum_rows - early)],
                here.at[1],
            ),
            pltpu.make_async_copy(o_part_hbm, o_sums, here.at[2]),
            pltpu.make_async_copy(pre_hbm, pre_ref, here.at[3]),
            pltpu.make_async_copy(full_q_hbm, full_q_ref, here.at[4]),
            pltpu.make_async_copy(full_kv_hbm, full_kv_ref, here.at[5]),
            pltpu.make_async_copy(tok_hbm, tok_ref, here.at[6]),
            pltpu.make_async_copy(mid_grad_hbm, mid_grad_ref, here.at[7]),
            pltpu.make_async_copy(normed_hbm, normed_ref, here.at[8]),
            pltpu.make_async_copy(middle_hbm, middle_ref, here.at[9]),
        ]
        first_loads = len(loads)
        for slot in range(4):
            row = pl.multiple_of(masked(dp, 2 * slot) * tok_rows, 16)
            loads.append(
                pltpu.make_async_copy(
                    prod_ref.at[pl.ds(row, tok_rows)],
                    own.at[pl.ds(slot * tok_rows, tok_rows)],
                    here.at[first_loads + slot],
                )
            )
        for one in loads:
            one.start()
        greet(wires, (1, 2, 4), True)
        summed = LineSum(wires, sums_own, total_ref, sums_land, LAST_CHUNKS, came=True)
        dense = PlaneReduce(
            wires, part, group, part, lambda slot: pl.multiple_of(masked(dp, 2 * slot) * group, 16),
            d_core, d_first, d_second, in_sums,
        )
        plane = PlaneReduce(
            wires, prod_ref, tok_rows, own, lambda slot: slot * tok_rows, core_in, first_in, second_in, moe
        )
        o_line = LineReduce(wires, o_sums, rows, o_land)
        in_line = LineReduce(wires, in_sums, rows, in_land)
        loads[0].wait()
        summed.begin()
        loads[1].wait()
        loads[2].wait()
        o_line.begin()
        for one in loads[3:first_loads]:
            one.wait()
        wide = 512

        @pl.loop(0, width // wide)
        def _(step):
            cut = pl.ds(pl.multiple_of(step * wide, wide), wide)
            normed_grad[:, cut] = dot(pre_ref[:, :q_width], full_q_ref[cut, :], 1, 1) + dot(
                pre_ref[:, q_width:], full_kv_ref[cut, : pre_width - q_width], 1, 1
            )

        summed.tick()
        gain_rows[...] = jnp.zeros_like(gain_rows)
        gain_rows[1:2, :] = gain_row_ref[0:1, :]
        tile = 32

        @pl.loop(0, tok_rows // tile)
        def _(step):
            cut = pl.ds(pl.multiple_of(step * tile, tile), tile)
            to_tokens, terms = norm_back(
                tok_ref[cut, :].astype(jnp.float32), gain_ref[0:1, :], normed_grad[cut, :]
            )
            tok_grad_ref[cut, :] = mid_grad_ref[cut, :] + to_tokens
            gain_rows[0:1, :] += jnp.sum(terms, axis=0, keepdims=True)

        summed.tick()
        o_line.event(0)
        part[:, pre_width:] = gain_rows[...].T.astype(jnp.bfloat16)

        @pl.loop(0, w_rows // 256)
        def _(step):
            cut = pl.ds(pl.multiple_of(step * 256, 256), 256)
            part[cut, :pre_width] = dot(normed_ref[:, cut], pre_ref[...], 0, 0).astype(jnp.bfloat16)

        dense.step(0)
        o_line.event(1)
        o_line.event(2)
        summed.tick(2)
        dense.step(1)
        o_line.event(3)
        summed.tick()
        dense.step(2)
        o_line.event(4)
        summed.tick()
        o_line.event(5)
        for one in loads[first_loads:]:
            one.wait()
        plane.step(0)
        summed.tick(2)
        plane.step(1)
        summed.tick()
        dense.step(3)
        plane.step(2)
        summed.tick(2)
        dense.step(4)
        dense.step(5)
        in_line.begin()
        summed.tick()
        in_line.event(0)
        summed.tick()
        plane.step(3)
        in_line.event(1)
        in_line.event(2)
        summed.tick(2)
        in_line.event(3)
        in_line.event(4)
        plane.step(4)
        summed.tick(2)
        in_line.event(5)
        plane.step(5)
        summed.tick(2)

        @pl.loop(0, tok_rows // tile)
        def _(step):
            cut = pl.ds(pl.multiple_of(step * tile, tile), tile)
            layer_ref[cut, :] = (middle_ref[cut, :] + moe[cut, :]).astype(jnp.bfloat16)

        o_line.finish((out_ref,))
        in_line.finish((wq_ref, wk_ref, wv_ref, gains_ref))
        summed.finish()

    f32, low = jnp.float32, jnp.bfloat16
    return pl.pallas_call(
        kernel,
        out_shape=(
            jax.ShapeDtypeStruct((sum_rows, width), low),
            jax.ShapeDtypeStruct((tok_rows, width), low),
            jax.ShapeDtypeStruct((tok_rows, width), f32),
            jax.ShapeDtypeStruct((rows, q_width), f32),
            jax.ShapeDtypeStruct((rows, (pre_width - q_width) // 2), f32),
            jax.ShapeDtypeStruct((rows, (pre_width - q_width) // 2), f32),
            jax.ShapeDtypeStruct((rows, LANES), f32),
            jax.ShapeDtypeStruct((rows, width), f32),
        ),
        in_specs=[ANY] * 7 + [VMEM, ANY, VMEM, ANY, ANY],
        out_specs=(VMEM,) * 8,
        scratch_shapes=[
            pltpu.VMEM((sum_rows, width), low),
            pltpu.VMEM((RING * CHUNK, width), low),
            pltpu.VMEM(full_q.shape, low),
            pltpu.VMEM(full_kv.shape, low),
            pltpu.VMEM((tok_rows, width), low),
            pltpu.VMEM((tok_rows, pre_width), low),
            pltpu.VMEM((tok_rows, width), low),
            pltpu.VMEM((tok_rows, width), f32),
            pltpu.VMEM((tok_rows, width), f32),
            pltpu.VMEM((4 * tok_rows, width), low),
        ]
        + PlaneReduce.scratch(tok_rows, width)
        + [pltpu.VMEM((tok_rows, width), f32), pltpu.VMEM((w_rows, in_width), low)]
        + PlaneReduce.scratch(group, in_width)
        + [
            pltpu.VMEM((group, in_width), low),
            LineReduce.scratch(rows, in_width),
            pltpu.VMEM((group, width), low),
            LineReduce.scratch(rows, width),
            pltpu.VMEM((tok_rows, width), f32),
            pltpu.VMEM((LANES, width), f32),
            pltpu.SemaphoreType.DMA((14,)),
        ]
        + sems(3 * len(LAST_CHUNKS) + 2 * PlaneReduce.COPIES + 2 * LineReduce.COPIES),
        compiler_params=kernel_params(4, 63),
        name="back_dense",
    )(
        sums_in, produced, full_q, full_kv, normed, grad_pre, tokens, gains, grad_mid, gain_row, w_out_part, middle
    )


def hand_over(sums_head, sums_tail, gains, *others):
    done, width = sum(FIRST_CHUNKS[:-CARRIED]), sums_head.shape[1]
    hidden_width = width // 2
    rows = 256
    head_steps, tail_steps = done // rows, sums_tail.shape[0] // rows
    down_steps = hidden_width // rows
    steps = head_steps + tail_steps
    count = len(others)

    def kernel(*refs):
        head_ref, tail_ref, gains_ref = refs[:3]
        down_ref, gate_ref, up_ref, attn_ref, moe_ref = refs[3 + count : 8 + count]
        step = pl.program_id(0)
        for source, target in zip(refs[3 : 3 + count], refs[8 + count :]):
            target[...] = source[...]

        @pl.when(step == 0)
        def _():
            turned_gains = gains_ref[...].T
            attn_ref[...] = turned_gains[0, :]
            moe_ref[...] = turned_gains[1, :]

        def put(values):
            @pl.when(step < down_steps)
            def _():
                down_ref[0] = values

            @pl.when(step >= down_steps)
            def _():
                gate_ref[0] = values[:, :hidden_width]
                up_ref[0] = values[:, hidden_width:]

        @pl.when(step < head_steps)
        def _():
            put(head_ref[...].astype(jnp.float32))

        @pl.when(step >= head_steps)
        def _():
            put(tail_ref[...].astype(jnp.float32))

    def by_rows(one):
        if one.shape[0] % (8 * 16):
            return pl.BlockSpec(one.shape, lambda i: (0, 0))
        return pl.BlockSpec((one.shape[0] // 8, one.shape[1]), lambda i: (jnp.minimum(i, 7), 0))

    f32 = jnp.float32
    in_shape = (1, rows, hidden_width)
    copied = [by_rows(one) for one in others]
    return pl.pallas_call(
        kernel,
        grid=(steps,),
        out_shape=(
            jax.ShapeDtypeStruct((1, hidden_width, width), f32),
            jax.ShapeDtypeStruct((1, width, hidden_width), f32),
            jax.ShapeDtypeStruct((1, width, hidden_width), f32),
            jax.ShapeDtypeStruct((gains.shape[0],), f32),
            jax.ShapeDtypeStruct((gains.shape[0],), f32),
        )
        + tuple(jax.ShapeDtypeStruct(one.shape, one.dtype) for one in others),
        in_specs=[
            pl.BlockSpec((rows, width), lambda i: (jnp.minimum(i, head_steps - 1), 0)),
            pl.BlockSpec((rows, width), lambda i: (jnp.maximum(i - head_steps, 0), 0)),
            pl.BlockSpec(gains.shape, lambda i: (0, 0)),
        ]
        + copied,
        out_specs=(
            pl.BlockSpec((1, rows, width), lambda i: (0, jnp.minimum(i, down_steps - 1), 0)),
            pl.BlockSpec(in_shape, lambda i: (0, jnp.maximum(i - down_steps, 0), 0)),
            pl.BlockSpec(in_shape, lambda i: (0, jnp.maximum(i - down_steps, 0), 0)),
            pl.BlockSpec((gains.shape[0],), lambda i: (0,)),
            pl.BlockSpec((gains.shape[0],), lambda i: (0,)),
        )
        + tuple(copied),
        compiler_params=pltpu.CompilerParams(vmem_limit_bytes=63 * MIB),
        name="hand_over",
    )(sums_head, sums_tail, gains, *others)


def on_plane_device(
    tokens,
    norm_attn,
    w_query,
    w_key,
    w_value,
    w_out,
    norm_moe,
    w_gate,
    w_up,
    w_down,
    routes,
    gate_values,
    lengths,
    cotangent,
):
    tok_rows = tokens.shape[0]
    ctx_size = lax.axis_size("ctx")
    ctx_place = lax.axis_index("ctx")
    group_places = jnp.arange(tok_rows * ctx_size, dtype=jnp.int32)
    seg_all, within_all = seq_tables(lengths[0], group_places)
    offset = ctx_place * tok_rows
    own_places = offset + jnp.arange(tok_rows, dtype=jnp.int32)
    within_own = lax.dynamic_slice_in_dim(within_all, offset, tok_rows)
    kv_columns = KVH * HD
    q_columns = HEADS * HD
    gains = jnp.pad(jnp.stack([norm_attn, norm_moe], axis=1), ((0, 0), (0, LANES - 2)))
    numbers = jnp.arange(8, dtype=jnp.int32)
    gates = jnp.sum(
        jnp.where(routes[None, :, :] == numbers[:, None, None], gate_values[None], 0.0), axis=2
    )
    half_size = HD // 2
    frequency = rope_base ** (-jnp.arange(half_size, dtype=jnp.float32) / half_size)
    angles = within_own.astype(jnp.float32)[:, None] * frequency[None, :]
    cosine = jnp.concatenate([jnp.cos(angles), jnp.cos(angles)], axis=1)
    sine = jnp.concatenate([-jnp.sin(angles), jnp.sin(angles)], axis=1)
    starts = jnp.broadcast_to((own_places - within_own)[None, :], (8, tok_rows))
    (
        full_q, full_kv, _, _, _, normed_low, middle, gain_rows, partial_sums, produced, sums_head, grad_mid, grad_pre,
        gain_row, w_out_part,
    ) = up_to_attention_back(
        w_query, w_key, w_value, gains, w_out, tokens, cotangent, gates, w_gate[0], w_up[0], w_down[0], starts, cosine,
        sine,
    )
    sums_tail, layer_out, grad_tokens, sum_q, sum_k, sum_v, sum_gains, sum_o = back_dense(
        partial_sums,
        produced,
        full_q,
        full_kv,
        normed_low,
        grad_pre,
        tokens,
        gain_rows,
        grad_mid,
        gain_row,
        w_out_part,
        middle,
    )
    down, gate, up, gain_attn, gain_moe, layer_out, grad_tokens, sum_q, sum_k, sum_v, sum_o = hand_over(
        sums_head, sums_tail, sum_gains, layer_out, grad_tokens, sum_q, sum_k, sum_v, sum_o
    )
    return (
        layer_out, grad_tokens, gain_attn, sum_q, sum_k, sum_v, sum_o, gain_moe, gate, up, down,
    )


def solution(mesh):
    on_plane = mesh.shape["dp"] == 8 and mesh.shape["ctx"] == LINE
    return jax.shard_map(
        on_plane_device if on_plane else on_device,
        mesh=mesh,
        in_specs=(
            P(("dp", "ctx"), None),
            P(("dp", "ctx")),
            P(("dp", "ctx"), None),
            P(("dp", "ctx"), None),
            P(("dp", "ctx"), None),
            P(("dp", "ctx"), None),
            P(("dp", "ctx")),
            P("dp", None, None),
            P("dp", None, None),
            P("dp", None, None),
            P(("dp", "ctx"), None),
            P(("dp", "ctx"), None),
            P("dp", None),
            P(("dp", "ctx"), None),
        ),
        out_specs=(
            P(("dp", "ctx"), None),
            P(("dp", "ctx"), None),
            P(("dp", "ctx")),
            P(("dp", "ctx"), None),
            P(("dp", "ctx"), None),
            P(("dp", "ctx"), None),
            P(("dp", "ctx"), None),
            P(("dp", "ctx")),
            P("dp", None, None),
            P("dp", None, None),
            P("dp", None, None),
        ),
        check_vma=False,
    )
```

```python
import math

import jax
import jax.numpy as jnp
from jax import lax
from jax.experimental import pallas as pl
from jax.experimental.pallas import tpu as pltpu
from jax.sharding import PartitionSpec as P

D = 1536
HEADS = 12
KVH = 2
HD = 128
TOP = 4
EXP_DEV = 1


epsilon = 1e-06
rope_base = 1000000.0
masked_score = -1e30


def rms_norm(values, gain):
    return values * lax.rsqrt(jnp.mean(values * values, axis=-1, keepdims=True) + epsilon) * gain


def rotate(values, within, direction):
    half_size = values.shape[-1] // 2
    frequency = rope_base ** (-jnp.arange(half_size, dtype=jnp.float32) / half_size)
    angles = direction * within.astype(jnp.float32)[:, None] * frequency[None, :]
    cosine = jnp.cos(angles)[:, None, :]
    sine = jnp.sin(angles)[:, None, :]
    first_half = values[..., :half_size]
    second = values[..., half_size:]
    return jnp.concatenate(
        [first_half * cosine - second * sine, second * cosine + first_half * sine], axis=-1
    )


def seq_tables(length_row, places):
    seq_ends = jnp.cumsum(length_row)
    passed = places[:, None] >= seq_ends[None, :]
    segment = jnp.sum(passed.astype(jnp.int32), axis=1)
    within = places - jnp.sum(jnp.where(passed, length_row[None, :], 0), axis=1)
    return (segment, within)


def collect_weights(gain_attn, w_query, w_key, w_value, w_out, gain_moe):
    return (
        lax.all_gather(gain_attn, ("dp", "ctx"), axis=0, tiled=True),
        lax.all_gather(w_query, ("dp", "ctx"), axis=0, tiled=True),
        lax.all_gather(w_key, ("dp", "ctx"), axis=0, tiled=True),
        lax.all_gather(w_value, ("dp", "ctx"), axis=0, tiled=True),
        lax.all_gather(w_out, ("dp", "ctx"), axis=0, tiled=True),
        lax.all_gather(gain_moe, ("dp", "ctx"), axis=0, tiled=True),
    )


def spread_grads(grad_gain_attn, grad_query, grad_key, grad_value, grad_outp, grad_gain_moe):
    return (
        lax.psum_scatter(grad_gain_attn, ("dp", "ctx"), scatter_dimension=0, tiled=True),
        lax.psum_scatter(grad_query, ("dp", "ctx"), scatter_dimension=0, tiled=True),
        lax.psum_scatter(grad_key, ("dp", "ctx"), scatter_dimension=0, tiled=True),
        lax.psum_scatter(grad_value, ("dp", "ctx"), scatter_dimension=0, tiled=True),
        lax.psum_scatter(grad_outp, ("dp", "ctx"), scatter_dimension=0, tiled=True),
        lax.psum_scatter(grad_gain_moe, ("dp", "ctx"), scatter_dimension=0, tiled=True),
    )


def on_device(
    tokens,
    norm_attn,
    w_query,
    w_key,
    w_value,
    w_out,
    norm_moe,
    w_gate,
    w_up,
    w_down,
    routes,
    gate_values,
    lengths,
    cotangent,
):
    tok_rows = tokens.shape[0]
    ctx_size = lax.axis_size("ctx")
    dp_size = lax.axis_size("dp")
    ctx_place = lax.axis_index("ctx")
    group_rows = tok_rows * ctx_size
    group_places = jnp.arange(group_rows, dtype=jnp.int32)
    seg_all, within_all = seq_tables(lengths[0], group_places)
    offset = ctx_place * tok_rows
    own_places = offset + jnp.arange(tok_rows, dtype=jnp.int32)
    seg_own = lax.dynamic_slice_in_dim(seg_all, offset, tok_rows)
    within_own = lax.dynamic_slice_in_dim(within_all, offset, tok_rows)
    allowed = (seg_own[:, None] == seg_all[None, :]) & (
        group_places[None, :] <= own_places[:, None]
    )
    gain_attn, full_q, full_k, full_v, full_o, gain_moe = collect_weights(
        norm_attn, w_query, w_key, w_value, w_out, norm_moe
    )
    gain_attn_f = gain_attn.astype(jnp.float32)
    gain_moe_f = gain_moe.astype(jnp.float32)
    inputs = tokens.astype(jnp.float32)
    normed_low = rms_norm(inputs, gain_attn_f).astype(jnp.bfloat16)
    query_pre = jnp.dot(normed_low, full_q, preferred_element_type=jnp.float32)
    key_pre = jnp.dot(normed_low, full_k, preferred_element_type=jnp.float32)
    value_pre = jnp.dot(normed_low, full_v, preferred_element_type=jnp.float32)
    query = rotate(query_pre.reshape(tok_rows, HEADS, HD), within_own, 1.0).astype(jnp.bfloat16)
    key_low = rotate(key_pre.reshape(tok_rows, KVH, HD), within_own, 1.0).astype(jnp.bfloat16)
    key_low = key_low.reshape(tok_rows, KVH * HD)
    value_low = value_pre.astype(jnp.bfloat16)
    all_keys, all_values = (
        lax.all_gather(key_low, "ctx", axis=0, tiled=True),
        lax.all_gather(value_low, "ctx", axis=0, tiled=True),
    )
    per_group = HEADS // KVH
    score_scale = HD ** (-0.5)
    query_groups = query.reshape(tok_rows, KVH, per_group, HD)

    def softmax_weights(group_number):
        keys_part = all_keys[:, group_number * HD : (group_number + 1) * HD]
        raw = jnp.einsum(
            "qjd,kd->jqk",
            query_groups[:, group_number],
            keys_part,
            preferred_element_type=jnp.float32,
        )
        scores = jnp.where(allowed[None], raw * score_scale, masked_score)
        row_top = jnp.max(scores, axis=-1, keepdims=True)
        expo = jnp.exp(scores - row_top)
        return expo / jnp.sum(expo, axis=-1, keepdims=True)

    mixed_parts = []
    for group_number in range(KVH):
        probs = softmax_weights(group_number)
        values_part = all_values[:, group_number * HD : (group_number + 1) * HD]
        mixed_group = jnp.einsum(
            "jqk,kd->qjd",
            probs.astype(jnp.bfloat16),
            values_part,
            preferred_element_type=jnp.float32,
        )
        mixed_parts.append(mixed_group.reshape(tok_rows, per_group * HD))
    mixed_low = jnp.concatenate(mixed_parts, axis=1).astype(jnp.bfloat16)
    middle = inputs + jnp.dot(mixed_low, full_o, preferred_element_type=jnp.float32)
    routed_low = rms_norm(middle, gain_moe_f).astype(jnp.bfloat16)
    experts_total = EXP_DEV * dp_size
    capacity = 3 * TOP * tok_rows // (2 * experts_total)
    assign_count = tok_rows * TOP
    flat_ids = routes.reshape(assign_count)
    onehot = (flat_ids[:, None] == jnp.arange(experts_total, dtype=jnp.int32)[None, :]).astype(
        jnp.int32
    )
    earlier = jnp.sum((jnp.cumsum(onehot, axis=0) - onehot) * onehot, axis=1)
    slot_index = flat_ids * capacity + earlier
    owner = (
        jnp.full((experts_total * capacity,), assign_count, jnp.int32)
        .at[slot_index]
        .set(jnp.arange(assign_count, dtype=jnp.int32))
    )
    padded = jnp.concatenate([routed_low, jnp.zeros((1, D), jnp.bfloat16)], axis=0)
    outgoing = padded[owner // TOP].reshape(experts_total, capacity, D)
    arrived = lax.all_to_all(outgoing, "dp", split_axis=0, concat_axis=0, tiled=True)
    arrived_sets = arrived.reshape(dp_size, EXP_DEV, capacity, D)
    gate_act = jnp.einsum(
        "secd,edf->secf", arrived_sets, w_gate, preferred_element_type=jnp.float32
    )
    up_act = jnp.einsum("secd,edf->secf", arrived_sets, w_up, preferred_element_type=jnp.float32)
    hidden_low = (jax.nn.silu(gate_act) * up_act).astype(jnp.bfloat16)
    produced = jnp.einsum("secf,efd->secd", hidden_low, w_down, preferred_element_type=jnp.float32)
    produced = produced.astype(jnp.bfloat16).reshape(experts_total, capacity, D)
    returned = lax.all_to_all(produced, "dp", split_axis=0, concat_axis=0, tiled=True)
    picked = returned.reshape(experts_total * capacity, D)[slot_index].reshape(tok_rows, TOP, D)
    moe_out = jnp.sum(picked.astype(jnp.float32) * gate_values[:, :, None], axis=1)
    layer_out = (middle + moe_out).astype(jnp.bfloat16)
    grad_out = cotangent.astype(jnp.float32)
    grad_assign = (grad_out[:, None, :] * gate_values[:, :, None]).astype(jnp.bfloat16)
    grad_padded = jnp.concatenate(
        [grad_assign.reshape(assign_count, D), jnp.zeros((1, D), jnp.bfloat16)], axis=0
    )
    grad_slots = grad_padded[owner].reshape(experts_total, capacity, D)
    grad_arrived = lax.all_to_all(grad_slots, "dp", split_axis=0, concat_axis=0, tiled=True)
    grad_arrived = grad_arrived.reshape(dp_size, EXP_DEV, capacity, D)
    grad_hidden = jnp.einsum(
        "secd,efd->secf", grad_arrived, w_down, preferred_element_type=jnp.float32
    )
    grad_w_down = jnp.einsum(
        "secf,secd->efd", hidden_low, grad_arrived, preferred_element_type=jnp.float32
    )
    glu_value, glu_pull = jax.vjp(
        lambda gate_in, up_in: jax.nn.silu(gate_in) * up_in, gate_act, up_act
    )
    grad_gate, grad_up = glu_pull(grad_hidden)
    grad_gate_low = grad_gate.astype(jnp.bfloat16)
    grad_up_low = grad_up.astype(jnp.bfloat16)
    grad_w_gate = jnp.einsum(
        "secd,secf->edf", arrived_sets, grad_gate_low, preferred_element_type=jnp.float32
    )
    grad_w_up = jnp.einsum(
        "secd,secf->edf", arrived_sets, grad_up_low, preferred_element_type=jnp.float32
    )
    grad_sent = jnp.einsum(
        "secf,edf->secd", grad_gate_low, w_gate, preferred_element_type=jnp.float32
    ) + jnp.einsum("secf,edf->secd", grad_up_low, w_up, preferred_element_type=jnp.float32)
    grad_sent = grad_sent.astype(jnp.bfloat16).reshape(experts_total, capacity, D)
    grad_back = lax.all_to_all(grad_sent, "dp", split_axis=0, concat_axis=0, tiled=True)
    grad_picked = grad_back.reshape(experts_total * capacity, D)[slot_index].reshape(
        tok_rows, TOP, D
    )
    grad_routed = jnp.sum(grad_picked.astype(jnp.float32), axis=1)
    expert_sums = (
        lax.psum(grad_w_gate.astype(jnp.bfloat16), "ctx").astype(jnp.float32),
        lax.psum(grad_w_up.astype(jnp.bfloat16), "ctx").astype(jnp.float32),
        lax.psum(grad_w_down.astype(jnp.bfloat16), "ctx").astype(jnp.float32),
    )
    norm_value, moe_pull = jax.vjp(rms_norm, middle, gain_moe_f)
    grad_mid_norm, grad_gain_moe = moe_pull(grad_routed)
    grad_middle = grad_out + grad_mid_norm
    grad_attn_low = grad_middle.astype(jnp.bfloat16)
    grad_w_out = jnp.einsum(
        "th,td->hd", mixed_low, grad_attn_low, preferred_element_type=jnp.float32
    )
    grad_mixed_low = jnp.einsum(
        "td,hd->th", grad_attn_low, full_o, preferred_element_type=jnp.float32
    ).astype(jnp.bfloat16)
    grad_mixed_groups = grad_mixed_low.reshape(tok_rows, KVH, per_group, HD)
    grad_query_parts = []
    prob_parts = []
    score_parts = []
    for group_number in range(KVH):
        probs = softmax_weights(group_number)
        keys_part = all_keys[:, group_number * HD : (group_number + 1) * HD]
        values_part = all_values[:, group_number * HD : (group_number + 1) * HD]
        grad_probs = jnp.einsum(
            "qjd,kd->jqk",
            grad_mixed_groups[:, group_number],
            values_part,
            preferred_element_type=jnp.float32,
        )
        grad_scores = probs * (grad_probs - jnp.sum(probs * grad_probs, axis=-1, keepdims=True))
        grad_raw_low = (grad_scores * score_scale).astype(jnp.bfloat16)
        grad_query_parts.append(
            jnp.einsum("jqk,kd->qjd", grad_raw_low, keys_part, preferred_element_type=jnp.float32)
        )
        prob_parts.append(probs.astype(jnp.bfloat16))
        score_parts.append(grad_raw_low)
    grad_query_rot = jnp.stack(grad_query_parts, axis=1).reshape(tok_rows, HEADS, HD)
    key_pieces = []
    value_pieces = []
    for group_number in range(KVH):
        score_piece = score_parts[group_number]
        prob_piece = prob_parts[group_number]
        key_pieces.append(
            jnp.einsum(
                "jqk,qjd->kd",
                score_piece,
                query_groups[:, group_number],
                preferred_element_type=jnp.float32,
            )
        )
        value_pieces.append(
            jnp.einsum(
                "jqk,qjd->kd",
                prob_piece,
                grad_mixed_groups[:, group_number],
                preferred_element_type=jnp.float32,
            )
        )
    key_value_grads = lax.psum_scatter(
        jnp.concatenate(key_pieces + value_pieces, axis=1).astype(jnp.bfloat16),
        "ctx",
        scatter_dimension=0,
        tiled=True,
    ).astype(jnp.float32)
    grad_query_low = (
        rotate(grad_query_rot, within_own, -1.0).astype(jnp.bfloat16).reshape(tok_rows, HEADS * HD)
    )
    grad_key_rot = key_value_grads[:, : KVH * HD].reshape(tok_rows, KVH, HD)
    grad_key_low = (
        rotate(grad_key_rot, within_own, -1.0).astype(jnp.bfloat16).reshape(tok_rows, KVH * HD)
    )
    grad_value_low = key_value_grads[:, KVH * HD :].astype(jnp.bfloat16)
    grad_w_query = jnp.einsum(
        "td,th->dh", normed_low, grad_query_low, preferred_element_type=jnp.float32
    )
    grad_w_key = jnp.einsum(
        "td,th->dh", normed_low, grad_key_low, preferred_element_type=jnp.float32
    )
    grad_w_value = jnp.einsum(
        "td,th->dh", normed_low, grad_value_low, preferred_element_type=jnp.float32
    )
    grad_normed = (
        jnp.einsum("th,dh->td", grad_query_low, full_q, preferred_element_type=jnp.float32)
        + jnp.einsum("th,dh->td", grad_key_low, full_k, preferred_element_type=jnp.float32)
        + jnp.einsum("th,dh->td", grad_value_low, full_v, preferred_element_type=jnp.float32)
    )
    first_value, attn_pull = jax.vjp(rms_norm, inputs, gain_attn_f)
    grad_inputs, grad_gain_attn = attn_pull(grad_normed)
    grad_tokens = grad_middle + grad_inputs
    dense_sums = spread_grads(
        grad_gain_attn, grad_w_query, grad_w_key, grad_w_value, grad_w_out, grad_gain_moe
    )
    return (
        layer_out,
        grad_tokens,
        dense_sums[0],
        dense_sums[1],
        dense_sums[2],
        dense_sums[3],
        dense_sums[4],
        dense_sums[5],
        expert_sums[0],
        expert_sums[1],
        expert_sums[2],
    )


MESH = pl.DeviceIdType.MESH
LANES = 128
MIB = 2**20
ANY = pl.BlockSpec(memory_space=pl.ANY)
VMEM = pl.BlockSpec(memory_space=pltpu.VMEM)


def flip(index, bit):
    return index + bit - 2 * bit * ((index // bit) % 2)


def masked(index, mask):
    for bit in (1, 2, 4):
        if mask & bit:
            index = flip(index, bit)
    return index


class Wires:
    def __init__(self, send, recv):
        self.send, self.recv, self.used = send, recv, 0
        self.dp, self.z = lax.axis_index("dp"), lax.axis_index("ctx")

    def take(self, count):
        first = self.used
        self.used += count
        return first

    def copy(self, src, dst, number, dp=None, z=None):
        return pltpu.make_async_remote_copy(
            src_ref=src,
            dst_ref=dst,
            send_sem=self.send.at[number],
            recv_sem=self.recv.at[number],
            device_id=(self.dp if dp is None else dp, self.z if z is None else z),
            device_id_type=MESH,
        )


def greet(wires, masks, line):
    barrier = pltpu.get_barrier_semaphore()
    dp, z = wires.dp, wires.z
    for mask in masks:
        pl.semaphore_signal(barrier, inc=1, device_id=(masked(dp, mask), z), device_id_type=MESH)
    for step in range(1, LINE) if line else ():
        pl.semaphore_signal(
            barrier, inc=1, device_id=(dp, lax.rem(z + step, LINE)), device_id_type=MESH
        )
    pl.semaphore_wait(barrier, len(masks) + (LINE - 1 if line else 0))


LINE = 4


class LineGather:
    COPIES = 2 * (LINE - 1)

    def __init__(self, wires, ref, rows_of):
        self.wires, self.ref, self.rows_of = wires, ref, rows_of
        self.first = wires.take(self.COPIES)

    def _copy(self, block, number, z):
        part = self.ref.at[self.rows_of(block)]
        return self.wires.copy(part, part, self.first + number, z=z)

    def start(self, step):
        z = self.wires.z

        @pl.when((z >= step) & (z < LINE - 1))
        def _():
            self._copy(z - step, step, z + 1).start()

        @pl.when((z + step < LINE) & (z > 0))
        def _():
            self._copy(z + step, LINE - 1 + step, z - 1).start()

    def wait(self, step):
        z = self.wires.z

        @pl.when(z - 1 - step >= 0)
        def _():
            self._copy(z - 1 - step, step, z).wait_recv()

        @pl.when(z + 1 + step < LINE)
        def _():
            self._copy(z + 1 + step, LINE - 1 + step, z).wait_recv()

    def finish(self):
        z = self.wires.z
        for step in range(LINE - 1):

            @pl.when((z >= step) & (z < LINE - 1))
            def _():
                self._copy(z - step, step, z + 1).wait_send()

            @pl.when((z + step < LINE) & (z > 0))
            def _():
                self._copy(z + step, LINE - 1 + step, z - 1).wait_send()


class PlaneGather:
    CHIP = (((2, 0, 0), (4, 0, 1)), ((4, 0, 0), (2, 0, 1)), ((4, 2, 0), (2, 4, 1)))
    CORE = (
        ((1, 0, 2),),
        ((1, 2, 0), (1, 4, 1)),
        ((1, 4, 0), (1, 2, 1)),
        ((1, 6, 0), (1, 6, 1)),
    )
    COPIES = 13

    def __init__(self, wires, ref, group):
        self.wires, self.ref, self.group = wires, ref, group
        first = wires.take(self.COPIES)
        self.number = {}
        for stage in self.CHIP + self.CORE:
            for one in stage:
                self.number[one] = first + len(self.number)
        self.core_left = [0, 1, 2, 3]

    def _copy(self, one, from_me):
        to, whose, half = one
        dp = self.wires.dp
        sender = dp if from_me else masked(dp, to)
        owner = masked(sender, whose)
        size = self.group if half == 2 else self.group // 2
        begin = owner * self.group + (self.group // 2 if half == 1 else 0)
        part = self.ref.at[pl.ds(pl.multiple_of(begin, 16), size)]
        return self.wires.copy(part, part, self.number[one], dp=masked(dp, to))

    def start(self, stage, far=True):
        for one in (self.CHIP[stage] if stage < 2 else ()) + self.CORE[stage]:
            self._copy(one, True).start()
        if stage == 1 and far:
            self.start_far()

    def start_one(self, number):
        self._copy((self.CHIP[0] + self.CORE[0])[number], True).start()

    def start_far(self):
        for one in self.CHIP[2]:
            self._copy(one, True).start()

    def wait(self, stage):
        for one in self.CHIP[stage]:
            self._copy(one, False).wait_recv()

    def wait_core(self, stage):
        self.core_left.remove(stage)
        for one in self.CORE[stage]:
            self._copy(one, False).wait_recv()

    def finish(self):
        for stage in list(self.core_left):
            self.wait_core(stage)
        for one in self.number:
            self._copy(one, True).wait_send()


def add_rows(out, out_row, left, left_row, right, right_row, rows):
    @pl.loop(0, rows // 16)
    def _(step):
        def cut(row):
            return pl.ds(pl.multiple_of(row + step * 16, 16), 16)

        out[cut(out_row), :] = (
            left[cut(left_row), :].astype(jnp.float32) + right[cut(right_row), :].astype(jnp.float32)
        ).astype(out.dtype)


class PlaneReduce:
    COPIES = 10
    STEPS = 6

    def __init__(self, wires, part, group, own, own_row, core_in, first_in, second_in, out):
        self.wires, self.part, self.group, self.half = wires, part, group, group // 2
        self.own, self.own_row, self.out = own, own_row, out
        self.core_in, self.first_in, self.second_in = core_in, first_in, second_in
        self.first = wires.take(self.COPIES)

    def _send(self, src, src_row, dst, dst_row, rows, number, to):
        return self.wires.copy(
            src.at[pl.ds(src_row, rows)],
            dst.at[pl.ds(dst_row, rows)],
            self.first + number,
            dp=masked(self.wires.dp, to),
        )

    def _core(self, slot):
        row = pl.multiple_of(masked(self.wires.dp, 1 + 2 * slot) * self.group, 16)
        return self._send(self.part, row, self.core_in, slot * self.group, self.group, slot, 1)

    def _far(self, number):
        g, h = self.group, self.half
        src_row, dst, dst_row, to = (
            (3 * g, self.first_in, h, 4),
            (3 * g + h, self.first_in, 3 * h, 2),
            (2 * g, self.first_in, 0, 4),
            (1 * g + h, self.first_in, 2 * h, 2),
            (1 * g, self.second_in, 0, 2),
            (2 * g + h, self.second_in, h, 4),
        )[number]
        return self._send(self.core_in, src_row, dst, dst_row, h, 4 + number, to)

    def _sum_core(self, slot):
        self._core(slot).wait()
        row = slot * self.group
        add_rows(self.core_in, row, self.own, self.own_row(slot), self.core_in, row, self.group)

    def _sum_far(self, number, row, in_row):
        self._far(number).wait()
        add_rows(self.core_in, row, self.core_in, row, self.first_in, in_row, self.half)

    def start_core(self, slot):
        self._core(slot).start()

    def step(self, number):
        g, h = self.group, self.half
        if number == 0:
            for slot in (3, 2, 1, 0):
                self.start_core(slot)
        elif number == 1:
            self._sum_core(3)
            self._far(0).start()
            self._far(1).start()
        elif number == 2:
            self._sum_core(2)
            self._far(2).start()
            self._sum_core(1)
            self._far(3).start()
            self._sum_core(0)
        elif number == 3:
            self._sum_far(0, 1 * g, h)
            self._far(4).start()
            self._sum_far(1, 2 * g + h, 3 * h)
            self._far(5).start()
        elif number == 4:
            self._sum_far(2, 0, 0)
            self._sum_far(3, h, 2 * h)
        elif self.out is None:
            self._far(4).wait()
            self._far(5).wait()
        else:
            self._far(4).wait()
            add_rows(self.out, 0, self.core_in, 0, self.second_in, 0, h)
            self._far(5).wait()
            add_rows(self.out, h, self.core_in, h, self.second_in, h, h)

    @staticmethod
    def scratch(group, columns):
        return [
            pltpu.VMEM((4 * group, columns), jnp.bfloat16),
            pltpu.VMEM((2 * group, columns), jnp.bfloat16),
            pltpu.VMEM((group, columns), jnp.bfloat16),
        ]


class LineReduce:
    COPIES = 2 * (LINE - 1) * LINE
    EVENTS = ((0, 0), (0, 1), (1, 0), (0, 2), (1, 1), (2, 0))

    def __init__(self, wires, part, rows, landing, ways=(1, -1)):
        self.wires, self.part, self.rows, self.landing, self.ways = wires, part, rows, landing, ways
        self.first = wires.take(self.COPIES)

    def _place(self, way, hop, nearer):
        return (LINE - 1 - nearer, hop) if way == 1 else (nearer, LINE - 1 - hop)

    def _copy(self, way, hop, nearer, z):
        side = self.ways.index(way)
        block, _ = self._place(way, hop, nearer)
        return self.wires.copy(
            self.part.at[pl.ds(block * self.rows, self.rows)],
            self.landing.at[pl.ds((side * LINE + block) * self.rows, self.rows)],
            self.first + (side * (LINE - 1) + hop) * LINE + nearer,
            z=z,
        )

    def _send(self, way, hop, nearer):
        z = self.wires.z

        @pl.when(z == self._place(way, hop, nearer)[1])
        def _():
            self._copy(way, hop, nearer, z + way).start()

    def begin(self):
        for nearer in range(LINE - 1):
            for way in self.ways:
                self._send(way, 0, nearer)

    def event(self, number):
        hop, nearer = self.EVENTS[number]
        z, rows = self.wires.z, self.rows
        for way in self.ways:
            block, source = self._place(way, hop, nearer)

            @pl.when(z == source + way)
            def _():
                self._copy(way, hop, nearer, z).wait_recv()
                landed = (self.ways.index(way) * LINE + block) * rows
                add_rows(
                    self.part, block * rows, self.part, block * rows, self.landing, landed, rows
                )
                if nearer < LINE - 2 - hop:
                    self._copy(way, hop + 1, nearer, z + way).start()

    def finish(self, outs):
        z, rows = self.wires.z, self.rows

        @pl.loop(0, rows // 16)
        def _(step):
            row = pl.multiple_of(z * rows + step * 16, 16)
            begin = 0
            for out in outs:
                out[pl.ds(pl.multiple_of(step * 16, 16), 16), :] = self.part[
                    pl.ds(row, 16), begin : begin + out.shape[1]
                ].astype(out.dtype)
                begin += out.shape[1]

        for hop, nearer in self.EVENTS:
            for way in self.ways:

                @pl.when(z == self._place(way, hop, nearer)[1])
                def _():
                    self._copy(way, hop, nearer, z + way).wait_send()

    @staticmethod
    def scratch(rows, columns, ways=2):
        return pltpu.VMEM(((ways * LINE - 1) * rows, columns), jnp.bfloat16)


def sems(count):
    return [pltpu.SemaphoreType.DMA((count,)), pltpu.SemaphoreType.DMA((count,))]


def kernel_params(collective_id, mib):
    return pltpu.CompilerParams(
        collective_id=collective_id, has_side_effects=True, vmem_limit_bytes=mib * MIB
    )


def dot(left, right, left_dim, right_dim):
    return lax.dot_general(
        left, right, (((left_dim,), (right_dim,)), ((), ())), preferred_element_type=jnp.float32
    )


def rows_at(begin, size):
    return pl.ds(pl.multiple_of(begin, 16), size)


CHUNK = 64
AHEAD = 3
CARRIED = 2
RING = 4
FIRST_CHUNKS = (CHUNK,) * 22
LAST_CHUNKS = (CHUNK,) * 16


class LineSum:
    def __init__(self, wires, own, out, landing, sizes, came=False, goes_on=False):
        self.wires, self.own, self.out, self.landing = wires, own, out, landing
        self.sizes, self.came, self.goes_on = sizes, came, goes_on
        self.all = len(sizes)
        self.chunks = self.all - (CARRIED if goes_on else 0)
        self.begun = CARRIED if came else 0
        self.now = self.begun
        self.first = wires.take(3 * self.all)
        z = wires.z
        self.inner = (z == 1) | (z == 2)
        self.outer = (z == 0) | (z == 3)
        self.end = 3 * (z - 1)
        self.near = 1 + z // 3
        self.peer = 3 - z

    def _row(self, chunk):
        return sum(self.sizes[:chunk])

    def _cut(self, ref, chunk):
        return ref.at[pl.ds(self._row(chunk), self.sizes[chunk])]

    def _slot(self, chunk):
        return chunk % RING * CHUNK

    def _in(self, chunk):
        return self.wires.copy(
            self._cut(self.own, chunk), self._cut(self.out, chunk), self.first + chunk, z=self.near
        )

    def _across(self, chunk):
        landed = self.landing.at[pl.ds(self._slot(chunk), self.sizes[chunk])]
        return self.wires.copy(
            self._cut(self.own, chunk), landed, self.first + self.all + chunk, z=self.peer
        )

    def _back(self, chunk, ref=None):
        number = self.first + 2 * self.all + chunk
        return self.wires.copy(
            self._cut(self.out if ref is None else ref, chunk), self._cut(self.out, chunk), number, z=self.end
        )

    def begin(self):
        @pl.when(self.outer)
        def _():
            for chunk in range(self.begun, min(self.begun + AHEAD, self.all)):
                self._in(chunk).start()

        if self.came:

            @pl.when(self.inner)
            def _():
                self._across(1).start()
                self._back(0, self.own).start()
                self.out[pl.ds(0, self.sizes[0]), :] = self.own[pl.ds(0, self.sizes[0]), :]

    def tick(self, count=1):
        for _ in range(count):
            if self.now < self.all + (0 if self.goes_on else 1):
                self._tick(self.now)
            self.now += 1

    def _tick(self, chunk):
        if chunk < self.all:

            @pl.when(self.outer)
            def _():
                self._in(chunk).wait_send()
                if chunk + AHEAD < self.all:
                    self._in(chunk + AHEAD).start()

        @pl.when(self.inner)
        def _():
            if chunk < self.all:
                row = self._row(chunk)
                self._in(chunk).wait_recv()
                add_rows(self.own, row, self.own, row, self.out, row, self.sizes[chunk])
                if chunk <= self.chunks:
                    self._across(chunk).start()
            if chunk >= 1:
                last = chunk - 1
                row, landed, rows = self._row(last), self._slot(last), self.sizes[last]
                self._across(last).wait_recv()
                if last < self.chunks:
                    add_rows(self.out, row, self.own, row, self.landing, landed, rows)
                    self._back(last).start()
                else:
                    self._across(last).wait_send()
                    add_rows(self.own, row, self.own, row, self.landing, landed, rows)

    def finish(self):
        self.tick(max(0, self.all + (0 if self.goes_on else 1) - self.now))

        @pl.when(self.outer)
        def _():
            for chunk in range(self.chunks):
                self._back(chunk).wait_recv()

        @pl.when(self.inner)
        def _():
            for chunk in range(1 if self.came else 0, self.chunks):
                self._across(chunk).wait_send()
            for chunk in range(self.chunks):
                self._back(chunk).wait_send()


def norm_back(values, gain, grad):
    scale = lax.rsqrt(jnp.mean(values * values, axis=-1, keepdims=True) + epsilon)
    normal = values * scale
    inner = grad * gain
    to_values = scale * (inner - normal * jnp.mean(inner * normal, axis=-1, keepdims=True))
    return to_values, grad * normal


def turned(values, cosine, sine):
    return values * cosine + pltpu.roll(values, HD // 2, 1) * sine


def up_to_attention_back(
    w_query, w_key, w_value, w_out, tokens, cotangent, w_gate, w_up, w_down, gain_attn, gain_moe, routes, gate_values,
    lengths,
):
    rows, width = w_query.shape
    key_width = w_key.shape[1]
    kv_width = key_width + w_value.shape[1]
    tok_rows = tokens.shape[0]
    keys = LINE * tok_rows
    planes = 8
    group = LINE * rows
    hidden_width = w_gate.shape[1]
    total_rows = planes * tok_rows
    sum_rows = width + hidden_width
    sent_rows, done_rows = sum(FIRST_CHUNKS), sum(FIRST_CHUNKS[:-CARRIED])
    score_scale = HD ** (-0.5)
    per_group = HEADS // KVH
    q_width = HEADS * HD

    def kernel(
        wq_ref, wk_ref, wv_ref, wo_ref, tok_hbm, cot_hbm, wg_ref, wu_ref, wd_ref, attn_ref, moe_ref, routes_ref,
        values_ref, lengths_ref,
        out_q, out_kv, out_o, query_hbm, mixed_hbm, normed_hbm, middle_hbm, gain_rows_ref, sums_ref, prod_ref, total_ref,
        grad_mid_hbm, grad_pre_ref, gain_row_ref, w_out_ref,
        w_in, w_down, x_all, y_all, hidden, grad_hidden, grad_in, sums, sums_land, all_gate, gate_t, all_kv, lse_ref,
        core_in, first_in, second_in, middle_ref, kv_land, cos_ref, sin_ref, both_gains, here, there, freed, send, recv,
    ):
        wires = Wires(send, recv)
        dp, z = wires.dp, wires.z

        def rows_begin(block):
            return pl.multiple_of(block * tok_rows, 16)

        def cut_of(block):
            return pl.ds(rows_begin(block), tok_rows)

        def gate_rows(block):
            return pl.ds(pl.multiple_of(block * planes, planes), planes)

        full_q = w_in
        full_kv = hidden.at[pl.ds(0, width), pl.ds(0, kv_width + LANES)]
        full_o = sums.at[pl.ds(0, width)]
        all_cot = y_all
        query_ref, mixed_ref, tok_ref, normed_ref, cot_ref = [
            grad_in.at[pl.ds(i * tok_rows, tok_rows)] for i in range(5)
        ]
        value_t = key_t = grad_in.at[pl.ds(5 * tok_rows, kv_width // 2), pl.ds(0, keys)]
        bias = grad_hidden.at[pl.ds(keys, keys), pl.ds(0, tok_rows)]
        full_o_ref = w_in
        part_o = y_all.at[pl.ds(0, width)]
        attn_low, mixed_grad = tok_ref, normed_ref
        kv_part = hidden.at[pl.ds(keys, keys), pl.ds(0, kv_width)]
        kv_grad = grad_hidden.at[pl.ds(0, keys), pl.ds(0, kv_width)]
        kv_out = grad_hidden.at[pl.ds(keys, tok_rows), pl.ds(tok_rows, kv_width)]

        own = rows_at((dp * LINE + z) * rows, rows)
        moves = [
            (wk_ref, full_kv.at[own, pl.ds(0, key_width)]),
            (wv_ref, full_kv.at[own, pl.ds(key_width, kv_width - key_width)]),
            (cot_hbm, all_cot.at[cut_of(dp)]),
            (wq_ref, full_q.at[own]),
            (wo_ref, full_o.at[own]),
            (tok_hbm, tok_ref),
            (wd_ref, w_down),
            (wg_ref, w_in.at[:, pl.ds(0, hidden_width)]),
            (wu_ref, w_in.at[:, pl.ds(hidden_width, hidden_width)]),
            (out_o, full_o_ref),
            (query_hbm, query_ref),
            (mixed_hbm, mixed_ref),
            (cot_hbm, cot_ref),
        ]
        moves = [pltpu.make_async_copy(a, b, here.at[i]) for i, (a, b) in enumerate(moves)]
        locals_, load_down, load_in, later = moves[:6], moves[6], moves[7:9], moves[9:]
        for one in locals_:
            one.start()
        load_down.start()
        both_gains[...] = jnp.zeros_like(both_gains)
        both_gains[0:1, :rows] = attn_ref[...].astype(jnp.float32)
        both_gains[1:2, :rows] = moe_ref[...].astype(jnp.float32)
        columns = jnp.concatenate([both_gains[...]] * (LANES // 8), axis=0).T
        full_kv[own, kv_width:] = columns[:rows, :].astype(jnp.bfloat16)
        numbers = lax.broadcasted_iota(jnp.int32, (planes, tok_rows), 0)
        gates = jnp.zeros((planes, tok_rows), jnp.float32)
        for place in range(routes_ref.shape[0]):
            named = routes_ref[place : place + 1, :] == numbers
            gates = gates + jnp.where(named, values_ref[place : place + 1, :], 0.0)
        all_gate[gate_rows(dp), :] = gates
        greet(wires, range(1, planes), True)
        for one in locals_:
            one.wait()

        def block_rows(block):
            return rows_at((dp * LINE + block) * rows, rows)

        line_kv, line_q, line_o = [LineGather(wires, r, block_rows) for r in (full_kv, full_q, full_o)]
        plane_kv, plane_q, plane_o = [PlaneGather(wires, r, group) for r in (full_kv, full_q, full_o)]
        plane_cot = PlaneGather(wires, all_cot, tok_rows)
        line_keys = LineGather(wires, all_kv, lambda block: rows_at(block * tok_rows, tok_rows))
        spread = PlaneGather(wires, x_all, tok_rows)
        plane = PlaneReduce(
            wires, y_all, tok_rows, y_all, lambda slot: rows_begin(masked(dp, 2 * slot)), core_in, first_in, second_in,
            None,
        )
        summed = LineSum(wires, sums, total_ref, sums_land, FIRST_CHUNKS, goes_on=True)
        dense = PlaneReduce(
            wires, part_o, group, part_o, lambda slot: pl.multiple_of(masked(dp, 2 * slot) * group, 16),
            core_in, first_in, second_in, w_out_ref,
        )
        line = LineReduce(wires, kv_part, tok_rows, kv_land, ways=(-1,))
        first = wires.take(planes - 1)

        def gate_copy(mask, owner):
            part = all_gate.at[gate_rows(owner)]
            return wires.copy(part, part, first + mask - 1, dp=masked(dp, mask))

        def starts_of(places):
            begin = jnp.zeros_like(places)
            edge = jnp.zeros((1, 1), jnp.int32)
            for number in range(lengths_ref.shape[1] - 1):
                edge = edge + lengths_ref[0:1, number : number + 1]
                begin = jnp.where(places >= edge, edge, begin)
            return begin

        def set_turns():
            places = lax.broadcasted_iota(jnp.int32, (tok_rows, HD), 0) + z * tok_rows
            lane = lax.broadcasted_iota(jnp.int32, (tok_rows, HD), 1)
            power = lax.rem(lane, HD // 2).astype(jnp.float32) * (-math.log(rope_base) / (HD // 2))
            angles = (places - starts_of(places)).astype(jnp.float32) * jnp.exp(power)
            cos_ref[...] = jnp.cos(angles)
            sine = jnp.sin(angles)
            sin_ref[...] = jnp.where(lane < HD // 2, -sine, sine)

        def set_bias():
            key_place = lax.broadcasted_iota(jnp.int32, (keys, tok_rows), 0)
            query_place = lax.broadcasted_iota(jnp.int32, (1, tok_rows), 1) + z * tok_rows
            allowed = (key_place >= starts_of(query_place)) & (key_place <= query_place)
            bias[...] = jnp.where(allowed, 0.0, masked_score)

        line_kv.start(0)
        plane_cot.start(0)
        for mask in range(1, planes):
            gate_copy(mask, dp).start()
        line_kv.wait(0)
        line_kv.start(1)
        set_turns()
        line_kv.wait(1)
        line_kv.start(2)
        line_q.start(0)
        line_kv.wait(2)
        plane_kv.start(0)
        plane_cot.wait(0)
        line_q.wait(0)
        line_q.start(1)
        plane_kv.wait(0)
        plane_kv.start(1)
        plane_cot.start(1, far=False)
        set_bias()
        line_q.wait(1)
        line_q.start(2)
        line_o.start(0)
        plane_kv.wait(1)
        plane_kv.start(2)
        plane_kv.wait(2)
        plane_kv.start(3)
        plane_kv.finish()
        line_q.wait(2)
        plane_q.start(0)

        gain_rows_ref[...] = full_kv[:, kv_width:].astype(jnp.float32).T[:8, :]
        tile = 32

        @pl.loop(0, tok_rows // tile)
        def _(step):
            cut = pl.ds(pl.multiple_of(step * tile, tile), tile)
            normed_ref[cut, :] = rms_norm(
                tok_ref[cut, :].astype(jnp.float32), gain_rows_ref[0:1, :]
            ).astype(jnp.bfloat16)

        own_keys = rows_at(z * tok_rows, tok_rows)
        pre = dot(normed_ref[...], full_kv[:, :kv_width], 1, 0)
        for pair in range(KVH):
            cut = slice(pair * HD, (pair + 1) * HD)
            all_kv[own_keys, cut] = turned(pre[:, cut], cos_ref[...], sin_ref[...]).astype(jnp.bfloat16)
        all_kv[own_keys, key_width:] = pre[:, key_width:].astype(jnp.bfloat16)
        line_keys.start(0)
        line_o.wait(0)
        line_o.start(1)
        plane_q.wait(0)
        plane_q.start(1)
        plane_cot.wait(1)
        plane_cot.start(2)
        line_keys.wait(0)
        line_keys.start(1)
        line_o.wait(1)
        line_o.start(2)
        line_keys.wait(1)
        line_keys.start(2)
        line_o.wait(2)
        plane_o.start(0)
        plane_q.wait(1)
        plane_q.start(2)
        plane_q.wait(2)
        plane_q.start(3)
        plane_q.finish()
        line_kv.finish()
        line_q.finish()
        saves = [
            (full_q, out_q),
            (full_kv, out_kv),
            (normed_ref, normed_hbm),
            (query_ref, query_hbm),
            (full_o, out_o),
            (mixed_ref, mixed_hbm),
            (middle_ref, middle_hbm),
        ]
        saves = [pltpu.make_async_copy(a, b, there.at[11 + i]) for i, (a, b) in enumerate(saves)]
        save_q, saves = saves[0], saves[1:]
        save_q.start()
        saves[0].start()
        saves[1].start()

        @pl.loop(0, HEADS // 2)
        def _(step):
            wide = pl.ds(pl.multiple_of(step * 2 * HD, 2 * HD), 2 * HD)
            pre_q = dot(normed_ref[...], full_q[:, wide], 1, 0)
            for one in range(2):
                query_ref[:, pl.ds(pl.multiple_of((2 * step + one) * HD, HD), HD)] = turned(
                    pre_q[:, one * HD : (one + 1) * HD], cos_ref[...], sin_ref[...]
                ).astype(jnp.bfloat16)

        saves[2].start()
        plane_o.wait(0)
        plane_o.start(1)
        save_q.wait()
        for one in load_in:
            one.start()
        line_keys.wait(2)
        value_t[...] = all_kv[:, key_width:].astype(jnp.float32).T.astype(jnp.bfloat16)
        lse_ref[...] = jnp.zeros_like(lse_ref)

        def attend(head):
            own_cut = pl.ds(pl.multiple_of(head * HD, HD), HD)
            key_cut = pl.ds(pl.multiple_of((head // per_group) * HD, HD), HD)
            scores = dot(all_kv[:, key_cut], query_ref[:, own_cut], 1, 1) * score_scale + bias[...]
            top = jnp.max(scores, axis=0, keepdims=True)
            expo = jnp.exp(scores - top)
            total = jnp.sum(expo, axis=0, keepdims=True)
            lse_ref[pl.ds(head, 1), :] = top + jnp.log(total)
            probs = (expo * (1.0 / total)).astype(jnp.bfloat16)
            mixed_ref[:, own_cut] = dot(value_t[key_cut, :], probs, 1, 0).T.astype(jnp.bfloat16)

        pl.loop(0, HEADS // 2)(attend)
        plane_cot.start_far()
        pl.loop(HEADS // 2, HEADS)(attend)
        plane_o.wait(1)
        plane_o.start(2)
        plane_o.wait(2)
        plane_o.start(3)
        plane_o.finish()
        line_o.finish()
        saves[3].start()
        saves[4].start()

        half_rows = tok_rows // 2
        for half in range(2):
            half_cut = pl.ds(half * half_rows, half_rows)

            @pl.loop(0, width // 512)
            def _(step):
                cut = pl.ds(pl.multiple_of(step * 512, 512), 512)
                middle_ref[half_cut, cut] = tok_ref[half_cut, cut].astype(jnp.float32) + dot(
                    mixed_ref[half_cut, :], full_o[:, cut], 1, 0
                )

            @pl.loop(0, half_rows // tile)
            def _(step):
                begin = half * half_rows + step * tile
                cut = pl.ds(pl.multiple_of(begin, tile), tile)
                x_all[pl.ds(pl.multiple_of(dp * tok_rows + begin, tile), tile), :] = rms_norm(
                    middle_ref[cut, :], gain_rows_ref[1:2, :]
                ).astype(jnp.bfloat16)

            spread.start_one(half)
        spread.start_one(2)
        saves[5].start()
        plane_cot.wait(2)
        plane_cot.start(3)
        plane_cot.finish()
        for mask in range(1, planes):
            gate_copy(mask, masked(dp, mask)).wait_recv()
        gate_t[...] = all_gate[...].T

        def gate_of(block):
            lane = lax.broadcasted_iota(jnp.int32, gate_t.shape, 1)
            return jnp.sum(jnp.where(lane == block * 8 + dp, gate_t[...], 0.0), axis=1, keepdims=True)

        def back_hidden(block):
            cut = cut_of(block)
            y_all[cut, :] = (y_all[cut, :].astype(jnp.float32) * gate_of(block)).astype(jnp.bfloat16)
            grad_hidden[cut, :] = dot(y_all[cut, :], w_down[...], 1, 1)

        def through(mask):
            cut = cut_of(masked(dp, mask))
            acts = dot(x_all[cut, :], w_in[...], 1, 0)
            gate_act, up_act = acts[:, :hidden_width], acts[:, hidden_width:]
            share = jax.nn.sigmoid(gate_act)
            silu = gate_act * share
            hidden[cut, :] = (silu * up_act).astype(jnp.bfloat16)
            grad = grad_hidden[cut, :]
            grad_in[cut, :hidden_width] = (
                grad * up_act * share * (1.0 + gate_act * (1.0 - share))
            ).astype(jnp.bfloat16)
            grad_in[cut, hidden_width:] = (grad * silu).astype(jnp.bfloat16)

        load_down.wait()
        pl.loop(0, 4)(back_hidden)
        spread.wait(0)
        spread.start(1)
        pl.loop(4, 8)(back_hidden)
        for one in load_in + saves:
            one.wait()
        through(0)
        spread.wait_core(0)
        through(1)
        spread.wait(1)
        spread.start(2)
        through(2)
        through(4)
        spread.wait_core(1)
        spread.wait_core(2)
        through(3)
        through(5)
        spread.wait(2)
        spread.start(3)
        through(6)
        spread.wait_core(3)
        through(7)

        def weights_down(step):
            cut = rows_at(step * 256, 256)
            sums[cut, :] = dot(hidden[:, cut], y_all[...], 0, 0).astype(jnp.bfloat16)

        def weights_in(step):
            cut = rows_at(step * 256, 256)
            out = rows_at(hidden_width + step * 256, 256)
            sums[out, :] = dot(x_all[:, cut], grad_in[...], 0, 0).astype(jnp.bfloat16)

        def save_sums(begin, end, number):
            rows = pl.ds(begin, end - begin)
            return pltpu.make_async_copy(sums.at[rows], sums_ref.at[rows], there.at[number])

        pl.loop(0, 1)(weights_down)
        summed.begin()
        pl.loop(1, 3)(weights_down)
        spread.finish()

        def input_grads(side):
            for slot in (3, 2, 1, 0):
                cut = cut_of(masked(dp, 2 * slot + side))
                y_all[cut, :] = dot(grad_in[cut, :], w_in[...], 1, 1).astype(jnp.bfloat16)
                if side:
                    plane.start_core(slot)

        input_grads(1)
        summed.tick()
        input_grads(0)
        summed.tick()
        later[0].start()
        plane.step(1)
        plane.step(2)
        summed.tick()
        pl.loop(0, 2)(weights_in)
        summed.tick()
        pl.loop(2, 4)(weights_in)
        summed.tick()
        plane.step(3)
        pl.loop(4, 6)(weights_in)
        summed.tick()
        for one in later[1:]:
            one.start()
        save = save_sums(sent_rows, sum_rows, 0)
        save.start()

        def save_made(block):
            return pltpu.make_async_copy(
                x_all.at[cut_of(block)], prod_ref.at[cut_of(block)], there.at[3 + block]
            )

        def make(block):
            made = dot(hidden[cut_of(block), :], w_down[...], 1, 0).astype(jnp.bfloat16).astype(jnp.float32)
            x_all[cut_of(block), :] = (made * gate_of(block)).astype(jnp.bfloat16)
            save_made(block).start()

        pl.loop(0, 4)(make)
        summed.tick()
        pl.loop(4, 8)(make)
        plane.step(4)
        summed.tick()
        set_bias()
        kv_grad[...] = jnp.zeros_like(kv_grad)
        gain_row_ref[...] = jnp.zeros_like(gain_row_ref)
        for one in later:
            one.wait()
        key_t[...] = all_kv[:, : kv_width // 2].astype(jnp.float32).T.astype(jnp.bfloat16)
        summed.tick()
        plane.step(5)

        tile = 32

        @pl.loop(0, tok_rows // tile)
        def _(step):
            cut = pl.ds(pl.multiple_of(step * tile, tile), tile)
            routed_grad = core_in[cut, :].astype(jnp.float32) + second_in[cut, :].astype(jnp.float32)
            to_middle, terms = norm_back(middle_ref[cut, :], gain_rows_ref[1:2, :], routed_grad)
            to_middle = cot_ref[cut, :].astype(jnp.float32) + to_middle
            middle_ref[cut, :] = to_middle
            attn_low[cut, :] = to_middle.astype(jnp.bfloat16)
            gain_row_ref[0:1, :] += jnp.sum(terms, axis=0, keepdims=True)

        for mask in (1, 2, 4):
            pl.semaphore_signal(freed, inc=1, device_id=(masked(dp, mask), z), device_id_type=MESH)
        save_mid = pltpu.make_async_copy(middle_ref, grad_mid_hbm, there.at[1])
        save_mid.start()
        summed.tick()
        wide = 512

        @pl.loop(0, width // wide)
        def _(step):
            cut = pl.ds(pl.multiple_of(step * wide, wide), wide)
            mixed_grad[:, cut] = dot(attn_low[...], full_o_ref[cut, :], 1, 1).astype(jnp.bfloat16)

        @pl.loop(0, width // 256)
        def _(step):
            cut = pl.ds(pl.multiple_of(step * 256, 256), 256)
            part_o[cut, :] = dot(mixed_ref[:, cut], attn_low[...], 0, 0).astype(jnp.bfloat16)

        pl.semaphore_wait(freed, 3)
        dense.step(0)
        summed.tick()

        def heads(first, last):
            @pl.loop(first, last)
            def _(head):
                own_cut = pl.ds(pl.multiple_of(head * HD, HD), HD)
                pair = head // per_group
                key_cut = pl.ds(pl.multiple_of(pair * HD, HD), HD)
                value_cut = pl.ds(pl.multiple_of((KVH + pair) * HD, HD), HD)
                q, do = query_ref[:, own_cut], mixed_grad[:, own_cut]
                k, v = all_kv[:, key_cut], all_kv[:, value_cut]
                scores = dot(k, q, 1, 1) * score_scale + bias[...]
                probs = jnp.exp(scores - lse_ref[pl.ds(head, 1), :])
                grad_probs = dot(v, do, 1, 1)
                inner = jnp.sum(probs * grad_probs, axis=0, keepdims=True)
                grad_raw = (probs * (grad_probs - inner) * score_scale).astype(jnp.bfloat16)
                kv_grad[:, value_cut] += dot(probs.astype(jnp.bfloat16), do, 1, 0)
                kv_grad[:, key_cut] += dot(grad_raw, q, 1, 0)
                to_query = dot(key_t[key_cut, :], grad_raw, 1, 0).T
                grad_pre_ref[:, own_cut] = turned(to_query, cos_ref[...], -sin_ref[...]).astype(
                    jnp.bfloat16
                )

        heads(0, 3)
        summed.tick()
        dense.step(1)
        dense.step(2)
        heads(3, 6)
        summed.tick()
        heads(6, 9)
        summed.tick()
        heads(9, 12)
        kv_part[...] = kv_grad[...].astype(jnp.bfloat16)
        line.begin()
        summed.tick()
        dense.step(3)
        summed.tick()
        line.event(0)
        summed.tick()
        dense.step(4)
        line.event(1)
        line.event(2)
        summed.tick()
        line.event(3)
        line.event(4)
        dense.step(5)
        summed.tick(max(0, summed.all - summed.now))
        save_last = save_sums(done_rows, sent_rows, 2)
        save_last.start()
        line.event(5)
        line.finish((kv_out,))
        for pair in range(KVH):
            cut = slice(pair * HD, (pair + 1) * HD)
            grad_pre_ref[:, q_width + pair * HD : q_width + (pair + 1) * HD] = turned(
                kv_out[:, cut], cos_ref[...], -sin_ref[...]
            ).astype(jnp.bfloat16)
        grad_pre_ref[:, q_width + kv_width // 2 :] = kv_out[:, kv_width // 2 :].astype(jnp.bfloat16)
        summed.finish()
        for block in range(8):
            save_made(block).wait()
        for one in (save, save_mid, save_last):
            one.wait()
        line_keys.finish()
        for mask in range(1, planes):
            gate_copy(mask, dp).wait_send()

    f32, low = jnp.float32, jnp.bfloat16
    copies = 4 * LineGather.COPIES + 5 * PlaneGather.COPIES + planes - 1
    copies += 2 * PlaneReduce.COPIES + 3 * len(FIRST_CHUNKS) + LineReduce.COPIES
    return pl.pallas_call(
        kernel,
        out_shape=(
            jax.ShapeDtypeStruct((width, width), low),
            jax.ShapeDtypeStruct((width, kv_width + LANES), low),
            jax.ShapeDtypeStruct((width, width), low),
            jax.ShapeDtypeStruct((tok_rows, width), low),
            jax.ShapeDtypeStruct((tok_rows, width), low),
            jax.ShapeDtypeStruct((tok_rows, width), low),
            jax.ShapeDtypeStruct((tok_rows, width), f32),
            jax.ShapeDtypeStruct((8, width), f32),
            jax.ShapeDtypeStruct((sum_rows, width), low),
            jax.ShapeDtypeStruct((total_rows, width), low),
            jax.ShapeDtypeStruct((sent_rows, width), low),
            jax.ShapeDtypeStruct((tok_rows, width), f32),
            jax.ShapeDtypeStruct((tok_rows, width + kv_width), low),
            jax.ShapeDtypeStruct((8, width), f32),
            jax.ShapeDtypeStruct((group, width), low),
        ),
        in_specs=[ANY] * 9 + [VMEM] * 5,
        out_specs=(ANY,) * 7 + (VMEM, ANY, ANY, VMEM, ANY, VMEM, VMEM, VMEM),
        scratch_shapes=[
            pltpu.VMEM((width, 2 * hidden_width), low),
            pltpu.VMEM((hidden_width, width), low),
            pltpu.VMEM((total_rows, width), low),
            pltpu.VMEM((total_rows, width), low),
            pltpu.VMEM((total_rows, hidden_width), low),
            pltpu.VMEM((total_rows, hidden_width), f32),
            pltpu.VMEM((total_rows, 2 * hidden_width), low),
            pltpu.VMEM((sum_rows, width), low),
            pltpu.VMEM((RING * CHUNK, width), low),
            pltpu.VMEM((planes * planes, tok_rows), f32),
            pltpu.VMEM((tok_rows, planes * planes), f32),
            pltpu.VMEM((keys, kv_width), low),
            pltpu.VMEM((16, tok_rows), f32),
        ]
        + PlaneReduce.scratch(tok_rows, width)
        + [
            pltpu.VMEM((tok_rows, width), f32),
            LineReduce.scratch(tok_rows, kv_width, 1),
            pltpu.VMEM((tok_rows, HD), f32),
            pltpu.VMEM((tok_rows, HD), f32),
            pltpu.VMEM((8, LANES), f32),
            pltpu.SemaphoreType.DMA((15,)),
            pltpu.SemaphoreType.DMA((18,)),
            pltpu.SemaphoreType.REGULAR,
        ]
        + sems(copies),
        compiler_params=kernel_params(1, 63),
        name="up_to_attention_back",
    )(
        w_query, w_key, w_value, w_out, tokens, cotangent, w_gate, w_up, w_down, gain_attn, gain_moe, routes, gate_values,
        lengths,
    )


def back_dense(sums_in, produced, full_q, full_kv, normed, grad_pre, tokens, gains, grad_mid, gain_row, w_out_part, middle):
    tok_rows, width = middle.shape
    q_width = full_q.shape[1]
    in_width = q_width + full_kv.shape[1]
    pre_width = in_width - LANES
    w_rows = width
    group, rows = w_rows // 8, w_rows // (8 * LINE)
    skipped, sum_rows = sum(FIRST_CHUNKS[:-CARRIED]), sum(LAST_CHUNKS)

    def kernel(
        sums_ref, prod_ref, full_q_hbm, full_kv_hbm, normed_hbm, pre_hbm, tok_hbm, gain_ref, mid_grad_hbm,
        gain_row_ref, o_part_hbm, middle_hbm,
        total_ref, layer_ref, tok_grad_ref, wq_ref, wk_ref, wv_ref, gains_ref, out_ref,
        sums_own, sums_land, full_q_ref, full_kv_ref, normed_ref, pre_ref, tok_ref, mid_grad_ref, middle_ref, own, core_in, first_in, second_in, moe, part, d_core, d_first, d_second, in_sums,
        in_land, o_sums, o_land, normed_grad, gain_rows, here, send, recv,
    ):
        wires = Wires(send, recv)
        dp, z = wires.dp, wires.z
        early = (CARRIED + AHEAD) * CHUNK
        loads = [
            pltpu.make_async_copy(sums_ref.at[pl.ds(skipped, early)], sums_own.at[pl.ds(0, early)], here.at[0]),
            pltpu.make_async_copy(
                sums_ref.at[pl.ds(skipped + early, sum_rows - early)],
                sums_own.at[pl.ds(early, sum_rows - early)],
                here.at[1],
            ),
            pltpu.make_async_copy(o_part_hbm, o_sums, here.at[2]),
            pltpu.make_async_copy(pre_hbm, pre_ref, here.at[3]),
            pltpu.make_async_copy(full_q_hbm, full_q_ref, here.at[4]),
            pltpu.make_async_copy(full_kv_hbm, full_kv_ref, here.at[5]),
            pltpu.make_async_copy(tok_hbm, tok_ref, here.at[6]),
            pltpu.make_async_copy(mid_grad_hbm, mid_grad_ref, here.at[7]),
            pltpu.make_async_copy(normed_hbm, normed_ref, here.at[8]),
            pltpu.make_async_copy(middle_hbm, middle_ref, here.at[9]),
        ]
        first_loads = len(loads)
        for slot in range(4):
            row = pl.multiple_of(masked(dp, 2 * slot) * tok_rows, 16)
            loads.append(
                pltpu.make_async_copy(
                    prod_ref.at[pl.ds(row, tok_rows)],
                    own.at[pl.ds(slot * tok_rows, tok_rows)],
                    here.at[first_loads + slot],
                )
            )
        for one in loads:
            one.start()
        greet(wires, (1, 2, 4), True)
        summed = LineSum(wires, sums_own, total_ref, sums_land, LAST_CHUNKS, came=True)
        dense = PlaneReduce(
            wires, part, group, part, lambda slot: pl.multiple_of(masked(dp, 2 * slot) * group, 16),
            d_core, d_first, d_second, in_sums,
        )
        plane = PlaneReduce(
            wires, prod_ref, tok_rows, own, lambda slot: slot * tok_rows, core_in, first_in, second_in, moe
        )
        o_line = LineReduce(wires, o_sums, rows, o_land)
        in_line = LineReduce(wires, in_sums, rows, in_land)
        loads[0].wait()
        summed.begin()
        loads[1].wait()
        loads[2].wait()
        o_line.begin()
        for one in loads[3:first_loads]:
            one.wait()
        wide = 512

        @pl.loop(0, width // wide)
        def _(step):
            cut = pl.ds(pl.multiple_of(step * wide, wide), wide)
            normed_grad[:, cut] = dot(pre_ref[:, :q_width], full_q_ref[cut, :], 1, 1) + dot(
                pre_ref[:, q_width:], full_kv_ref[cut, : pre_width - q_width], 1, 1
            )

        summed.tick()
        gain_rows[...] = jnp.zeros_like(gain_rows)
        gain_rows[1:2, :] = gain_row_ref[0:1, :]
        tile = 32

        @pl.loop(0, tok_rows // tile)
        def _(step):
            cut = pl.ds(pl.multiple_of(step * tile, tile), tile)
            to_tokens, terms = norm_back(
                tok_ref[cut, :].astype(jnp.float32), gain_ref[0:1, :], normed_grad[cut, :]
            )
            tok_grad_ref[cut, :] = mid_grad_ref[cut, :] + to_tokens
            gain_rows[0:1, :] += jnp.sum(terms, axis=0, keepdims=True)

        summed.tick()
        o_line.event(0)
        part[:, pre_width:] = gain_rows[...].T.astype(jnp.bfloat16)

        @pl.loop(0, w_rows // 256)
        def _(step):
            cut = pl.ds(pl.multiple_of(step * 256, 256), 256)
            part[cut, :pre_width] = dot(normed_ref[:, cut], pre_ref[...], 0, 0).astype(jnp.bfloat16)

        dense.step(0)
        o_line.event(1)
        o_line.event(2)
        summed.tick(2)
        dense.step(1)
        o_line.event(3)
        summed.tick()
        dense.step(2)
        o_line.event(4)
        summed.tick()
        o_line.event(5)
        for one in loads[first_loads:]:
            one.wait()
        plane.step(0)
        summed.tick(2)
        dense.step(3)
        plane.step(1)
        plane.step(2)
        summed.tick(2)
        dense.step(4)
        dense.step(5)
        in_line.begin()
        summed.tick()
        in_line.event(0)
        summed.tick()
        plane.step(3)
        in_line.event(1)
        in_line.event(2)
        summed.tick(2)
        in_line.event(3)
        in_line.event(4)
        plane.step(4)
        summed.tick(2)
        in_line.event(5)
        plane.step(5)
        summed.tick(2)

        @pl.loop(0, tok_rows // tile)
        def _(step):
            cut = pl.ds(pl.multiple_of(step * tile, tile), tile)
            layer_ref[cut, :] = (middle_ref[cut, :] + moe[cut, :]).astype(jnp.bfloat16)

        o_line.finish((out_ref,))
        in_line.finish((wq_ref, wk_ref, wv_ref, gains_ref))
        summed.finish()

    f32, low = jnp.float32, jnp.bfloat16
    return pl.pallas_call(
        kernel,
        out_shape=(
            jax.ShapeDtypeStruct((sum_rows, width), low),
            jax.ShapeDtypeStruct((tok_rows, width), low),
            jax.ShapeDtypeStruct((tok_rows, width), f32),
            jax.ShapeDtypeStruct((rows, q_width), f32),
            jax.ShapeDtypeStruct((rows, (pre_width - q_width) // 2), f32),
            jax.ShapeDtypeStruct((rows, (pre_width - q_width) // 2), f32),
            jax.ShapeDtypeStruct((rows, LANES), f32),
            jax.ShapeDtypeStruct((rows, width), f32),
        ),
        in_specs=[ANY] * 7 + [VMEM, ANY, VMEM, ANY, ANY],
        out_specs=(VMEM,) * 8,
        scratch_shapes=[
            pltpu.VMEM((sum_rows, width), low),
            pltpu.VMEM((RING * CHUNK, width), low),
            pltpu.VMEM(full_q.shape, low),
            pltpu.VMEM(full_kv.shape, low),
            pltpu.VMEM((tok_rows, width), low),
            pltpu.VMEM((tok_rows, pre_width), low),
            pltpu.VMEM((tok_rows, width), low),
            pltpu.VMEM((tok_rows, width), f32),
            pltpu.VMEM((tok_rows, width), f32),
            pltpu.VMEM((4 * tok_rows, width), low),
        ]
        + PlaneReduce.scratch(tok_rows, width)
        + [pltpu.VMEM((tok_rows, width), f32), pltpu.VMEM((w_rows, in_width), low)]
        + PlaneReduce.scratch(group, in_width)
        + [
            pltpu.VMEM((group, in_width), low),
            LineReduce.scratch(rows, in_width),
            pltpu.VMEM((group, width), low),
            LineReduce.scratch(rows, width),
            pltpu.VMEM((tok_rows, width), f32),
            pltpu.VMEM((LANES, width), f32),
            pltpu.SemaphoreType.DMA((14,)),
        ]
        + sems(3 * len(LAST_CHUNKS) + 2 * PlaneReduce.COPIES + 2 * LineReduce.COPIES),
        compiler_params=kernel_params(4, 63),
        name="back_dense",
    )(
        sums_in, produced, full_q, full_kv, normed, grad_pre, tokens, gains, grad_mid, gain_row, w_out_part, middle
    )


def hand_over(sums_head, sums_tail, gains, *others):
    done, width = sum(FIRST_CHUNKS[:-CARRIED]), sums_head.shape[1]
    hidden_width = width // 2
    rows = 256
    head_steps, tail_steps = done // rows, sums_tail.shape[0] // rows
    down_steps = hidden_width // rows
    steps = head_steps + tail_steps
    count = len(others)

    def kernel(*refs):
        head_ref, tail_ref, gains_ref = refs[:3]
        down_ref, gate_ref, up_ref, attn_ref, moe_ref = refs[3 + count : 8 + count]
        step = pl.program_id(0)
        for source, target in zip(refs[3 : 3 + count], refs[8 + count :]):
            target[...] = source[...]

        @pl.when(step == 0)
        def _():
            turned_gains = gains_ref[...].T
            attn_ref[...] = turned_gains[0, :]
            moe_ref[...] = turned_gains[1, :]

        def put(values):
            @pl.when(step < down_steps)
            def _():
                down_ref[0] = values

            @pl.when(step >= down_steps)
            def _():
                gate_ref[0] = values[:, :hidden_width]
                up_ref[0] = values[:, hidden_width:]

        @pl.when(step < head_steps)
        def _():
            put(head_ref[...].astype(jnp.float32))

        @pl.when(step >= head_steps)
        def _():
            put(tail_ref[...].astype(jnp.float32))

    def by_rows(one):
        if one.shape[0] % (8 * 16):
            return pl.BlockSpec(one.shape, lambda i: (0, 0))
        return pl.BlockSpec((one.shape[0] // 8, one.shape[1]), lambda i: (jnp.minimum(i, 7), 0))

    f32 = jnp.float32
    in_shape = (1, rows, hidden_width)
    copied = [by_rows(one) for one in others]
    return pl.pallas_call(
        kernel,
        grid=(steps,),
        out_shape=(
            jax.ShapeDtypeStruct((1, hidden_width, width), f32),
            jax.ShapeDtypeStruct((1, width, hidden_width), f32),
            jax.ShapeDtypeStruct((1, width, hidden_width), f32),
            jax.ShapeDtypeStruct((gains.shape[0],), f32),
            jax.ShapeDtypeStruct((gains.shape[0],), f32),
        )
        + tuple(jax.ShapeDtypeStruct(one.shape, one.dtype) for one in others),
        in_specs=[
            pl.BlockSpec((rows, width), lambda i: (jnp.minimum(i, head_steps - 1), 0)),
            pl.BlockSpec((rows, width), lambda i: (jnp.maximum(i - head_steps, 0), 0)),
            pl.BlockSpec(gains.shape, lambda i: (0, 0)),
        ]
        + copied,
        out_specs=(
            pl.BlockSpec((1, rows, width), lambda i: (0, jnp.minimum(i, down_steps - 1), 0)),
            pl.BlockSpec(in_shape, lambda i: (0, jnp.maximum(i - down_steps, 0), 0)),
            pl.BlockSpec(in_shape, lambda i: (0, jnp.maximum(i - down_steps, 0), 0)),
            pl.BlockSpec((gains.shape[0],), lambda i: (0,)),
            pl.BlockSpec((gains.shape[0],), lambda i: (0,)),
        )
        + tuple(copied),
        compiler_params=pltpu.CompilerParams(vmem_limit_bytes=63 * MIB),
        name="hand_over",
    )(sums_head, sums_tail, gains, *others)


def on_plane_device(
    tokens,
    norm_attn,
    w_query,
    w_key,
    w_value,
    w_out,
    norm_moe,
    w_gate,
    w_up,
    w_down,
    routes,
    gate_values,
    lengths,
    cotangent,
):
    (
        full_q, full_kv, _, _, _, normed_low, middle, gain_rows, partial_sums, produced, sums_head, grad_mid, grad_pre,
        gain_row, w_out_part,
    ) = up_to_attention_back(
        w_query, w_key, w_value, w_out, tokens, cotangent, w_gate[0], w_up[0], w_down[0], norm_attn[None], norm_moe[None],
        routes.T, gate_values.T, lengths,
    )
    sums_tail, layer_out, grad_tokens, sum_q, sum_k, sum_v, sum_gains, sum_o = back_dense(
        partial_sums,
        produced,
        full_q,
        full_kv,
        normed_low,
        grad_pre,
        tokens,
        gain_rows,
        grad_mid,
        gain_row,
        w_out_part,
        middle,
    )
    down, gate, up, gain_attn, gain_moe, layer_out, grad_tokens, sum_q, sum_k, sum_v, sum_o = hand_over(
        sums_head, sums_tail, sum_gains, layer_out, grad_tokens, sum_q, sum_k, sum_v, sum_o
    )
    return (
        layer_out, grad_tokens, gain_attn, sum_q, sum_k, sum_v, sum_o, gain_moe, gate, up, down,
    )


def solution(mesh):
    on_plane = mesh.shape["dp"] == 8 and mesh.shape["ctx"] == LINE
    return jax.shard_map(
        on_plane_device if on_plane else on_device,
        mesh=mesh,
        in_specs=(
            P(("dp", "ctx"), None),
            P(("dp", "ctx")),
            P(("dp", "ctx"), None),
            P(("dp", "ctx"), None),
            P(("dp", "ctx"), None),
            P(("dp", "ctx"), None),
            P(("dp", "ctx")),
            P("dp", None, None),
            P("dp", None, None),
            P("dp", None, None),
            P(("dp", "ctx"), None),
            P(("dp", "ctx"), None),
            P("dp", None),
            P(("dp", "ctx"), None),
        ),
        out_specs=(
            P(("dp", "ctx"), None),
            P(("dp", "ctx"), None),
            P(("dp", "ctx")),
            P(("dp", "ctx"), None),
            P(("dp", "ctx"), None),
            P(("dp", "ctx"), None),
            P(("dp", "ctx"), None),
            P(("dp", "ctx")),
            P("dp", None, None),
            P("dp", None, None),
            P("dp", None, None),
        ),
        check_vma=False,
    )
```

```python
import math

import jax
import jax.numpy as jnp
from jax import lax
from jax.experimental import pallas as pl
from jax.experimental.pallas import tpu as pltpu
from jax.sharding import PartitionSpec as P

D = 1536
HEADS = 12
KVH = 2
HD = 128
TOP = 4
EXP_DEV = 1


epsilon = 1e-06
rope_base = 1000000.0
masked_score = -1e30


def rms_norm(values, gain):
    return values * lax.rsqrt(jnp.mean(values * values, axis=-1, keepdims=True) + epsilon) * gain


def rotate(values, within, direction):
    half_size = values.shape[-1] // 2
    frequency = rope_base ** (-jnp.arange(half_size, dtype=jnp.float32) / half_size)
    angles = direction * within.astype(jnp.float32)[:, None] * frequency[None, :]
    cosine = jnp.cos(angles)[:, None, :]
    sine = jnp.sin(angles)[:, None, :]
    first_half = values[..., :half_size]
    second = values[..., half_size:]
    return jnp.concatenate(
        [first_half * cosine - second * sine, second * cosine + first_half * sine], axis=-1
    )


def seq_tables(length_row, places):
    seq_ends = jnp.cumsum(length_row)
    passed = places[:, None] >= seq_ends[None, :]
    segment = jnp.sum(passed.astype(jnp.int32), axis=1)
    within = places - jnp.sum(jnp.where(passed, length_row[None, :], 0), axis=1)
    return (segment, within)


def collect_weights(gain_attn, w_query, w_key, w_value, w_out, gain_moe):
    return (
        lax.all_gather(gain_attn, ("dp", "ctx"), axis=0, tiled=True),
        lax.all_gather(w_query, ("dp", "ctx"), axis=0, tiled=True),
        lax.all_gather(w_key, ("dp", "ctx"), axis=0, tiled=True),
        lax.all_gather(w_value, ("dp", "ctx"), axis=0, tiled=True),
        lax.all_gather(w_out, ("dp", "ctx"), axis=0, tiled=True),
        lax.all_gather(gain_moe, ("dp", "ctx"), axis=0, tiled=True),
    )


def spread_grads(grad_gain_attn, grad_query, grad_key, grad_value, grad_outp, grad_gain_moe):
    return (
        lax.psum_scatter(grad_gain_attn, ("dp", "ctx"), scatter_dimension=0, tiled=True),
        lax.psum_scatter(grad_query, ("dp", "ctx"), scatter_dimension=0, tiled=True),
        lax.psum_scatter(grad_key, ("dp", "ctx"), scatter_dimension=0, tiled=True),
        lax.psum_scatter(grad_value, ("dp", "ctx"), scatter_dimension=0, tiled=True),
        lax.psum_scatter(grad_outp, ("dp", "ctx"), scatter_dimension=0, tiled=True),
        lax.psum_scatter(grad_gain_moe, ("dp", "ctx"), scatter_dimension=0, tiled=True),
    )


def on_device(
    tokens,
    norm_attn,
    w_query,
    w_key,
    w_value,
    w_out,
    norm_moe,
    w_gate,
    w_up,
    w_down,
    routes,
    gate_values,
    lengths,
    cotangent,
):
    tok_rows = tokens.shape[0]
    ctx_size = lax.axis_size("ctx")
    dp_size = lax.axis_size("dp")
    ctx_place = lax.axis_index("ctx")
    group_rows = tok_rows * ctx_size
    group_places = jnp.arange(group_rows, dtype=jnp.int32)
    seg_all, within_all = seq_tables(lengths[0], group_places)
    offset = ctx_place * tok_rows
    own_places = offset + jnp.arange(tok_rows, dtype=jnp.int32)
    seg_own = lax.dynamic_slice_in_dim(seg_all, offset, tok_rows)
    within_own = lax.dynamic_slice_in_dim(within_all, offset, tok_rows)
    allowed = (seg_own[:, None] == seg_all[None, :]) & (
        group_places[None, :] <= own_places[:, None]
    )
    gain_attn, full_q, full_k, full_v, full_o, gain_moe = collect_weights(
        norm_attn, w_query, w_key, w_value, w_out, norm_moe
    )
    gain_attn_f = gain_attn.astype(jnp.float32)
    gain_moe_f = gain_moe.astype(jnp.float32)
    inputs = tokens.astype(jnp.float32)
    normed_low = rms_norm(inputs, gain_attn_f).astype(jnp.bfloat16)
    query_pre = jnp.dot(normed_low, full_q, preferred_element_type=jnp.float32)
    key_pre = jnp.dot(normed_low, full_k, preferred_element_type=jnp.float32)
    value_pre = jnp.dot(normed_low, full_v, preferred_element_type=jnp.float32)
    query = rotate(query_pre.reshape(tok_rows, HEADS, HD), within_own, 1.0).astype(jnp.bfloat16)
    key_low = rotate(key_pre.reshape(tok_rows, KVH, HD), within_own, 1.0).astype(jnp.bfloat16)
    key_low = key_low.reshape(tok_rows, KVH * HD)
    value_low = value_pre.astype(jnp.bfloat16)
    all_keys, all_values = (
        lax.all_gather(key_low, "ctx", axis=0, tiled=True),
        lax.all_gather(value_low, "ctx", axis=0, tiled=True),
    )
    per_group = HEADS // KVH
    score_scale = HD ** (-0.5)
    query_groups = query.reshape(tok_rows, KVH, per_group, HD)

    def softmax_weights(group_number):
        keys_part = all_keys[:, group_number * HD : (group_number + 1) * HD]
        raw = jnp.einsum(
            "qjd,kd->jqk",
            query_groups[:, group_number],
            keys_part,
            preferred_element_type=jnp.float32,
        )
        scores = jnp.where(allowed[None], raw * score_scale, masked_score)
        row_top = jnp.max(scores, axis=-1, keepdims=True)
        expo = jnp.exp(scores - row_top)
        return expo / jnp.sum(expo, axis=-1, keepdims=True)

    mixed_parts = []
    for group_number in range(KVH):
        probs = softmax_weights(group_number)
        values_part = all_values[:, group_number * HD : (group_number + 1) * HD]
        mixed_group = jnp.einsum(
            "jqk,kd->qjd",
            probs.astype(jnp.bfloat16),
            values_part,
            preferred_element_type=jnp.float32,
        )
        mixed_parts.append(mixed_group.reshape(tok_rows, per_group * HD))
    mixed_low = jnp.concatenate(mixed_parts, axis=1).astype(jnp.bfloat16)
    middle = inputs + jnp.dot(mixed_low, full_o, preferred_element_type=jnp.float32)
    routed_low = rms_norm(middle, gain_moe_f).astype(jnp.bfloat16)
    experts_total = EXP_DEV * dp_size
    capacity = 3 * TOP * tok_rows // (2 * experts_total)
    assign_count = tok_rows * TOP
    flat_ids = routes.reshape(assign_count)
    onehot = (flat_ids[:, None] == jnp.arange(experts_total, dtype=jnp.int32)[None, :]).astype(
        jnp.int32
    )
    earlier = jnp.sum((jnp.cumsum(onehot, axis=0) - onehot) * onehot, axis=1)
    slot_index = flat_ids * capacity + earlier
    owner = (
        jnp.full((experts_total * capacity,), assign_count, jnp.int32)
        .at[slot_index]
        .set(jnp.arange(assign_count, dtype=jnp.int32))
    )
    padded = jnp.concatenate([routed_low, jnp.zeros((1, D), jnp.bfloat16)], axis=0)
    outgoing = padded[owner // TOP].reshape(experts_total, capacity, D)
    arrived = lax.all_to_all(outgoing, "dp", split_axis=0, concat_axis=0, tiled=True)
    arrived_sets = arrived.reshape(dp_size, EXP_DEV, capacity, D)
    gate_act = jnp.einsum(
        "secd,edf->secf", arrived_sets, w_gate, preferred_element_type=jnp.float32
    )
    up_act = jnp.einsum("secd,edf->secf", arrived_sets, w_up, preferred_element_type=jnp.float32)
    hidden_low = (jax.nn.silu(gate_act) * up_act).astype(jnp.bfloat16)
    produced = jnp.einsum("secf,efd->secd", hidden_low, w_down, preferred_element_type=jnp.float32)
    produced = produced.astype(jnp.bfloat16).reshape(experts_total, capacity, D)
    returned = lax.all_to_all(produced, "dp", split_axis=0, concat_axis=0, tiled=True)
    picked = returned.reshape(experts_total * capacity, D)[slot_index].reshape(tok_rows, TOP, D)
    moe_out = jnp.sum(picked.astype(jnp.float32) * gate_values[:, :, None], axis=1)
    layer_out = (middle + moe_out).astype(jnp.bfloat16)
    grad_out = cotangent.astype(jnp.float32)
    grad_assign = (grad_out[:, None, :] * gate_values[:, :, None]).astype(jnp.bfloat16)
    grad_padded = jnp.concatenate(
        [grad_assign.reshape(assign_count, D), jnp.zeros((1, D), jnp.bfloat16)], axis=0
    )
    grad_slots = grad_padded[owner].reshape(experts_total, capacity, D)
    grad_arrived = lax.all_to_all(grad_slots, "dp", split_axis=0, concat_axis=0, tiled=True)
    grad_arrived = grad_arrived.reshape(dp_size, EXP_DEV, capacity, D)
    grad_hidden = jnp.einsum(
        "secd,efd->secf", grad_arrived, w_down, preferred_element_type=jnp.float32
    )
    grad_w_down = jnp.einsum(
        "secf,secd->efd", hidden_low, grad_arrived, preferred_element_type=jnp.float32
    )
    glu_value, glu_pull = jax.vjp(
        lambda gate_in, up_in: jax.nn.silu(gate_in) * up_in, gate_act, up_act
    )
    grad_gate, grad_up = glu_pull(grad_hidden)
    grad_gate_low = grad_gate.astype(jnp.bfloat16)
    grad_up_low = grad_up.astype(jnp.bfloat16)
    grad_w_gate = jnp.einsum(
        "secd,secf->edf", arrived_sets, grad_gate_low, preferred_element_type=jnp.float32
    )
    grad_w_up = jnp.einsum(
        "secd,secf->edf", arrived_sets, grad_up_low, preferred_element_type=jnp.float32
    )
    grad_sent = jnp.einsum(
        "secf,edf->secd", grad_gate_low, w_gate, preferred_element_type=jnp.float32
    ) + jnp.einsum("secf,edf->secd", grad_up_low, w_up, preferred_element_type=jnp.float32)
    grad_sent = grad_sent.astype(jnp.bfloat16).reshape(experts_total, capacity, D)
    grad_back = lax.all_to_all(grad_sent, "dp", split_axis=0, concat_axis=0, tiled=True)
    grad_picked = grad_back.reshape(experts_total * capacity, D)[slot_index].reshape(
        tok_rows, TOP, D
    )
    grad_routed = jnp.sum(grad_picked.astype(jnp.float32), axis=1)
    expert_sums = (
        lax.psum(grad_w_gate.astype(jnp.bfloat16), "ctx").astype(jnp.float32),
        lax.psum(grad_w_up.astype(jnp.bfloat16), "ctx").astype(jnp.float32),
        lax.psum(grad_w_down.astype(jnp.bfloat16), "ctx").astype(jnp.float32),
    )
    norm_value, moe_pull = jax.vjp(rms_norm, middle, gain_moe_f)
    grad_mid_norm, grad_gain_moe = moe_pull(grad_routed)
    grad_middle = grad_out + grad_mid_norm
    grad_attn_low = grad_middle.astype(jnp.bfloat16)
    grad_w_out = jnp.einsum(
        "th,td->hd", mixed_low, grad_attn_low, preferred_element_type=jnp.float32
    )
    grad_mixed_low = jnp.einsum(
        "td,hd->th", grad_attn_low, full_o, preferred_element_type=jnp.float32
    ).astype(jnp.bfloat16)
    grad_mixed_groups = grad_mixed_low.reshape(tok_rows, KVH, per_group, HD)
    grad_query_parts = []
    prob_parts = []
    score_parts = []
    for group_number in range(KVH):
        probs = softmax_weights(group_number)
        keys_part = all_keys[:, group_number * HD : (group_number + 1) * HD]
        values_part = all_values[:, group_number * HD : (group_number + 1) * HD]
        grad_probs = jnp.einsum(
            "qjd,kd->jqk",
            grad_mixed_groups[:, group_number],
            values_part,
            preferred_element_type=jnp.float32,
        )
        grad_scores = probs * (grad_probs - jnp.sum(probs * grad_probs, axis=-1, keepdims=True))
        grad_raw_low = (grad_scores * score_scale).astype(jnp.bfloat16)
        grad_query_parts.append(
            jnp.einsum("jqk,kd->qjd", grad_raw_low, keys_part, preferred_element_type=jnp.float32)
        )
        prob_parts.append(probs.astype(jnp.bfloat16))
        score_parts.append(grad_raw_low)
    grad_query_rot = jnp.stack(grad_query_parts, axis=1).reshape(tok_rows, HEADS, HD)
    key_pieces = []
    value_pieces = []
    for group_number in range(KVH):
        score_piece = score_parts[group_number]
        prob_piece = prob_parts[group_number]
        key_pieces.append(
            jnp.einsum(
                "jqk,qjd->kd",
                score_piece,
                query_groups[:, group_number],
                preferred_element_type=jnp.float32,
            )
        )
        value_pieces.append(
            jnp.einsum(
                "jqk,qjd->kd",
                prob_piece,
                grad_mixed_groups[:, group_number],
                preferred_element_type=jnp.float32,
            )
        )
    key_value_grads = lax.psum_scatter(
        jnp.concatenate(key_pieces + value_pieces, axis=1).astype(jnp.bfloat16),
        "ctx",
        scatter_dimension=0,
        tiled=True,
    ).astype(jnp.float32)
    grad_query_low = (
        rotate(grad_query_rot, within_own, -1.0).astype(jnp.bfloat16).reshape(tok_rows, HEADS * HD)
    )
    grad_key_rot = key_value_grads[:, : KVH * HD].reshape(tok_rows, KVH, HD)
    grad_key_low = (
        rotate(grad_key_rot, within_own, -1.0).astype(jnp.bfloat16).reshape(tok_rows, KVH * HD)
    )
    grad_value_low = key_value_grads[:, KVH * HD :].astype(jnp.bfloat16)
    grad_w_query = jnp.einsum(
        "td,th->dh", normed_low, grad_query_low, preferred_element_type=jnp.float32
    )
    grad_w_key = jnp.einsum(
        "td,th->dh", normed_low, grad_key_low, preferred_element_type=jnp.float32
    )
    grad_w_value = jnp.einsum(
        "td,th->dh", normed_low, grad_value_low, preferred_element_type=jnp.float32
    )
    grad_normed = (
        jnp.einsum("th,dh->td", grad_query_low, full_q, preferred_element_type=jnp.float32)
        + jnp.einsum("th,dh->td", grad_key_low, full_k, preferred_element_type=jnp.float32)
        + jnp.einsum("th,dh->td", grad_value_low, full_v, preferred_element_type=jnp.float32)
    )
    first_value, attn_pull = jax.vjp(rms_norm, inputs, gain_attn_f)
    grad_inputs, grad_gain_attn = attn_pull(grad_normed)
    grad_tokens = grad_middle + grad_inputs
    dense_sums = spread_grads(
        grad_gain_attn, grad_w_query, grad_w_key, grad_w_value, grad_w_out, grad_gain_moe
    )
    return (
        layer_out,
        grad_tokens,
        dense_sums[0],
        dense_sums[1],
        dense_sums[2],
        dense_sums[3],
        dense_sums[4],
        dense_sums[5],
        expert_sums[0],
        expert_sums[1],
        expert_sums[2],
    )


MESH = pl.DeviceIdType.MESH
LANES = 128
MIB = 2**20
ANY = pl.BlockSpec(memory_space=pl.ANY)
VMEM = pl.BlockSpec(memory_space=pltpu.VMEM)


def flip(index, bit):
    return index + bit - 2 * bit * ((index // bit) % 2)


def masked(index, mask):
    for bit in (1, 2, 4):
        if mask & bit:
            index = flip(index, bit)
    return index


class Wires:
    def __init__(self, send, recv):
        self.send, self.recv, self.used = send, recv, 0
        self.dp, self.z = lax.axis_index("dp"), lax.axis_index("ctx")

    def take(self, count):
        first = self.used
        self.used += count
        return first

    def copy(self, src, dst, number, dp=None, z=None):
        return pltpu.make_async_remote_copy(
            src_ref=src,
            dst_ref=dst,
            send_sem=self.send.at[number],
            recv_sem=self.recv.at[number],
            device_id=(self.dp if dp is None else dp, self.z if z is None else z),
            device_id_type=MESH,
        )


def greet(wires, masks, line):
    barrier = pltpu.get_barrier_semaphore()
    dp, z = wires.dp, wires.z
    for mask in masks:
        pl.semaphore_signal(barrier, inc=1, device_id=(masked(dp, mask), z), device_id_type=MESH)
    for step in range(1, LINE) if line else ():
        pl.semaphore_signal(
            barrier, inc=1, device_id=(dp, lax.rem(z + step, LINE)), device_id_type=MESH
        )
    pl.semaphore_wait(barrier, len(masks) + (LINE - 1 if line else 0))


LINE = 4


class LineGather:
    COPIES = 2 * (LINE - 1)

    def __init__(self, wires, ref, rows_of):
        self.wires, self.ref, self.rows_of = wires, ref, rows_of
        self.first = wires.take(self.COPIES)

    def _copy(self, block, number, z):
        part = self.ref.at[self.rows_of(block)]
        return self.wires.copy(part, part, self.first + number, z=z)

    def start(self, step):
        z = self.wires.z

        @pl.when((z >= step) & (z < LINE - 1))
        def _():
            self._copy(z - step, step, z + 1).start()

        @pl.when((z + step < LINE) & (z > 0))
        def _():
            self._copy(z + step, LINE - 1 + step, z - 1).start()

    def wait(self, step):
        z = self.wires.z

        @pl.when(z - 1 - step >= 0)
        def _():
            self._copy(z - 1 - step, step, z).wait_recv()

        @pl.when(z + 1 + step < LINE)
        def _():
            self._copy(z + 1 + step, LINE - 1 + step, z).wait_recv()

    def finish(self):
        z = self.wires.z
        for step in range(LINE - 1):

            @pl.when((z >= step) & (z < LINE - 1))
            def _():
                self._copy(z - step, step, z + 1).wait_send()

            @pl.when((z + step < LINE) & (z > 0))
            def _():
                self._copy(z + step, LINE - 1 + step, z - 1).wait_send()


class PlaneGather:
    CHIP = (((2, 0, 0), (4, 0, 1)), ((4, 0, 0), (2, 0, 1)), ((4, 2, 0), (2, 4, 1)))
    CORE = (
        ((1, 0, 2),),
        ((1, 2, 0), (1, 4, 1)),
        ((1, 4, 0), (1, 2, 1)),
        ((1, 6, 0), (1, 6, 1)),
    )
    COPIES = 13

    def __init__(self, wires, ref, group):
        self.wires, self.ref, self.group = wires, ref, group
        first = wires.take(self.COPIES)
        self.number = {}
        for stage in self.CHIP + self.CORE:
            for one in stage:
                self.number[one] = first + len(self.number)
        self.core_left = [0, 1, 2, 3]

    def _copy(self, one, from_me):
        to, whose, half = one
        dp = self.wires.dp
        sender = dp if from_me else masked(dp, to)
        owner = masked(sender, whose)
        size = self.group if half == 2 else self.group // 2
        begin = owner * self.group + (self.group // 2 if half == 1 else 0)
        part = self.ref.at[pl.ds(pl.multiple_of(begin, 16), size)]
        return self.wires.copy(part, part, self.number[one], dp=masked(dp, to))

    def start(self, stage, far=True):
        for one in (self.CHIP[stage] if stage < 2 else ()) + self.CORE[stage]:
            self._copy(one, True).start()
        if stage == 1 and far:
            self.start_far()

    def start_one(self, number):
        self._copy((self.CHIP[0] + self.CORE[0])[number], True).start()

    def start_far(self):
        for one in self.CHIP[2]:
            self._copy(one, True).start()

    def wait(self, stage):
        for one in self.CHIP[stage]:
            self._copy(one, False).wait_recv()

    def wait_core(self, stage):
        self.core_left.remove(stage)
        for one in self.CORE[stage]:
            self._copy(one, False).wait_recv()

    def finish(self):
        for stage in list(self.core_left):
            self.wait_core(stage)
        for one in self.number:
            self._copy(one, True).wait_send()


def add_rows(out, out_row, left, left_row, right, right_row, rows):
    @pl.loop(0, rows // 16)
    def _(step):
        def cut(row):
            return pl.ds(pl.multiple_of(row + step * 16, 16), 16)

        out[cut(out_row), :] = (
            left[cut(left_row), :].astype(jnp.float32) + right[cut(right_row), :].astype(jnp.float32)
        ).astype(out.dtype)


class PlaneReduce:
    COPIES = 10
    STEPS = 6

    def __init__(self, wires, part, group, own, own_row, core_in, first_in, second_in, out):
        self.wires, self.part, self.group, self.half = wires, part, group, group // 2
        self.own, self.own_row, self.out = own, own_row, out
        self.core_in, self.first_in, self.second_in = core_in, first_in, second_in
        self.first = wires.take(self.COPIES)

    def _send(self, src, src_row, dst, dst_row, rows, number, to):
        return self.wires.copy(
            src.at[pl.ds(src_row, rows)],
            dst.at[pl.ds(dst_row, rows)],
            self.first + number,
            dp=masked(self.wires.dp, to),
        )

    def _core(self, slot):
        row = pl.multiple_of(masked(self.wires.dp, 1 + 2 * slot) * self.group, 16)
        return self._send(self.part, row, self.core_in, slot * self.group, self.group, slot, 1)

    def _far(self, number):
        g, h = self.group, self.half
        src_row, dst, dst_row, to = (
            (3 * g, self.first_in, h, 4),
            (3 * g + h, self.first_in, 3 * h, 2),
            (2 * g, self.first_in, 0, 4),
            (1 * g + h, self.first_in, 2 * h, 2),
            (1 * g, self.second_in, 0, 2),
            (2 * g + h, self.second_in, h, 4),
        )[number]
        return self._send(self.core_in, src_row, dst, dst_row, h, 4 + number, to)

    def _sum_core(self, slot):
        self._core(slot).wait()
        row = slot * self.group
        add_rows(self.core_in, row, self.own, self.own_row(slot), self.core_in, row, self.group)

    def _sum_far(self, number, row, in_row):
        self._far(number).wait()
        add_rows(self.core_in, row, self.core_in, row, self.first_in, in_row, self.half)

    def start_core(self, slot):
        self._core(slot).start()

    def step(self, number):
        g, h = self.group, self.half
        if number == 0:
            for slot in (3, 2, 1, 0):
                self.start_core(slot)
        elif number == 1:
            self._sum_core(3)
            self._far(0).start()
            self._far(1).start()
        elif number == 2:
            self._sum_core(2)
            self._far(2).start()
            self._sum_core(1)
            self._far(3).start()
            self._sum_core(0)
        elif number == 3:
            self._sum_far(0, 1 * g, h)
            self._far(4).start()
            self._sum_far(1, 2 * g + h, 3 * h)
            self._far(5).start()
        elif number == 4:
            self._sum_far(2, 0, 0)
            self._sum_far(3, h, 2 * h)
        elif self.out is None:
            self._far(4).wait()
            self._far(5).wait()
        else:
            self._far(4).wait()
            add_rows(self.out, 0, self.core_in, 0, self.second_in, 0, h)
            self._far(5).wait()
            add_rows(self.out, h, self.core_in, h, self.second_in, h, h)

    @staticmethod
    def scratch(group, columns):
        return [
            pltpu.VMEM((4 * group, columns), jnp.bfloat16),
            pltpu.VMEM((2 * group, columns), jnp.bfloat16),
            pltpu.VMEM((group, columns), jnp.bfloat16),
        ]


class LineReduce:
    COPIES = 2 * (LINE - 1) * LINE
    EVENTS = ((0, 0), (0, 1), (1, 0), (0, 2), (1, 1), (2, 0))

    def __init__(self, wires, part, rows, landing, ways=(1, -1)):
        self.wires, self.part, self.rows, self.landing, self.ways = wires, part, rows, landing, ways
        self.first = wires.take(self.COPIES)

    def _place(self, way, hop, nearer):
        return (LINE - 1 - nearer, hop) if way == 1 else (nearer, LINE - 1 - hop)

    def _copy(self, way, hop, nearer, z):
        side = self.ways.index(way)
        block, _ = self._place(way, hop, nearer)
        return self.wires.copy(
            self.part.at[pl.ds(block * self.rows, self.rows)],
            self.landing.at[pl.ds((side * LINE + block) * self.rows, self.rows)],
            self.first + (side * (LINE - 1) + hop) * LINE + nearer,
            z=z,
        )

    def _send(self, way, hop, nearer):
        z = self.wires.z

        @pl.when(z == self._place(way, hop, nearer)[1])
        def _():
            self._copy(way, hop, nearer, z + way).start()

    def begin(self):
        for nearer in range(LINE - 1):
            for way in self.ways:
                self._send(way, 0, nearer)

    def event(self, number):
        hop, nearer = self.EVENTS[number]
        z, rows = self.wires.z, self.rows
        for way in self.ways:
            block, source = self._place(way, hop, nearer)

            @pl.when(z == source + way)
            def _():
                self._copy(way, hop, nearer, z).wait_recv()
                landed = (self.ways.index(way) * LINE + block) * rows
                add_rows(
                    self.part, block * rows, self.part, block * rows, self.landing, landed, rows
                )
                if nearer < LINE - 2 - hop:
                    self._copy(way, hop + 1, nearer, z + way).start()

    def finish(self, outs):
        z, rows = self.wires.z, self.rows

        @pl.loop(0, rows // 16)
        def _(step):
            row = pl.multiple_of(z * rows + step * 16, 16)
            begin = 0
            for out in outs:
                out[pl.ds(pl.multiple_of(step * 16, 16), 16), :] = self.part[
                    pl.ds(row, 16), begin : begin + out.shape[1]
                ].astype(out.dtype)
                begin += out.shape[1]

        for hop, nearer in self.EVENTS:
            for way in self.ways:

                @pl.when(z == self._place(way, hop, nearer)[1])
                def _():
                    self._copy(way, hop, nearer, z + way).wait_send()

    @staticmethod
    def scratch(rows, columns, ways=2):
        return pltpu.VMEM(((ways * LINE - 1) * rows, columns), jnp.bfloat16)


def sems(count):
    return [pltpu.SemaphoreType.DMA((count,)), pltpu.SemaphoreType.DMA((count,))]


def kernel_params(collective_id, mib):
    return pltpu.CompilerParams(
        collective_id=collective_id, has_side_effects=True, vmem_limit_bytes=mib * MIB
    )


def dot(left, right, left_dim, right_dim):
    return lax.dot_general(
        left, right, (((left_dim,), (right_dim,)), ((), ())), preferred_element_type=jnp.float32
    )


def rows_at(begin, size):
    return pl.ds(pl.multiple_of(begin, 16), size)


CHUNK = 64
AHEAD = 3
CARRIED = 2
RING = 4
FIRST_CHUNKS = (CHUNK,) * 22
LAST_CHUNKS = (CHUNK,) * 16


class LineSum:
    def __init__(self, wires, own, out, landing, sizes, came=False, goes_on=False):
        self.wires, self.own, self.out, self.landing = wires, own, out, landing
        self.sizes, self.came, self.goes_on = sizes, came, goes_on
        self.all = len(sizes)
        self.chunks = self.all - (CARRIED if goes_on else 0)
        self.begun = CARRIED if came else 0
        self.now = self.begun
        self.first = wires.take(3 * self.all)
        z = wires.z
        self.inner = (z == 1) | (z == 2)
        self.outer = (z == 0) | (z == 3)
        self.end = 3 * (z - 1)
        self.near = 1 + z // 3
        self.peer = 3 - z

    def _row(self, chunk):
        return sum(self.sizes[:chunk])

    def _cut(self, ref, chunk):
        return ref.at[pl.ds(self._row(chunk), self.sizes[chunk])]

    def _slot(self, chunk):
        return chunk % RING * CHUNK

    def _in(self, chunk):
        return self.wires.copy(
            self._cut(self.own, chunk), self._cut(self.out, chunk), self.first + chunk, z=self.near
        )

    def _across(self, chunk):
        landed = self.landing.at[pl.ds(self._slot(chunk), self.sizes[chunk])]
        return self.wires.copy(
            self._cut(self.own, chunk), landed, self.first + self.all + chunk, z=self.peer
        )

    def _back(self, chunk, ref=None):
        number = self.first + 2 * self.all + chunk
        return self.wires.copy(
            self._cut(self.out if ref is None else ref, chunk), self._cut(self.out, chunk), number, z=self.end
        )

    def begin(self):
        @pl.when(self.outer)
        def _():
            for chunk in range(self.begun, min(self.begun + AHEAD, self.all)):
                self._in(chunk).start()

        if self.came:

            @pl.when(self.inner)
            def _():
                self._across(1).start()
                self._back(0, self.own).start()
                self.out[pl.ds(0, self.sizes[0]), :] = self.own[pl.ds(0, self.sizes[0]), :]

    def tick(self, count=1):
        for _ in range(count):
            if self.now < self.all + (0 if self.goes_on else 1):
                self._tick(self.now)
            self.now += 1

    def _tick(self, chunk):
        if chunk < self.all:

            @pl.when(self.outer)
            def _():
                self._in(chunk).wait_send()
                if chunk + AHEAD < self.all:
                    self._in(chunk + AHEAD).start()

        @pl.when(self.inner)
        def _():
            if chunk < self.all:
                row = self._row(chunk)
                self._in(chunk).wait_recv()
                add_rows(self.own, row, self.own, row, self.out, row, self.sizes[chunk])
                if chunk <= self.chunks:
                    self._across(chunk).start()
            if chunk >= 1:
                last = chunk - 1
                row, landed, rows = self._row(last), self._slot(last), self.sizes[last]
                self._across(last).wait_recv()
                if last < self.chunks:
                    add_rows(self.out, row, self.own, row, self.landing, landed, rows)
                    self._back(last).start()
                else:
                    self._across(last).wait_send()
                    add_rows(self.own, row, self.own, row, self.landing, landed, rows)

    def finish(self):
        self.tick(max(0, self.all + (0 if self.goes_on else 1) - self.now))

        @pl.when(self.outer)
        def _():
            for chunk in range(self.chunks):
                self._back(chunk).wait_recv()

        @pl.when(self.inner)
        def _():
            for chunk in range(1 if self.came else 0, self.chunks):
                self._across(chunk).wait_send()
            for chunk in range(self.chunks):
                self._back(chunk).wait_send()


def norm_back(values, gain, grad):
    scale = lax.rsqrt(jnp.mean(values * values, axis=-1, keepdims=True) + epsilon)
    normal = values * scale
    inner = grad * gain
    to_values = scale * (inner - normal * jnp.mean(inner * normal, axis=-1, keepdims=True))
    return to_values, grad * normal


def turned(values, cosine, sine):
    return values * cosine + pltpu.roll(values, HD // 2, 1) * sine


def up_to_attention_back(
    w_query, w_key, w_value, w_out, tokens, cotangent, w_gate, w_up, w_down, gain_attn, gain_moe, routes, gate_values,
    lengths,
):
    rows, width = w_query.shape
    key_width = w_key.shape[1]
    kv_width = key_width + w_value.shape[1]
    tok_rows = tokens.shape[0]
    keys = LINE * tok_rows
    planes = 8
    group = LINE * rows
    hidden_width = w_gate.shape[1]
    total_rows = planes * tok_rows
    sum_rows = width + hidden_width
    sent_rows, done_rows = sum(FIRST_CHUNKS), sum(FIRST_CHUNKS[:-CARRIED])
    score_scale = HD ** (-0.5)
    per_group = HEADS // KVH
    q_width = HEADS * HD

    def kernel(
        wq_ref, wk_ref, wv_ref, wo_ref, tok_hbm, cot_hbm, wg_ref, wu_ref, wd_ref, attn_ref, moe_ref, routes_ref,
        values_ref, lengths_ref,
        out_q, out_kv, out_o, query_hbm, mixed_hbm, normed_hbm, middle_hbm, gain_rows_ref, sums_ref, prod_ref, total_ref,
        grad_mid_hbm, grad_pre_ref, gain_row_ref, w_out_ref,
        w_in, w_down, x_all, y_all, hidden, grad_hidden, grad_in, sums, sums_land, all_gate, gate_t, all_kv, lse_ref,
        core_in, first_in, second_in, middle_ref, kv_land, cos_ref, sin_ref, both_gains, here, there, freed, send, recv,
    ):
        wires = Wires(send, recv)
        dp, z = wires.dp, wires.z

        def rows_begin(block):
            return pl.multiple_of(block * tok_rows, 16)

        def cut_of(block):
            return pl.ds(rows_begin(block), tok_rows)

        def gate_rows(block):
            return pl.ds(pl.multiple_of(block * planes, planes), planes)

        full_q = w_in
        full_kv = hidden.at[pl.ds(0, width), pl.ds(0, kv_width + LANES)]
        full_o = sums.at[pl.ds(0, width)]
        all_cot = y_all
        query_ref, mixed_ref, tok_ref, normed_ref, cot_ref = [
            grad_in.at[pl.ds(i * tok_rows, tok_rows)] for i in range(5)
        ]
        value_t = key_t = grad_in.at[pl.ds(5 * tok_rows, kv_width // 2), pl.ds(0, keys)]
        bias = grad_hidden.at[pl.ds(keys, keys), pl.ds(0, tok_rows)]
        full_o_ref = w_in
        part_o = y_all.at[pl.ds(0, width)]
        attn_low, mixed_grad = tok_ref, normed_ref
        kv_part = hidden.at[pl.ds(keys, keys), pl.ds(0, kv_width)]
        kv_grad = grad_hidden.at[pl.ds(0, keys), pl.ds(0, kv_width)]
        kv_out = grad_hidden.at[pl.ds(keys, tok_rows), pl.ds(tok_rows, kv_width)]

        own = rows_at((dp * LINE + z) * rows, rows)
        moves = [
            (wk_ref, full_kv.at[own, pl.ds(0, key_width)]),
            (wv_ref, full_kv.at[own, pl.ds(key_width, kv_width - key_width)]),
            (cot_hbm, all_cot.at[cut_of(dp)]),
            (wq_ref, full_q.at[own]),
            (wo_ref, full_o.at[own]),
            (tok_hbm, tok_ref),
            (wd_ref, w_down),
            (wg_ref, w_in.at[:, pl.ds(0, hidden_width)]),
            (wu_ref, w_in.at[:, pl.ds(hidden_width, hidden_width)]),
            (out_o, full_o_ref),
            (query_hbm, query_ref),
            (mixed_hbm, mixed_ref),
            (cot_hbm, cot_ref),
        ]
        moves = [pltpu.make_async_copy(a, b, here.at[i]) for i, (a, b) in enumerate(moves)]
        locals_, load_down, load_in, later = moves[:6], moves[6], moves[7:9], moves[9:]
        for one in locals_:
            one.start()
        load_down.start()
        both_gains[...] = jnp.zeros_like(both_gains)
        both_gains[0:1, :rows] = attn_ref[...].astype(jnp.float32)
        both_gains[1:2, :rows] = moe_ref[...].astype(jnp.float32)
        columns = jnp.concatenate([both_gains[...]] * (LANES // 8), axis=0).T
        full_kv[own, kv_width:] = columns[:rows, :].astype(jnp.bfloat16)
        numbers = lax.broadcasted_iota(jnp.int32, (planes, tok_rows), 0)
        gates = jnp.zeros((planes, tok_rows), jnp.float32)
        for place in range(routes_ref.shape[0]):
            named = routes_ref[place : place + 1, :] == numbers
            gates = gates + jnp.where(named, values_ref[place : place + 1, :], 0.0)
        all_gate[gate_rows(dp), :] = gates
        greet(wires, range(1, planes), True)
        for one in locals_:
            one.wait()

        def block_rows(block):
            return rows_at((dp * LINE + block) * rows, rows)

        line_kv, line_q, line_o = [LineGather(wires, r, block_rows) for r in (full_kv, full_q, full_o)]
        plane_kv, plane_q, plane_o = [PlaneGather(wires, r, group) for r in (full_kv, full_q, full_o)]
        plane_cot = PlaneGather(wires, all_cot, tok_rows)
        line_keys = LineGather(wires, all_kv, lambda block: rows_at(block * tok_rows, tok_rows))
        spread = PlaneGather(wires, x_all, tok_rows)
        plane = PlaneReduce(
            wires, y_all, tok_rows, y_all, lambda slot: rows_begin(masked(dp, 2 * slot)), core_in, first_in, second_in,
            None,
        )
        summed = LineSum(wires, sums, total_ref, sums_land, FIRST_CHUNKS, goes_on=True)
        dense = PlaneReduce(
            wires, part_o, group, part_o, lambda slot: pl.multiple_of(masked(dp, 2 * slot) * group, 16),
            core_in, first_in, second_in, w_out_ref,
        )
        line = LineReduce(wires, kv_part, tok_rows, kv_land, ways=(-1,))
        first = wires.take(planes - 1)

        def gate_copy(mask, owner):
            part = all_gate.at[gate_rows(owner)]
            return wires.copy(part, part, first + mask - 1, dp=masked(dp, mask))

        def starts_of(places):
            begin = jnp.zeros_like(places)
            edge = jnp.zeros((1, 1), jnp.int32)
            for number in range(lengths_ref.shape[1] - 1):
                edge = edge + lengths_ref[0:1, number : number + 1]
                begin = jnp.where(places >= edge, edge, begin)
            return begin

        def set_turns():
            places = lax.broadcasted_iota(jnp.int32, (tok_rows, HD), 0) + z * tok_rows
            lane = lax.broadcasted_iota(jnp.int32, (tok_rows, HD), 1)
            power = lax.rem(lane, HD // 2).astype(jnp.float32) * (-math.log(rope_base) / (HD // 2))
            angles = (places - starts_of(places)).astype(jnp.float32) * jnp.exp(power)
            cos_ref[...] = jnp.cos(angles)
            sine = jnp.sin(angles)
            sin_ref[...] = jnp.where(lane < HD // 2, -sine, sine)

        def set_bias():
            key_place = lax.broadcasted_iota(jnp.int32, (keys, tok_rows), 0)
            query_place = lax.broadcasted_iota(jnp.int32, (1, tok_rows), 1) + z * tok_rows
            allowed = (key_place >= starts_of(query_place)) & (key_place <= query_place)
            bias[...] = jnp.where(allowed, 0.0, masked_score)

        line_kv.start(0)
        plane_cot.start(0)
        for mask in range(1, planes):
            gate_copy(mask, dp).start()
        line_kv.wait(0)
        line_kv.start(1)
        set_turns()
        line_kv.wait(1)
        line_kv.start(2)
        line_q.start(0)
        line_kv.wait(2)
        plane_kv.start(0)
        plane_cot.wait(0)
        line_q.wait(0)
        line_q.start(1)
        plane_kv.wait(0)
        plane_kv.start(1)
        plane_cot.start(1, far=False)
        set_bias()
        line_q.wait(1)
        line_q.start(2)
        line_o.start(0)
        plane_kv.wait(1)
        plane_kv.start(2)
        plane_kv.wait(2)
        plane_kv.start(3)
        plane_kv.finish()
        line_q.wait(2)
        plane_q.start(0)

        gain_rows_ref[...] = full_kv[:, kv_width:].astype(jnp.float32).T[:8, :]
        tile = 32

        @pl.loop(0, tok_rows // tile)
        def _(step):
            cut = pl.ds(pl.multiple_of(step * tile, tile), tile)
            normed_ref[cut, :] = rms_norm(
                tok_ref[cut, :].astype(jnp.float32), gain_rows_ref[0:1, :]
            ).astype(jnp.bfloat16)

        own_keys = rows_at(z * tok_rows, tok_rows)
        pre = dot(normed_ref[...], full_kv[:, :kv_width], 1, 0)
        for pair in range(KVH):
            cut = slice(pair * HD, (pair + 1) * HD)
            all_kv[own_keys, cut] = turned(pre[:, cut], cos_ref[...], sin_ref[...]).astype(jnp.bfloat16)
        all_kv[own_keys, key_width:] = pre[:, key_width:].astype(jnp.bfloat16)
        line_keys.start(0)
        line_o.wait(0)
        line_o.start(1)
        plane_q.wait(0)
        plane_q.start(1)
        plane_cot.wait(1)
        plane_cot.start(2)
        line_keys.wait(0)
        line_keys.start(1)
        line_o.wait(1)
        line_o.start(2)
        line_keys.wait(1)
        line_keys.start(2)
        line_o.wait(2)
        plane_o.start(0)
        plane_q.wait(1)
        plane_q.start(2)
        plane_q.wait(2)
        plane_q.start(3)
        plane_q.finish()
        line_kv.finish()
        line_q.finish()
        saves = [
            (full_q, out_q),
            (full_kv, out_kv),
            (normed_ref, normed_hbm),
            (query_ref, query_hbm),
            (full_o, out_o),
            (mixed_ref, mixed_hbm),
            (middle_ref, middle_hbm),
        ]
        saves = [pltpu.make_async_copy(a, b, there.at[11 + i]) for i, (a, b) in enumerate(saves)]
        save_q, saves = saves[0], saves[1:]
        save_q.start()
        saves[0].start()
        saves[1].start()

        @pl.loop(0, HEADS // 2)
        def _(step):
            wide = pl.ds(pl.multiple_of(step * 2 * HD, 2 * HD), 2 * HD)
            pre_q = dot(normed_ref[...], full_q[:, wide], 1, 0)
            for one in range(2):
                query_ref[:, pl.ds(pl.multiple_of((2 * step + one) * HD, HD), HD)] = turned(
                    pre_q[:, one * HD : (one + 1) * HD], cos_ref[...], sin_ref[...]
                ).astype(jnp.bfloat16)

        saves[2].start()
        plane_o.wait(0)
        plane_o.start(1)
        save_q.wait()
        for one in load_in:
            one.start()
        line_keys.wait(2)
        value_t[...] = all_kv[:, key_width:].astype(jnp.float32).T.astype(jnp.bfloat16)
        lse_ref[...] = jnp.zeros_like(lse_ref)

        def attend(head):
            own_cut = pl.ds(pl.multiple_of(head * HD, HD), HD)
            key_cut = pl.ds(pl.multiple_of((head // per_group) * HD, HD), HD)
            scores = dot(all_kv[:, key_cut], query_ref[:, own_cut], 1, 1) * score_scale + bias[...]
            top = jnp.max(scores, axis=0, keepdims=True)
            expo = jnp.exp(scores - top)
            total = jnp.sum(expo, axis=0, keepdims=True)
            lse_ref[pl.ds(head, 1), :] = top + jnp.log(total)
            probs = (expo * (1.0 / total)).astype(jnp.bfloat16)
            mixed_ref[:, own_cut] = dot(value_t[key_cut, :], probs, 1, 0).T.astype(jnp.bfloat16)

        pl.loop(0, HEADS // 2)(attend)
        plane_cot.start_far()
        pl.loop(HEADS // 2, HEADS)(attend)
        plane_o.wait(1)
        plane_o.start(2)
        plane_o.wait(2)
        plane_o.start(3)
        plane_o.finish()
        line_o.finish()
        saves[3].start()
        saves[4].start()

        half_rows = tok_rows // 2
        for half in range(2):
            half_cut = pl.ds(half * half_rows, half_rows)

            @pl.loop(0, width // 512)
            def _(step):
                cut = pl.ds(pl.multiple_of(step * 512, 512), 512)
                middle_ref[half_cut, cut] = tok_ref[half_cut, cut].astype(jnp.float32) + dot(
                    mixed_ref[half_cut, :], full_o[:, cut], 1, 0
                )

            @pl.loop(0, half_rows // tile)
            def _(step):
                begin = half * half_rows + step * tile
                cut = pl.ds(pl.multiple_of(begin, tile), tile)
                x_all[pl.ds(pl.multiple_of(dp * tok_rows + begin, tile), tile), :] = rms_norm(
                    middle_ref[cut, :], gain_rows_ref[1:2, :]
                ).astype(jnp.bfloat16)

            spread.start_one(half)
        spread.start_one(2)
        saves[5].start()
        plane_cot.wait(2)
        plane_cot.start(3)
        plane_cot.finish()
        for mask in range(1, planes):
            gate_copy(mask, masked(dp, mask)).wait_recv()
        gate_t[...] = all_gate[...].T

        def gate_of(block):
            lane = lax.broadcasted_iota(jnp.int32, gate_t.shape, 1)
            return jnp.sum(jnp.where(lane == block * 8 + dp, gate_t[...], 0.0), axis=1, keepdims=True)

        def back_hidden(block):
            cut = cut_of(block)
            y_all[cut, :] = (y_all[cut, :].astype(jnp.float32) * gate_of(block)).astype(jnp.bfloat16)
            grad_hidden[cut, :] = dot(y_all[cut, :], w_down[...], 1, 1)

        def through(mask):
            cut = cut_of(masked(dp, mask))
            acts = dot(x_all[cut, :], w_in[...], 1, 0)
            gate_act, up_act = acts[:, :hidden_width], acts[:, hidden_width:]
            share = jax.nn.sigmoid(gate_act)
            silu = gate_act * share
            hidden[cut, :] = (silu * up_act).astype(jnp.bfloat16)
            grad = grad_hidden[cut, :]
            grad_in[cut, :hidden_width] = (
                grad * up_act * share * (1.0 + gate_act * (1.0 - share))
            ).astype(jnp.bfloat16)
            grad_in[cut, hidden_width:] = (grad * silu).astype(jnp.bfloat16)

        load_down.wait()
        pl.loop(0, 4)(back_hidden)
        spread.wait(0)
        spread.start(1)
        pl.loop(4, 8)(back_hidden)
        for one in load_in + saves:
            one.wait()
        through(0)
        spread.wait_core(0)
        through(1)
        spread.wait(1)
        spread.start(2)
        through(2)
        through(4)
        spread.wait_core(1)
        spread.wait_core(2)
        through(3)
        through(5)
        spread.wait(2)
        spread.start(3)
        through(6)
        spread.wait_core(3)
        through(7)

        def weights_down(step):
            cut = rows_at(step * 256, 256)
            sums[cut, :] = dot(hidden[:, cut], y_all[...], 0, 0).astype(jnp.bfloat16)

        def weights_in(step):
            cut = rows_at(step * 256, 256)
            out = rows_at(hidden_width + step * 256, 256)
            sums[out, :] = dot(x_all[:, cut], grad_in[...], 0, 0).astype(jnp.bfloat16)

        def save_sums(begin, end, number):
            rows = pl.ds(begin, end - begin)
            return pltpu.make_async_copy(sums.at[rows], sums_ref.at[rows], there.at[number])

        pl.loop(0, 1)(weights_down)
        summed.begin()
        pl.loop(1, 3)(weights_down)
        spread.finish()

        def input_grads(side):
            for slot in (3, 2, 1, 0):
                cut = cut_of(masked(dp, 2 * slot + side))
                y_all[cut, :] = dot(grad_in[cut, :], w_in[...], 1, 1).astype(jnp.bfloat16)
                if side:
                    plane.start_core(slot)

        input_grads(1)
        summed.tick()
        input_grads(0)
        summed.tick()
        later[0].start()
        plane.step(1)
        plane.step(2)
        summed.tick()
        pl.loop(0, 2)(weights_in)
        summed.tick()
        pl.loop(2, 4)(weights_in)
        summed.tick()
        plane.step(3)
        pl.loop(4, 6)(weights_in)
        summed.tick()
        for one in later[1:]:
            one.start()
        save = save_sums(sent_rows, sum_rows, 0)
        save.start()

        def save_made(block):
            return pltpu.make_async_copy(
                x_all.at[cut_of(block)], prod_ref.at[cut_of(block)], there.at[3 + block]
            )

        def make(block):
            made = dot(hidden[cut_of(block), :], w_down[...], 1, 0).astype(jnp.bfloat16).astype(jnp.float32)
            x_all[cut_of(block), :] = (made * gate_of(block)).astype(jnp.bfloat16)
            save_made(block).start()

        pl.loop(0, 4)(make)
        summed.tick()
        pl.loop(4, 8)(make)
        plane.step(4)
        summed.tick()
        set_bias()
        kv_grad[...] = jnp.zeros_like(kv_grad)
        gain_row_ref[...] = jnp.zeros_like(gain_row_ref)
        for one in later:
            one.wait()
        key_t[...] = all_kv[:, : kv_width // 2].astype(jnp.float32).T.astype(jnp.bfloat16)
        summed.tick()
        plane.step(5)

        tile = 32

        @pl.loop(0, tok_rows // tile)
        def _(step):
            cut = pl.ds(pl.multiple_of(step * tile, tile), tile)
            routed_grad = core_in[cut, :].astype(jnp.float32) + second_in[cut, :].astype(jnp.float32)
            to_middle, terms = norm_back(middle_ref[cut, :], gain_rows_ref[1:2, :], routed_grad)
            to_middle = cot_ref[cut, :].astype(jnp.float32) + to_middle
            middle_ref[cut, :] = to_middle
            attn_low[cut, :] = to_middle.astype(jnp.bfloat16)
            gain_row_ref[0:1, :] += jnp.sum(terms, axis=0, keepdims=True)

        for mask in (1, 2, 4):
            pl.semaphore_signal(freed, inc=1, device_id=(masked(dp, mask), z), device_id_type=MESH)
        save_mid = pltpu.make_async_copy(middle_ref, grad_mid_hbm, there.at[1])
        save_mid.start()
        summed.tick()
        wide = 512

        @pl.loop(0, width // wide)
        def _(step):
            cut = pl.ds(pl.multiple_of(step * wide, wide), wide)
            mixed_grad[:, cut] = dot(attn_low[...], full_o_ref[cut, :], 1, 1).astype(jnp.bfloat16)

        @pl.loop(0, width // 256)
        def _(step):
            cut = pl.ds(pl.multiple_of(step * 256, 256), 256)
            part_o[cut, :] = dot(mixed_ref[:, cut], attn_low[...], 0, 0).astype(jnp.bfloat16)

        pl.semaphore_wait(freed, 3)
        dense.step(0)
        summed.tick()

        def heads(first, last):
            @pl.loop(first, last)
            def _(head):
                own_cut = pl.ds(pl.multiple_of(head * HD, HD), HD)
                pair = head // per_group
                key_cut = pl.ds(pl.multiple_of(pair * HD, HD), HD)
                value_cut = pl.ds(pl.multiple_of((KVH + pair) * HD, HD), HD)
                q, do = query_ref[:, own_cut], mixed_grad[:, own_cut]
                k, v = all_kv[:, key_cut], all_kv[:, value_cut]
                scores = dot(k, q, 1, 1) * score_scale + bias[...]
                probs = jnp.exp(scores - lse_ref[pl.ds(head, 1), :])
                grad_probs = dot(v, do, 1, 1)
                inner = jnp.sum(probs * grad_probs, axis=0, keepdims=True)
                grad_raw = (probs * (grad_probs - inner) * score_scale).astype(jnp.bfloat16)
                kv_grad[:, value_cut] += dot(probs.astype(jnp.bfloat16), do, 1, 0)
                kv_grad[:, key_cut] += dot(grad_raw, q, 1, 0)
                to_query = dot(key_t[key_cut, :], grad_raw, 1, 0).T
                grad_pre_ref[:, own_cut] = turned(to_query, cos_ref[...], -sin_ref[...]).astype(
                    jnp.bfloat16
                )

        heads(0, 3)
        summed.tick()
        dense.step(1)
        dense.step(2)
        heads(3, 6)
        summed.tick()
        heads(6, 9)
        summed.tick()
        heads(9, 12)
        kv_part[...] = kv_grad[...].astype(jnp.bfloat16)
        line.begin()
        summed.tick()
        dense.step(3)
        summed.tick()
        line.event(0)
        summed.tick()
        dense.step(4)
        line.event(1)
        line.event(2)
        summed.tick()
        line.event(3)
        line.event(4)
        dense.step(5)
        line.event(5)
        line.finish((kv_out,))
        for pair in range(KVH):
            cut = slice(pair * HD, (pair + 1) * HD)
            grad_pre_ref[:, q_width + pair * HD : q_width + (pair + 1) * HD] = turned(
                kv_out[:, cut], cos_ref[...], -sin_ref[...]
            ).astype(jnp.bfloat16)
        grad_pre_ref[:, q_width + kv_width // 2 :] = kv_out[:, kv_width // 2 :].astype(jnp.bfloat16)
        for block in range(8):
            save_made(block).wait()
        save.wait()
        save_mid.wait()
        line_keys.finish()
        for mask in range(1, planes):
            gate_copy(mask, dp).wait_send()
        summed.tick(max(0, summed.all - summed.now))
        save_last = save_sums(done_rows, sent_rows, 2)
        save_last.start()
        summed.finish()
        save_last.wait()

    f32, low = jnp.float32, jnp.bfloat16
    copies = 4 * LineGather.COPIES + 5 * PlaneGather.COPIES + planes - 1
    copies += 2 * PlaneReduce.COPIES + 3 * len(FIRST_CHUNKS) + LineReduce.COPIES
    return pl.pallas_call(
        kernel,
        out_shape=(
            jax.ShapeDtypeStruct((width, width), low),
            jax.ShapeDtypeStruct((width, kv_width + LANES), low),
            jax.ShapeDtypeStruct((width, width), low),
            jax.ShapeDtypeStruct((tok_rows, width), low),
            jax.ShapeDtypeStruct((tok_rows, width), low),
            jax.ShapeDtypeStruct((tok_rows, width), low),
            jax.ShapeDtypeStruct((tok_rows, width), f32),
            jax.ShapeDtypeStruct((8, width), f32),
            jax.ShapeDtypeStruct((sum_rows, width), low),
            jax.ShapeDtypeStruct((total_rows, width), low),
            jax.ShapeDtypeStruct((sent_rows, width), low),
            jax.ShapeDtypeStruct((tok_rows, width), f32),
            jax.ShapeDtypeStruct((tok_rows, width + kv_width), low),
            jax.ShapeDtypeStruct((8, width), f32),
            jax.ShapeDtypeStruct((group, width), low),
        ),
        in_specs=[ANY] * 9 + [VMEM] * 5,
        out_specs=(ANY,) * 7 + (VMEM, ANY, ANY, VMEM, ANY, VMEM, VMEM, VMEM),
        scratch_shapes=[
            pltpu.VMEM((width, 2 * hidden_width), low),
            pltpu.VMEM((hidden_width, width), low),
            pltpu.VMEM((total_rows, width), low),
            pltpu.VMEM((total_rows, width), low),
            pltpu.VMEM((total_rows, hidden_width), low),
            pltpu.VMEM((total_rows, hidden_width), f32),
            pltpu.VMEM((total_rows, 2 * hidden_width), low),
            pltpu.VMEM((sum_rows, width), low),
            pltpu.VMEM((RING * CHUNK, width), low),
            pltpu.VMEM((planes * planes, tok_rows), f32),
            pltpu.VMEM((tok_rows, planes * planes), f32),
            pltpu.VMEM((keys, kv_width), low),
            pltpu.VMEM((16, tok_rows), f32),
        ]
        + PlaneReduce.scratch(tok_rows, width)
        + [
            pltpu.VMEM((tok_rows, width), f32),
            LineReduce.scratch(tok_rows, kv_width, 1),
            pltpu.VMEM((tok_rows, HD), f32),
            pltpu.VMEM((tok_rows, HD), f32),
            pltpu.VMEM((8, LANES), f32),
            pltpu.SemaphoreType.DMA((15,)),
            pltpu.SemaphoreType.DMA((18,)),
            pltpu.SemaphoreType.REGULAR,
        ]
        + sems(copies),
        compiler_params=kernel_params(1, 63),
        name="up_to_attention_back",
    )(
        w_query, w_key, w_value, w_out, tokens, cotangent, w_gate, w_up, w_down, gain_attn, gain_moe, routes, gate_values,
        lengths,
    )


def back_dense(sums_in, produced, full_q, full_kv, normed, grad_pre, tokens, gains, grad_mid, gain_row, w_out_part, middle):
    tok_rows, width = middle.shape
    q_width = full_q.shape[1]
    in_width = q_width + full_kv.shape[1]
    pre_width = in_width - LANES
    w_rows = width
    group, rows = w_rows // 8, w_rows // (8 * LINE)
    skipped, sum_rows = sum(FIRST_CHUNKS[:-CARRIED]), sum(LAST_CHUNKS)

    def kernel(
        sums_ref, prod_ref, full_q_hbm, full_kv_hbm, normed_hbm, pre_hbm, tok_hbm, gain_ref, mid_grad_hbm,
        gain_row_ref, o_part_hbm, middle_hbm,
        total_ref, layer_ref, tok_grad_ref, wq_ref, wk_ref, wv_ref, gains_ref, out_ref,
        sums_own, sums_land, full_q_ref, full_kv_ref, normed_ref, pre_ref, tok_ref, mid_grad_ref, middle_ref, own, core_in, first_in, second_in, moe, part, d_core, d_first, d_second, in_sums,
        in_land, o_sums, o_land, normed_grad, gain_rows, here, send, recv,
    ):
        wires = Wires(send, recv)
        dp, z = wires.dp, wires.z
        early = (CARRIED + AHEAD) * CHUNK
        loads = [
            pltpu.make_async_copy(sums_ref.at[pl.ds(skipped, early)], sums_own.at[pl.ds(0, early)], here.at[0]),
            pltpu.make_async_copy(
                sums_ref.at[pl.ds(skipped + early, sum_rows - early)],
                sums_own.at[pl.ds(early, sum_rows - early)],
                here.at[1],
            ),
            pltpu.make_async_copy(o_part_hbm, o_sums, here.at[2]),
            pltpu.make_async_copy(pre_hbm, pre_ref, here.at[3]),
            pltpu.make_async_copy(full_q_hbm, full_q_ref, here.at[4]),
            pltpu.make_async_copy(full_kv_hbm, full_kv_ref, here.at[5]),
            pltpu.make_async_copy(tok_hbm, tok_ref, here.at[6]),
            pltpu.make_async_copy(mid_grad_hbm, mid_grad_ref, here.at[7]),
            pltpu.make_async_copy(normed_hbm, normed_ref, here.at[8]),
            pltpu.make_async_copy(middle_hbm, middle_ref, here.at[9]),
        ]
        first_loads = len(loads)
        for slot in range(4):
            row = pl.multiple_of(masked(dp, 2 * slot) * tok_rows, 16)
            loads.append(
                pltpu.make_async_copy(
                    prod_ref.at[pl.ds(row, tok_rows)],
                    own.at[pl.ds(slot * tok_rows, tok_rows)],
                    here.at[first_loads + slot],
                )
            )
        for one in loads:
            one.start()
        greet(wires, (1, 2, 4), True)
        summed = LineSum(wires, sums_own, total_ref, sums_land, LAST_CHUNKS, came=True)
        dense = PlaneReduce(
            wires, part, group, part, lambda slot: pl.multiple_of(masked(dp, 2 * slot) * group, 16),
            d_core, d_first, d_second, in_sums,
        )
        plane = PlaneReduce(
            wires, prod_ref, tok_rows, own, lambda slot: slot * tok_rows, core_in, first_in, second_in, moe
        )
        o_line = LineReduce(wires, o_sums, rows, o_land)
        in_line = LineReduce(wires, in_sums, rows, in_land)
        loads[0].wait()
        summed.begin()
        loads[1].wait()
        loads[2].wait()
        o_line.begin()
        for one in loads[3:first_loads]:
            one.wait()
        wide = 512

        @pl.loop(0, width // wide)
        def _(step):
            cut = pl.ds(pl.multiple_of(step * wide, wide), wide)
            normed_grad[:, cut] = dot(pre_ref[:, :q_width], full_q_ref[cut, :], 1, 1) + dot(
                pre_ref[:, q_width:], full_kv_ref[cut, : pre_width - q_width], 1, 1
            )

        summed.tick()
        gain_rows[...] = jnp.zeros_like(gain_rows)
        gain_rows[1:2, :] = gain_row_ref[0:1, :]
        tile = 32

        @pl.loop(0, tok_rows // tile)
        def _(step):
            cut = pl.ds(pl.multiple_of(step * tile, tile), tile)
            to_tokens, terms = norm_back(
                tok_ref[cut, :].astype(jnp.float32), gain_ref[0:1, :], normed_grad[cut, :]
            )
            tok_grad_ref[cut, :] = mid_grad_ref[cut, :] + to_tokens
            gain_rows[0:1, :] += jnp.sum(terms, axis=0, keepdims=True)

        summed.tick()
        o_line.event(0)
        part[:, pre_width:] = gain_rows[...].T.astype(jnp.bfloat16)

        @pl.loop(0, w_rows // 256)
        def _(step):
            cut = pl.ds(pl.multiple_of(step * 256, 256), 256)
            part[cut, :pre_width] = dot(normed_ref[:, cut], pre_ref[...], 0, 0).astype(jnp.bfloat16)

        dense.step(0)
        o_line.event(1)
        o_line.event(2)
        summed.tick(2)
        dense.step(1)
        o_line.event(3)
        summed.tick()
        dense.step(2)
        o_line.event(4)
        summed.tick()
        o_line.event(5)
        for one in loads[first_loads:]:
            one.wait()
        plane.step(0)
        summed.tick(2)
        dense.step(3)
        plane.step(1)
        plane.step(2)
        summed.tick(2)
        dense.step(4)
        dense.step(5)
        in_line.begin()
        summed.tick()
        in_line.event(0)
        summed.tick()
        plane.step(3)
        in_line.event(1)
        in_line.event(2)
        summed.tick(2)
        in_line.event(3)
        o_line.finish((out_ref,))
        in_line.event(4)
        plane.step(4)
        summed.tick(2)
        in_line.event(5)
        in_line.finish((wq_ref, wk_ref, wv_ref, gains_ref))
        plane.step(5)

        @pl.loop(0, tok_rows // tile)
        def _(step):
            cut = pl.ds(pl.multiple_of(step * tile, tile), tile)
            layer_ref[cut, :] = (middle_ref[cut, :] + moe[cut, :]).astype(jnp.bfloat16)

        summed.finish()

    f32, low = jnp.float32, jnp.bfloat16
    return pl.pallas_call(
        kernel,
        out_shape=(
            jax.ShapeDtypeStruct((sum_rows, width), low),
            jax.ShapeDtypeStruct((tok_rows, width), low),
            jax.ShapeDtypeStruct((tok_rows, width), f32),
            jax.ShapeDtypeStruct((rows, q_width), f32),
            jax.ShapeDtypeStruct((rows, (pre_width - q_width) // 2), f32),
            jax.ShapeDtypeStruct((rows, (pre_width - q_width) // 2), f32),
            jax.ShapeDtypeStruct((rows, LANES), f32),
            jax.ShapeDtypeStruct((rows, width), f32),
        ),
        in_specs=[ANY] * 7 + [VMEM, ANY, VMEM, ANY, ANY],
        out_specs=(VMEM,) * 8,
        scratch_shapes=[
            pltpu.VMEM((sum_rows, width), low),
            pltpu.VMEM((RING * CHUNK, width), low),
            pltpu.VMEM(full_q.shape, low),
            pltpu.VMEM(full_kv.shape, low),
            pltpu.VMEM((tok_rows, width), low),
            pltpu.VMEM((tok_rows, pre_width), low),
            pltpu.VMEM((tok_rows, width), low),
            pltpu.VMEM((tok_rows, width), f32),
            pltpu.VMEM((tok_rows, width), f32),
            pltpu.VMEM((4 * tok_rows, width), low),
        ]
        + PlaneReduce.scratch(tok_rows, width)
        + [pltpu.VMEM((tok_rows, width), f32), pltpu.VMEM((w_rows, in_width), low)]
        + PlaneReduce.scratch(group, in_width)
        + [
            pltpu.VMEM((group, in_width), low),
            LineReduce.scratch(rows, in_width),
            pltpu.VMEM((group, width), low),
            LineReduce.scratch(rows, width),
            pltpu.VMEM((tok_rows, width), f32),
            pltpu.VMEM((LANES, width), f32),
            pltpu.SemaphoreType.DMA((14,)),
        ]
        + sems(3 * len(LAST_CHUNKS) + 2 * PlaneReduce.COPIES + 2 * LineReduce.COPIES),
        compiler_params=kernel_params(4, 63),
        name="back_dense",
    )(
        sums_in, produced, full_q, full_kv, normed, grad_pre, tokens, gains, grad_mid, gain_row, w_out_part, middle
    )


def hand_over(sums_head, sums_tail, gains, *others):
    done, width = sum(FIRST_CHUNKS[:-CARRIED]), sums_head.shape[1]
    hidden_width = width // 2
    rows, tile = 256, 32
    count, steps = len(others), (hidden_width + width) // rows

    def kernel(*refs):
        head_ref, tail_ref, gains_ref = refs[:3]
        ins, outs = refs[3 : 3 + count], refs[8 + count : 8 + 2 * count]
        down_ref, gate_ref, up_ref, attn_ref, moe_ref = refs[3 + count : 8 + count]
        low, wide, gate, up = refs[8 + 2 * count : 12 + 2 * count]
        held, load, save = refs[12 + 2 * count : 12 + 3 * count], refs[-2], refs[-1]
        loads, saves = [], []
        for step in range(steps):
            begin = step * rows
            source, start = (head_ref, begin) if begin < done else (tail_ref, begin - done)
            loads.append(
                pltpu.make_async_copy(source.at[pl.ds(start, rows)], low.at[pl.ds(begin, rows)], load.at[step])
            )
        for number in range(count):
            loads.append(pltpu.make_async_copy(ins[number], held[number], load.at[steps + number]))
        for one in loads:
            one.start()

        def go(source, target, number):
            saves.append(pltpu.make_async_copy(source, target, save.at[number]))
            saves[-1].start()

        for step in range(steps):
            begin = step * rows
            loads[step].wait()
            down = begin < hidden_width
            place = begin if down else begin - hidden_width

            @pl.loop(0, rows // tile)
            def _(part):
                values = low[pl.ds(pl.multiple_of(begin + part * tile, tile), tile), :].astype(jnp.float32)
                cut = pl.ds(pl.multiple_of(place + part * tile, tile), tile)
                if down:
                    wide[cut, :] = values
                else:
                    gate[cut, :] = values[:, :hidden_width]
                    up[cut, :] = values[:, hidden_width:]

            cut = pl.ds(place, rows)
            if down:
                go(wide.at[cut], down_ref.at[0, cut], step)
            else:
                go(gate.at[cut], gate_ref.at[0, cut], step)
                go(up.at[cut], up_ref.at[0, cut], steps + step)
        for number in range(count):
            loads[steps + number].wait()
            go(held[number], outs[number], 2 * steps + number)
        turned_gains = gains_ref[...].T
        attn_ref[...] = turned_gains[0, :]
        moe_ref[...] = turned_gains[1, :]
        for one in saves:
            one.wait()

    f32 = jnp.float32
    return pl.pallas_call(
        kernel,
        out_shape=(
            jax.ShapeDtypeStruct((1, hidden_width, width), f32),
            jax.ShapeDtypeStruct((1, width, hidden_width), f32),
            jax.ShapeDtypeStruct((1, width, hidden_width), f32),
            jax.ShapeDtypeStruct((gains.shape[0],), f32),
            jax.ShapeDtypeStruct((gains.shape[0],), f32),
        )
        + tuple(jax.ShapeDtypeStruct(one.shape, one.dtype) for one in others),
        in_specs=[ANY, ANY, VMEM] + [ANY] * count,
        out_specs=(ANY, ANY, ANY, VMEM, VMEM) + (ANY,) * count,
        scratch_shapes=[
            pltpu.VMEM((hidden_width + width, width), jnp.bfloat16),
            pltpu.VMEM((hidden_width, width), f32),
            pltpu.VMEM((width, hidden_width), f32),
            pltpu.VMEM((width, hidden_width), f32),
        ]
        + [pltpu.VMEM(one.shape, one.dtype) for one in others]
        + [pltpu.SemaphoreType.DMA((steps + count,)), pltpu.SemaphoreType.DMA((2 * steps + count,))],
        compiler_params=pltpu.CompilerParams(vmem_limit_bytes=63 * MIB),
        name="hand_over",
    )(sums_head, sums_tail, gains, *others)


def on_plane_device(
    tokens,
    norm_attn,
    w_query,
    w_key,
    w_value,
    w_out,
    norm_moe,
    w_gate,
    w_up,
    w_down,
    routes,
    gate_values,
    lengths,
    cotangent,
):
    (
        full_q, full_kv, _, _, _, normed_low, middle, gain_rows, partial_sums, produced, sums_head, grad_mid, grad_pre,
        gain_row, w_out_part,
    ) = up_to_attention_back(
        w_query, w_key, w_value, w_out, tokens, cotangent, w_gate[0], w_up[0], w_down[0], norm_attn[None], norm_moe[None],
        routes.T, gate_values.T, lengths,
    )
    sums_tail, layer_out, grad_tokens, sum_q, sum_k, sum_v, sum_gains, sum_o = back_dense(
        partial_sums,
        produced,
        full_q,
        full_kv,
        normed_low,
        grad_pre,
        tokens,
        gain_rows,
        grad_mid,
        gain_row,
        w_out_part,
        middle,
    )
    down, gate, up, gain_attn, gain_moe, layer_out, grad_tokens, sum_q, sum_k, sum_v, sum_o = hand_over(
        sums_head, sums_tail, sum_gains, layer_out, grad_tokens, sum_q, sum_k, sum_v, sum_o
    )
    return (
        layer_out, grad_tokens, gain_attn, sum_q, sum_k, sum_v, sum_o, gain_moe, gate, up, down,
    )


def solution(mesh):
    on_plane = mesh.shape["dp"] == 8 and mesh.shape["ctx"] == LINE
    return jax.shard_map(
        on_plane_device if on_plane else on_device,
        mesh=mesh,
        in_specs=(
            P(("dp", "ctx"), None),
            P(("dp", "ctx")),
            P(("dp", "ctx"), None),
            P(("dp", "ctx"), None),
            P(("dp", "ctx"), None),
            P(("dp", "ctx"), None),
            P(("dp", "ctx")),
            P("dp", None, None),
            P("dp", None, None),
            P("dp", None, None),
            P(("dp", "ctx"), None),
            P(("dp", "ctx"), None),
            P("dp", None),
            P(("dp", "ctx"), None),
        ),
        out_specs=(
            P(("dp", "ctx"), None),
            P(("dp", "ctx"), None),
            P(("dp", "ctx")),
            P(("dp", "ctx"), None),
            P(("dp", "ctx"), None),
            P(("dp", "ctx"), None),
            P(("dp", "ctx"), None),
            P(("dp", "ctx")),
            P("dp", None, None),
            P("dp", None, None),
            P("dp", None, None),
        ),
        check_vma=False,
    )
```
